32 devices in a mesh: flow: 8 (over z, y), trans: 4 (over x, core).
Axes of the slice: x: 2, y: 2, z: 4, core: 2. Of those that a mesh axis runs over, the one named last changes fastest.
Arguments:
- concentration: float32 [4, 128, 64, 256], P(None, 'flow', 'trans'), may hold values from 0 to 2
- stratum: int32 [128, 64, 256], P('flow', 'trans'), may hold values from 0 to 15
- porosity: float32 [16], replicated, may hold values from 0.1 to 0.4
- dispersion_table: float32 [16, 2], replicated, may hold values from 512 to 15360
- transverse_table: float32 [16], replicated, may hold values from 0.2 to 2
- exchange_table: float32 [16], replicated, may hold values from 0.01 to 0.2
- decay_table: float32 [16], replicated, may hold values from 0.01 to 0.2
Outputs:
- new_concentration: float32 [4, 128, 64, 256], P(None, 'flow', 'trans')
The draws below stay inside these ranges and needn't reach their ends.
All inputs are finite; a program needn't handle non-finite values.
Results may differ from the reference program's by a relative error of at most 0.001.
Values sent between devices are 32-bit elements; how exact they have to be, the bound alone decides.
No kernel may reach another device: no remote copies, remote signals or barrier semaphores. Data moves between devices by JAX's collectives and lax.ppermute only.
A program may use at most 128 MiB of HBM per device.

```python
import math
import jax
import jax.numpy as jnp
from jax import lax

NZ = 256
STRATA = 16
NX = 128
NY = 64


def draw_concentration(key, part):
    rough_key = jax.random.fold_in(key, 11)
    phase_key = jax.random.fold_in(key, 23)
    rough = jax.random.uniform(rough_key, (4, NX, NY, NZ), jnp.float32)
    phase = jax.random.uniform(phase_key, (4, 1, 1, 1), jnp.float32)
    along = (jnp.arange(NX, dtype=jnp.float32)[None, :, None, None] + 0.5) / NX
    smooth = 0.9 + 0.4 * jnp.sin(2.0 * math.pi * (along + phase))
    values = smooth + (rough - 0.5)
    return values.astype(jnp.float32)


def touch_ends(values, rng, low, top_value):
    index_at = [jax.random.randint(jax.random.fold_in(rng, axis), (), 0, length) for axis, length in enumerate(values.shape)]
    longest = values.shape.index(max(values.shape))
    neighbour = index_at[:longest] + [(index_at[longest] + 1) % values.shape[longest]] + index_at[longest + 1:]
    return values.at[tuple(index_at)].set(low).at[tuple(neighbour)].set(top_value)


def setup_inputs(seed: int = 0) -> dict:
    arg_keys = jax.random.split(jax.random.key(seed), 8)
    return {
        "concentration": draw_concentration(jax.random.fold_in(arg_keys[7], 71), 0),
        "stratum": touch_ends(jax.random.randint(arg_keys[1], (NX, NY, NZ), 0, STRATA), jax.random.fold_in(arg_keys[1], 1), 0, STRATA - 1).astype(jnp.int32),
        "porosity": jnp.clip(jax.random.uniform(arg_keys[2], (STRATA,), jnp.float32, 0.1, 0.4), 0.1, 0.4),
        "dispersion_table": jnp.clip(jnp.exp(jax.random.uniform(arg_keys[3], (STRATA, 2), jnp.float32, math.log(512.0), math.log(15360.0))), 512.0, 15360.0),
        "transverse_table": jnp.clip(jnp.exp(jax.random.uniform(arg_keys[4], (STRATA,), jnp.float32, math.log(0.2), math.log(2.0))), 0.2, 2.0),
        "exchange_table": jnp.clip(jnp.exp(jax.random.uniform(arg_keys[5], (STRATA,), jnp.float32, math.log(0.01), math.log(0.2))), 0.01, 0.2),
        "decay_table": jnp.clip(jnp.exp(jax.random.uniform(arg_keys[6], (STRATA,), jnp.float32, math.log(0.01), math.log(0.2))), 0.01, 0.2),
    }


def harmonic(first, second):
    return 2.0 * first * second / (first + second)

def assemble(diagonal, exchange, decay):
    nothing = jnp.zeros_like(exchange)
    block_rows = [[diagonal[0] + exchange + decay, nothing, -exchange, nothing], [-decay, diagonal[1] + exchange, nothing, -exchange], [-exchange, nothing, diagonal[2] + exchange + decay, nothing], [nothing, -exchange, -decay, diagonal[3] + exchange]]
    return jnp.stack([jnp.stack(entries) for entries in block_rows])

def cells_last(field):
    return jnp.moveaxis(field, 0, -1)

def line_solve(diagonal, exchange, decay, left_face, right_face, source):
    unit_block = jnp.eye(4, dtype=diagonal.dtype)
    line_count = diagonal.shape[1]

    def forward(state_pair, inputs_cell):
        upper_prev, vector_prev = state_pair
        diagonal_cell, exchange_cell, decay_cell, left_num, right_num, forcing = inputs_cell
        cell_block = jnp.moveaxis(assemble(jnp.transpose(diagonal_cell), exchange_cell, decay_cell), -1, 0)
        pivot_block = cell_block + left_num[:, :, None] * upper_prev
        columns = jnp.concatenate([-(right_num[:, None, :] * unit_block), (forcing + left_num * vector_prev)[:, :, None]], axis=2)
        solved = jnp.linalg.solve(pivot_block, columns)
        upper_part = solved[:, :, :4]
        vector_part = solved[:, :, 4]
        return ((upper_part, vector_part), (upper_part, vector_part))
    start_pair = (jnp.zeros((line_count, 4, 4), diagonal.dtype), jnp.zeros((line_count, 4), diagonal.dtype))
    ignored, stored = lax.scan(forward, start_pair, (diagonal, exchange, decay, left_face, right_face, source))

    def backward(following, inputs_cell):
        upper_part, vector_part = inputs_cell
        current = vector_part - jnp.einsum('bmn,bn->bm', upper_part, following)
        return (current, current)
    final_state, result = lax.scan(backward, jnp.zeros((line_count, 4), diagonal.dtype), stored, reverse=True)
    return result

def reference(concentration, stratum, porosity, dispersion_table, transverse_table, exchange_table, decay_table):
    transverse = transverse_table[stratum]
    padded_mobile = jnp.pad(concentration[:2], ((0, 0), (0, 0), (1, 1), (1, 1)))
    padded_trans = jnp.pad(transverse, ((0, 0), (1, 1), (1, 1)))

    def plane_solve(row_index):
        strata_row = lax.dynamic_index_in_dim(stratum, row_index, 1, keepdims=False)
        conc_row = lax.dynamic_index_in_dim(concentration, row_index, 2, keepdims=False)
        mobile_window = lax.dynamic_slice_in_dim(padded_mobile, row_index, 3, 2)
        trans_window = lax.dynamic_slice_in_dim(padded_trans, row_index, 3, 1)
        centre_num = trans_window[:, 1, 1:NZ + 1]
        centre_conc = mobile_window[:, :, 1, 1:NZ + 1]
        flux = jnp.zeros_like(centre_conc)
        for offset_y, offset_z in ((2, 1), (0, 1), (1, 2), (1, 0)):
            neighbour_num = trans_window[:, offset_y, offset_z:offset_z + NZ]
            neighbour_conc = mobile_window[:, :, offset_y, offset_z:offset_z + NZ]
            flux = flux + harmonic(centre_num, neighbour_num) * (neighbour_conc - centre_conc)
        porosity_cell = porosity[strata_row]
        dispersion = jnp.moveaxis(dispersion_table[strata_row], -1, 0)
        exchange = exchange_table[strata_row]
        decay = decay_table[strata_row]
        padded_flow = jnp.pad(dispersion, ((0, 0), (1, 1), (0, 0)))
        right_mobile = harmonic(dispersion, padded_flow[:, 2:])
        left_mobile = harmonic(dispersion, padded_flow[:, :-2])
        zero_faces = jnp.zeros_like(left_mobile)
        left_face = jnp.concatenate([left_mobile, zero_faces])
        right_face = jnp.concatenate([right_mobile, zero_faces])
        capacity = jnp.stack([porosity_cell, porosity_cell, 1.0 - porosity_cell, 1.0 - porosity_cell])
        source = capacity * conc_row + jnp.concatenate([flux, jnp.zeros_like(flux)])
        diagonal = capacity + jnp.concatenate([left_mobile + right_mobile, zero_faces])
        return line_solve(cells_last(diagonal), exchange, decay, cells_last(left_face), cells_last(right_face), cells_last(source))
    solved = lax.map(plane_solve, jnp.arange(NY, dtype=jnp.int32))
    return jnp.transpose(solved, (3, 1, 0, 2))
```

```python
import functools

import jax
import jax.numpy as jnp
from jax import lax
from jax.experimental import pallas as pl
from jax.experimental.pallas import tpu as pltpu
from jax.sharding import PartitionSpec as P

SUB, LANE = 8, 128
POR, DISP_A, DISP_B, TRANS, EXCH, DECAY = range(6)
ZA_LL, ZA_LR, ZA_RR, ZB_LL, ZB_LR, ZB_RR, C_LL, C_LR, C_RL, C_RR, FA_L, FA_R, FB_L, FB_R = range(14)
QUANTITIES = 14
CURRENTS = 4
VMEM_LIMIT = 40 * 1024 * 1024


def recip(x):
    return 1.0 / x


def lookup(row, index):
    tiles = []
    for y in range(0, index.shape[0], SUB):
        across = [
            jnp.take_along_axis(
                row, index[y : y + SUB, z : z + LANE], axis=1, mode="promise_in_bounds"
            )
            for z in range(0, index.shape[1], LANE)
        ]
        tiles.append(jnp.concatenate(across, axis=1))
    return jnp.concatenate(tiles, axis=0)


def derived(tab_ref):
    por, disp_a, disp_b, trans, exch, decay = [
        jnp.broadcast_to(tab_ref[k : k + 1, :], (SUB, LANE)) for k in range(6)
    ]
    immobile = 1.0 - por
    over_a = 1.0 / (immobile + exch + decay)
    over_b = 1.0 / (immobile + exch)
    beta = immobile * over_a
    gamma = exch * over_a
    share_b = exch * over_b
    return dict(
        por=por,
        shunt_a=por + decay + exch * (immobile + decay) * over_a,
        shunt_b=por + exch * immobile * over_b,
        half_a=0.5 / disp_a,
        half_b=0.5 / disp_b,
        half_t=0.5 / trans,
        beta=beta,
        gamma=gamma,
        alpha_a=exch * beta,
        alpha_b=share_b * immobile,
        kappa=decay + share_b * decay * gamma,
        delta=share_b * decay * beta,
        free_b=immobile * over_b,
        share_b=share_b,
        decay_b=decay * over_b,
    )


def chunk_of(peers, planes_y, planes_z):
    if peers <= planes_y:
        return planes_y // peers, planes_z
    return 1, planes_y * planes_z // peers


def chunk_place(which, block, planes_z):
    rows, width = block
    across = planes_z // width
    return (which // across) * rows, (which % across) * width


def shifted_difference(value, axis):
    return pltpu.roll(value, value.shape[axis] - 1, axis) - value


def local_kernel(
    block,
    tab_ref,
    stratum_ref,
    conc_ref,
    pay_ref,
    edge_ref,
    pass_a_ref,
    drop_a_ref,
    pass_b_ref,
    drop_b_ref,
    over_ref,
    source_a_ref,
    source_b_ref,
    head_a,
    head_b,
    kappa_ref,
    left_a,
    right_a,
    left_b,
    right_b,
    adj_l,
    adj_r,
):
    n, planes_y, planes_z = stratum_ref.shape
    numbers = derived(tab_ref)

    cond_a = cond_b = half_a = half_b = through_a = through_b = None
    for i in range(n):
        index = stratum_ref[i]
        shunt_a, shunt_b = lookup(numbers["shunt_a"], index), lookup(numbers["shunt_b"], index)
        new_a, new_b = lookup(numbers["half_a"], index), lookup(numbers["half_b"], index)
        kappa_ref[i] = lookup(numbers["kappa"], index)
        if i == 0:
            first_half_a, first_half_b = new_a, new_b
            cond_a, cond_b = shunt_a, shunt_b
            through_a = through_b = jnp.ones_like(shunt_a)
        else:
            face_a, face_b = half_a + new_a, half_b + new_b
            pass_a, pass_b = recip(1.0 + face_a * cond_a), recip(1.0 + face_b * cond_b)
            cond_a, cond_b = shunt_a + cond_a * pass_a, shunt_b + cond_b * pass_b
            pass_a_ref[i], pass_b_ref[i] = pass_a, pass_b
            drop_a_ref[i], drop_b_ref[i] = face_a * pass_a, face_b * pass_b
            through_a, through_b = through_a * pass_a, through_b * pass_b
        head_a[i], head_b[i] = through_a, through_b
        half_a, half_b = new_a, new_b
    over_a, over_b = recip(cond_a), recip(cond_b)
    over_ref[0], over_ref[1] = over_a, over_b

    r_a, r_b = over_a, over_b
    l_a, l_b = through_a * over_a, through_b * over_b
    couple = [None] * 4
    for i in reversed(range(n)):
        if i < n - 1:
            pass_a, pass_b = pass_a_ref[i + 1], pass_b_ref[i + 1]
            l_a = pass_a * l_a + drop_a_ref[i + 1] * head_a[i]
            l_b = pass_b * l_b + drop_b_ref[i + 1] * head_b[i]
            r_a, r_b = pass_a * r_a, pass_b * r_b
        left_a[i], right_a[i], left_b[i], right_b[i] = l_a, r_a, l_b, r_b
        kappa = kappa_ref[i]
        k_l, k_r = kappa * l_a, kappa * r_a
        terms = [l_b * k_l, l_b * k_r, r_b * k_l, r_b * k_r]
        couple = [t if c is None else c + t for c, t in zip(couple, terms)]

    g_l = g_r = None
    for i in range(n):
        kappa = kappa_ref[i]
        s_l, s_r = kappa * left_b[i], kappa * right_b[i]
        if i > 0:
            pass_a = pass_a_ref[i]
            s_l, s_r = s_l + pass_a * g_l, s_r + pass_a * g_r
        g_l, g_r = s_l, s_r
        adj_l[i], adj_r[i] = g_l, g_r

    lane = lax.broadcasted_iota(jnp.int32, (planes_y, planes_z), 1)
    line = lax.broadcasted_iota(jnp.int32, (planes_y, planes_z), 0)
    inside = (line < planes_y - 1, lane < planes_z - 1)
    w_l, w_r = adj_l[n - 1] * over_a, adj_r[n - 1] * over_a
    free = [None] * 4
    for i in reversed(range(n)):
        if i < n - 1:
            pass_a, drop_a = pass_a_ref[i + 1], drop_a_ref[i + 1]
            w_l, w_r = pass_a * w_l + drop_a * adj_l[i], pass_a * w_r + drop_a * adj_r[i]
        adj_l[i], adj_r[i] = w_l, w_r
        index = stratum_ref[i]
        half_t = lookup(numbers["half_t"], index)
        por = lookup(numbers["por"], index)
        c0, c1, c2, c3 = [conc_ref[k, i] for k in range(4)]
        source_a = por * c0 + lookup(numbers["alpha_a"], index) * c2
        source_b = (
            por * c1
            + lookup(numbers["alpha_b"], index) * c3
            + lookup(numbers["delta"], index) * c2
        )
        for axis in (0, 1):
            last = half_t.shape[axis] - 1
            face = jnp.where(
                inside[axis], recip(half_t + pltpu.roll(half_t, last, axis)), 0.0
            )
            flow_a = face * shifted_difference(c0, axis)
            flow_b = face * shifted_difference(c1, axis)
            source_a = source_a + (flow_a - pltpu.roll(flow_a, 1, axis))
            source_b = source_b + (flow_b - pltpu.roll(flow_b, 1, axis))
        source_a_ref[i], source_b_ref[i] = source_a, source_b
        terms = [
            left_a[i] * source_a,
            right_a[i] * source_a,
            left_b[i] * source_b + w_l * source_a,
            right_b[i] * source_b + w_r * source_a,
        ]
        free = [t if f is None else f + t for f, t in zip(free, terms)]

    quantities = [
        left_a[0] + first_half_a,
        right_a[0],
        over_a + half_a,
        left_b[0] + first_half_b,
        right_b[0],
        over_b + half_b,
        *couple,
        *free,
    ]
    rows, width = block
    for p in range(pay_ref.shape[0]):
        y, z = chunk_place(p, block, planes_z)
        for q, value in enumerate(quantities):
            pay_ref[p, q * rows : (q + 1) * rows, :] = value[y : y + rows, z : z + width]
    for k, ref in enumerate((left_a, right_a, left_b, right_b, adj_l, adj_r)):
        edge_ref[0, k] = ref[:, 0, :]
        edge_ref[1, k] = ref[:, planes_y - 1, :]


def border_kernel(
    block,
    tab_ref,
    own_lo_ref,
    own_hi_ref,
    next_lo_ref,
    next_hi_ref,
    edge_ref,
    pay_ref,
    out_ref,
    flow_ref,
):
    peers = pay_ref.shape[0]
    rows, width = block
    planes_z = own_lo_ref.shape[2]
    half_row = 0.5 / jnp.broadcast_to(tab_ref[TRANS : TRANS + 1, :], (SUB, LANE))
    out_ref[...] = pay_ref[...]
    for side, (own_ref, next_ref) in enumerate(
        ((own_lo_ref, next_lo_ref), (own_hi_ref, next_hi_ref))
    ):
        own_id = own_ref[2].astype(jnp.int32) - 1
        next_id = next_ref[2].astype(jnp.int32) - 1
        present = next_id >= 0
        half = lookup(half_row, own_id) + lookup(half_row, jnp.maximum(next_id, 0))
        face = jnp.where(present, recip(half), 0.0)
        flow_a = face * (next_ref[0] - own_ref[0])
        flow_b = face * (next_ref[1] - own_ref[1])
        flow_ref[side, 0], flow_ref[side, 1] = flow_a, flow_b
        l_a, r_a, l_b, r_b, w_l, w_r = [edge_ref[side, k] for k in range(6)]
        changes = {
            FA_L: l_a * flow_a,
            FA_R: r_a * flow_a,
            FB_L: l_b * flow_b + w_l * flow_a,
            FB_R: r_b * flow_b + w_r * flow_a,
        }
        across = planes_z // width
        for q, change in changes.items():
            total = jnp.sum(change, axis=0, keepdims=True)
            for part in range(across):
                p = part if side == 0 else peers - across + part
                row = q * rows + (0 if side == 0 else rows - 1)
                out_ref[p, row : row + 1, :] = (
                    pay_ref[p, row : row + 1, :] + total[:, part * width : (part + 1) * width]
                )


def chain_kernel(block, pay_ref, out_ref):
    peers = pay_ref.shape[0]
    rows, width = block

    def take(segment, q):
        return pay_ref[segment, q * rows : (q + 1) * rows, :]

    count = peers - 1
    pass_a, over_a, rhs_a = [None] * count, [None] * count, [None] * count
    pass_b, over_b = [None] * count, [None] * count
    for k in range(count):
        diag_a = take(k, ZA_RR) + take(k + 1, ZA_LL)
        diag_b = take(k, ZB_RR) + take(k + 1, ZB_LL)
        rhs = take(k, FA_R) - take(k + 1, FA_L)
        if k > 0:
            off_a, off_b = take(k, ZA_LR), take(k, ZB_LR)
            ratio_a = off_a * over_a[k - 1]
            pass_a[k - 1] = ratio_a
            diag_a = diag_a - off_a * ratio_a
            rhs = rhs + ratio_a * rhs_a[k - 1]
            ratio_b = off_b * over_b[k - 1]
            pass_b[k - 1] = ratio_b
            diag_b = diag_b - off_b * ratio_b
        over_a[k], over_b[k], rhs_a[k] = recip(diag_a), recip(diag_b), rhs
    current_a = [None] * count
    for k in reversed(range(count)):
        value = rhs_a[k] * over_a[k]
        if k < count - 1:
            value = value + pass_a[k] * current_a[k + 1]
        current_a[k] = value
    nothing = jnp.zeros((rows, width), jnp.float32)
    into = [nothing] + current_a + [nothing]
    rhs_b = [None] * count
    for k in range(count):
        rhs = (
            take(k, FB_R)
            - take(k + 1, FB_L)
            + take(k, C_RL) * into[k]
            - (take(k, C_RR) + take(k + 1, C_LL)) * into[k + 1]
            + take(k + 1, C_LR) * into[k + 2]
        )
        if k > 0:
            rhs = rhs + pass_b[k - 1] * rhs_b[k - 1]
        rhs_b[k] = rhs
    current_b = [None] * count
    for k in reversed(range(count)):
        value = rhs_b[k] * over_b[k]
        if k < count - 1:
            value = value + pass_b[k] * current_b[k + 1]
        current_b[k] = value
    into_b = [nothing] + current_b + [nothing]
    for k in range(peers):
        values = (into[k], -into[k + 1], into_b[k], -into_b[k + 1])
        for q, value in enumerate(values):
            out_ref[k, q * rows : (q + 1) * rows, :] = value


def final_kernel(
    block,
    tab_ref,
    stratum_ref,
    conc_ref,
    pass_a_ref,
    drop_a_ref,
    pass_b_ref,
    drop_b_ref,
    over_ref,
    source_a_ref,
    source_b_ref,
    flow_ref,
    current_ref,
    out_ref,
    gather_a,
    gather_b,
):
    n, planes_y, planes_z = stratum_ref.shape
    peers = current_ref.shape[0]
    rows, width = block
    numbers = derived(tab_ref)
    across = planes_z // width

    def plane(q):
        lines = []
        for p in range(0, peers, across):
            pieces = [current_ref[p + j, q * rows : (q + 1) * rows, :] for j in range(across)]
            lines.append(jnp.concatenate(pieces, axis=1) if across > 1 else pieces[0])
        return jnp.concatenate(lines, axis=0)

    line = lax.broadcasted_iota(jnp.int32, (planes_y, planes_z), 0)
    first_line, last_line = line == 0, line == planes_y - 1

    def with_border(source, component, i):
        low = jnp.broadcast_to(flow_ref[0, component, i : i + 1, :], source.shape)
        high = jnp.broadcast_to(flow_ref[1, component, i : i + 1, :], source.shape)
        return source + jnp.where(first_line, low, jnp.where(last_line, high, 0.0))

    value = plane(0)
    for i in range(n):
        value = with_border(source_a_ref[i], 0, i) + value
        if i < n - 1:
            gather_a[i] = value
            value = pass_a_ref[i + 1] * value
    x = (value + plane(1)) * over_ref[0]
    for i in reversed(range(n)):
        if i < n - 1:
            x = pass_a_ref[i + 1] * x + drop_a_ref[i + 1] * gather_a[i]
        out_ref[0, i] = x
    value = plane(2)
    for i in range(n):
        kappa = lookup(numbers["kappa"], stratum_ref[i])
        value = with_border(source_b_ref[i], 1, i) + kappa * out_ref[0, i] + value
        if i < n - 1:
            gather_b[i] = value
            value = pass_b_ref[i + 1] * value
    x = (value + plane(3)) * over_ref[1]
    for i in reversed(range(n)):
        if i < n - 1:
            x = pass_b_ref[i + 1] * x + drop_b_ref[i + 1] * gather_b[i]
        out_ref[1, i] = x
        index = stratum_ref[i]
        x2 = (
            lookup(numbers["beta"], index) * conc_ref[2, i]
            + lookup(numbers["gamma"], index) * out_ref[0, i]
        )
        out_ref[2, i] = x2
        out_ref[3, i] = (
            lookup(numbers["free_b"], index) * conc_ref[3, i]
            + lookup(numbers["share_b"], index) * x
            + lookup(numbers["decay_b"], index) * x2
        )


def call(kernel, outs, scratch=()):
    return pl.pallas_call(
        kernel,
        out_shape=[jax.ShapeDtypeStruct(shape, jnp.float32) for shape in outs],
        scratch_shapes=[pltpu.VMEM(shape, jnp.float32) for shape in scratch],
        compiler_params=pltpu.CompilerParams(vmem_limit_bytes=VMEM_LIMIT),
    )


def per_device(
    concentration,
    stratum,
    porosity,
    dispersion_table,
    transverse_table,
    exchange_table,
    decay_table,
):
    n, planes_y, planes_z = stratum.shape
    peers = lax.axis_size("flow")
    block = chunk_of(peers, planes_y, planes_z)
    rows, width = block
    cells = (n, planes_y, planes_z)

    numbered = (stratum + 1).astype(jnp.float32)
    own_lo = jnp.concatenate([concentration[:2, :, 0], numbered[None, :, 0]])
    own_hi = jnp.concatenate([concentration[:2, :, -1], numbered[None, :, -1]])
    groups = lax.axis_size("trans")
    up = [(i, i + 1) for i in range(groups - 1)]
    down = [(i + 1, i) for i in range(groups - 1)]
    next_lo = lax.ppermute(own_hi, "trans", up)
    next_hi = lax.ppermute(own_lo, "trans", down)

    table = jnp.stack(
        [
            porosity,
            dispersion_table[:, 0],
            dispersion_table[:, 1],
            transverse_table,
            exchange_table,
            decay_table,
        ]
    )
    strata = porosity.shape[0]
    table = jnp.pad(table, ((0, SUB - 6), (0, LANE - strata)), constant_values=0.5)

    pay_shape = (peers, QUANTITIES * rows, width)
    pay, edge, pass_a, drop_a, pass_b, drop_b, over, source_a, source_b = call(
        functools.partial(local_kernel, block),
        [pay_shape, (2, 6, n, planes_z), cells, cells, cells, cells, (2, planes_y, planes_z), cells, cells],
        [cells] * 9,
    )(table, stratum, concentration)
    pay, flow = call(
        functools.partial(border_kernel, block), [pay_shape, (2, 2, n, planes_z)]
    )(table, own_lo, own_hi, next_lo, next_hi, edge, pay)
    gathered = lax.all_to_all(pay, "flow", 0, 0, tiled=True)
    (currents,) = call(
        functools.partial(chain_kernel, block), [(peers, CURRENTS * rows, width)]
    )(gathered)
    currents = lax.all_to_all(currents, "flow", 0, 0, tiled=True)
    (out,) = call(
        functools.partial(final_kernel, block), [(4,) + cells], [cells] * 2
    )(
        table,
        stratum,
        concentration,
        pass_a,
        drop_a,
        pass_b,
        drop_b,
        over,
        source_a,
        source_b,
        flow,
        currents,
    )
    return out


def solution(mesh):
    in_specs = (P(None, "flow", "trans", None), P("flow", "trans", None), P(), P(), P(), P(), P())
    out_specs = P(None, "flow", "trans", None)
    return jax.shard_map(
        per_device, mesh=mesh, in_specs=in_specs, out_specs=out_specs, check_vma=False
    )
```

```python
import functools

import jax
import jax.numpy as jnp
from jax import lax
from jax.experimental import pallas as pl
from jax.experimental.pallas import tpu as pltpu
from jax.sharding import PartitionSpec as P

SUB, LANE = 8, 128
ZA_LL, ZA_LR, ZA_RR, ZB_LL, ZB_LR, ZB_RR, C_LL, C_LR, C_RL, C_RR, FA_L, FA_R, FB_L, FB_R = range(14)
QUANTITIES = 14
CURRENTS = 4
VMEM_LIMIT = 40 * 1024 * 1024


def recip(x):
    return 1.0 / x


def lookup(row, index):
    tiles = []
    for y in range(0, index.shape[0], SUB):
        across = [
            jnp.take_along_axis(
                row, index[y : y + SUB, z : z + LANE], axis=1, mode="promise_in_bounds"
            )
            for z in range(0, index.shape[1], LANE)
        ]
        tiles.append(jnp.concatenate(across, axis=1))
    return jnp.concatenate(tiles, axis=0)


NUMBERS = (
    "por",
    "shunt_a",
    "shunt_b",
    "half_a",
    "half_b",
    "half_t",
    "beta",
    "gamma",
    "alpha_a",
    "alpha_b",
    "kappa",
    "delta",
    "free_b",
    "share_b",
    "decay_b",
)


def derive(por, disp_a, disp_b, trans, exch, decay):
    immobile = 1.0 - por
    over_a = 1.0 / (immobile + exch + decay)
    over_b = 1.0 / (immobile + exch)
    beta = immobile * over_a
    gamma = exch * over_a
    share_b = exch * over_b
    return dict(
        por=por,
        shunt_a=por + decay + exch * (immobile + decay) * over_a,
        shunt_b=por + exch * immobile * over_b,
        half_a=0.5 / disp_a,
        half_b=0.5 / disp_b,
        half_t=0.5 / trans,
        beta=beta,
        gamma=gamma,
        alpha_a=exch * beta,
        alpha_b=share_b * immobile,
        kappa=decay + share_b * decay * gamma,
        delta=share_b * decay * beta,
        free_b=immobile * over_b,
        share_b=share_b,
        decay_b=decay * over_b,
    )


class Numbers:
    def __init__(self, tab_ref):
        self.tab_ref = tab_ref

    def __call__(self, name, index):
        k = NUMBERS.index(name)
        row = jnp.broadcast_to(self.tab_ref[k : k + 1, :], (SUB, LANE))
        return lookup(row, index)


def chunk_of(peers, planes_y, planes_z):
    if peers <= planes_y:
        return planes_y // peers, planes_z
    return 1, planes_y * planes_z // peers


def chunk_place(which, block, planes_z):
    rows, width = block
    across = planes_z // width
    return (which // across) * rows, (which % across) * width


def shifted_difference(value, axis):
    return pltpu.roll(value, value.shape[axis] - 1, axis) - value


def pack_kernel(
    conc_hbm,
    stratum_hbm,
    por_hbm,
    disp_hbm,
    trans_hbm,
    exch_hbm,
    decay_hbm,
    lo_ref,
    hi_ref,
    tab_ref,
    conc_ref,
    stratum_ref,
    por_ref,
    disp_ref,
    trans_ref,
    exch_ref,
    decay_ref,
    raw,
    sems,
):
    moves = [
        (stratum_hbm, stratum_ref),
        (conc_hbm.at[0:2], conc_ref.at[0:2]),
        (por_hbm, por_ref),
        (disp_hbm, disp_ref),
        (trans_hbm, trans_ref),
        (exch_hbm, exch_ref),
        (decay_hbm, decay_ref),
        (conc_hbm.at[2:4], conc_ref.at[2:4]),
    ]
    copies = [pltpu.make_async_copy(src, dst, sems.at[k]) for k, (src, dst) in enumerate(moves)]
    for copy in copies:
        copy.start()
    raw[...] = jnp.full(raw.shape, 0.5, jnp.float32)
    for copy in copies[2:7]:
        copy.wait()
    strata = por_ref.shape[1]
    raw[0:1, 0:strata] = por_ref[...]
    raw[1:3, 0:strata] = disp_ref[...]
    raw[3:4, 0:strata] = trans_ref[...]
    raw[4:5, 0:strata] = exch_ref[...]
    raw[5:6, 0:strata] = decay_ref[...]
    made = derive(*[raw[k : k + 1, :] for k in range(6)])
    for k, name in enumerate(NUMBERS):
        tab_ref[k : k + 1, :] = made[name]
    tab_ref[len(NUMBERS) : 2 * SUB, :] = raw[0 : 2 * SUB - len(NUMBERS), :]
    copies[0].wait()
    last = stratum_ref.shape[1] - 1
    for ref, y in ((lo_ref, 0), (hi_ref, last)):
        ref[2] = (stratum_ref[:, y, :] + 1).astype(jnp.float32)
    copies[1].wait()
    for ref, y in ((lo_ref, 0), (hi_ref, last)):
        ref[0] = conc_ref[0, :, y, :]
        ref[1] = conc_ref[1, :, y, :]
    copies[7].wait()


def local_kernel(
    block,
    tab_ref,
    stratum_ref,
    conc_ref,
    pay_ref,
    edge_ref,
    pass_a_ref,
    drop_a_ref,
    pass_b_ref,
    drop_b_ref,
    over_ref,
    source_a_ref,
    source_b_ref,
    head_a,
    head_b,
    kappa_ref,
    left_a,
    right_a,
    left_b,
    right_b,
    adj_l,
    adj_r,
):
    n, planes_y, planes_z = stratum_ref.shape
    number = Numbers(tab_ref)

    cond_a = cond_b = half_a = half_b = through_a = through_b = None
    for i in range(n):
        index = stratum_ref[i]
        shunt_a, shunt_b = number("shunt_a", index), number("shunt_b", index)
        new_a, new_b = number("half_a", index), number("half_b", index)
        kappa_ref[i] = number("kappa", index)
        if i == 0:
            first_half_a, first_half_b = new_a, new_b
            cond_a, cond_b = shunt_a, shunt_b
            through_a = through_b = jnp.ones_like(shunt_a)
        else:
            face_a, face_b = half_a + new_a, half_b + new_b
            pass_a, pass_b = recip(1.0 + face_a * cond_a), recip(1.0 + face_b * cond_b)
            cond_a, cond_b = shunt_a + cond_a * pass_a, shunt_b + cond_b * pass_b
            pass_a_ref[i], pass_b_ref[i] = pass_a, pass_b
            drop_a_ref[i], drop_b_ref[i] = face_a * pass_a, face_b * pass_b
            through_a, through_b = through_a * pass_a, through_b * pass_b
        head_a[i], head_b[i] = through_a, through_b
        half_a, half_b = new_a, new_b
    over_a, over_b = recip(cond_a), recip(cond_b)
    over_ref[0], over_ref[1] = over_a, over_b

    r_a, r_b = over_a, over_b
    l_a, l_b = through_a * over_a, through_b * over_b
    couple = [None] * 4
    for i in reversed(range(n)):
        if i < n - 1:
            pass_a, pass_b = pass_a_ref[i + 1], pass_b_ref[i + 1]
            l_a = pass_a * l_a + drop_a_ref[i + 1] * head_a[i]
            l_b = pass_b * l_b + drop_b_ref[i + 1] * head_b[i]
            r_a, r_b = pass_a * r_a, pass_b * r_b
        left_a[i], right_a[i], left_b[i], right_b[i] = l_a, r_a, l_b, r_b
        kappa = kappa_ref[i]
        k_l, k_r = kappa * l_a, kappa * r_a
        terms = [l_b * k_l, l_b * k_r, r_b * k_l, r_b * k_r]
        couple = [t if c is None else c + t for c, t in zip(couple, terms)]

    g_l = g_r = None
    for i in range(n):
        kappa = kappa_ref[i]
        s_l, s_r = kappa * left_b[i], kappa * right_b[i]
        if i > 0:
            pass_a = pass_a_ref[i]
            s_l, s_r = s_l + pass_a * g_l, s_r + pass_a * g_r
        g_l, g_r = s_l, s_r
        adj_l[i], adj_r[i] = g_l, g_r

    lane = lax.broadcasted_iota(jnp.int32, (planes_y, planes_z), 1)
    line = lax.broadcasted_iota(jnp.int32, (planes_y, planes_z), 0)
    inside = (line < planes_y - 1, lane < planes_z - 1)
    w_l, w_r = adj_l[n - 1] * over_a, adj_r[n - 1] * over_a
    free = [None] * 4
    for i in reversed(range(n)):
        if i < n - 1:
            pass_a, drop_a = pass_a_ref[i + 1], drop_a_ref[i + 1]
            w_l, w_r = pass_a * w_l + drop_a * adj_l[i], pass_a * w_r + drop_a * adj_r[i]
        adj_l[i], adj_r[i] = w_l, w_r
        index = stratum_ref[i]
        half_t = number("half_t", index)
        por = number("por", index)
        c0, c1, c2, c3 = [conc_ref[k, i] for k in range(4)]
        source_a = por * c0 + number("alpha_a", index) * c2
        source_b = (
            por * c1
            + number("alpha_b", index) * c3
            + number("delta", index) * c2
        )
        for axis in (0, 1):
            last = half_t.shape[axis] - 1
            face = jnp.where(
                inside[axis], recip(half_t + pltpu.roll(half_t, last, axis)), 0.0
            )
            flow_a = face * shifted_difference(c0, axis)
            flow_b = face * shifted_difference(c1, axis)
            source_a = source_a + (flow_a - pltpu.roll(flow_a, 1, axis))
            source_b = source_b + (flow_b - pltpu.roll(flow_b, 1, axis))
        source_a_ref[i], source_b_ref[i] = source_a, source_b
        terms = [
            left_a[i] * source_a,
            right_a[i] * source_a,
            left_b[i] * source_b + w_l * source_a,
            right_b[i] * source_b + w_r * source_a,
        ]
        free = [t if f is None else f + t for f, t in zip(free, terms)]

    quantities = [
        left_a[0] + first_half_a,
        right_a[0],
        over_a + half_a,
        left_b[0] + first_half_b,
        right_b[0],
        over_b + half_b,
        *couple,
        *free,
    ]
    rows, width = block
    for p in range(pay_ref.shape[0]):
        y, z = chunk_place(p, block, planes_z)
        for q, value in enumerate(quantities):
            pay_ref[p, q * rows : (q + 1) * rows, :] = value[y : y + rows, z : z + width]
    for k, ref in enumerate((left_a, right_a, left_b, right_b, adj_l, adj_r)):
        edge_ref[0, k] = ref[:, 0, :]
        edge_ref[1, k] = ref[:, planes_y - 1, :]


def border_kernel(
    block,
    tab_ref,
    own_lo_ref,
    own_hi_ref,
    next_lo_ref,
    next_hi_ref,
    edge_ref,
    pay_ref,
    out_ref,
    flow_ref,
):
    peers = pay_ref.shape[0]
    rows, width = block
    planes_z = own_lo_ref.shape[2]
    number = Numbers(tab_ref)
    out_ref[...] = pay_ref[...]
    for side, (own_ref, next_ref) in enumerate(
        ((own_lo_ref, next_lo_ref), (own_hi_ref, next_hi_ref))
    ):
        own_id = own_ref[2].astype(jnp.int32) - 1
        next_id = next_ref[2].astype(jnp.int32) - 1
        present = next_id >= 0
        half = number("half_t", own_id) + number("half_t", jnp.maximum(next_id, 0))
        face = jnp.where(present, recip(half), 0.0)
        flow_a = face * (next_ref[0] - own_ref[0])
        flow_b = face * (next_ref[1] - own_ref[1])
        flow_ref[side, 0], flow_ref[side, 1] = flow_a, flow_b
        l_a, r_a, l_b, r_b, w_l, w_r = [edge_ref[side, k] for k in range(6)]
        changes = {
            FA_L: l_a * flow_a,
            FA_R: r_a * flow_a,
            FB_L: l_b * flow_b + w_l * flow_a,
            FB_R: r_b * flow_b + w_r * flow_a,
        }
        across = planes_z // width
        for q, change in changes.items():
            total = jnp.sum(change, axis=0, keepdims=True)
            for part in range(across):
                p = part if side == 0 else peers - across + part
                row = q * rows + (0 if side == 0 else rows - 1)
                out_ref[p, row : row + 1, :] = (
                    pay_ref[p, row : row + 1, :] + total[:, part * width : (part + 1) * width]
                )


def chain_kernel(block, pay_ref, out_ref):
    peers = pay_ref.shape[0]
    rows, width = block

    def take(segment, q):
        return pay_ref[segment, q * rows : (q + 1) * rows, :]

    count = peers - 1
    pass_a, over_a, rhs_a = [None] * count, [None] * count, [None] * count
    pass_b, over_b = [None] * count, [None] * count
    for k in range(count):
        diag_a = take(k, ZA_RR) + take(k + 1, ZA_LL)
        diag_b = take(k, ZB_RR) + take(k + 1, ZB_LL)
        rhs = take(k, FA_R) - take(k + 1, FA_L)
        if k > 0:
            off_a, off_b = take(k, ZA_LR), take(k, ZB_LR)
            ratio_a = off_a * over_a[k - 1]
            pass_a[k - 1] = ratio_a
            diag_a = diag_a - off_a * ratio_a
            rhs = rhs + ratio_a * rhs_a[k - 1]
            ratio_b = off_b * over_b[k - 1]
            pass_b[k - 1] = ratio_b
            diag_b = diag_b - off_b * ratio_b
        over_a[k], over_b[k], rhs_a[k] = recip(diag_a), recip(diag_b), rhs
    current_a = [None] * count
    for k in reversed(range(count)):
        value = rhs_a[k] * over_a[k]
        if k < count - 1:
            value = value + pass_a[k] * current_a[k + 1]
        current_a[k] = value
    nothing = jnp.zeros((rows, width), jnp.float32)
    into = [nothing] + current_a + [nothing]
    rhs_b = [None] * count
    for k in range(count):
        rhs = (
            take(k, FB_R)
            - take(k + 1, FB_L)
            + take(k, C_RL) * into[k]
            - (take(k, C_RR) + take(k + 1, C_LL)) * into[k + 1]
            + take(k + 1, C_LR) * into[k + 2]
        )
        if k > 0:
            rhs = rhs + pass_b[k - 1] * rhs_b[k - 1]
        rhs_b[k] = rhs
    current_b = [None] * count
    for k in reversed(range(count)):
        value = rhs_b[k] * over_b[k]
        if k < count - 1:
            value = value + pass_b[k] * current_b[k + 1]
        current_b[k] = value
    into_b = [nothing] + current_b + [nothing]
    for k in range(peers):
        values = (into[k], -into[k + 1], into_b[k], -into_b[k + 1])
        for q, value in enumerate(values):
            out_ref[k, q * rows : (q + 1) * rows, :] = value


def final_kernel(
    block,
    tab_ref,
    stratum_ref,
    conc_ref,
    pass_a_ref,
    drop_a_ref,
    pass_b_ref,
    drop_b_ref,
    over_ref,
    source_a_ref,
    source_b_ref,
    flow_ref,
    current_ref,
    out_ref,
    gather_a,
    gather_b,
):
    n, planes_y, planes_z = stratum_ref.shape
    peers = current_ref.shape[0]
    rows, width = block
    number = Numbers(tab_ref)
    across = planes_z // width

    def plane(q):
        lines = []
        for p in range(0, peers, across):
            pieces = [current_ref[p + j, q * rows : (q + 1) * rows, :] for j in range(across)]
            lines.append(jnp.concatenate(pieces, axis=1) if across > 1 else pieces[0])
        return jnp.concatenate(lines, axis=0)

    line = lax.broadcasted_iota(jnp.int32, (planes_y, planes_z), 0)
    first_line, last_line = line == 0, line == planes_y - 1

    def with_border(source, component, i):
        low = jnp.broadcast_to(flow_ref[0, component, i : i + 1, :], source.shape)
        high = jnp.broadcast_to(flow_ref[1, component, i : i + 1, :], source.shape)
        return source + jnp.where(first_line, low, jnp.where(last_line, high, 0.0))

    value = plane(0)
    for i in range(n):
        value = with_border(source_a_ref[i], 0, i) + value
        if i < n - 1:
            gather_a[i] = value
            value = pass_a_ref[i + 1] * value
    x = (value + plane(1)) * over_ref[0]
    for i in reversed(range(n)):
        if i < n - 1:
            x = pass_a_ref[i + 1] * x + drop_a_ref[i + 1] * gather_a[i]
        out_ref[0, i] = x
    value = plane(2)
    for i in range(n):
        kappa = number("kappa", stratum_ref[i])
        value = with_border(source_b_ref[i], 1, i) + kappa * out_ref[0, i] + value
        if i < n - 1:
            gather_b[i] = value
            value = pass_b_ref[i + 1] * value
    x = (value + plane(3)) * over_ref[1]
    for i in reversed(range(n)):
        if i < n - 1:
            x = pass_b_ref[i + 1] * x + drop_b_ref[i + 1] * gather_b[i]
        out_ref[1, i] = x
        index = stratum_ref[i]
        x2 = (
            number("beta", index) * conc_ref[2, i]
            + number("gamma", index) * out_ref[0, i]
        )
        out_ref[2, i] = x2
        out_ref[3, i] = (
            number("free_b", index) * conc_ref[3, i]
            + number("share_b", index) * x
            + number("decay_b", index) * x2
        )


def call(kernel, outs, scratch=()):
    return pl.pallas_call(
        kernel,
        out_shape=[jax.ShapeDtypeStruct(shape, jnp.float32) for shape in outs],
        scratch_shapes=[pltpu.VMEM(shape, jnp.float32) for shape in scratch],
        compiler_params=pltpu.CompilerParams(vmem_limit_bytes=VMEM_LIMIT),
    )


def per_device(
    concentration,
    stratum,
    porosity,
    dispersion_table,
    transverse_table,
    exchange_table,
    decay_table,
):
    n, planes_y, planes_z = stratum.shape
    peers = lax.axis_size("flow")
    block = chunk_of(peers, planes_y, planes_z)
    rows, width = block
    cells = (n, planes_y, planes_z)

    halo = (3, n, planes_z)
    strata = porosity.shape[0]
    hbm = pl.BlockSpec(memory_space=pltpu.HBM)
    own_lo, own_hi, table, concentration, stratum = pl.pallas_call(
        pack_kernel,
        out_shape=[
            jax.ShapeDtypeStruct(halo, jnp.float32),
            jax.ShapeDtypeStruct(halo, jnp.float32),
            jax.ShapeDtypeStruct((2 * SUB, LANE), jnp.float32),
            jax.ShapeDtypeStruct(concentration.shape, jnp.float32),
            jax.ShapeDtypeStruct(cells, jnp.int32),
        ],
        in_specs=[hbm] * 7,
        scratch_shapes=[
            pltpu.VMEM((1, strata), jnp.float32),
            pltpu.VMEM((2, strata), jnp.float32),
            pltpu.VMEM((1, strata), jnp.float32),
            pltpu.VMEM((1, strata), jnp.float32),
            pltpu.VMEM((1, strata), jnp.float32),
            pltpu.VMEM((SUB, LANE), jnp.float32),
            pltpu.SemaphoreType.DMA((8,)),
        ],
        compiler_params=pltpu.CompilerParams(vmem_limit_bytes=VMEM_LIMIT),
    )(
        *[
            pltpu.with_memory_space_constraint(value, pltpu.HBM)
            for value in (
                concentration,
                stratum,
                porosity[None],
                dispersion_table.T,
                transverse_table[None],
                exchange_table[None],
                decay_table[None],
            )
        ]
    )
    groups = lax.axis_size("trans")
    up = [(i, i + 1) for i in range(groups - 1)]
    down = [(i + 1, i) for i in range(groups - 1)]
    next_lo = lax.ppermute(own_hi, "trans", up)
    next_hi = lax.ppermute(own_lo, "trans", down)

    pay_shape = (peers, QUANTITIES * rows, width)
    pay, edge, pass_a, drop_a, pass_b, drop_b, over, source_a, source_b = call(
        functools.partial(local_kernel, block),
        [pay_shape, (2, 6, n, planes_z), cells, cells, cells, cells, (2, planes_y, planes_z), cells, cells],
        [cells] * 9,
    )(table, stratum, concentration)
    pay, flow = call(
        functools.partial(border_kernel, block), [pay_shape, (2, 2, n, planes_z)]
    )(table, own_lo, own_hi, next_lo, next_hi, edge, pay)
    gathered = lax.all_to_all(pay, "flow", 0, 0, tiled=True)
    (currents,) = call(
        functools.partial(chain_kernel, block), [(peers, CURRENTS * rows, width)]
    )(gathered)
    currents = lax.all_to_all(currents, "flow", 0, 0, tiled=True)
    (out,) = call(
        functools.partial(final_kernel, block), [(4,) + cells], [cells] * 2
    )(
        table,
        stratum,
        concentration,
        pass_a,
        drop_a,
        pass_b,
        drop_b,
        over,
        source_a,
        source_b,
        flow,
        currents,
    )
    return out


def solution(mesh):
    in_specs = (P(None, "flow", "trans", None), P("flow", "trans", None), P(), P(), P(), P(), P())
    out_specs = P(None, "flow", "trans", None)
    return jax.shard_map(
        per_device, mesh=mesh, in_specs=in_specs, out_specs=out_specs, check_vma=False
    )
```

```python
import functools

import jax
import jax.numpy as jnp
from jax import lax
from jax.experimental import pallas as pl
from jax.experimental.pallas import tpu as pltpu
from jax.sharding import PartitionSpec as P

SUB, LANE = 8, 128
ZA_LL, ZA_LR, ZA_RR, ZB_LL, ZB_LR, ZB_RR, C_LL, C_LR, C_RL, C_RR, FA_L, FA_R, FB_L, FB_R = range(14)
QUANTITIES = 14
CURRENTS = 4
VMEM_LIMIT = 40 * 1024 * 1024


def recip(x):
    return 1.0 / x


def lookup(row, index):
    tiles = []
    for y in range(0, index.shape[0], SUB):
        across = [
            jnp.take_along_axis(
                row, index[y : y + SUB, z : z + LANE], axis=1, mode="promise_in_bounds"
            )
            for z in range(0, index.shape[1], LANE)
        ]
        tiles.append(jnp.concatenate(across, axis=1))
    return jnp.concatenate(tiles, axis=0)


NUMBERS = (
    "por",
    "shunt_a",
    "shunt_b",
    "half_a",
    "half_b",
    "half_t",
    "beta",
    "gamma",
    "alpha_a",
    "alpha_b",
    "kappa",
    "delta",
    "free_b",
    "share_b",
    "decay_b",
)


def derive(por, disp_a, disp_b, trans, exch, decay):
    immobile = 1.0 - por
    over_a = 1.0 / (immobile + exch + decay)
    over_b = 1.0 / (immobile + exch)
    beta = immobile * over_a
    gamma = exch * over_a
    share_b = exch * over_b
    return dict(
        por=por,
        shunt_a=por + decay + exch * (immobile + decay) * over_a,
        shunt_b=por + exch * immobile * over_b,
        half_a=0.5 / disp_a,
        half_b=0.5 / disp_b,
        half_t=0.5 / trans,
        beta=beta,
        gamma=gamma,
        alpha_a=exch * beta,
        alpha_b=share_b * immobile,
        kappa=decay + share_b * decay * gamma,
        delta=share_b * decay * beta,
        free_b=immobile * over_b,
        share_b=share_b,
        decay_b=decay * over_b,
    )


class Numbers:
    def __init__(self, tab_ref):
        self.tab_ref = tab_ref

    def __call__(self, name, index):
        k = NUMBERS.index(name)
        row = jnp.broadcast_to(self.tab_ref[k : k + 1, :], (SUB, LANE))
        return lookup(row, index)


def chunk_of(peers, planes_y, planes_z):
    if peers <= planes_y:
        return planes_y // peers, planes_z
    return 1, planes_y * planes_z // peers


def chunk_rows(block):
    return block[0] * block[1] // LANE


def store_chunks(ref, q, value, block):
    rows, width = block
    across = value.shape[1] // width
    base = q * chunk_rows(block)
    for p in range(ref.shape[0]):
        y, z = (p // across) * rows, (p % across) * width
        for k in range(width // LANE):
            low = z + k * LANE
            ref[p, base + k * rows : base + (k + 1) * rows, :] = value[
                y : y + rows, low : low + LANE
            ]


def load_chunks(ref, q, block, planes_z):
    rows, width = block
    across = planes_z // width
    base = q * chunk_rows(block)
    lines = []
    for p in range(0, ref.shape[0], across):
        pieces = [
            ref[p + j, base + k * rows : base + (k + 1) * rows, :]
            for j in range(across)
            for k in range(width // LANE)
        ]
        lines.append(jnp.concatenate(pieces, axis=1))
    return jnp.concatenate(lines, axis=0)


def shifted_difference(value, axis):
    return pltpu.roll(value, value.shape[axis] - 1, axis) - value


def pack_kernel(
    conc_hbm,
    stratum_hbm,
    por_hbm,
    disp_hbm,
    trans_hbm,
    exch_hbm,
    decay_hbm,
    lo_ref,
    hi_ref,
    tab_ref,
    conc_ref,
    stratum_ref,
    por_ref,
    disp_ref,
    trans_ref,
    exch_ref,
    decay_ref,
    raw,
    sems,
):
    moves = [
        (stratum_hbm, stratum_ref),
        (conc_hbm.at[0:2], conc_ref.at[0:2]),
        (por_hbm, por_ref),
        (disp_hbm, disp_ref),
        (trans_hbm, trans_ref),
        (exch_hbm, exch_ref),
        (decay_hbm, decay_ref),
        (conc_hbm.at[2:4], conc_ref.at[2:4]),
    ]
    copies = [pltpu.make_async_copy(src, dst, sems.at[k]) for k, (src, dst) in enumerate(moves)]
    for copy in copies:
        copy.start()
    raw[...] = jnp.full(raw.shape, 0.5, jnp.float32)
    for copy in copies[2:7]:
        copy.wait()
    strata = por_ref.shape[1]
    raw[0:1, 0:strata] = por_ref[...]
    raw[1:3, 0:strata] = disp_ref[...]
    raw[3:4, 0:strata] = trans_ref[...]
    raw[4:5, 0:strata] = exch_ref[...]
    raw[5:6, 0:strata] = decay_ref[...]
    made = derive(*[raw[k : k + 1, :] for k in range(6)])
    for k, name in enumerate(NUMBERS):
        tab_ref[k : k + 1, :] = made[name]
    tab_ref[len(NUMBERS) : 2 * SUB, :] = raw[0 : 2 * SUB - len(NUMBERS), :]
    copies[0].wait()
    last = stratum_ref.shape[1] - 1
    for ref, y in ((lo_ref, 0), (hi_ref, last)):
        ref[2] = (stratum_ref[:, y, :] + 1).astype(jnp.float32)
    copies[1].wait()
    for ref, y in ((lo_ref, 0), (hi_ref, last)):
        ref[0] = conc_ref[0, :, y, :]
        ref[1] = conc_ref[1, :, y, :]
    copies[7].wait()


def local_kernel(
    tab_ref,
    stratum_ref,
    conc_ref,
    pay_ref,
    edge_ref,
    pass_a_ref,
    drop_a_ref,
    pass_b_ref,
    drop_b_ref,
    over_ref,
    source_a_ref,
    source_b_ref,
    head_a,
    head_b,
    kappa_ref,
    left_a,
    right_a,
    left_b,
    right_b,
    adj_l,
    adj_r,
):
    n, planes_y, planes_z = stratum_ref.shape
    number = Numbers(tab_ref)

    cond_a = cond_b = half_a = half_b = through_a = through_b = None
    for i in range(n):
        index = stratum_ref[i]
        shunt_a, shunt_b = number("shunt_a", index), number("shunt_b", index)
        new_a, new_b = number("half_a", index), number("half_b", index)
        kappa_ref[i] = number("kappa", index)
        if i == 0:
            first_half_a, first_half_b = new_a, new_b
            cond_a, cond_b = shunt_a, shunt_b
            through_a = through_b = jnp.ones_like(shunt_a)
        else:
            face_a, face_b = half_a + new_a, half_b + new_b
            pass_a, pass_b = recip(1.0 + face_a * cond_a), recip(1.0 + face_b * cond_b)
            cond_a, cond_b = shunt_a + cond_a * pass_a, shunt_b + cond_b * pass_b
            pass_a_ref[i], pass_b_ref[i] = pass_a, pass_b
            drop_a_ref[i], drop_b_ref[i] = face_a * pass_a, face_b * pass_b
            through_a, through_b = through_a * pass_a, through_b * pass_b
        head_a[i], head_b[i] = through_a, through_b
        half_a, half_b = new_a, new_b
    over_a, over_b = recip(cond_a), recip(cond_b)
    over_ref[0], over_ref[1] = over_a, over_b

    r_a, r_b = over_a, over_b
    l_a, l_b = through_a * over_a, through_b * over_b
    couple = [None] * 4
    for i in reversed(range(n)):
        if i < n - 1:
            pass_a, pass_b = pass_a_ref[i + 1], pass_b_ref[i + 1]
            l_a = pass_a * l_a + drop_a_ref[i + 1] * head_a[i]
            l_b = pass_b * l_b + drop_b_ref[i + 1] * head_b[i]
            r_a, r_b = pass_a * r_a, pass_b * r_b
        left_a[i], right_a[i], left_b[i], right_b[i] = l_a, r_a, l_b, r_b
        kappa = kappa_ref[i]
        k_l, k_r = kappa * l_a, kappa * r_a
        terms = [l_b * k_l, l_b * k_r, r_b * k_l, r_b * k_r]
        couple = [t if c is None else c + t for c, t in zip(couple, terms)]

    g_l = g_r = None
    for i in range(n):
        kappa = kappa_ref[i]
        s_l, s_r = kappa * left_b[i], kappa * right_b[i]
        if i > 0:
            pass_a = pass_a_ref[i]
            s_l, s_r = s_l + pass_a * g_l, s_r + pass_a * g_r
        g_l, g_r = s_l, s_r
        adj_l[i], adj_r[i] = g_l, g_r

    lane = lax.broadcasted_iota(jnp.int32, (planes_y, planes_z), 1)
    line = lax.broadcasted_iota(jnp.int32, (planes_y, planes_z), 0)
    inside = (line < planes_y - 1, lane < planes_z - 1)
    w_l, w_r = adj_l[n - 1] * over_a, adj_r[n - 1] * over_a
    free = [None] * 4
    for i in reversed(range(n)):
        if i < n - 1:
            pass_a, drop_a = pass_a_ref[i + 1], drop_a_ref[i + 1]
            w_l, w_r = pass_a * w_l + drop_a * adj_l[i], pass_a * w_r + drop_a * adj_r[i]
        adj_l[i], adj_r[i] = w_l, w_r
        index = stratum_ref[i]
        half_t = number("half_t", index)
        por = number("por", index)
        c0, c1, c2, c3 = [conc_ref[k, i] for k in range(4)]
        source_a = por * c0 + number("alpha_a", index) * c2
        source_b = (
            por * c1
            + number("alpha_b", index) * c3
            + number("delta", index) * c2
        )
        for axis in (0, 1):
            last = half_t.shape[axis] - 1
            face = jnp.where(
                inside[axis], recip(half_t + pltpu.roll(half_t, last, axis)), 0.0
            )
            flow_a = face * shifted_difference(c0, axis)
            flow_b = face * shifted_difference(c1, axis)
            source_a = source_a + (flow_a - pltpu.roll(flow_a, 1, axis))
            source_b = source_b + (flow_b - pltpu.roll(flow_b, 1, axis))
        source_a_ref[i], source_b_ref[i] = source_a, source_b
        terms = [
            left_a[i] * source_a,
            right_a[i] * source_a,
            left_b[i] * source_b + w_l * source_a,
            right_b[i] * source_b + w_r * source_a,
        ]
        free = [t if f is None else f + t for f, t in zip(free, terms)]

    quantities = [
        left_a[0] + first_half_a,
        right_a[0],
        over_a + half_a,
        left_b[0] + first_half_b,
        right_b[0],
        over_b + half_b,
        *couple,
        *free,
    ]
    half = planes_y // 2
    for q, value in enumerate(quantities):
        pay_ref[0, q] = value[:half]
        pay_ref[1, q] = value[half:]
    for k, ref in enumerate((left_a, right_a, left_b, right_b, adj_l, adj_r)):
        edge_ref[0, k] = ref[:, 0, :]
        edge_ref[1, k] = ref[:, planes_y - 1, :]


def border_kernel(
    tab_ref,
    own_lo_ref,
    own_hi_ref,
    next_lo_ref,
    next_hi_ref,
    edge_ref,
    pay_ref,
    out_ref,
    flow_ref,
):
    number = Numbers(tab_ref)
    out_ref[...] = pay_ref[...]
    for side, (own_ref, next_ref) in enumerate(
        ((own_lo_ref, next_lo_ref), (own_hi_ref, next_hi_ref))
    ):
        own_id = own_ref[2].astype(jnp.int32) - 1
        next_id = next_ref[2].astype(jnp.int32) - 1
        present = next_id >= 0
        half = number("half_t", own_id) + number("half_t", jnp.maximum(next_id, 0))
        face = jnp.where(present, recip(half), 0.0)
        flow_a = face * (next_ref[0] - own_ref[0])
        flow_b = face * (next_ref[1] - own_ref[1])
        flow_ref[side, 0], flow_ref[side, 1] = flow_a, flow_b
        l_a, r_a, l_b, r_b, w_l, w_r = [edge_ref[side, k] for k in range(6)]
        changes = {
            FA_L: l_a * flow_a,
            FA_R: r_a * flow_a,
            FB_L: l_b * flow_b + w_l * flow_a,
            FB_R: r_b * flow_b + w_r * flow_a,
        }
        row = 0 if side == 0 else pay_ref.shape[2] - 1
        for q, change in changes.items():
            total = jnp.sum(change, axis=0, keepdims=True)
            out_ref[side, q, row : row + 1, :] = pay_ref[side, q, row : row + 1, :] + total


def merge_kernel(block, pay_ref, out_ref, keep_ref):
    one = [pay_ref[0, q] for q in range(QUANTITIES)]
    two = [pay_ref[1, q] for q in range(QUANTITIES)]
    over_a = recip(one[ZA_RR] + two[ZA_LL])
    over_b = recip(one[ZB_RR] + two[ZB_LL])
    across = one[C_RR] + two[C_LL]
    free_a = over_a * (one[FA_R] - two[FA_L])
    from_l, from_r = over_a * one[ZA_LR], over_a * two[ZA_LR]
    free_b = over_b * (one[FB_R] - two[FB_L] - across * free_a)
    from_l_b, from_r_b = over_b * one[ZB_LR], over_b * two[ZB_LR]
    cross_l = over_b * (one[C_RL] - across * from_l)
    cross_r = over_b * (two[C_LR] - across * from_r)
    merged = {
        ZA_LL: one[ZA_LL] - one[ZA_LR] * from_l,
        ZA_LR: one[ZA_LR] * from_r,
        ZA_RR: two[ZA_RR] - two[ZA_LR] * from_r,
        ZB_LL: one[ZB_LL] - one[ZB_LR] * from_l_b,
        ZB_LR: one[ZB_LR] * from_r_b,
        ZB_RR: two[ZB_RR] - two[ZB_LR] * from_r_b,
        C_LL: one[C_LL] - one[ZB_LR] * cross_l - one[C_LR] * from_l,
        C_LR: one[ZB_LR] * cross_r + one[C_LR] * from_r,
        C_RL: two[ZB_LR] * cross_l + two[C_RL] * from_l,
        C_RR: two[C_RR] - two[ZB_LR] * cross_r - two[C_RL] * from_r,
        FA_L: one[FA_L] - one[ZA_LR] * free_a,
        FA_R: two[FA_R] + two[ZA_LR] * free_a,
        FB_L: one[FB_L] - one[ZB_LR] * free_b - one[C_LR] * free_a,
        FB_R: two[FB_R] + two[ZB_LR] * free_b + two[C_RL] * free_a,
    }
    for q, value in merged.items():
        store_chunks(out_ref, q, value, block)
    for k, value in enumerate(
        (free_a, from_l, from_r, free_b, from_l_b, from_r_b, cross_l, cross_r)
    ):
        keep_ref[k] = value


def split_kernel(block, current_ref, keep_ref, out_ref):
    planes_z = keep_ref.shape[2]
    l_a, r_a, l_b, r_b = [load_chunks(current_ref, q, block, planes_z) for q in range(CURRENTS)]
    free_a, from_l, from_r, free_b, from_l_b, from_r_b, cross_l, cross_r = [
        keep_ref[k] for k in range(8)
    ]
    middle_a = free_a + from_l * l_a - from_r * r_a
    middle_b = free_b + from_l_b * l_b - from_r_b * r_b + cross_l * l_a - cross_r * r_a
    for q, value in enumerate((l_a, -middle_a, l_b, -middle_b)):
        out_ref[0, q] = value
    for q, value in enumerate((middle_a, r_a, middle_b, r_b)):
        out_ref[1, q] = value


def chain_kernel(block, pay_ref, out_ref):
    peers = pay_ref.shape[0]
    rows = chunk_rows(block)

    def take(segment, q):
        return pay_ref[segment, q * rows : (q + 1) * rows, :]

    count = peers - 1
    pass_a, over_a, rhs_a = [None] * count, [None] * count, [None] * count
    pass_b, over_b = [None] * count, [None] * count
    for k in range(count):
        diag_a = take(k, ZA_RR) + take(k + 1, ZA_LL)
        diag_b = take(k, ZB_RR) + take(k + 1, ZB_LL)
        rhs = take(k, FA_R) - take(k + 1, FA_L)
        if k > 0:
            off_a, off_b = take(k, ZA_LR), take(k, ZB_LR)
            ratio_a = off_a * over_a[k - 1]
            pass_a[k - 1] = ratio_a
            diag_a = diag_a - off_a * ratio_a
            rhs = rhs + ratio_a * rhs_a[k - 1]
            ratio_b = off_b * over_b[k - 1]
            pass_b[k - 1] = ratio_b
            diag_b = diag_b - off_b * ratio_b
        over_a[k], over_b[k], rhs_a[k] = recip(diag_a), recip(diag_b), rhs
    current_a = [None] * count
    for k in reversed(range(count)):
        value = rhs_a[k] * over_a[k]
        if k < count - 1:
            value = value + pass_a[k] * current_a[k + 1]
        current_a[k] = value
    nothing = jnp.zeros((rows, LANE), jnp.float32)
    into = [nothing] + current_a + [nothing]
    rhs_b = [None] * count
    for k in range(count):
        rhs = (
            take(k, FB_R)
            - take(k + 1, FB_L)
            + take(k, C_RL) * into[k]
            - (take(k, C_RR) + take(k + 1, C_LL)) * into[k + 1]
            + take(k + 1, C_LR) * into[k + 2]
        )
        if k > 0:
            rhs = rhs + pass_b[k - 1] * rhs_b[k - 1]
        rhs_b[k] = rhs
    current_b = [None] * count
    for k in reversed(range(count)):
        value = rhs_b[k] * over_b[k]
        if k < count - 1:
            value = value + pass_b[k] * current_b[k + 1]
        current_b[k] = value
    into_b = [nothing] + current_b + [nothing]
    for k in range(peers):
        values = (into[k], -into[k + 1], into_b[k], -into_b[k + 1])
        for q, value in enumerate(values):
            out_ref[k, q * rows : (q + 1) * rows, :] = value


def final_kernel(
    tab_ref,
    stratum_ref,
    conc_ref,
    pass_a_ref,
    drop_a_ref,
    pass_b_ref,
    drop_b_ref,
    over_ref,
    source_a_ref,
    source_b_ref,
    flow_ref,
    current_ref,
    out_ref,
    gather_a,
    gather_b,
):
    n, planes_y, planes_z = stratum_ref.shape
    number = Numbers(tab_ref)

    def plane(q):
        return jnp.concatenate([current_ref[0, q], current_ref[1, q]], axis=0)

    line = lax.broadcasted_iota(jnp.int32, (planes_y, planes_z), 0)
    first_line, last_line = line == 0, line == planes_y - 1

    def with_border(source, component, i):
        low = jnp.broadcast_to(flow_ref[0, component, i : i + 1, :], source.shape)
        high = jnp.broadcast_to(flow_ref[1, component, i : i + 1, :], source.shape)
        return source + jnp.where(first_line, low, jnp.where(last_line, high, 0.0))

    value = plane(0)
    for i in range(n):
        value = with_border(source_a_ref[i], 0, i) + value
        if i < n - 1:
            gather_a[i] = value
            value = pass_a_ref[i + 1] * value
    x = (value + plane(1)) * over_ref[0]
    for i in reversed(range(n)):
        if i < n - 1:
            x = pass_a_ref[i + 1] * x + drop_a_ref[i + 1] * gather_a[i]
        out_ref[0, i] = x
    value = plane(2)
    for i in range(n):
        kappa = number("kappa", stratum_ref[i])
        value = with_border(source_b_ref[i], 1, i) + kappa * out_ref[0, i] + value
        if i < n - 1:
            gather_b[i] = value
            value = pass_b_ref[i + 1] * value
    x = (value + plane(3)) * over_ref[1]
    for i in reversed(range(n)):
        if i < n - 1:
            x = pass_b_ref[i + 1] * x + drop_b_ref[i + 1] * gather_b[i]
        out_ref[1, i] = x
        index = stratum_ref[i]
        x2 = (
            number("beta", index) * conc_ref[2, i]
            + number("gamma", index) * out_ref[0, i]
        )
        out_ref[2, i] = x2
        out_ref[3, i] = (
            number("free_b", index) * conc_ref[3, i]
            + number("share_b", index) * x
            + number("decay_b", index) * x2
        )


def call(kernel, outs, scratch=()):
    return pl.pallas_call(
        kernel,
        out_shape=[jax.ShapeDtypeStruct(shape, jnp.float32) for shape in outs],
        scratch_shapes=[pltpu.VMEM(shape, jnp.float32) for shape in scratch],
        compiler_params=pltpu.CompilerParams(vmem_limit_bytes=VMEM_LIMIT),
    )


def per_device(
    concentration,
    stratum,
    porosity,
    dispersion_table,
    transverse_table,
    exchange_table,
    decay_table,
):
    n, planes_y, planes_z = stratum.shape
    peers = lax.axis_size("flow")
    others = peers // 2
    half = planes_y // 2
    block = chunk_of(others, half, planes_z)
    rows = chunk_rows(block)
    pairs = [[2 * m, 2 * m + 1] for m in range(others)]
    sides = [[2 * m + r for m in range(others)] for r in range(2)]
    cells = (n, planes_y, planes_z)

    halo = (3, n, planes_z)
    strata = porosity.shape[0]
    hbm = pl.BlockSpec(memory_space=pltpu.HBM)
    own_lo, own_hi, table, concentration, stratum = pl.pallas_call(
        pack_kernel,
        out_shape=[
            jax.ShapeDtypeStruct(halo, jnp.float32),
            jax.ShapeDtypeStruct(halo, jnp.float32),
            jax.ShapeDtypeStruct((2 * SUB, LANE), jnp.float32),
            jax.ShapeDtypeStruct(concentration.shape, jnp.float32),
            jax.ShapeDtypeStruct(cells, jnp.int32),
        ],
        in_specs=[hbm] * 7,
        scratch_shapes=[
            pltpu.VMEM((1, strata), jnp.float32),
            pltpu.VMEM((2, strata), jnp.float32),
            pltpu.VMEM((1, strata), jnp.float32),
            pltpu.VMEM((1, strata), jnp.float32),
            pltpu.VMEM((1, strata), jnp.float32),
            pltpu.VMEM((SUB, LANE), jnp.float32),
            pltpu.SemaphoreType.DMA((8,)),
        ],
        compiler_params=pltpu.CompilerParams(vmem_limit_bytes=VMEM_LIMIT),
    )(
        *[
            pltpu.with_memory_space_constraint(value, pltpu.HBM)
            for value in (
                concentration,
                stratum,
                porosity[None],
                dispersion_table.T,
                transverse_table[None],
                exchange_table[None],
                decay_table[None],
            )
        ]
    )
    groups = lax.axis_size("trans")
    up = [(i, i + 1) for i in range(groups - 1)]
    down = [(i + 1, i) for i in range(groups - 1)]
    next_lo = lax.ppermute(own_hi, "trans", up)
    next_hi = lax.ppermute(own_lo, "trans", down)

    pay_shape = (2, QUANTITIES, half, planes_z)
    pay, edge, pass_a, drop_a, pass_b, drop_b, over, source_a, source_b = call(
        local_kernel,
        [pay_shape, (2, 6, n, planes_z), cells, cells, cells, cells, (2, planes_y, planes_z), cells, cells],
        [cells] * 9,
    )(table, stratum, concentration)
    pay, flow = call(border_kernel, [pay_shape, (2, 2, n, planes_z)])(
        table, own_lo, own_hi, next_lo, next_hi, edge, pay
    )
    pay = lax.all_to_all(pay, "flow", 0, 0, axis_index_groups=pairs, tiled=True)
    pay, keep = call(
        functools.partial(merge_kernel, block),
        [(others, QUANTITIES * rows, LANE), (8, half, planes_z)],
    )(pay)
    pay = lax.all_to_all(pay, "flow", 0, 0, axis_index_groups=sides, tiled=True)
    (currents,) = call(
        functools.partial(chain_kernel, block), [(others, CURRENTS * rows, LANE)]
    )(pay)
    currents = lax.all_to_all(currents, "flow", 0, 0, axis_index_groups=sides, tiled=True)
    (currents,) = call(
        functools.partial(split_kernel, block), [(2, CURRENTS, half, planes_z)]
    )(currents, keep)
    currents = lax.all_to_all(currents, "flow", 0, 0, axis_index_groups=pairs, tiled=True)
    (out,) = call(final_kernel, [(4,) + cells], [cells] * 2)(
        table,
        stratum,
        concentration,
        pass_a,
        drop_a,
        pass_b,
        drop_b,
        over,
        source_a,
        source_b,
        flow,
        currents,
    )
    return out


def solution(mesh):
    in_specs = (P(None, "flow", "trans", None), P("flow", "trans", None), P(), P(), P(), P(), P())
    out_specs = P(None, "flow", "trans", None)
    return jax.shard_map(
        per_device, mesh=mesh, in_specs=in_specs, out_specs=out_specs, check_vma=False
    )
```

```python
import functools

import jax
import jax.numpy as jnp
from jax import lax
from jax.experimental import pallas as pl
from jax.experimental.pallas import tpu as pltpu
from jax.sharding import PartitionSpec as P

SUB, LANE = 8, 128
ZA_LL, ZA_LR, ZA_RR, ZB_LL, ZB_LR, ZB_RR, C_LL, C_LR, C_RL, C_RR, FA_L, FA_R, FB_L, FB_R = range(14)
QUANTITIES = 14
CURRENTS = 4
VMEM_LIMIT = 40 * 1024 * 1024


def recip(x):
    return 1.0 / x


def lookup(row, index):
    tiles = []
    for y in range(0, index.shape[0], SUB):
        across = [
            jnp.take_along_axis(
                row, index[y : y + SUB, z : z + LANE], axis=1, mode="promise_in_bounds"
            )
            for z in range(0, index.shape[1], LANE)
        ]
        tiles.append(jnp.concatenate(across, axis=1))
    return jnp.concatenate(tiles, axis=0)


NUMBERS = (
    "por",
    "shunt_a",
    "shunt_b",
    "half_a",
    "half_b",
    "half_t",
    "beta",
    "gamma",
    "alpha_a",
    "alpha_b",
    "kappa",
    "delta",
    "free_b",
    "share_b",
    "decay_b",
)


def derive(por, disp_a, disp_b, trans, exch, decay):
    immobile = 1.0 - por
    over_a = 1.0 / (immobile + exch + decay)
    over_b = 1.0 / (immobile + exch)
    beta = immobile * over_a
    gamma = exch * over_a
    share_b = exch * over_b
    return dict(
        por=por,
        shunt_a=por + decay + exch * (immobile + decay) * over_a,
        shunt_b=por + exch * immobile * over_b,
        half_a=0.5 / disp_a,
        half_b=0.5 / disp_b,
        half_t=0.5 / trans,
        beta=beta,
        gamma=gamma,
        alpha_a=exch * beta,
        alpha_b=share_b * immobile,
        kappa=decay + share_b * decay * gamma,
        delta=share_b * decay * beta,
        free_b=immobile * over_b,
        share_b=share_b,
        decay_b=decay * over_b,
    )


class Numbers:
    def __init__(self, tab_ref):
        self.tab_ref = tab_ref

    def __call__(self, name, index):
        k = NUMBERS.index(name)
        row = jnp.broadcast_to(self.tab_ref[k : k + 1, :], (SUB, LANE))
        return lookup(row, index)


def shifted_difference(value, axis):
    return pltpu.roll(value, value.shape[axis] - 1, axis) - value


def pack_kernel(
    conc_hbm,
    stratum_hbm,
    por_hbm,
    disp_hbm,
    trans_hbm,
    exch_hbm,
    decay_hbm,
    lo_ref,
    hi_ref,
    tab_ref,
    conc_ref,
    stratum_ref,
    por_ref,
    disp_ref,
    trans_ref,
    exch_ref,
    decay_ref,
    raw,
    sems,
):
    moves = [
        (stratum_hbm, stratum_ref),
        (conc_hbm.at[0:2], conc_ref.at[0:2]),
        (por_hbm, por_ref),
        (disp_hbm, disp_ref),
        (trans_hbm, trans_ref),
        (exch_hbm, exch_ref),
        (decay_hbm, decay_ref),
        (conc_hbm.at[2:4], conc_ref.at[2:4]),
    ]
    copies = [pltpu.make_async_copy(src, dst, sems.at[k]) for k, (src, dst) in enumerate(moves)]
    for copy in copies:
        copy.start()
    raw[...] = jnp.full(raw.shape, 0.5, jnp.float32)
    for copy in copies[2:7]:
        copy.wait()
    strata = por_ref.shape[1]
    raw[0:1, 0:strata] = por_ref[...]
    raw[1:3, 0:strata] = disp_ref[...]
    raw[3:4, 0:strata] = trans_ref[...]
    raw[4:5, 0:strata] = exch_ref[...]
    raw[5:6, 0:strata] = decay_ref[...]
    made = derive(*[raw[k : k + 1, :] for k in range(6)])
    for k, name in enumerate(NUMBERS):
        tab_ref[k : k + 1, :] = made[name]
    tab_ref[len(NUMBERS) : 2 * SUB, :] = raw[0 : 2 * SUB - len(NUMBERS), :]
    copies[0].wait()
    last = stratum_ref.shape[1] - 1
    for ref, y in ((lo_ref, 0), (hi_ref, last)):
        ref[2] = (stratum_ref[:, y, :] + 1).astype(jnp.float32)
    copies[1].wait()
    for ref, y in ((lo_ref, 0), (hi_ref, last)):
        ref[0] = conc_ref[0, :, y, :]
        ref[1] = conc_ref[1, :, y, :]
    copies[7].wait()


def local_kernel(
    tab_ref,
    stratum_ref,
    conc_ref,
    pay_ref,
    edge_ref,
    pass_a_ref,
    drop_a_ref,
    pass_b_ref,
    drop_b_ref,
    over_ref,
    source_a_ref,
    source_b_ref,
    head_a,
    head_b,
    kappa_ref,
    left_a,
    right_a,
    left_b,
    right_b,
    adj_l,
    adj_r,
):
    n, planes_y, planes_z = stratum_ref.shape
    number = Numbers(tab_ref)

    cond_a = cond_b = half_a = half_b = through_a = through_b = None
    for i in range(n):
        index = stratum_ref[i]
        shunt_a, shunt_b = number("shunt_a", index), number("shunt_b", index)
        new_a, new_b = number("half_a", index), number("half_b", index)
        kappa_ref[i] = number("kappa", index)
        if i == 0:
            first_half_a, first_half_b = new_a, new_b
            cond_a, cond_b = shunt_a, shunt_b
            through_a = through_b = jnp.ones_like(shunt_a)
        else:
            face_a, face_b = half_a + new_a, half_b + new_b
            pass_a, pass_b = recip(1.0 + face_a * cond_a), recip(1.0 + face_b * cond_b)
            cond_a, cond_b = shunt_a + cond_a * pass_a, shunt_b + cond_b * pass_b
            pass_a_ref[i], pass_b_ref[i] = pass_a, pass_b
            drop_a_ref[i], drop_b_ref[i] = face_a * pass_a, face_b * pass_b
            through_a, through_b = through_a * pass_a, through_b * pass_b
        head_a[i], head_b[i] = through_a, through_b
        half_a, half_b = new_a, new_b
    over_a, over_b = recip(cond_a), recip(cond_b)
    over_ref[0], over_ref[1] = over_a, over_b

    r_a, r_b = over_a, over_b
    l_a, l_b = through_a * over_a, through_b * over_b
    couple = [None] * 4
    for i in reversed(range(n)):
        if i < n - 1:
            pass_a, pass_b = pass_a_ref[i + 1], pass_b_ref[i + 1]
            l_a = pass_a * l_a + drop_a_ref[i + 1] * head_a[i]
            l_b = pass_b * l_b + drop_b_ref[i + 1] * head_b[i]
            r_a, r_b = pass_a * r_a, pass_b * r_b
        left_a[i], right_a[i], left_b[i], right_b[i] = l_a, r_a, l_b, r_b
        kappa = kappa_ref[i]
        k_l, k_r = kappa * l_a, kappa * r_a
        terms = [l_b * k_l, l_b * k_r, r_b * k_l, r_b * k_r]
        couple = [t if c is None else c + t for c, t in zip(couple, terms)]

    g_l = g_r = None
    for i in range(n):
        kappa = kappa_ref[i]
        s_l, s_r = kappa * left_b[i], kappa * right_b[i]
        if i > 0:
            pass_a = pass_a_ref[i]
            s_l, s_r = s_l + pass_a * g_l, s_r + pass_a * g_r
        g_l, g_r = s_l, s_r
        adj_l[i], adj_r[i] = g_l, g_r

    lane = lax.broadcasted_iota(jnp.int32, (planes_y, planes_z), 1)
    line = lax.broadcasted_iota(jnp.int32, (planes_y, planes_z), 0)
    inside = (line < planes_y - 1, lane < planes_z - 1)
    w_l, w_r = adj_l[n - 1] * over_a, adj_r[n - 1] * over_a
    free = [None] * 4
    for i in reversed(range(n)):
        if i < n - 1:
            pass_a, drop_a = pass_a_ref[i + 1], drop_a_ref[i + 1]
            w_l, w_r = pass_a * w_l + drop_a * adj_l[i], pass_a * w_r + drop_a * adj_r[i]
        adj_l[i], adj_r[i] = w_l, w_r
        index = stratum_ref[i]
        half_t = number("half_t", index)
        por = number("por", index)
        c0, c1, c2, c3 = [conc_ref[k, i] for k in range(4)]
        source_a = por * c0 + number("alpha_a", index) * c2
        source_b = (
            por * c1
            + number("alpha_b", index) * c3
            + number("delta", index) * c2
        )
        for axis in (0, 1):
            last = half_t.shape[axis] - 1
            face = jnp.where(
                inside[axis], recip(half_t + pltpu.roll(half_t, last, axis)), 0.0
            )
            flow_a = face * shifted_difference(c0, axis)
            flow_b = face * shifted_difference(c1, axis)
            source_a = source_a + (flow_a - pltpu.roll(flow_a, 1, axis))
            source_b = source_b + (flow_b - pltpu.roll(flow_b, 1, axis))
        source_a_ref[i], source_b_ref[i] = source_a, source_b
        terms = [
            left_a[i] * source_a,
            right_a[i] * source_a,
            left_b[i] * source_b + w_l * source_a,
            right_b[i] * source_b + w_r * source_a,
        ]
        free = [t if f is None else f + t for f, t in zip(free, terms)]

    quantities = [
        left_a[0] + first_half_a,
        right_a[0],
        over_a + half_a,
        left_b[0] + first_half_b,
        right_b[0],
        over_b + half_b,
        *couple,
        *free,
    ]
    for q, value in enumerate(quantities):
        pay_ref[q] = value
    for k, ref in enumerate((left_a, right_a, left_b, right_b, adj_l, adj_r)):
        edge_ref[0, k] = ref[:, 0, :]
        edge_ref[1, k] = ref[:, planes_y - 1, :]


def side_of(axis, stride):
    return (lax.axis_index(axis) // stride) % 2 == 1


def border_kernel(
    tab_ref,
    own_lo_ref,
    own_hi_ref,
    next_lo_ref,
    next_hi_ref,
    edge_ref,
    pay_ref,
    keep_ref,
    send_ref,
    flow_ref,
):
    number = Numbers(tab_ref)
    half = pay_ref.shape[1] // 2
    second = side_of("flow", 1)
    low, high = pay_ref[:, :half], pay_ref[:, half:]
    keep_ref[...] = jnp.where(second, high, low)
    send_ref[...] = jnp.where(second, low, high)
    for side, (own_ref, next_ref) in enumerate(
        ((own_lo_ref, next_lo_ref), (own_hi_ref, next_hi_ref))
    ):
        own_id = own_ref[2].astype(jnp.int32) - 1
        next_id = next_ref[2].astype(jnp.int32) - 1
        present = next_id >= 0
        resist = number("half_t", own_id) + number("half_t", jnp.maximum(next_id, 0))
        face = jnp.where(present, recip(resist), 0.0)
        flow_a = face * (next_ref[0] - own_ref[0])
        flow_b = face * (next_ref[1] - own_ref[1])
        flow_ref[side, 0], flow_ref[side, 1] = flow_a, flow_b
        l_a, r_a, l_b, r_b, w_l, w_r = [edge_ref[side, k] for k in range(6)]
        changes = {
            FA_L: l_a * flow_a,
            FA_R: r_a * flow_a,
            FB_L: l_b * flow_b + w_l * flow_a,
            FB_R: r_b * flow_b + w_r * flow_a,
        }
        row = 0 if side == 0 else half - 1
        kept = second if side == 1 else jnp.logical_not(second)
        for q, change in changes.items():
            total = jnp.sum(change, axis=0, keepdims=True)
            keep_ref[q, row : row + 1, :] += jnp.where(kept, total, 0.0)
            send_ref[q, row : row + 1, :] += jnp.where(kept, 0.0, total)


FACE_L = (ZA_LL, ZB_LL, C_LL, FA_L, FB_L)
FACE_R = (ZA_RR, ZB_RR, C_RR, FA_R, FB_R)
KEPT = 8


def merge(one, two):
    over_a = recip(one[ZA_RR] + two[ZA_LL])
    over_b = recip(one[ZB_RR] + two[ZB_LL])
    across = one[C_RR] + two[C_LL]
    free_a = over_a * (one[FA_R] - two[FA_L])
    from_l, from_r = over_a * one[ZA_LR], over_a * two[ZA_LR]
    free_b = over_b * (one[FB_R] - two[FB_L] - across * free_a)
    from_l_b, from_r_b = over_b * one[ZB_LR], over_b * two[ZB_LR]
    cross_l = over_b * (one[C_RL] - across * from_l)
    cross_r = over_b * (two[C_LR] - across * from_r)
    merged = {
        ZA_LL: one[ZA_LL] - one[ZA_LR] * from_l,
        ZA_LR: one[ZA_LR] * from_r,
        ZA_RR: two[ZA_RR] - two[ZA_LR] * from_r,
        ZB_LL: one[ZB_LL] - one[ZB_LR] * from_l_b,
        ZB_LR: one[ZB_LR] * from_r_b,
        ZB_RR: two[ZB_RR] - two[ZB_LR] * from_r_b,
        C_LL: one[C_LL] - one[ZB_LR] * cross_l - one[C_LR] * from_l,
        C_LR: one[ZB_LR] * cross_r + one[C_LR] * from_r,
        C_RL: two[ZB_LR] * cross_l + two[C_RL] * from_l,
        C_RR: two[C_RR] - two[ZB_LR] * cross_r - two[C_RL] * from_r,
        FA_L: one[FA_L] - one[ZA_LR] * free_a,
        FA_R: two[FA_R] + two[ZA_LR] * free_a,
        FB_L: one[FB_L] - one[ZB_LR] * free_b - one[C_LR] * free_a,
        FB_R: two[FB_R] + two[ZB_LR] * free_b + two[C_RL] * free_a,
    }
    return merged, (free_a, from_l, from_r, free_b, from_l_b, from_r_b, cross_l, cross_r)


def between(kept, ends):
    free_a, from_l, from_r, free_b, from_l_b, from_r_b, cross_l, cross_r = kept
    l_a, r_a, l_b, r_b = ends
    middle_a = free_a + from_l * l_a - from_r * r_a
    middle_b = free_b + from_l_b * l_b - from_r_b * r_b + cross_l * l_a - cross_r * r_a
    return middle_a, middle_b


def merge_kernel(stride, last, own_ref, other_ref, out_ref, kept_ref, *face_ref):
    second = side_of("flow", stride)
    own = [own_ref[q] for q in range(QUANTITIES)]
    other = [other_ref[q] for q in range(QUANTITIES)]
    one = [jnp.where(second, b, a) for a, b in zip(own, other)]
    two = [jnp.where(second, a, b) for a, b in zip(own, other)]
    merged, kept = merge(one, two)
    for q, value in merged.items():
        out_ref[q] = value
    for k, value in enumerate(kept):
        kept_ref[k] = value
    if last:
        after = side_of("flow", 2 * stride)
        for k, (l, r) in enumerate(zip(FACE_L, FACE_R)):
            face_ref[0][k] = jnp.where(after, merged[l], merged[r])


def close_kernel(strides, own_ref, other_ref, *refs):
    kept_refs, mine_ref, send_ref = refs[:-2], refs[-2], refs[-1]
    stride = strides[-1]
    second = side_of("flow", stride)
    own = [jnp.where(second, own_ref[l], own_ref[r]) for l, r in zip(FACE_L, FACE_R)]
    z_a, z_b, couple, f_a, f_b = [own[k] + other_ref[k] for k in range(3)] + [
        jnp.where(second, other_ref[k] - own[k], own[k] - other_ref[k]) for k in (3, 4)
    ]
    current_a = recip(z_a) * f_a
    current_b = recip(z_b) * (f_b - couple * current_a)
    nothing = jnp.zeros_like(current_a)

    def side_ends(after, middle_a, middle_b, ends):
        l_a, r_a, l_b, r_b = ends
        return (
            jnp.where(after, middle_a, l_a),
            jnp.where(after, r_a, -middle_a),
            jnp.where(after, middle_b, l_b),
            jnp.where(after, r_b, -middle_b),
        )

    ends = side_ends(second, current_a, current_b, (nothing,) * 4)
    for stride, kept_ref in reversed(list(zip(strides[:-1], kept_refs))):
        middle_a, middle_b = between([kept_ref[k] for k in range(KEPT)], ends)
        after = side_of("flow", stride)
        if stride == 1:
            other_ends = side_ends(jnp.logical_not(after), middle_a, middle_b, ends)
            for q, value in enumerate(other_ends):
                send_ref[q] = value
        ends = side_ends(after, middle_a, middle_b, ends)
    for q, value in enumerate(ends):
        mine_ref[q] = value


def final_kernel(
    tab_ref,
    stratum_ref,
    conc_ref,
    pass_a_ref,
    drop_a_ref,
    pass_b_ref,
    drop_b_ref,
    over_ref,
    source_a_ref,
    source_b_ref,
    flow_ref,
    mine_ref,
    current_ref,
    out_ref,
    gather_a,
    gather_b,
):
    n, planes_y, planes_z = stratum_ref.shape
    number = Numbers(tab_ref)

    second = side_of("flow", 1)

    def plane(q):
        mine, other = mine_ref[q], current_ref[q]
        halves = [jnp.where(second, other, mine), jnp.where(second, mine, other)]
        return jnp.concatenate(halves, axis=0)

    line = lax.broadcasted_iota(jnp.int32, (planes_y, planes_z), 0)
    first_line, last_line = line == 0, line == planes_y - 1

    def with_border(source, component, i):
        low = jnp.broadcast_to(flow_ref[0, component, i : i + 1, :], source.shape)
        high = jnp.broadcast_to(flow_ref[1, component, i : i + 1, :], source.shape)
        return source + jnp.where(first_line, low, jnp.where(last_line, high, 0.0))

    value = plane(0)
    for i in range(n):
        value = with_border(source_a_ref[i], 0, i) + value
        if i < n - 1:
            gather_a[i] = value
            value = pass_a_ref[i + 1] * value
    x = (value + plane(1)) * over_ref[0]
    for i in reversed(range(n)):
        if i < n - 1:
            x = pass_a_ref[i + 1] * x + drop_a_ref[i + 1] * gather_a[i]
        out_ref[0, i] = x
    value = plane(2)
    for i in range(n):
        kappa = number("kappa", stratum_ref[i])
        value = with_border(source_b_ref[i], 1, i) + kappa * out_ref[0, i] + value
        if i < n - 1:
            gather_b[i] = value
            value = pass_b_ref[i + 1] * value
    x = (value + plane(3)) * over_ref[1]
    for i in reversed(range(n)):
        if i < n - 1:
            x = pass_b_ref[i + 1] * x + drop_b_ref[i + 1] * gather_b[i]
        out_ref[1, i] = x
        index = stratum_ref[i]
        x2 = (
            number("beta", index) * conc_ref[2, i]
            + number("gamma", index) * out_ref[0, i]
        )
        out_ref[2, i] = x2
        out_ref[3, i] = (
            number("free_b", index) * conc_ref[3, i]
            + number("share_b", index) * x
            + number("decay_b", index) * x2
        )


def call(kernel, outs, scratch=()):
    return pl.pallas_call(
        kernel,
        out_shape=[jax.ShapeDtypeStruct(shape, jnp.float32) for shape in outs],
        scratch_shapes=[pltpu.VMEM(shape, jnp.float32) for shape in scratch],
        compiler_params=pltpu.CompilerParams(vmem_limit_bytes=VMEM_LIMIT),
    )


def per_device(
    concentration,
    stratum,
    porosity,
    dispersion_table,
    transverse_table,
    exchange_table,
    decay_table,
):
    n, planes_y, planes_z = stratum.shape
    peers = lax.axis_size("flow")
    half = planes_y // 2
    strides = [1 << k for k in range(peers.bit_length() - 1)]
    cells = (n, planes_y, planes_z)

    halo = (3, n, planes_z)
    strata = porosity.shape[0]
    hbm = pl.BlockSpec(memory_space=pltpu.HBM)
    own_lo, own_hi, table, concentration, stratum = pl.pallas_call(
        pack_kernel,
        out_shape=[
            jax.ShapeDtypeStruct(halo, jnp.float32),
            jax.ShapeDtypeStruct(halo, jnp.float32),
            jax.ShapeDtypeStruct((2 * SUB, LANE), jnp.float32),
            jax.ShapeDtypeStruct(concentration.shape, jnp.float32),
            jax.ShapeDtypeStruct(cells, jnp.int32),
        ],
        in_specs=[hbm] * 7,
        scratch_shapes=[
            pltpu.VMEM((1, strata), jnp.float32),
            pltpu.VMEM((2, strata), jnp.float32),
            pltpu.VMEM((1, strata), jnp.float32),
            pltpu.VMEM((1, strata), jnp.float32),
            pltpu.VMEM((1, strata), jnp.float32),
            pltpu.VMEM((SUB, LANE), jnp.float32),
            pltpu.SemaphoreType.DMA((8,)),
        ],
        compiler_params=pltpu.CompilerParams(vmem_limit_bytes=VMEM_LIMIT),
    )(
        *[
            pltpu.with_memory_space_constraint(value, pltpu.HBM)
            for value in (
                concentration,
                stratum,
                porosity[None],
                dispersion_table.T,
                transverse_table[None],
                exchange_table[None],
                decay_table[None],
            )
        ]
    )
    groups = lax.axis_size("trans")
    up = [(i, i + 1) for i in range(groups - 1)]
    down = [(i + 1, i) for i in range(groups - 1)]
    next_lo = lax.ppermute(own_hi, "trans", up)
    next_hi = lax.ppermute(own_lo, "trans", down)

    def exchange(value, stride):
        return lax.ppermute(value, "flow", [(i, i ^ stride) for i in range(peers)])

    pay, edge, pass_a, drop_a, pass_b, drop_b, over, source_a, source_b = call(
        local_kernel,
        [
            (QUANTITIES, planes_y, planes_z),
            (2, 6, n, planes_z),
            *[cells] * 4,
            (2, planes_y, planes_z),
            *[cells] * 2,
        ],
        [cells] * 9,
    )(table, stratum, concentration)
    block_shape = (QUANTITIES, half, planes_z)
    block, send, flow = call(border_kernel, [block_shape, block_shape, (2, 2, n, planes_z)])(
        table, own_lo, own_hi, next_lo, next_hi, edge, pay
    )
    kept = []
    for stride in strides[:-1]:
        other = exchange(send, stride)
        last = stride == strides[-2]
        block, keep, *face = call(
            functools.partial(merge_kernel, stride, last),
            [block_shape, (KEPT, half, planes_z)] + [(5, half, planes_z)] * last,
        )(block, other)
        kept.append(keep)
        send = face[0] if last else block
    ends_shape = (CURRENTS, half, planes_z)
    mine, send = call(functools.partial(close_kernel, strides), [ends_shape, ends_shape])(
        block, exchange(send, strides[-1]), *kept
    )
    currents = exchange(send, 1)
    (out,) = call(final_kernel, [(4,) + cells], [cells] * 2)(
        table,
        stratum,
        concentration,
        pass_a,
        drop_a,
        pass_b,
        drop_b,
        over,
        source_a,
        source_b,
        flow,
        mine,
        currents,
    )
    return out


def solution(mesh):
    in_specs = (P(None, "flow", "trans", None), P("flow", "trans", None), P(), P(), P(), P(), P())
    out_specs = P(None, "flow", "trans", None)
    return jax.shard_map(
        per_device, mesh=mesh, in_specs=in_specs, out_specs=out_specs, check_vma=False
    )
```

```python
import functools

import jax
import jax.numpy as jnp
from jax import lax
from jax.experimental import pallas as pl
from jax.experimental.pallas import tpu as pltpu
from jax.sharding import PartitionSpec as P

SUB, LANE = 8, 128
ZA_LL, ZA_LR, ZA_RR, ZB_LL, ZB_LR, ZB_RR, C_LL, C_LR, C_RL, C_RR, FA_L, FA_R, FB_L, FB_R = range(14)
QUANTITIES = 14
CURRENTS = 4
VMEM_LIMIT = 40 * 1024 * 1024


def recip(x):
    return 1.0 / x


def lookup(row, index):
    tiles = []
    for y in range(0, index.shape[0], SUB):
        across = [
            jnp.take_along_axis(
                row, index[y : y + SUB, z : z + LANE], axis=1, mode="promise_in_bounds"
            )
            for z in range(0, index.shape[1], LANE)
        ]
        tiles.append(jnp.concatenate(across, axis=1))
    return jnp.concatenate(tiles, axis=0)


NUMBERS = (
    "por",
    "shunt_a",
    "shunt_b",
    "half_a",
    "half_b",
    "half_t",
    "beta",
    "gamma",
    "alpha_a",
    "alpha_b",
    "kappa",
    "delta",
    "free_b",
    "share_b",
    "decay_b",
)


def derive(por, disp_a, disp_b, trans, exch, decay):
    immobile = 1.0 - por
    over_a = 1.0 / (immobile + exch + decay)
    over_b = 1.0 / (immobile + exch)
    beta = immobile * over_a
    gamma = exch * over_a
    share_b = exch * over_b
    return dict(
        por=por,
        shunt_a=por + decay + exch * (immobile + decay) * over_a,
        shunt_b=por + exch * immobile * over_b,
        half_a=0.5 / disp_a,
        half_b=0.5 / disp_b,
        half_t=0.5 / trans,
        beta=beta,
        gamma=gamma,
        alpha_a=exch * beta,
        alpha_b=share_b * immobile,
        kappa=decay + share_b * decay * gamma,
        delta=share_b * decay * beta,
        free_b=immobile * over_b,
        share_b=share_b,
        decay_b=decay * over_b,
    )


class Numbers:
    def __init__(self, tab_ref):
        self.tab_ref = tab_ref

    def __call__(self, name, index):
        k = NUMBERS.index(name)
        row = jnp.broadcast_to(self.tab_ref[k : k + 1, :], (SUB, LANE))
        return lookup(row, index)


def shifted_difference(value, axis):
    return pltpu.roll(value, value.shape[axis] - 1, axis) - value


def side_of(axis, stride):
    return (lax.axis_index(axis) // stride) % 2 == 1


def pack_kernel(
    conc_hbm,
    stratum_hbm,
    por_hbm,
    disp_hbm,
    trans_hbm,
    exch_hbm,
    decay_hbm,
    early_ref,
    late_ref,
    tab_ref,
    conc_ref,
    stratum_ref,
    por_ref,
    disp_ref,
    trans_ref,
    exch_ref,
    decay_ref,
    raw,
    sems,
):
    moves = [
        (stratum_hbm, stratum_ref),
        (conc_hbm.at[0:2], conc_ref.at[0:2]),
        (por_hbm, por_ref),
        (disp_hbm, disp_ref),
        (trans_hbm, trans_ref),
        (exch_hbm, exch_ref),
        (decay_hbm, decay_ref),
        (conc_hbm.at[2:4], conc_ref.at[2:4]),
    ]
    copies = [pltpu.make_async_copy(src, dst, sems.at[k]) for k, (src, dst) in enumerate(moves)]
    for copy in copies:
        copy.start()
    raw[...] = jnp.full(raw.shape, 0.5, jnp.float32)
    for copy in copies[2:7]:
        copy.wait()
    strata = por_ref.shape[1]
    raw[0:1, 0:strata] = por_ref[...]
    raw[1:3, 0:strata] = disp_ref[...]
    raw[3:4, 0:strata] = trans_ref[...]
    raw[4:5, 0:strata] = exch_ref[...]
    raw[5:6, 0:strata] = decay_ref[...]
    made = derive(*[raw[k : k + 1, :] for k in range(6)])
    for k, name in enumerate(NUMBERS):
        tab_ref[k : k + 1, :] = made[name]
    tab_ref[len(NUMBERS) : 2 * SUB, :] = raw[0 : 2 * SUB - len(NUMBERS), :]
    odd = side_of("trans", 1)
    last = stratum_ref.shape[1] - 1

    def put(k, low, high):
        early_ref[k] = jnp.where(odd, low, high)
        late_ref[k] = jnp.where(odd, high, low)

    copies[0].wait()
    numbered = [(stratum_ref[:, y, :] + 1).astype(jnp.float32) for y in (0, last)]
    put(2, *numbered)
    copies[1].wait()
    for k in (0, 1):
        put(k, conc_ref[k, :, 0, :], conc_ref[k, :, last, :])
    copies[7].wait()


def local_kernel(
    tab_ref,
    stratum_ref,
    conc_ref,
    pay_ref,
    edge_ref,
    pass_a_ref,
    drop_a_ref,
    pass_b_ref,
    drop_b_ref,
    over_ref,
    source_a_ref,
    source_b_ref,
    head_a,
    head_b,
    kappa_ref,
    left_a,
    right_a,
    left_b,
    right_b,
    adj_l,
    adj_r,
):
    n, planes_y, planes_z = stratum_ref.shape
    number = Numbers(tab_ref)

    cond_a = cond_b = half_a = half_b = through_a = through_b = None
    for i in range(n):
        index = stratum_ref[i]
        shunt_a, shunt_b = number("shunt_a", index), number("shunt_b", index)
        new_a, new_b = number("half_a", index), number("half_b", index)
        kappa_ref[i] = number("kappa", index)
        if i == 0:
            first_half_a, first_half_b = new_a, new_b
            cond_a, cond_b = shunt_a, shunt_b
            through_a = through_b = jnp.ones_like(shunt_a)
        else:
            face_a, face_b = half_a + new_a, half_b + new_b
            pass_a, pass_b = recip(1.0 + face_a * cond_a), recip(1.0 + face_b * cond_b)
            cond_a, cond_b = shunt_a + cond_a * pass_a, shunt_b + cond_b * pass_b
            pass_a_ref[i], pass_b_ref[i] = pass_a, pass_b
            drop_a_ref[i], drop_b_ref[i] = face_a * pass_a, face_b * pass_b
            through_a, through_b = through_a * pass_a, through_b * pass_b
        head_a[i], head_b[i] = through_a, through_b
        half_a, half_b = new_a, new_b
    over_a, over_b = recip(cond_a), recip(cond_b)
    over_ref[0], over_ref[1] = over_a, over_b

    r_a, r_b = over_a, over_b
    l_a, l_b = through_a * over_a, through_b * over_b
    couple = [None] * 4
    for i in reversed(range(n)):
        if i < n - 1:
            pass_a, pass_b = pass_a_ref[i + 1], pass_b_ref[i + 1]
            l_a = pass_a * l_a + drop_a_ref[i + 1] * head_a[i]
            l_b = pass_b * l_b + drop_b_ref[i + 1] * head_b[i]
            r_a, r_b = pass_a * r_a, pass_b * r_b
        left_a[i], right_a[i], left_b[i], right_b[i] = l_a, r_a, l_b, r_b
        kappa = kappa_ref[i]
        k_l, k_r = kappa * l_a, kappa * r_a
        terms = [l_b * k_l, l_b * k_r, r_b * k_l, r_b * k_r]
        couple = [t if c is None else c + t for c, t in zip(couple, terms)]

    g_l = g_r = None
    for i in range(n):
        kappa = kappa_ref[i]
        s_l, s_r = kappa * left_b[i], kappa * right_b[i]
        if i > 0:
            pass_a = pass_a_ref[i]
            s_l, s_r = s_l + pass_a * g_l, s_r + pass_a * g_r
        g_l, g_r = s_l, s_r
        adj_l[i], adj_r[i] = g_l, g_r

    lane = lax.broadcasted_iota(jnp.int32, (planes_y, planes_z), 1)
    line = lax.broadcasted_iota(jnp.int32, (planes_y, planes_z), 0)
    inside = (line < planes_y - 1, lane < planes_z - 1)
    w_l, w_r = adj_l[n - 1] * over_a, adj_r[n - 1] * over_a
    free = [None] * 4
    for i in reversed(range(n)):
        if i < n - 1:
            pass_a, drop_a = pass_a_ref[i + 1], drop_a_ref[i + 1]
            w_l, w_r = pass_a * w_l + drop_a * adj_l[i], pass_a * w_r + drop_a * adj_r[i]
        adj_l[i], adj_r[i] = w_l, w_r
        index = stratum_ref[i]
        half_t = number("half_t", index)
        por = number("por", index)
        c0, c1, c2, c3 = [conc_ref[k, i] for k in range(4)]
        source_a = por * c0 + number("alpha_a", index) * c2
        source_b = (
            por * c1
            + number("alpha_b", index) * c3
            + number("delta", index) * c2
        )
        for axis in (0, 1):
            last = half_t.shape[axis] - 1
            face = jnp.where(
                inside[axis], recip(half_t + pltpu.roll(half_t, last, axis)), 0.0
            )
            flow_a = face * shifted_difference(c0, axis)
            flow_b = face * shifted_difference(c1, axis)
            source_a = source_a + (flow_a - pltpu.roll(flow_a, 1, axis))
            source_b = source_b + (flow_b - pltpu.roll(flow_b, 1, axis))
        source_a_ref[i], source_b_ref[i] = source_a, source_b
        terms = [
            left_a[i] * source_a,
            right_a[i] * source_a,
            left_b[i] * source_b + w_l * source_a,
            right_b[i] * source_b + w_r * source_a,
        ]
        free = [t if f is None else f + t for f, t in zip(free, terms)]

    quantities = [
        left_a[0] + first_half_a,
        right_a[0],
        over_a + half_a,
        left_b[0] + first_half_b,
        right_b[0],
        over_b + half_b,
        *couple,
        *free,
    ]
    for q, value in enumerate(quantities):
        pay_ref[q] = value
    for k, ref in enumerate((left_a, right_a, left_b, right_b, adj_l, adj_r)):
        edge_ref[0, k] = ref[:, 0, :]
        edge_ref[1, k] = ref[:, planes_y - 1, :]


def border_kernel(
    tab_ref,
    early_ref,
    late_ref,
    beyond_early_ref,
    beyond_late_ref,
    edge_ref,
    pay_ref,
    keep_ref,
    send_ref,
    flow_ref,
):
    number = Numbers(tab_ref)
    half = pay_ref.shape[1] // 2
    second = side_of("flow", 1)
    low, high = pay_ref[:, :half], pay_ref[:, half:]
    keep_ref[...] = jnp.where(second, high, low)
    send_ref[...] = jnp.where(second, low, high)
    odd = side_of("trans", 1)
    for side in range(2):
        early = odd if side == 0 else jnp.logical_not(odd)
        own = jnp.where(early, early_ref[...], late_ref[...])
        beyond = jnp.where(early, beyond_early_ref[...], beyond_late_ref[...])
        own_id = own[2].astype(jnp.int32) - 1
        next_id = beyond[2].astype(jnp.int32) - 1
        present = next_id >= 0
        resist = number("half_t", own_id) + number("half_t", jnp.maximum(next_id, 0))
        face = jnp.where(present, recip(resist), 0.0)
        flow_a = face * (beyond[0] - own[0])
        flow_b = face * (beyond[1] - own[1])
        flow_ref[side, 0], flow_ref[side, 1] = flow_a, flow_b
        l_a, r_a, l_b, r_b, w_l, w_r = [edge_ref[side, k] for k in range(6)]
        changes = {
            FA_L: l_a * flow_a,
            FA_R: r_a * flow_a,
            FB_L: l_b * flow_b + w_l * flow_a,
            FB_R: r_b * flow_b + w_r * flow_a,
        }
        row = 0 if side == 0 else half - 1
        kept = second if side == 1 else jnp.logical_not(second)
        for q, change in changes.items():
            total = jnp.sum(change, axis=0, keepdims=True)
            keep_ref[q, row : row + 1, :] += jnp.where(kept, total, 0.0)
            send_ref[q, row : row + 1, :] += jnp.where(kept, 0.0, total)


FACE_L = (ZA_LL, ZB_LL, C_LL, FA_L, FB_L)
FACE_R = (ZA_RR, ZB_RR, C_RR, FA_R, FB_R)
KEPT = 8


def merge(one, two):
    over_a = recip(one[ZA_RR] + two[ZA_LL])
    over_b = recip(one[ZB_RR] + two[ZB_LL])
    across = one[C_RR] + two[C_LL]
    free_a = over_a * (one[FA_R] - two[FA_L])
    from_l, from_r = over_a * one[ZA_LR], over_a * two[ZA_LR]
    free_b = over_b * (one[FB_R] - two[FB_L] - across * free_a)
    from_l_b, from_r_b = over_b * one[ZB_LR], over_b * two[ZB_LR]
    cross_l = over_b * (one[C_RL] - across * from_l)
    cross_r = over_b * (two[C_LR] - across * from_r)
    merged = {
        ZA_LL: one[ZA_LL] - one[ZA_LR] * from_l,
        ZA_LR: one[ZA_LR] * from_r,
        ZA_RR: two[ZA_RR] - two[ZA_LR] * from_r,
        ZB_LL: one[ZB_LL] - one[ZB_LR] * from_l_b,
        ZB_LR: one[ZB_LR] * from_r_b,
        ZB_RR: two[ZB_RR] - two[ZB_LR] * from_r_b,
        C_LL: one[C_LL] - one[ZB_LR] * cross_l - one[C_LR] * from_l,
        C_LR: one[ZB_LR] * cross_r + one[C_LR] * from_r,
        C_RL: two[ZB_LR] * cross_l + two[C_RL] * from_l,
        C_RR: two[C_RR] - two[ZB_LR] * cross_r - two[C_RL] * from_r,
        FA_L: one[FA_L] - one[ZA_LR] * free_a,
        FA_R: two[FA_R] + two[ZA_LR] * free_a,
        FB_L: one[FB_L] - one[ZB_LR] * free_b - one[C_LR] * free_a,
        FB_R: two[FB_R] + two[ZB_LR] * free_b + two[C_RL] * free_a,
    }
    return merged, (free_a, from_l, from_r, free_b, from_l_b, from_r_b, cross_l, cross_r)


def between(kept, ends):
    free_a, from_l, from_r, free_b, from_l_b, from_r_b, cross_l, cross_r = kept
    l_a, r_a, l_b, r_b = ends
    middle_a = free_a + from_l * l_a - from_r * r_a
    middle_b = free_b + from_l_b * l_b - from_r_b * r_b + cross_l * l_a - cross_r * r_a
    return middle_a, middle_b


def merge_kernel(stride, last, own_ref, other_ref, out_ref, kept_ref, *face_ref):
    second = side_of("flow", stride)
    own = [own_ref[q] for q in range(QUANTITIES)]
    other = [other_ref[q] for q in range(QUANTITIES)]
    one = [jnp.where(second, b, a) for a, b in zip(own, other)]
    two = [jnp.where(second, a, b) for a, b in zip(own, other)]
    merged, kept = merge(one, two)
    for q, value in merged.items():
        out_ref[q] = value
    for k, value in enumerate(kept):
        kept_ref[k] = value
    if last:
        after = side_of("flow", 2 * stride)
        for k, (l, r) in enumerate(zip(FACE_L, FACE_R)):
            face_ref[0][k] = jnp.where(after, merged[l], merged[r])


def close_kernel(strides, own_ref, other_ref, *refs):
    kept_refs, mine_ref, send_ref = refs[:-2], refs[-2], refs[-1]
    stride = strides[-1]
    second = side_of("flow", stride)
    own = [jnp.where(second, own_ref[l], own_ref[r]) for l, r in zip(FACE_L, FACE_R)]
    z_a, z_b, couple, f_a, f_b = [own[k] + other_ref[k] for k in range(3)] + [
        jnp.where(second, other_ref[k] - own[k], own[k] - other_ref[k]) for k in (3, 4)
    ]
    current_a = recip(z_a) * f_a
    current_b = recip(z_b) * (f_b - couple * current_a)
    nothing = jnp.zeros_like(current_a)

    def side_ends(after, middle_a, middle_b, ends):
        l_a, r_a, l_b, r_b = ends
        return (
            jnp.where(after, middle_a, l_a),
            jnp.where(after, r_a, -middle_a),
            jnp.where(after, middle_b, l_b),
            jnp.where(after, r_b, -middle_b),
        )

    ends = side_ends(second, current_a, current_b, (nothing,) * 4)
    for stride, kept_ref in reversed(list(zip(strides[:-1], kept_refs))):
        middle_a, middle_b = between([kept_ref[k] for k in range(KEPT)], ends)
        after = side_of("flow", stride)
        if stride == 1:
            other_ends = side_ends(jnp.logical_not(after), middle_a, middle_b, ends)
            for q, value in enumerate(other_ends):
                send_ref[q] = value
        ends = side_ends(after, middle_a, middle_b, ends)
    for q, value in enumerate(ends):
        mine_ref[q] = value


def final_kernel(
    tab_ref,
    stratum_ref,
    conc_ref,
    pass_a_ref,
    drop_a_ref,
    pass_b_ref,
    drop_b_ref,
    over_ref,
    source_a_ref,
    source_b_ref,
    flow_ref,
    mine_ref,
    current_ref,
    out_ref,
    gather_a,
    gather_b,
):
    n, planes_y, planes_z = stratum_ref.shape
    number = Numbers(tab_ref)

    second = side_of("flow", 1)

    def plane(q):
        mine, other = mine_ref[q], current_ref[q]
        halves = [jnp.where(second, other, mine), jnp.where(second, mine, other)]
        return jnp.concatenate(halves, axis=0)

    line = lax.broadcasted_iota(jnp.int32, (planes_y, planes_z), 0)
    first_line, last_line = line == 0, line == planes_y - 1

    def with_border(source, component, i):
        low = jnp.broadcast_to(flow_ref[0, component, i : i + 1, :], source.shape)
        high = jnp.broadcast_to(flow_ref[1, component, i : i + 1, :], source.shape)
        return source + jnp.where(first_line, low, jnp.where(last_line, high, 0.0))

    value = plane(0)
    for i in range(n):
        value = with_border(source_a_ref[i], 0, i) + value
        if i < n - 1:
            gather_a[i] = value
            value = pass_a_ref[i + 1] * value
    x = (value + plane(1)) * over_ref[0]
    for i in reversed(range(n)):
        if i < n - 1:
            x = pass_a_ref[i + 1] * x + drop_a_ref[i + 1] * gather_a[i]
        out_ref[0, i] = x
    value = plane(2)
    for i in range(n):
        kappa = number("kappa", stratum_ref[i])
        value = with_border(source_b_ref[i], 1, i) + kappa * out_ref[0, i] + value
        if i < n - 1:
            gather_b[i] = value
            value = pass_b_ref[i + 1] * value
    x = (value + plane(3)) * over_ref[1]
    for i in reversed(range(n)):
        if i < n - 1:
            x = pass_b_ref[i + 1] * x + drop_b_ref[i + 1] * gather_b[i]
        out_ref[1, i] = x
        index = stratum_ref[i]
        x2 = (
            number("beta", index) * conc_ref[2, i]
            + number("gamma", index) * out_ref[0, i]
        )
        out_ref[2, i] = x2
        out_ref[3, i] = (
            number("free_b", index) * conc_ref[3, i]
            + number("share_b", index) * x
            + number("decay_b", index) * x2
        )


def call(kernel, outs, scratch=()):
    return pl.pallas_call(
        kernel,
        out_shape=[jax.ShapeDtypeStruct(shape, jnp.float32) for shape in outs],
        scratch_shapes=[pltpu.VMEM(shape, jnp.float32) for shape in scratch],
        compiler_params=pltpu.CompilerParams(vmem_limit_bytes=VMEM_LIMIT),
    )


def per_device(
    concentration,
    stratum,
    porosity,
    dispersion_table,
    transverse_table,
    exchange_table,
    decay_table,
):
    n, planes_y, planes_z = stratum.shape
    peers = lax.axis_size("flow")
    half = planes_y // 2
    strides = [1 << k for k in range(peers.bit_length() - 1)]
    cells = (n, planes_y, planes_z)

    halo = (3, n, planes_z)
    strata = porosity.shape[0]
    hbm = pl.BlockSpec(memory_space=pltpu.HBM)
    early, late, table, concentration, stratum = pl.pallas_call(
        pack_kernel,
        out_shape=[
            jax.ShapeDtypeStruct(halo, jnp.float32),
            jax.ShapeDtypeStruct(halo, jnp.float32),
            jax.ShapeDtypeStruct((2 * SUB, LANE), jnp.float32),
            jax.ShapeDtypeStruct(concentration.shape, jnp.float32),
            jax.ShapeDtypeStruct(cells, jnp.int32),
        ],
        in_specs=[hbm] * 7,
        scratch_shapes=[
            pltpu.VMEM((1, strata), jnp.float32),
            pltpu.VMEM((2, strata), jnp.float32),
            pltpu.VMEM((1, strata), jnp.float32),
            pltpu.VMEM((1, strata), jnp.float32),
            pltpu.VMEM((1, strata), jnp.float32),
            pltpu.VMEM((SUB, LANE), jnp.float32),
            pltpu.SemaphoreType.DMA((8,)),
        ],
        compiler_params=pltpu.CompilerParams(vmem_limit_bytes=VMEM_LIMIT),
    )(
        *[
            pltpu.with_memory_space_constraint(value, pltpu.HBM)
            for value in (
                concentration,
                stratum,
                porosity[None],
                dispersion_table.T,
                transverse_table[None],
                exchange_table[None],
                decay_table[None],
            )
        ]
    )
    groups = lax.axis_size("trans")
    def swap(value, start):
        low = range(start, groups - 1, 2)
        pairs = [(i, i + 1) for i in low] + [(i + 1, i) for i in low]
        return lax.ppermute(value, "trans", pairs)

    beyond_early, beyond_late = swap(early, 0), swap(late, 1)

    def exchange(value, stride):
        return lax.ppermute(value, "flow", [(i, i ^ stride) for i in range(peers)])

    pay, edge, pass_a, drop_a, pass_b, drop_b, over, source_a, source_b = call(
        local_kernel,
        [
            (QUANTITIES, planes_y, planes_z),
            (2, 6, n, planes_z),
            *[cells] * 4,
            (2, planes_y, planes_z),
            *[cells] * 2,
        ],
        [cells] * 9,
    )(table, stratum, concentration)
    block_shape = (QUANTITIES, half, planes_z)
    block, send, flow = call(border_kernel, [block_shape, block_shape, (2, 2, n, planes_z)])(
        table, early, late, beyond_early, beyond_late, edge, pay
    )
    kept = []
    for stride in strides[:-1]:
        other = exchange(send, stride)
        last = stride == strides[-2]
        block, keep, *face = call(
            functools.partial(merge_kernel, stride, last),
            [block_shape, (KEPT, half, planes_z)] + [(5, half, planes_z)] * last,
        )(block, other)
        kept.append(keep)
        send = face[0] if last else block
    ends_shape = (CURRENTS, half, planes_z)
    mine, send = call(functools.partial(close_kernel, strides), [ends_shape, ends_shape])(
        block, exchange(send, strides[-1]), *kept
    )
    currents = exchange(send, 1)
    (out,) = call(final_kernel, [(4,) + cells], [cells] * 2)(
        table,
        stratum,
        concentration,
        pass_a,
        drop_a,
        pass_b,
        drop_b,
        over,
        source_a,
        source_b,
        flow,
        mine,
        currents,
    )
    return out


def solution(mesh):
    in_specs = (P(None, "flow", "trans", None), P("flow", "trans", None), P(), P(), P(), P(), P())
    out_specs = P(None, "flow", "trans", None)
    return jax.shard_map(
        per_device, mesh=mesh, in_specs=in_specs, out_specs=out_specs, check_vma=False
    )
```

```python
import functools

import jax
import jax.numpy as jnp
from jax import lax
from jax.experimental import pallas as pl
from jax.experimental.pallas import tpu as pltpu
from jax.sharding import PartitionSpec as P

SUB, LANE = 8, 128
ZA_LL, ZA_LR, ZA_RR, ZB_LL, ZB_LR, ZB_RR, C_LL, C_LR, C_RL, C_RR, FA_L, FA_R, FB_L, FB_R = range(14)
QUANTITIES = 14
CURRENTS = 4
VMEM_LIMIT = 40 * 1024 * 1024


def recip(x):
    return 1.0 / x


def lookup(row, index):
    tiles = []
    for y in range(0, index.shape[0], SUB):
        across = [
            jnp.take_along_axis(
                row, index[y : y + SUB, z : z + LANE], axis=1, mode="promise_in_bounds"
            )
            for z in range(0, index.shape[1], LANE)
        ]
        tiles.append(jnp.concatenate(across, axis=1))
    return jnp.concatenate(tiles, axis=0)


NUMBERS = (
    "por",
    "shunt_a",
    "shunt_b",
    "half_a",
    "half_b",
    "half_t",
    "beta",
    "gamma",
    "alpha_a",
    "alpha_b",
    "kappa",
    "delta",
    "free_b",
    "share_b",
    "decay_b",
)


def derive(por, disp_a, disp_b, trans, exch, decay):
    immobile = 1.0 - por
    over_a = 1.0 / (immobile + exch + decay)
    over_b = 1.0 / (immobile + exch)
    beta = immobile * over_a
    gamma = exch * over_a
    share_b = exch * over_b
    return dict(
        por=por,
        shunt_a=por + decay + exch * (immobile + decay) * over_a,
        shunt_b=por + exch * immobile * over_b,
        half_a=0.5 / disp_a,
        half_b=0.5 / disp_b,
        half_t=0.5 / trans,
        beta=beta,
        gamma=gamma,
        alpha_a=exch * beta,
        alpha_b=share_b * immobile,
        kappa=decay + share_b * decay * gamma,
        delta=share_b * decay * beta,
        free_b=immobile * over_b,
        share_b=share_b,
        decay_b=decay * over_b,
    )


class Numbers:
    def __init__(self, tab_ref):
        self.tab_ref = tab_ref

    def __call__(self, name, index):
        k = NUMBERS.index(name)
        row = jnp.broadcast_to(self.tab_ref[k : k + 1, :], (SUB, LANE))
        return lookup(row, index)


def shifted_difference(value, axis):
    return pltpu.roll(value, value.shape[axis] - 1, axis) - value


def side_of(axis, stride):
    return (lax.axis_index(axis) // stride) % 2 == 1


def pack_kernel(
    conc_hbm,
    stratum_hbm,
    por_hbm,
    disp_hbm,
    trans_hbm,
    exch_hbm,
    decay_hbm,
    early_ref,
    late_ref,
    tab_ref,
    conc_ref,
    stratum_ref,
    por_ref,
    disp_ref,
    trans_ref,
    exch_ref,
    decay_ref,
    raw,
    sems,
):
    moves = [
        (stratum_hbm, stratum_ref),
        (conc_hbm.at[0:2], conc_ref.at[0:2]),
        (por_hbm, por_ref),
        (disp_hbm, disp_ref),
        (trans_hbm, trans_ref),
        (exch_hbm, exch_ref),
        (decay_hbm, decay_ref),
        (conc_hbm.at[2:4], conc_ref.at[2:4]),
    ]
    copies = [pltpu.make_async_copy(src, dst, sems.at[k]) for k, (src, dst) in enumerate(moves)]
    for copy in copies:
        copy.start()
    raw[...] = jnp.full(raw.shape, 0.5, jnp.float32)
    for copy in copies[2:7]:
        copy.wait()
    strata = por_ref.shape[1]
    raw[0:1, 0:strata] = por_ref[...]
    raw[1:3, 0:strata] = disp_ref[...]
    raw[3:4, 0:strata] = trans_ref[...]
    raw[4:5, 0:strata] = exch_ref[...]
    raw[5:6, 0:strata] = decay_ref[...]
    made = derive(*[raw[k : k + 1, :] for k in range(6)])
    for k, name in enumerate(NUMBERS):
        tab_ref[k : k + 1, :] = made[name]
    tab_ref[len(NUMBERS) : 2 * SUB, :] = raw[0 : 2 * SUB - len(NUMBERS), :]
    odd = side_of("trans", 1)
    last = stratum_ref.shape[1] - 1

    def put(k, low, high):
        early_ref[k] = jnp.where(odd, low, high)
        late_ref[k] = jnp.where(odd, high, low)

    copies[0].wait()
    numbered = [(stratum_ref[:, y, :] + 1).astype(jnp.float32) for y in (0, last)]
    put(2, *numbered)
    copies[1].wait()
    for k in (0, 1):
        put(k, conc_ref[k, :, 0, :], conc_ref[k, :, last, :])
    copies[7].wait()


def half_of(kept):
    second = lax.axis_index("flow") % 2
    return second if kept else 1 - second


def local_kernel(
    kept,
    tab_ref,
    stratum_ref,
    conc_ref,
    pay_ref,
    edge_ref,
    pass_a_ref,
    drop_a_ref,
    pass_b_ref,
    drop_b_ref,
    over_ref,
    source_a_ref,
    source_b_ref,
    head_a,
    head_b,
    kappa_ref,
    left_a,
    right_a,
    left_b,
    right_b,
    adj_l,
    adj_r,
):
    n, planes_y, planes_z = stratum_ref.shape
    half = planes_y // 2
    which = half_of(kept)
    rows = pl.ds(pl.multiple_of(which * half, half), half)
    other_rows = pl.ds(pl.multiple_of((1 - which) * half, half), half)
    number = Numbers(tab_ref)

    cond_a = cond_b = half_a = half_b = through_a = through_b = None
    for i in range(n):
        index = stratum_ref[i, rows, :]
        shunt_a, shunt_b = number("shunt_a", index), number("shunt_b", index)
        new_a, new_b = number("half_a", index), number("half_b", index)
        kappa_ref[i] = number("kappa", index)
        if i == 0:
            first_half_a, first_half_b = new_a, new_b
            cond_a, cond_b = shunt_a, shunt_b
            through_a = through_b = jnp.ones_like(shunt_a)
        else:
            face_a, face_b = half_a + new_a, half_b + new_b
            pass_a, pass_b = recip(1.0 + face_a * cond_a), recip(1.0 + face_b * cond_b)
            cond_a, cond_b = shunt_a + cond_a * pass_a, shunt_b + cond_b * pass_b
            pass_a_ref[i], pass_b_ref[i] = pass_a, pass_b
            drop_a_ref[i], drop_b_ref[i] = face_a * pass_a, face_b * pass_b
            through_a, through_b = through_a * pass_a, through_b * pass_b
        head_a[i], head_b[i] = through_a, through_b
        half_a, half_b = new_a, new_b
    over_a, over_b = recip(cond_a), recip(cond_b)
    over_ref[0], over_ref[1] = over_a, over_b

    r_a, r_b = over_a, over_b
    l_a, l_b = through_a * over_a, through_b * over_b
    couple = [None] * 4
    for i in reversed(range(n)):
        if i < n - 1:
            pass_a, pass_b = pass_a_ref[i + 1], pass_b_ref[i + 1]
            l_a = pass_a * l_a + drop_a_ref[i + 1] * head_a[i]
            l_b = pass_b * l_b + drop_b_ref[i + 1] * head_b[i]
            r_a, r_b = pass_a * r_a, pass_b * r_b
        left_a[i], right_a[i], left_b[i], right_b[i] = l_a, r_a, l_b, r_b
        kappa = kappa_ref[i]
        k_l, k_r = kappa * l_a, kappa * r_a
        terms = [l_b * k_l, l_b * k_r, r_b * k_l, r_b * k_r]
        couple = [t if c is None else c + t for c, t in zip(couple, terms)]

    g_l = g_r = None
    for i in range(n):
        kappa = kappa_ref[i]
        s_l, s_r = kappa * left_b[i], kappa * right_b[i]
        if i > 0:
            pass_a = pass_a_ref[i]
            s_l, s_r = s_l + pass_a * g_l, s_r + pass_a * g_r
        g_l, g_r = s_l, s_r
        adj_l[i], adj_r[i] = g_l, g_r

    lane = lax.broadcasted_iota(jnp.int32, (half, planes_z), 1)
    line = lax.broadcasted_iota(jnp.int32, (half, planes_z), 0)
    inside = (line < half - 1, lane < planes_z - 1)
    meets = line == (half - 1) * (1 - which)
    shift = jnp.where(which == 0, half - 1, 1)
    w_l, w_r = adj_l[n - 1] * over_a, adj_r[n - 1] * over_a
    free = [None] * 4
    for i in reversed(range(n)):
        if i < n - 1:
            pass_a, drop_a = pass_a_ref[i + 1], drop_a_ref[i + 1]
            w_l, w_r = pass_a * w_l + drop_a * adj_l[i], pass_a * w_r + drop_a * adj_r[i]
        adj_l[i], adj_r[i] = w_l, w_r
        index = stratum_ref[i, rows, :]
        half_t = number("half_t", index)
        por = number("por", index)
        c0, c1, c2, c3 = [conc_ref[k, i, rows, :] for k in range(4)]
        source_a = por * c0 + number("alpha_a", index) * c2
        source_b = (
            por * c1
            + number("alpha_b", index) * c3
            + number("delta", index) * c2
        )
        for axis in (0, 1):
            last = half_t.shape[axis] - 1
            face = jnp.where(
                inside[axis], recip(half_t + pltpu.roll(half_t, last, axis)), 0.0
            )
            flow_a = face * shifted_difference(c0, axis)
            flow_b = face * shifted_difference(c1, axis)
            source_a = source_a + (flow_a - pltpu.roll(flow_a, 1, axis))
            source_b = source_b + (flow_b - pltpu.roll(flow_b, 1, axis))
        beyond_t = pltpu.roll(number("half_t", stratum_ref[i, other_rows, :]), shift, 0)
        face = jnp.where(meets, recip(half_t + beyond_t), 0.0)
        source_a = source_a + face * (pltpu.roll(conc_ref[0, i, other_rows, :], shift, 0) - c0)
        source_b = source_b + face * (pltpu.roll(conc_ref[1, i, other_rows, :], shift, 0) - c1)
        source_a_ref[i], source_b_ref[i] = source_a, source_b
        terms = [
            left_a[i] * source_a,
            right_a[i] * source_a,
            left_b[i] * source_b + w_l * source_a,
            right_b[i] * source_b + w_r * source_a,
        ]
        free = [t if f is None else f + t for f, t in zip(free, terms)]

    quantities = [
        left_a[0] + first_half_a,
        right_a[0],
        over_a + half_a,
        left_b[0] + first_half_b,
        right_b[0],
        over_b + half_b,
        *couple,
        *free,
    ]
    for q, value in enumerate(quantities):
        pay_ref[q] = value
    for k, ref in enumerate((left_a, right_a, left_b, right_b, adj_l, adj_r)):
        edge_ref[k] = jnp.where(which == 0, ref[:, 0, :], ref[:, half - 1, :])


def border_kernel(
    kept,
    tab_ref,
    early_ref,
    late_ref,
    beyond_early_ref,
    beyond_late_ref,
    edge_ref,
    pay_ref,
    out_ref,
    flow_ref,
):
    number = Numbers(tab_ref)
    half = pay_ref.shape[1]
    low = half_of(kept) == 0
    early = side_of("trans", 1) == low
    own = jnp.where(early, early_ref[...], late_ref[...])
    beyond = jnp.where(early, beyond_early_ref[...], beyond_late_ref[...])
    own_id = own[2].astype(jnp.int32) - 1
    next_id = beyond[2].astype(jnp.int32) - 1
    resist = number("half_t", own_id) + number("half_t", jnp.maximum(next_id, 0))
    face = jnp.where(next_id >= 0, recip(resist), 0.0)
    flow_a = face * (beyond[0] - own[0])
    flow_b = face * (beyond[1] - own[1])
    flow_ref[0], flow_ref[1] = flow_a, flow_b
    l_a, r_a, l_b, r_b, w_l, w_r = [edge_ref[k] for k in range(6)]
    changes = {
        FA_L: l_a * flow_a,
        FA_R: r_a * flow_a,
        FB_L: l_b * flow_b + w_l * flow_a,
        FB_R: r_b * flow_b + w_r * flow_a,
    }
    line = lax.broadcasted_iota(jnp.int32, pay_ref.shape[1:], 0)
    outer = line == jnp.where(low, 0, half - 1)
    for q in range(QUANTITIES):
        value = pay_ref[q]
        if q in changes:
            total = jnp.sum(changes[q], axis=0, keepdims=True)
            value = value + jnp.where(outer, total, 0.0)
        out_ref[q] = value


FACE_L = (ZA_LL, ZB_LL, C_LL, FA_L, FB_L)
FACE_R = (ZA_RR, ZB_RR, C_RR, FA_R, FB_R)
KEPT = 8


def merge(one, two):
    over_a = recip(one[ZA_RR] + two[ZA_LL])
    over_b = recip(one[ZB_RR] + two[ZB_LL])
    across = one[C_RR] + two[C_LL]
    free_a = over_a * (one[FA_R] - two[FA_L])
    from_l, from_r = over_a * one[ZA_LR], over_a * two[ZA_LR]
    free_b = over_b * (one[FB_R] - two[FB_L] - across * free_a)
    from_l_b, from_r_b = over_b * one[ZB_LR], over_b * two[ZB_LR]
    cross_l = over_b * (one[C_RL] - across * from_l)
    cross_r = over_b * (two[C_LR] - across * from_r)
    merged = {
        ZA_LL: one[ZA_LL] - one[ZA_LR] * from_l,
        ZA_LR: one[ZA_LR] * from_r,
        ZA_RR: two[ZA_RR] - two[ZA_LR] * from_r,
        ZB_LL: one[ZB_LL] - one[ZB_LR] * from_l_b,
        ZB_LR: one[ZB_LR] * from_r_b,
        ZB_RR: two[ZB_RR] - two[ZB_LR] * from_r_b,
        C_LL: one[C_LL] - one[ZB_LR] * cross_l - one[C_LR] * from_l,
        C_LR: one[ZB_LR] * cross_r + one[C_LR] * from_r,
        C_RL: two[ZB_LR] * cross_l + two[C_RL] * from_l,
        C_RR: two[C_RR] - two[ZB_LR] * cross_r - two[C_RL] * from_r,
        FA_L: one[FA_L] - one[ZA_LR] * free_a,
        FA_R: two[FA_R] + two[ZA_LR] * free_a,
        FB_L: one[FB_L] - one[ZB_LR] * free_b - one[C_LR] * free_a,
        FB_R: two[FB_R] + two[ZB_LR] * free_b + two[C_RL] * free_a,
    }
    return merged, (free_a, from_l, from_r, free_b, from_l_b, from_r_b, cross_l, cross_r)


def between(kept, ends):
    free_a, from_l, from_r, free_b, from_l_b, from_r_b, cross_l, cross_r = kept
    l_a, r_a, l_b, r_b = ends
    middle_a = free_a + from_l * l_a - from_r * r_a
    middle_b = free_b + from_l_b * l_b - from_r_b * r_b + cross_l * l_a - cross_r * r_a
    return middle_a, middle_b


def merge_kernel(stride, last, own_ref, other_ref, out_ref, kept_ref, *face_ref):
    second = side_of("flow", stride)
    own = [own_ref[q] for q in range(QUANTITIES)]
    other = [other_ref[q] for q in range(QUANTITIES)]
    one = [jnp.where(second, b, a) for a, b in zip(own, other)]
    two = [jnp.where(second, a, b) for a, b in zip(own, other)]
    merged, kept = merge(one, two)
    for q, value in merged.items():
        out_ref[q] = value
    for k, value in enumerate(kept):
        kept_ref[k] = value
    if last:
        after = side_of("flow", 2 * stride)
        for k, (l, r) in enumerate(zip(FACE_L, FACE_R)):
            face_ref[0][k] = jnp.where(after, merged[l], merged[r])


def close_kernel(strides, own_ref, other_ref, *refs):
    kept_refs, mine_ref, send_ref = refs[:-2], refs[-2], refs[-1]
    stride = strides[-1]
    second = side_of("flow", stride)
    own = [jnp.where(second, own_ref[l], own_ref[r]) for l, r in zip(FACE_L, FACE_R)]
    z_a, z_b, couple, f_a, f_b = [own[k] + other_ref[k] for k in range(3)] + [
        jnp.where(second, other_ref[k] - own[k], own[k] - other_ref[k]) for k in (3, 4)
    ]
    current_a = recip(z_a) * f_a
    current_b = recip(z_b) * (f_b - couple * current_a)
    nothing = jnp.zeros_like(current_a)

    def side_ends(after, middle_a, middle_b, ends):
        l_a, r_a, l_b, r_b = ends
        return (
            jnp.where(after, middle_a, l_a),
            jnp.where(after, r_a, -middle_a),
            jnp.where(after, middle_b, l_b),
            jnp.where(after, r_b, -middle_b),
        )

    ends = side_ends(second, current_a, current_b, (nothing,) * 4)
    for stride, kept_ref in reversed(list(zip(strides[:-1], kept_refs))):
        middle_a, middle_b = between([kept_ref[k] for k in range(KEPT)], ends)
        after = side_of("flow", stride)
        if stride == 1:
            other_ends = side_ends(jnp.logical_not(after), middle_a, middle_b, ends)
            for q, value in enumerate(other_ends):
                send_ref[q] = value
        ends = side_ends(after, middle_a, middle_b, ends)
    for q, value in enumerate(ends):
        mine_ref[q] = value


def final_kernel(
    kept,
    tab_ref,
    stratum_ref,
    conc_ref,
    pass_a_ref,
    drop_a_ref,
    pass_b_ref,
    drop_b_ref,
    over_ref,
    source_a_ref,
    source_b_ref,
    flow_ref,
    current_ref,
    *refs,
):
    out_hbm, gather_a, gather_b, made, sems = refs[-5:]
    n, planes_y, planes_z = stratum_ref.shape
    half = planes_y // 2
    which = half_of(kept)
    rows = pl.ds(pl.multiple_of(which * half, half), half)
    number = Numbers(tab_ref)
    line = lax.broadcasted_iota(jnp.int32, (half, planes_z), 0)
    outer = line == (half - 1) * which

    def with_border(source, component, i):
        flow = jnp.broadcast_to(flow_ref[component, i : i + 1, :], source.shape)
        return source + jnp.where(outer, flow, 0.0)

    l_a, r_a, l_b, r_b = [current_ref[q] for q in range(CURRENTS)]
    value = l_a
    for i in range(n):
        value = with_border(source_a_ref[i], 0, i) + value
        if i < n - 1:
            gather_a[i] = value
            value = pass_a_ref[i + 1] * value
    x = (value + r_a) * over_ref[0]
    for i in reversed(range(n)):
        if i < n - 1:
            x = pass_a_ref[i + 1] * x + drop_a_ref[i + 1] * gather_a[i]
        made[0, i] = x
    value = l_b
    for i in range(n):
        kappa = number("kappa", stratum_ref[i, rows, :])
        value = with_border(source_b_ref[i], 1, i) + kappa * made[0, i] + value
        if i < n - 1:
            gather_b[i] = value
            value = pass_b_ref[i + 1] * value
    x = (value + r_b) * over_ref[1]
    copies = []
    for i in reversed(range(n)):
        if i < n - 1:
            x = pass_b_ref[i + 1] * x + drop_b_ref[i + 1] * gather_b[i]
        made[1, i] = x
        index = stratum_ref[i, rows, :]
        x2 = number("beta", index) * conc_ref[2, i, rows, :] + number("gamma", index) * made[0, i]
        made[2, i] = x2
        made[3, i] = (
            number("free_b", index) * conc_ref[3, i, rows, :]
            + number("share_b", index) * x
            + number("decay_b", index) * x2
        )
        copies.append(
            pltpu.make_async_copy(made.at[:, i], out_hbm.at[:, i, rows, :], sems.at[i])
        )
        copies[-1].start()
    for copy in copies:
        copy.wait()


def call(kernel, outs, scratch=()):
    return pl.pallas_call(
        kernel,
        out_shape=[jax.ShapeDtypeStruct(shape, jnp.float32) for shape in outs],
        scratch_shapes=[pltpu.VMEM(shape, jnp.float32) for shape in scratch],
        compiler_params=pltpu.CompilerParams(vmem_limit_bytes=VMEM_LIMIT),
    )


def per_device(
    concentration,
    stratum,
    porosity,
    dispersion_table,
    transverse_table,
    exchange_table,
    decay_table,
):
    n, planes_y, planes_z = stratum.shape
    peers = lax.axis_size("flow")
    half = planes_y // 2
    strides = [1 << k for k in range(peers.bit_length() - 1)]
    cells = (n, planes_y, planes_z)

    halo = (3, n, planes_z)
    strata = porosity.shape[0]
    hbm = pl.BlockSpec(memory_space=pltpu.HBM)
    early, late, table, concentration, stratum = pl.pallas_call(
        pack_kernel,
        out_shape=[
            jax.ShapeDtypeStruct(halo, jnp.float32),
            jax.ShapeDtypeStruct(halo, jnp.float32),
            jax.ShapeDtypeStruct((2 * SUB, LANE), jnp.float32),
            jax.ShapeDtypeStruct(concentration.shape, jnp.float32),
            jax.ShapeDtypeStruct(cells, jnp.int32),
        ],
        in_specs=[hbm] * 7,
        scratch_shapes=[
            pltpu.VMEM((1, strata), jnp.float32),
            pltpu.VMEM((2, strata), jnp.float32),
            pltpu.VMEM((1, strata), jnp.float32),
            pltpu.VMEM((1, strata), jnp.float32),
            pltpu.VMEM((1, strata), jnp.float32),
            pltpu.VMEM((SUB, LANE), jnp.float32),
            pltpu.SemaphoreType.DMA((8,)),
        ],
        compiler_params=pltpu.CompilerParams(vmem_limit_bytes=VMEM_LIMIT),
    )(
        *[
            pltpu.with_memory_space_constraint(value, pltpu.HBM)
            for value in (
                concentration,
                stratum,
                porosity[None],
                dispersion_table.T,
                transverse_table[None],
                exchange_table[None],
                decay_table[None],
            )
        ]
    )
    groups = lax.axis_size("trans")
    def swap(value, start):
        low = range(start, groups - 1, 2)
        pairs = [(i, i + 1) for i in low] + [(i + 1, i) for i in low]
        return lax.ppermute(value, "trans", pairs)

    beyond_early, beyond_late = swap(early, 0), swap(late, 1)

    def exchange(value, stride):
        return lax.ppermute(value, "flow", [(i, i ^ stride) for i in range(peers)])

    half_cells = (n, half, planes_z)
    block_shape = (QUANTITIES, half, planes_z)

    def local(kept):
        pay, edge, *rest = call(
            functools.partial(local_kernel, kept),
            [
                block_shape,
                (6, n, planes_z),
                *[half_cells] * 4,
                (2, half, planes_z),
                *[half_cells] * 2,
            ],
            [half_cells] * 9,
        )(table, stratum, concentration)
        pay, flow = call(
            functools.partial(border_kernel, kept), [block_shape, (2, n, planes_z)]
        )(table, early, late, beyond_early, beyond_late, edge, pay)
        return pay, (*rest, flow)

    send, sent_rest = local(False)
    block, kept_rest = local(True)
    kept = []
    for stride in strides[:-1]:
        other = exchange(send, stride)
        last = stride == strides[-2]
        block, keep, *face = call(
            functools.partial(merge_kernel, stride, last),
            [block_shape, (KEPT, half, planes_z)] + [(5, half, planes_z)] * last,
        )(block, other)
        kept.append(keep)
        send = face[0] if last else block
    ends_shape = (CURRENTS, half, planes_z)
    mine, send = call(functools.partial(close_kernel, strides), [ends_shape, ends_shape])(
        block, exchange(send, strides[-1]), *kept
    )
    currents = exchange(send, 1)
    def final(kept, rest, currents, *before):
        whole = jax.ShapeDtypeStruct((4,) + cells, jnp.float32)
        vmem = pl.BlockSpec(memory_space=pltpu.VMEM)
        return pl.pallas_call(
            functools.partial(final_kernel, kept),
            out_shape=whole,
            in_specs=[vmem] * 12 + [hbm] * len(before),
            out_specs=hbm,
            scratch_shapes=[
                pltpu.VMEM(half_cells, jnp.float32),
                pltpu.VMEM(half_cells, jnp.float32),
                pltpu.VMEM((4,) + half_cells, jnp.float32),
                pltpu.SemaphoreType.DMA((n,)),
            ],
            input_output_aliases={12: 0} if before else {},
            compiler_params=pltpu.CompilerParams(vmem_limit_bytes=VMEM_LIMIT),
        )(table, stratum, concentration, *rest, currents, *before)

    out = final(True, kept_rest, mine)
    return final(False, sent_rest, currents, out)


def solution(mesh):
    in_specs = (P(None, "flow", "trans", None), P("flow", "trans", None), P(), P(), P(), P(), P())
    out_specs = P(None, "flow", "trans", None)
    return jax.shard_map(
        per_device, mesh=mesh, in_specs=in_specs, out_specs=out_specs, check_vma=False
    )
```

```python
import functools

import jax
import jax.numpy as jnp
from jax import lax
from jax.experimental import pallas as pl
from jax.experimental.pallas import tpu as pltpu
from jax.sharding import PartitionSpec as P

SUB, LANE = 8, 128
ZA_LL, ZA_LR, ZA_RR, ZB_LL, ZB_LR, ZB_RR, C_LL, C_LR, C_RL, C_RR, FA_L, FA_R, FB_L, FB_R = range(14)
QUANTITIES = 14
CURRENTS = 4
KEPT = 8
PIECES = 2
VMEM_LIMIT = 40 * 1024 * 1024


def recip(x):
    return 1.0 / x


def lookup(row, index):
    tiles = []
    for y in range(0, index.shape[0], SUB):
        across = [
            jnp.take_along_axis(
                row, index[y : y + SUB, z : z + LANE], axis=1, mode="promise_in_bounds"
            )
            for z in range(0, index.shape[1], LANE)
        ]
        tiles.append(jnp.concatenate(across, axis=1))
    return jnp.concatenate(tiles, axis=0)


NUMBERS = (
    "por",
    "shunt_a",
    "shunt_b",
    "half_a",
    "half_b",
    "half_t",
    "beta",
    "gamma",
    "alpha_a",
    "alpha_b",
    "kappa",
    "delta",
    "free_b",
    "share_b",
    "decay_b",
)


def derive(por, disp_a, disp_b, trans, exch, decay):
    immobile = 1.0 - por
    over_a = 1.0 / (immobile + exch + decay)
    over_b = 1.0 / (immobile + exch)
    beta = immobile * over_a
    gamma = exch * over_a
    share_b = exch * over_b
    return dict(
        por=por,
        shunt_a=por + decay + exch * (immobile + decay) * over_a,
        shunt_b=por + exch * immobile * over_b,
        half_a=0.5 / disp_a,
        half_b=0.5 / disp_b,
        half_t=0.5 / trans,
        beta=beta,
        gamma=gamma,
        alpha_a=exch * beta,
        alpha_b=share_b * immobile,
        kappa=decay + share_b * decay * gamma,
        delta=share_b * decay * beta,
        free_b=immobile * over_b,
        share_b=share_b,
        decay_b=decay * over_b,
    )


class Numbers:
    def __init__(self, tab_ref):
        self.tab_ref = tab_ref

    def __call__(self, name, index):
        k = NUMBERS.index(name)
        row = jnp.broadcast_to(self.tab_ref[k : k + 1, :], (SUB, LANE))
        return lookup(row, index)


def shifted_difference(value, axis):
    return pltpu.roll(value, value.shape[axis] - 1, axis) - value


def side_of(axis, stride):
    return (lax.axis_index(axis) // stride) % 2 == 1


def pack_kernel(
    conc_hbm,
    stratum_hbm,
    por_hbm,
    disp_hbm,
    trans_hbm,
    exch_hbm,
    decay_hbm,
    early_ref,
    late_ref,
    tab_ref,
    conc_ref,
    stratum_ref,
    por_ref,
    disp_ref,
    trans_ref,
    exch_ref,
    decay_ref,
    raw,
    sems,
):
    moves = [
        (stratum_hbm, stratum_ref),
        (conc_hbm.at[0:2], conc_ref.at[0:2]),
        (por_hbm, por_ref),
        (disp_hbm, disp_ref),
        (trans_hbm, trans_ref),
        (exch_hbm, exch_ref),
        (decay_hbm, decay_ref),
        (conc_hbm.at[2:4], conc_ref.at[2:4]),
    ]
    copies = [pltpu.make_async_copy(src, dst, sems.at[k]) for k, (src, dst) in enumerate(moves)]
    for copy in copies:
        copy.start()
    raw[...] = jnp.full(raw.shape, 0.5, jnp.float32)
    for copy in copies[2:7]:
        copy.wait()
    strata = por_ref.shape[1]
    raw[0:1, 0:strata] = por_ref[...]
    raw[1:3, 0:strata] = disp_ref[...]
    raw[3:4, 0:strata] = trans_ref[...]
    raw[4:5, 0:strata] = exch_ref[...]
    raw[5:6, 0:strata] = decay_ref[...]
    made = derive(*[raw[k : k + 1, :] for k in range(6)])
    for k, name in enumerate(NUMBERS):
        tab_ref[k : k + 1, :] = made[name]
    tab_ref[len(NUMBERS) : 2 * SUB, :] = raw[0 : 2 * SUB - len(NUMBERS), :]
    odd = side_of("trans", 1)
    last = stratum_ref.shape[1] - 1

    def put(k, low, high):
        early_ref[k] = jnp.where(odd, low, high)
        late_ref[k] = jnp.where(odd, high, low)

    copies[0].wait()
    numbered = [(stratum_ref[:, y, :] + 1).astype(jnp.float32) for y in (0, last)]
    put(2, *numbered)
    copies[1].wait()
    for k in (0, 1):
        put(k, conc_ref[k, :, 0, :], conc_ref[k, :, last, :])
    copies[7].wait()


def half_of(kept):
    second = lax.axis_index("flow") % 2
    return second if kept else 1 - second


def local_kernel(
    kept,
    tab_ref,
    stratum_ref,
    conc_ref,
    pay_ref,
    edge_ref,
    pass_a_ref,
    drop_a_ref,
    pass_b_ref,
    drop_b_ref,
    over_ref,
    source_a_ref,
    source_b_ref,
    head_a,
    head_b,
    kappa_ref,
    left_a,
    right_a,
    left_b,
    right_b,
    adj_l,
    adj_r,
):
    n, planes_y, planes_z = stratum_ref.shape
    half = planes_y // 2
    which = half_of(kept)
    rows = pl.ds(pl.multiple_of(which * half, half), half)
    other_rows = pl.ds(pl.multiple_of((1 - which) * half, half), half)
    number = Numbers(tab_ref)

    pieces = range(PIECES)
    m = n // PIECES
    firsts, lasts = [s * m for s in pieces], [s * m + m - 1 for s in pieces]

    cond_a, cond_b, half_a, half_b, through_a, through_b = [[None] * PIECES for _ in range(6)]
    first_half_a, first_half_b = [None] * PIECES, [None] * PIECES
    for j in range(m):
        for s in pieces:
            i = firsts[s] + j
            index = stratum_ref[i, rows, :]
            shunt_a, shunt_b = number("shunt_a", index), number("shunt_b", index)
            new_a, new_b = number("half_a", index), number("half_b", index)
            kappa_ref[i] = number("kappa", index)
            if j == 0:
                first_half_a[s], first_half_b[s] = new_a, new_b
                cond_a[s], cond_b[s] = shunt_a, shunt_b
                through_a[s] = through_b[s] = jnp.ones_like(shunt_a)
            else:
                face_a, face_b = half_a[s] + new_a, half_b[s] + new_b
                pass_a, pass_b = recip(1.0 + face_a * cond_a[s]), recip(1.0 + face_b * cond_b[s])
                cond_a[s], cond_b[s] = shunt_a + cond_a[s] * pass_a, shunt_b + cond_b[s] * pass_b
                pass_a_ref[i], pass_b_ref[i] = pass_a, pass_b
                drop_a_ref[i], drop_b_ref[i] = face_a * pass_a, face_b * pass_b
                through_a[s], through_b[s] = through_a[s] * pass_a, through_b[s] * pass_b
            head_a[i], head_b[i] = through_a[s], through_b[s]
            half_a[s], half_b[s] = new_a, new_b
    over_a, over_b = [recip(c) for c in cond_a], [recip(c) for c in cond_b]
    for s in pieces:
        over_ref[0, s], over_ref[1, s] = over_a[s], over_b[s]

    r_a, r_b = list(over_a), list(over_b)
    l_a = [t * o for t, o in zip(through_a, over_a)]
    l_b = [t * o for t, o in zip(through_b, over_b)]
    couple = [[None] * 4 for _ in pieces]
    for j in reversed(range(m)):
        for s in pieces:
            i = firsts[s] + j
            if j < m - 1:
                pass_a, pass_b = pass_a_ref[i + 1], pass_b_ref[i + 1]
                l_a[s] = pass_a * l_a[s] + drop_a_ref[i + 1] * head_a[i]
                l_b[s] = pass_b * l_b[s] + drop_b_ref[i + 1] * head_b[i]
                r_a[s], r_b[s] = pass_a * r_a[s], pass_b * r_b[s]
            left_a[i], right_a[i], left_b[i], right_b[i] = l_a[s], r_a[s], l_b[s], r_b[s]
            kappa = kappa_ref[i]
            k_l, k_r = kappa * l_a[s], kappa * r_a[s]
            terms = [l_b[s] * k_l, l_b[s] * k_r, r_b[s] * k_l, r_b[s] * k_r]
            couple[s] = [t if c is None else c + t for c, t in zip(couple[s], terms)]

    g_l, g_r = [None] * PIECES, [None] * PIECES
    for j in range(m):
        for s in pieces:
            i = firsts[s] + j
            kappa = kappa_ref[i]
            s_l, s_r = kappa * left_b[i], kappa * right_b[i]
            if j > 0:
                pass_a = pass_a_ref[i]
                s_l, s_r = s_l + pass_a * g_l[s], s_r + pass_a * g_r[s]
            g_l[s], g_r[s] = s_l, s_r
            adj_l[i], adj_r[i] = s_l, s_r

    lane = lax.broadcasted_iota(jnp.int32, (half, planes_z), 1)
    line = lax.broadcasted_iota(jnp.int32, (half, planes_z), 0)
    inside = (line < half - 1, lane < planes_z - 1)
    meets = line == (half - 1) * (1 - which)
    shift = jnp.where(which == 0, half - 1, 1)
    w_l = [adj_l[lasts[s]] * over_a[s] for s in pieces]
    w_r = [adj_r[lasts[s]] * over_a[s] for s in pieces]
    free = [[None] * 4 for _ in pieces]
    for j in reversed(range(m)):
        for s in pieces:
            i = firsts[s] + j
            if j < m - 1:
                pass_a, drop_a = pass_a_ref[i + 1], drop_a_ref[i + 1]
                w_l[s] = pass_a * w_l[s] + drop_a * adj_l[i]
                w_r[s] = pass_a * w_r[s] + drop_a * adj_r[i]
            adj_l[i], adj_r[i] = w_l[s], w_r[s]
            index = stratum_ref[i, rows, :]
            half_t = number("half_t", index)
            por = number("por", index)
            c0, c1, c2, c3 = [conc_ref[k, i, rows, :] for k in range(4)]
            source_a = por * c0 + number("alpha_a", index) * c2
            source_b = por * c1 + number("alpha_b", index) * c3 + number("delta", index) * c2
            for axis in (0, 1):
                last = half_t.shape[axis] - 1
                face = jnp.where(
                    inside[axis], recip(half_t + pltpu.roll(half_t, last, axis)), 0.0
                )
                flow_a = face * shifted_difference(c0, axis)
                flow_b = face * shifted_difference(c1, axis)
                source_a = source_a + (flow_a - pltpu.roll(flow_a, 1, axis))
                source_b = source_b + (flow_b - pltpu.roll(flow_b, 1, axis))
            beyond_t = pltpu.roll(number("half_t", stratum_ref[i, other_rows, :]), shift, 0)
            face = jnp.where(meets, recip(half_t + beyond_t), 0.0)
            source_a = source_a + face * (pltpu.roll(conc_ref[0, i, other_rows, :], shift, 0) - c0)
            source_b = source_b + face * (pltpu.roll(conc_ref[1, i, other_rows, :], shift, 0) - c1)
            source_a_ref[i], source_b_ref[i] = source_a, source_b
            terms = [
                left_a[i] * source_a,
                right_a[i] * source_a,
                left_b[i] * source_b + w_l[s] * source_a,
                right_b[i] * source_b + w_r[s] * source_a,
            ]
            free[s] = [t if f is None else f + t for f, t in zip(free[s], terms)]

    for s in pieces:
        quantities = [
            l_a[s] + first_half_a[s],
            r_a[s],
            over_a[s] + half_a[s],
            l_b[s] + first_half_b[s],
            r_b[s],
            over_b[s] + half_b[s],
            *couple[s],
            *free[s],
        ]
        for q, value in enumerate(quantities):
            pay_ref[s, q] = value
    for k, ref in enumerate((left_a, right_a, left_b, right_b, adj_l, adj_r)):
        edge_ref[k] = jnp.where(which == 0, ref[:, 0, :], ref[:, half - 1, :])


def border_kernel(
    kept,
    tab_ref,
    early_ref,
    late_ref,
    beyond_early_ref,
    beyond_late_ref,
    edge_ref,
    pay_ref,
    out_ref,
    kept_ref,
    flow_ref,
):
    number = Numbers(tab_ref)
    n, planes_z = edge_ref.shape[1:]
    m = n // PIECES
    half = pay_ref.shape[2]
    low = half_of(kept) == 0
    early = side_of("trans", 1) == low
    own = jnp.where(early, early_ref[...], late_ref[...])
    beyond = jnp.where(early, beyond_early_ref[...], beyond_late_ref[...])
    own_id = own[2].astype(jnp.int32) - 1
    next_id = beyond[2].astype(jnp.int32) - 1
    resist = number("half_t", own_id) + number("half_t", next_id)
    end = jnp.where(low, 0, lax.axis_size("trans") - 1)
    face = jnp.where(lax.axis_index("trans") != end, recip(resist), 0.0)
    flow_a = face * (beyond[0] - own[0])
    flow_b = face * (beyond[1] - own[1])
    flow_ref[0], flow_ref[1] = flow_a, flow_b
    l_a, r_a, l_b, r_b, w_l, w_r = [edge_ref[k] for k in range(6)]
    changes = {
        FA_L: l_a * flow_a,
        FA_R: r_a * flow_a,
        FB_L: l_b * flow_b + w_l * flow_a,
        FB_R: r_b * flow_b + w_r * flow_a,
    }
    line = lax.broadcasted_iota(jnp.int32, (half, planes_z), 0)
    outer = line == jnp.where(low, 0, half - 1)
    blocks = []
    for s in range(PIECES):
        values = {q: pay_ref[s, q] for q in range(QUANTITIES)}
        for q, change in changes.items():
            total = jnp.sum(change[s * m : (s + 1) * m], axis=0, keepdims=True)
            values[q] = values[q] + jnp.where(outer, total, 0.0)
        blocks.append(values)
    slot = 0
    while len(blocks) > 1:
        joined = []
        for one, two in zip(blocks[::2], blocks[1::2]):
            merged, parts = merge(one, two)
            for k, value in enumerate(parts):
                kept_ref[slot, k] = value
            slot += 1
            joined.append(merged)
        blocks = joined
    for q in range(QUANTITIES):
        out_ref[q] = blocks[0][q]


FACE_L = (ZA_LL, ZB_LL, C_LL, FA_L, FB_L)
FACE_R = (ZA_RR, ZB_RR, C_RR, FA_R, FB_R)


def merge(one, two):
    over_a = recip(one[ZA_RR] + two[ZA_LL])
    over_b = recip(one[ZB_RR] + two[ZB_LL])
    across = one[C_RR] + two[C_LL]
    free_a = over_a * (one[FA_R] - two[FA_L])
    from_l, from_r = over_a * one[ZA_LR], over_a * two[ZA_LR]
    free_b = over_b * (one[FB_R] - two[FB_L] - across * free_a)
    from_l_b, from_r_b = over_b * one[ZB_LR], over_b * two[ZB_LR]
    cross_l = over_b * (one[C_RL] - across * from_l)
    cross_r = over_b * (two[C_LR] - across * from_r)
    merged = {
        ZA_LL: one[ZA_LL] - one[ZA_LR] * from_l,
        ZA_LR: one[ZA_LR] * from_r,
        ZA_RR: two[ZA_RR] - two[ZA_LR] * from_r,
        ZB_LL: one[ZB_LL] - one[ZB_LR] * from_l_b,
        ZB_LR: one[ZB_LR] * from_r_b,
        ZB_RR: two[ZB_RR] - two[ZB_LR] * from_r_b,
        C_LL: one[C_LL] - one[ZB_LR] * cross_l - one[C_LR] * from_l,
        C_LR: one[ZB_LR] * cross_r + one[C_LR] * from_r,
        C_RL: two[ZB_LR] * cross_l + two[C_RL] * from_l,
        C_RR: two[C_RR] - two[ZB_LR] * cross_r - two[C_RL] * from_r,
        FA_L: one[FA_L] - one[ZA_LR] * free_a,
        FA_R: two[FA_R] + two[ZA_LR] * free_a,
        FB_L: one[FB_L] - one[ZB_LR] * free_b - one[C_LR] * free_a,
        FB_R: two[FB_R] + two[ZB_LR] * free_b + two[C_RL] * free_a,
    }
    return merged, (free_a, from_l, from_r, free_b, from_l_b, from_r_b, cross_l, cross_r)


def between(kept, ends):
    free_a, from_l, from_r, free_b, from_l_b, from_r_b, cross_l, cross_r = kept
    l_a, r_a, l_b, r_b = ends
    middle_a = free_a + from_l * l_a - from_r * r_a
    middle_b = free_b + from_l_b * l_b - from_r_b * r_b + cross_l * l_a - cross_r * r_a
    return middle_a, middle_b


def merge_kernel(stride, last, own_ref, other_ref, out_ref, kept_ref, *face_ref):
    second = side_of("flow", stride)
    own = [own_ref[q] for q in range(QUANTITIES)]
    other = [other_ref[q] for q in range(QUANTITIES)]
    one = [jnp.where(second, b, a) for a, b in zip(own, other)]
    two = [jnp.where(second, a, b) for a, b in zip(own, other)]
    merged, kept = merge(one, two)
    for q, value in merged.items():
        out_ref[q] = value
    for k, value in enumerate(kept):
        kept_ref[k] = value
    if last:
        after = side_of("flow", 2 * stride)
        for k, (l, r) in enumerate(zip(FACE_L, FACE_R)):
            face_ref[0][k] = jnp.where(after, merged[l], merged[r])


def close_kernel(strides, own_ref, other_ref, *refs):
    kept_refs, mine_ref, send_ref = refs[:-2], refs[-2], refs[-1]
    stride = strides[-1]
    second = side_of("flow", stride)
    own = [jnp.where(second, own_ref[l], own_ref[r]) for l, r in zip(FACE_L, FACE_R)]
    z_a, z_b, couple, f_a, f_b = [own[k] + other_ref[k] for k in range(3)] + [
        jnp.where(second, other_ref[k] - own[k], own[k] - other_ref[k]) for k in (3, 4)
    ]
    current_a = recip(z_a) * f_a
    current_b = recip(z_b) * (f_b - couple * current_a)
    nothing = jnp.zeros_like(current_a)

    def side_ends(after, middle_a, middle_b, ends):
        l_a, r_a, l_b, r_b = ends
        return (
            jnp.where(after, middle_a, l_a),
            jnp.where(after, r_a, -middle_a),
            jnp.where(after, middle_b, l_b),
            jnp.where(after, r_b, -middle_b),
        )

    ends = side_ends(second, current_a, current_b, (nothing,) * 4)
    for stride, kept_ref in reversed(list(zip(strides[:-1], kept_refs))):
        middle_a, middle_b = between([kept_ref[k] for k in range(KEPT)], ends)
        after = side_of("flow", stride)
        if stride == 1:
            other_ends = side_ends(jnp.logical_not(after), middle_a, middle_b, ends)
            for q, value in enumerate(other_ends):
                send_ref[q] = value
        ends = side_ends(after, middle_a, middle_b, ends)
    for q, value in enumerate(ends):
        mine_ref[q] = value


def final_kernel(
    kept,
    tab_ref,
    stratum_ref,
    conc_ref,
    pass_a_ref,
    drop_a_ref,
    pass_b_ref,
    drop_b_ref,
    over_ref,
    source_a_ref,
    source_b_ref,
    kept_ref,
    flow_ref,
    current_ref,
    *refs,
):
    out_hbm, gather_a, gather_b, made, sems = refs[-5:]
    n, planes_y, planes_z = stratum_ref.shape
    half = planes_y // 2
    which = half_of(kept)
    rows = pl.ds(pl.multiple_of(which * half, half), half)
    number = Numbers(tab_ref)
    line = lax.broadcasted_iota(jnp.int32, (half, planes_z), 0)
    outer = line == (half - 1) * which

    def with_border(source, component, i):
        flow = jnp.broadcast_to(flow_ref[component, i : i + 1, :], source.shape)
        return source + jnp.where(outer, flow, 0.0)

    ends = [tuple(current_ref[q] for q in range(CURRENTS))]
    slot = PIECES - 1
    while len(ends) < PIECES:
        slot -= len(ends)
        parts = []
        for k, (l_a, r_a, l_b, r_b) in enumerate(ends):
            values = [kept_ref[slot + k, v] for v in range(KEPT)]
            middle_a, middle_b = between(values, (l_a, r_a, l_b, r_b))
            parts += [(l_a, -middle_a, l_b, -middle_b), (middle_a, r_a, middle_b, r_b)]
        ends = parts

    pieces = range(PIECES)
    m = n // PIECES
    values = [ends[s][0] for s in pieces]
    for j in range(m):
        for s in pieces:
            i = s * m + j
            values[s] = with_border(source_a_ref[i], 0, i) + values[s]
            if j < m - 1:
                gather_a[i] = values[s]
                values[s] = pass_a_ref[i + 1] * values[s]
    x = [(values[s] + ends[s][1]) * over_ref[0, s] for s in pieces]
    for j in reversed(range(m)):
        for s in pieces:
            i = s * m + j
            if j < m - 1:
                x[s] = pass_a_ref[i + 1] * x[s] + drop_a_ref[i + 1] * gather_a[i]
            made[0, i] = x[s]
    values = [ends[s][2] for s in pieces]
    for j in range(m):
        for s in pieces:
            i = s * m + j
            kappa = number("kappa", stratum_ref[i, rows, :])
            values[s] = with_border(source_b_ref[i], 1, i) + kappa * made[0, i] + values[s]
            if j < m - 1:
                gather_b[i] = values[s]
                values[s] = pass_b_ref[i + 1] * values[s]
    x = [(values[s] + ends[s][3]) * over_ref[1, s] for s in pieces]
    copies = []
    for j in reversed(range(m)):
        for s in pieces:
            i = s * m + j
            if j < m - 1:
                x[s] = pass_b_ref[i + 1] * x[s] + drop_b_ref[i + 1] * gather_b[i]
            made[1, i] = x[s]
            index = stratum_ref[i, rows, :]
            x2 = (
                number("beta", index) * conc_ref[2, i, rows, :]
                + number("gamma", index) * made[0, i]
            )
            made[2, i] = x2
            made[3, i] = (
                number("free_b", index) * conc_ref[3, i, rows, :]
                + number("share_b", index) * x[s]
                + number("decay_b", index) * x2
            )
            copies.append(
                pltpu.make_async_copy(made.at[:, i], out_hbm.at[:, i, rows, :], sems.at[i])
            )
            copies[-1].start()
    for copy in copies:
        copy.wait()


def call(kernel, outs, scratch=()):
    return pl.pallas_call(
        kernel,
        out_shape=[jax.ShapeDtypeStruct(shape, jnp.float32) for shape in outs],
        scratch_shapes=[pltpu.VMEM(shape, jnp.float32) for shape in scratch],
        compiler_params=pltpu.CompilerParams(vmem_limit_bytes=VMEM_LIMIT),
    )


def per_device(
    concentration,
    stratum,
    porosity,
    dispersion_table,
    transverse_table,
    exchange_table,
    decay_table,
):
    n, planes_y, planes_z = stratum.shape
    peers = lax.axis_size("flow")
    half = planes_y // 2
    strides = [1 << k for k in range(peers.bit_length() - 1)]
    cells = (n, planes_y, planes_z)

    halo = (3, n, planes_z)
    strata = porosity.shape[0]
    hbm = pl.BlockSpec(memory_space=pltpu.HBM)
    early, late, table, concentration, stratum = pl.pallas_call(
        pack_kernel,
        out_shape=[
            jax.ShapeDtypeStruct(halo, jnp.float32),
            jax.ShapeDtypeStruct(halo, jnp.float32),
            jax.ShapeDtypeStruct((2 * SUB, LANE), jnp.float32),
            jax.ShapeDtypeStruct(concentration.shape, jnp.float32),
            jax.ShapeDtypeStruct(cells, jnp.int32),
        ],
        in_specs=[hbm] * 7,
        scratch_shapes=[
            pltpu.VMEM((1, strata), jnp.float32),
            pltpu.VMEM((2, strata), jnp.float32),
            pltpu.VMEM((1, strata), jnp.float32),
            pltpu.VMEM((1, strata), jnp.float32),
            pltpu.VMEM((1, strata), jnp.float32),
            pltpu.VMEM((SUB, LANE), jnp.float32),
            pltpu.SemaphoreType.DMA((8,)),
        ],
        compiler_params=pltpu.CompilerParams(vmem_limit_bytes=VMEM_LIMIT),
    )(
        *[
            pltpu.with_memory_space_constraint(value, pltpu.HBM)
            for value in (
                concentration,
                stratum,
                porosity[None],
                dispersion_table.T,
                transverse_table[None],
                exchange_table[None],
                decay_table[None],
            )
        ]
    )
    groups = lax.axis_size("trans")
    def swap(value, start):
        low = range(start, groups - 1, 2)
        pairs = [(i, i + 1) for i in low] + [(i + 1, i) for i in low]
        if start:
            pairs += [(0, groups - 1), (groups - 1, 0)]
        return lax.ppermute(value, "trans", pairs)

    beyond_early, beyond_late = swap(early, 0), swap(late, 1)

    def exchange(value, stride):
        return lax.ppermute(value, "flow", [(i, i ^ stride) for i in range(peers)])

    half_cells = (n, half, planes_z)
    block_shape = (QUANTITIES, half, planes_z)

    def local(kept):
        pay, edge, *rest = call(
            functools.partial(local_kernel, kept),
            [
                (PIECES,) + block_shape,
                (6, n, planes_z),
                *[half_cells] * 4,
                (2, PIECES, half, planes_z),
                *[half_cells] * 2,
            ],
            [half_cells] * 9,
        )(table, stratum, concentration)
        pay, parts, flow = call(
            functools.partial(border_kernel, kept),
            [block_shape, (PIECES - 1, KEPT, half, planes_z), (2, n, planes_z)],
        )(table, early, late, beyond_early, beyond_late, edge, pay)
        return pay, (*rest, parts, flow)

    send, sent_rest = local(False)
    block, kept_rest = local(True)
    kept = []
    for stride in strides[:-1]:
        other = exchange(send, stride)
        last = stride == strides[-2]
        block, keep, *face = call(
            functools.partial(merge_kernel, stride, last),
            [block_shape, (KEPT, half, planes_z)] + [(5, half, planes_z)] * last,
        )(block, other)
        kept.append(keep)
        send = face[0] if last else block
    ends_shape = (CURRENTS, half, planes_z)
    mine, send = call(functools.partial(close_kernel, strides), [ends_shape, ends_shape])(
        block, exchange(send, strides[-1]), *kept
    )
    currents = exchange(send, 1)
    def final(kept, rest, currents, *before):
        whole = jax.ShapeDtypeStruct((4,) + cells, jnp.float32)
        vmem = pl.BlockSpec(memory_space=pltpu.VMEM)
        return pl.pallas_call(
            functools.partial(final_kernel, kept),
            out_shape=whole,
            in_specs=[vmem] * 13 + [hbm] * len(before),
            out_specs=hbm,
            scratch_shapes=[
                pltpu.VMEM(half_cells, jnp.float32),
                pltpu.VMEM(half_cells, jnp.float32),
                pltpu.VMEM((4,) + half_cells, jnp.float32),
                pltpu.SemaphoreType.DMA((n,)),
            ],
            input_output_aliases={13: 0} if before else {},
            compiler_params=pltpu.CompilerParams(vmem_limit_bytes=VMEM_LIMIT),
        )(table, stratum, concentration, *rest, currents, *before)

    out = final(True, kept_rest, mine)
    return final(False, sent_rest, currents, out)


def solution(mesh):
    in_specs = (P(None, "flow", "trans", None), P("flow", "trans", None), P(), P(), P(), P(), P())
    out_specs = P(None, "flow", "trans", None)
    return jax.shard_map(
        per_device, mesh=mesh, in_specs=in_specs, out_specs=out_specs, check_vma=False
    )
```

```python
import functools

import jax
import jax.numpy as jnp
from jax import lax
from jax.experimental import pallas as pl
from jax.experimental.pallas import tpu as pltpu
from jax.sharding import PartitionSpec as P

SUB, LANE = 8, 128
ZA_LL, ZA_LR, ZA_RR, ZB_LL, ZB_LR, ZB_RR, C_LL, C_LR, C_RL, C_RR, FA_L, FA_R, FB_L, FB_R = range(14)
QUANTITIES = 14
CURRENTS = 4
KEPT = 8
PIECES = 4
VMEM_LIMIT = 40 * 1024 * 1024


def recip(x):
    return 1.0 / x


def lookup(row, index):
    tiles = []
    for y in range(0, index.shape[0], SUB):
        across = [
            jnp.take_along_axis(
                row, index[y : y + SUB, z : z + LANE], axis=1, mode="promise_in_bounds"
            )
            for z in range(0, index.shape[1], LANE)
        ]
        tiles.append(jnp.concatenate(across, axis=1))
    return jnp.concatenate(tiles, axis=0)


NUMBERS = (
    "por",
    "shunt_a",
    "shunt_b",
    "half_a",
    "half_b",
    "half_t",
    "beta",
    "gamma",
    "alpha_a",
    "alpha_b",
    "kappa",
    "delta",
    "free_b",
    "share_b",
    "decay_b",
)


def derive(por, disp_a, disp_b, trans, exch, decay):
    immobile = 1.0 - por
    over_a = 1.0 / (immobile + exch + decay)
    over_b = 1.0 / (immobile + exch)
    beta = immobile * over_a
    gamma = exch * over_a
    share_b = exch * over_b
    return dict(
        por=por,
        shunt_a=por + decay + exch * (immobile + decay) * over_a,
        shunt_b=por + exch * immobile * over_b,
        half_a=0.5 / disp_a,
        half_b=0.5 / disp_b,
        half_t=0.5 / trans,
        beta=beta,
        gamma=gamma,
        alpha_a=exch * beta,
        alpha_b=share_b * immobile,
        kappa=decay + share_b * decay * gamma,
        delta=share_b * decay * beta,
        free_b=immobile * over_b,
        share_b=share_b,
        decay_b=decay * over_b,
    )


class Numbers:
    def __init__(self, tab_ref):
        self.tab_ref = tab_ref

    def __call__(self, name, index):
        k = NUMBERS.index(name)
        row = jnp.broadcast_to(self.tab_ref[k : k + 1, :], (SUB, LANE))
        return lookup(row, index)


def shifted_difference(value, axis):
    return pltpu.roll(value, value.shape[axis] - 1, axis) - value


def side_of(axis, stride):
    return (lax.axis_index(axis) // stride) % 2 == 1


def pack_kernel(
    conc_hbm,
    stratum_hbm,
    por_hbm,
    disp_hbm,
    trans_hbm,
    exch_hbm,
    decay_hbm,
    early_ref,
    late_ref,
    tab_ref,
    conc_ref,
    stratum_ref,
    por_ref,
    disp_ref,
    trans_ref,
    exch_ref,
    decay_ref,
    raw,
    sems,
):
    moves = [
        (stratum_hbm, stratum_ref),
        (conc_hbm.at[0:2], conc_ref.at[0:2]),
        (por_hbm, por_ref),
        (disp_hbm, disp_ref),
        (trans_hbm, trans_ref),
        (exch_hbm, exch_ref),
        (decay_hbm, decay_ref),
        (conc_hbm.at[2:4], conc_ref.at[2:4]),
    ]
    copies = [pltpu.make_async_copy(src, dst, sems.at[k]) for k, (src, dst) in enumerate(moves)]
    for copy in copies:
        copy.start()
    raw[...] = jnp.full(raw.shape, 0.5, jnp.float32)
    for copy in copies[2:7]:
        copy.wait()
    strata = por_ref.shape[1]
    raw[0:1, 0:strata] = por_ref[...]
    raw[1:3, 0:strata] = disp_ref[...]
    raw[3:4, 0:strata] = trans_ref[...]
    raw[4:5, 0:strata] = exch_ref[...]
    raw[5:6, 0:strata] = decay_ref[...]
    made = derive(*[raw[k : k + 1, :] for k in range(6)])
    for k, name in enumerate(NUMBERS):
        tab_ref[k : k + 1, :] = made[name]
    tab_ref[len(NUMBERS) : 2 * SUB, :] = raw[0 : 2 * SUB - len(NUMBERS), :]
    odd = side_of("trans", 1)
    last = stratum_ref.shape[1] - 1

    def put(k, low, high):
        early_ref[k] = jnp.where(odd, low, high)
        late_ref[k] = jnp.where(odd, high, low)

    copies[0].wait()
    numbered = [(stratum_ref[:, y, :] + 1).astype(jnp.float32) for y in (0, last)]
    put(2, *numbered)
    copies[1].wait()
    for k in (0, 1):
        put(k, conc_ref[k, :, 0, :], conc_ref[k, :, last, :])
    copies[7].wait()


def half_of(kept):
    second = lax.axis_index("flow") % 2
    return second if kept else 1 - second


def local_kernel(
    kept,
    tab_ref,
    stratum_ref,
    conc_ref,
    pay_ref,
    edge_ref,
    pass_a_ref,
    drop_a_ref,
    pass_b_ref,
    drop_b_ref,
    over_ref,
    source_a_ref,
    source_b_ref,
    head_a,
    head_b,
    kappa_ref,
    left_a,
    right_a,
    left_b,
    right_b,
    adj_l,
    adj_r,
):
    n, planes_y, planes_z = stratum_ref.shape
    half = planes_y // 2
    which = half_of(kept)
    rows = pl.ds(pl.multiple_of(which * half, half), half)
    other_rows = pl.ds(pl.multiple_of((1 - which) * half, half), half)
    number = Numbers(tab_ref)

    pieces = range(PIECES)
    m = n // PIECES
    shape = (half, planes_z)
    zero, one = jnp.zeros(shape, jnp.float32), jnp.ones(shape, jnp.float32)

    def from_left(j, carry):
        after = []
        for s, (cond_a, cond_b, half_a, half_b, through_a, through_b) in zip(pieces, carry):
            i = s * m + j
            index = stratum_ref[i, rows, :]
            new_a, new_b = number("half_a", index), number("half_b", index)
            face_a, face_b = half_a + new_a, half_b + new_b
            pass_a, pass_b = recip(1.0 + face_a * cond_a), recip(1.0 + face_b * cond_b)
            cond_a = number("shunt_a", index) + cond_a * pass_a
            cond_b = number("shunt_b", index) + cond_b * pass_b
            through_a, through_b = through_a * pass_a, through_b * pass_b
            kappa_ref[i] = number("kappa", index)
            pass_a_ref[i], pass_b_ref[i] = pass_a, pass_b
            drop_a_ref[i], drop_b_ref[i] = face_a * pass_a, face_b * pass_b
            head_a[i], head_b[i] = through_a, through_b
            after.append((cond_a, cond_b, new_a, new_b, through_a, through_b))
        return after

    ahead = lax.fori_loop(0, m, from_left, [(zero, zero, zero, zero, one, one)] * PIECES)
    over_a, over_b = [recip(c[0]) for c in ahead], [recip(c[1]) for c in ahead]
    for s in pieces:
        over_ref[0, s], over_ref[1, s] = over_a[s], over_b[s]

    def from_right(back, carry):
        after = []
        for s, (next_pass, next_drop, next_pass_b, next_drop_b, l_a, r_a, l_b, r_b, *couple) in zip(
            pieces, carry
        ):
            i = s * m + (m - 1 - back)
            l_a = next_pass * l_a + next_drop * head_a[i]
            l_b = next_pass_b * l_b + next_drop_b * head_b[i]
            r_a, r_b = next_pass * r_a, next_pass_b * r_b
            left_a[i], right_a[i], left_b[i], right_b[i] = l_a, r_a, l_b, r_b
            kappa = kappa_ref[i]
            k_l, k_r = kappa * l_a, kappa * r_a
            terms = [l_b * k_l, l_b * k_r, r_b * k_l, r_b * k_r]
            couple = [c + t for c, t in zip(couple, terms)]
            passes = (pass_a_ref[i], drop_a_ref[i], pass_b_ref[i], drop_b_ref[i])
            after.append((*passes, l_a, r_a, l_b, r_b, *couple))
        return after

    responses = lax.fori_loop(
        0,
        m,
        from_right,
        [(one, a, one, b, zero, a, zero, b, zero, zero, zero, zero) for a, b in zip(over_a, over_b)],
    )

    def share(j, carry):
        after = []
        for s, (g_l, g_r) in zip(pieces, carry):
            i = s * m + j
            kappa, pass_a = kappa_ref[i], pass_a_ref[i]
            g_l = kappa * left_b[i] + pass_a * g_l
            g_r = kappa * right_b[i] + pass_a * g_r
            adj_l[i], adj_r[i] = g_l, g_r
            after.append((g_l, g_r))
        return after

    lax.fori_loop(0, m, share, [(zero, zero)] * PIECES)

    lane = lax.broadcasted_iota(jnp.int32, shape, 1)
    line = lax.broadcasted_iota(jnp.int32, shape, 0)
    inside = (line < half - 1, lane < planes_z - 1)
    meets = line == (half - 1) * (1 - which)
    shift = jnp.where(which == 0, half - 1, 1)

    def sources(back, carry):
        after = []
        for s, (next_pass, next_drop, w_l, w_r, *free) in zip(pieces, carry):
            i = s * m + (m - 1 - back)
            w_l = next_pass * w_l + next_drop * adj_l[i]
            w_r = next_pass * w_r + next_drop * adj_r[i]
            adj_l[i], adj_r[i] = w_l, w_r
            index = stratum_ref[i, rows, :]
            half_t = number("half_t", index)
            por = number("por", index)
            c0, c1, c2, c3 = [conc_ref[k, i, rows, :] for k in range(4)]
            source_a = por * c0 + number("alpha_a", index) * c2
            source_b = por * c1 + number("alpha_b", index) * c3 + number("delta", index) * c2
            for axis in (0, 1):
                last = half_t.shape[axis] - 1
                face = jnp.where(
                    inside[axis], recip(half_t + pltpu.roll(half_t, last, axis)), 0.0
                )
                flow_a = face * shifted_difference(c0, axis)
                flow_b = face * shifted_difference(c1, axis)
                source_a = source_a + (flow_a - pltpu.roll(flow_a, 1, axis))
                source_b = source_b + (flow_b - pltpu.roll(flow_b, 1, axis))
            beyond_t = pltpu.roll(number("half_t", stratum_ref[i, other_rows, :]), shift, 0)
            face = jnp.where(meets, recip(half_t + beyond_t), 0.0)
            beyond_a = pltpu.roll(conc_ref[0, i, other_rows, :], shift, 0)
            beyond_b = pltpu.roll(conc_ref[1, i, other_rows, :], shift, 0)
            source_a = source_a + face * (beyond_a - c0)
            source_b = source_b + face * (beyond_b - c1)
            source_a_ref[i], source_b_ref[i] = source_a, source_b
            terms = [
                left_a[i] * source_a,
                right_a[i] * source_a,
                left_b[i] * source_b + w_l * source_a,
                right_b[i] * source_b + w_r * source_a,
            ]
            free = [f + t for f, t in zip(free, terms)]
            after.append((pass_a_ref[i], drop_a_ref[i], w_l, w_r, *free))
        return after

    totals = lax.fori_loop(0, m, sources, [(one, a) + (zero,) * 6 for a in over_a])
    for s in pieces:
        l_a, r_a, l_b, r_b, *couple = responses[s][4:]
        first = stratum_ref[s * m, rows, :]
        quantities = [
            l_a + number("half_a", first),
            r_a,
            over_a[s] + ahead[s][2],
            l_b + number("half_b", first),
            r_b,
            over_b[s] + ahead[s][3],
            *couple,
            *totals[s][4:],
        ]
        for q, value in enumerate(quantities):
            pay_ref[s, q] = value
    for k, ref in enumerate((left_a, right_a, left_b, right_b, adj_l, adj_r)):
        edge_ref[k] = jnp.where(which == 0, ref[:, 0, :], ref[:, half - 1, :])


def border_kernel(
    kept,
    tab_ref,
    early_ref,
    late_ref,
    beyond_early_ref,
    beyond_late_ref,
    edge_ref,
    pay_ref,
    out_ref,
    kept_ref,
    flow_ref,
):
    number = Numbers(tab_ref)
    n, planes_z = edge_ref.shape[1:]
    m = n // PIECES
    half = pay_ref.shape[2]
    low = half_of(kept) == 0
    early = side_of("trans", 1) == low
    own = jnp.where(early, early_ref[...], late_ref[...])
    beyond = jnp.where(early, beyond_early_ref[...], beyond_late_ref[...])
    own_id = own[2].astype(jnp.int32) - 1
    next_id = beyond[2].astype(jnp.int32) - 1
    resist = number("half_t", own_id) + number("half_t", next_id)
    end = jnp.where(low, 0, lax.axis_size("trans") - 1)
    face = jnp.where(lax.axis_index("trans") != end, recip(resist), 0.0)
    flow_a = face * (beyond[0] - own[0])
    flow_b = face * (beyond[1] - own[1])
    flow_ref[0], flow_ref[1] = flow_a, flow_b
    l_a, r_a, l_b, r_b, w_l, w_r = [edge_ref[k] for k in range(6)]
    changes = {
        FA_L: l_a * flow_a,
        FA_R: r_a * flow_a,
        FB_L: l_b * flow_b + w_l * flow_a,
        FB_R: r_b * flow_b + w_r * flow_a,
    }
    line = lax.broadcasted_iota(jnp.int32, (half, planes_z), 0)
    outer = line == jnp.where(low, 0, half - 1)
    blocks = []
    for s in range(PIECES):
        values = {q: pay_ref[s, q] for q in range(QUANTITIES)}
        for q, change in changes.items():
            total = jnp.sum(change[s * m : (s + 1) * m], axis=0, keepdims=True)
            values[q] = values[q] + jnp.where(outer, total, 0.0)
        blocks.append(values)
    slot = 0
    while len(blocks) > 1:
        joined = []
        for one, two in zip(blocks[::2], blocks[1::2]):
            merged, parts = merge(one, two)
            for k, value in enumerate(parts):
                kept_ref[slot, k] = value
            slot += 1
            joined.append(merged)
        blocks = joined
    for q in range(QUANTITIES):
        out_ref[q] = blocks[0][q]


FACE_L = (ZA_LL, ZB_LL, C_LL, FA_L, FB_L)
FACE_R = (ZA_RR, ZB_RR, C_RR, FA_R, FB_R)


def merge(one, two):
    over_a = recip(one[ZA_RR] + two[ZA_LL])
    over_b = recip(one[ZB_RR] + two[ZB_LL])
    across = one[C_RR] + two[C_LL]
    free_a = over_a * (one[FA_R] - two[FA_L])
    from_l, from_r = over_a * one[ZA_LR], over_a * two[ZA_LR]
    free_b = over_b * (one[FB_R] - two[FB_L] - across * free_a)
    from_l_b, from_r_b = over_b * one[ZB_LR], over_b * two[ZB_LR]
    cross_l = over_b * (one[C_RL] - across * from_l)
    cross_r = over_b * (two[C_LR] - across * from_r)
    merged = {
        ZA_LL: one[ZA_LL] - one[ZA_LR] * from_l,
        ZA_LR: one[ZA_LR] * from_r,
        ZA_RR: two[ZA_RR] - two[ZA_LR] * from_r,
        ZB_LL: one[ZB_LL] - one[ZB_LR] * from_l_b,
        ZB_LR: one[ZB_LR] * from_r_b,
        ZB_RR: two[ZB_RR] - two[ZB_LR] * from_r_b,
        C_LL: one[C_LL] - one[ZB_LR] * cross_l - one[C_LR] * from_l,
        C_LR: one[ZB_LR] * cross_r + one[C_LR] * from_r,
        C_RL: two[ZB_LR] * cross_l + two[C_RL] * from_l,
        C_RR: two[C_RR] - two[ZB_LR] * cross_r - two[C_RL] * from_r,
        FA_L: one[FA_L] - one[ZA_LR] * free_a,
        FA_R: two[FA_R] + two[ZA_LR] * free_a,
        FB_L: one[FB_L] - one[ZB_LR] * free_b - one[C_LR] * free_a,
        FB_R: two[FB_R] + two[ZB_LR] * free_b + two[C_RL] * free_a,
    }
    return merged, (free_a, from_l, from_r, free_b, from_l_b, from_r_b, cross_l, cross_r)


def between(kept, ends):
    free_a, from_l, from_r, free_b, from_l_b, from_r_b, cross_l, cross_r = kept
    l_a, r_a, l_b, r_b = ends
    middle_a = free_a + from_l * l_a - from_r * r_a
    middle_b = free_b + from_l_b * l_b - from_r_b * r_b + cross_l * l_a - cross_r * r_a
    return middle_a, middle_b


def merge_kernel(stride, last, own_ref, other_ref, out_ref, kept_ref, *face_ref):
    second = side_of("flow", stride)
    own = [own_ref[q] for q in range(QUANTITIES)]
    other = [other_ref[q] for q in range(QUANTITIES)]
    one = [jnp.where(second, b, a) for a, b in zip(own, other)]
    two = [jnp.where(second, a, b) for a, b in zip(own, other)]
    merged, kept = merge(one, two)
    for q, value in merged.items():
        out_ref[q] = value
    for k, value in enumerate(kept):
        kept_ref[k] = value
    if last:
        after = side_of("flow", 2 * stride)
        for k, (l, r) in enumerate(zip(FACE_L, FACE_R)):
            face_ref[0][k] = jnp.where(after, merged[l], merged[r])


def close_kernel(strides, own_ref, other_ref, *refs):
    kept_refs, mine_ref, send_ref = refs[:-2], refs[-2], refs[-1]
    stride = strides[-1]
    second = side_of("flow", stride)
    own = [jnp.where(second, own_ref[l], own_ref[r]) for l, r in zip(FACE_L, FACE_R)]
    z_a, z_b, couple, f_a, f_b = [own[k] + other_ref[k] for k in range(3)] + [
        jnp.where(second, other_ref[k] - own[k], own[k] - other_ref[k]) for k in (3, 4)
    ]
    current_a = recip(z_a) * f_a
    current_b = recip(z_b) * (f_b - couple * current_a)
    nothing = jnp.zeros_like(current_a)

    def side_ends(after, middle_a, middle_b, ends):
        l_a, r_a, l_b, r_b = ends
        return (
            jnp.where(after, middle_a, l_a),
            jnp.where(after, r_a, -middle_a),
            jnp.where(after, middle_b, l_b),
            jnp.where(after, r_b, -middle_b),
        )

    ends = side_ends(second, current_a, current_b, (nothing,) * 4)
    for stride, kept_ref in reversed(list(zip(strides[:-1], kept_refs))):
        middle_a, middle_b = between([kept_ref[k] for k in range(KEPT)], ends)
        after = side_of("flow", stride)
        if stride == 1:
            other_ends = side_ends(jnp.logical_not(after), middle_a, middle_b, ends)
            for q, value in enumerate(other_ends):
                send_ref[q] = value
        ends = side_ends(after, middle_a, middle_b, ends)
    for q, value in enumerate(ends):
        mine_ref[q] = value


def final_kernel(
    kept,
    tab_ref,
    stratum_ref,
    conc_ref,
    pass_a_ref,
    drop_a_ref,
    pass_b_ref,
    drop_b_ref,
    over_ref,
    source_a_ref,
    source_b_ref,
    kept_ref,
    flow_ref,
    current_ref,
    *refs,
):
    out_hbm, gather_a, gather_b, made, sems = refs[-5:]
    n, planes_y, planes_z = stratum_ref.shape
    half = planes_y // 2
    which = half_of(kept)
    rows = pl.ds(pl.multiple_of(which * half, half), half)
    number = Numbers(tab_ref)
    line = lax.broadcasted_iota(jnp.int32, (half, planes_z), 0)
    outer = line == (half - 1) * which

    def with_border(source, component, i):
        flow = jnp.broadcast_to(flow_ref[component, pl.ds(i, 1), :], source.shape)
        return source + jnp.where(outer, flow, 0.0)

    ends = [tuple(current_ref[q] for q in range(CURRENTS))]
    slot = PIECES - 1
    while len(ends) < PIECES:
        slot -= len(ends)
        parts = []
        for k, (l_a, r_a, l_b, r_b) in enumerate(ends):
            values = [kept_ref[slot + k, v] for v in range(KEPT)]
            middle_a, middle_b = between(values, (l_a, r_a, l_b, r_b))
            parts += [(l_a, -middle_a, l_b, -middle_b), (middle_a, r_a, middle_b, r_b)]
        ends = parts

    pieces = range(PIECES)
    m = n // PIECES
    one = jnp.ones((half, planes_z), jnp.float32)

    def collect_a(j, carry):
        after = []
        for s, value in zip(pieces, carry):
            i = s * m + j
            gather_a[i] = with_border(source_a_ref[i], 0, i) + pass_a_ref[i] * value
            after.append(gather_a[i])
        return after

    def solve_a(back, carry):
        after = []
        for s, (next_pass, next_drop, x) in zip(pieces, carry):
            i = s * m + (m - 1 - back)
            x = next_pass * x + next_drop * gather_a[i]
            made[0, i] = x
            after.append((pass_a_ref[i], drop_a_ref[i], x))
        return after

    def collect_b(j, carry):
        after = []
        for s, value in zip(pieces, carry):
            i = s * m + j
            kappa = number("kappa", stratum_ref[i, rows, :])
            source = with_border(source_b_ref[i], 1, i) + kappa * made[0, i]
            gather_b[i] = source + pass_b_ref[i] * value
            after.append(gather_b[i])
        return after

    def result(i):
        return pltpu.make_async_copy(made.at[:, i], out_hbm.at[:, i, rows, :], sems.at[i])

    def solve_b(back, carry):
        after = []
        for s, (next_pass, next_drop, x) in zip(pieces, carry):
            i = s * m + (m - 1 - back)
            x = next_pass * x + next_drop * gather_b[i]
            made[1, i] = x
            index = stratum_ref[i, rows, :]
            x2 = (
                number("beta", index) * conc_ref[2, i, rows, :]
                + number("gamma", index) * made[0, i]
            )
            made[2, i] = x2
            made[3, i] = (
                number("free_b", index) * conc_ref[3, i, rows, :]
                + number("share_b", index) * x
                + number("decay_b", index) * x2
            )
            after.append((pass_b_ref[i], drop_b_ref[i], x))
        for s in pieces:
            result(s * m + (m - 1 - back)).start()
        return after

    lax.fori_loop(0, m, collect_a, [ends[s][0] for s in pieces])
    start = [(one, over_ref[0, s], ends[s][1] * over_ref[0, s]) for s in pieces]
    lax.fori_loop(0, m, solve_a, start)
    lax.fori_loop(0, m, collect_b, [ends[s][2] for s in pieces])
    start = [(one, over_ref[1, s], ends[s][3] * over_ref[1, s]) for s in pieces]
    lax.fori_loop(0, m, solve_b, start)
    for i in range(n):
        result(i).wait()


def call(kernel, outs, scratch=()):
    return pl.pallas_call(
        kernel,
        out_shape=[jax.ShapeDtypeStruct(shape, jnp.float32) for shape in outs],
        scratch_shapes=[pltpu.VMEM(shape, jnp.float32) for shape in scratch],
        compiler_params=pltpu.CompilerParams(vmem_limit_bytes=VMEM_LIMIT),
    )


def per_device(
    concentration,
    stratum,
    porosity,
    dispersion_table,
    transverse_table,
    exchange_table,
    decay_table,
):
    n, planes_y, planes_z = stratum.shape
    peers = lax.axis_size("flow")
    half = planes_y // 2
    strides = [1 << k for k in range(peers.bit_length() - 1)]
    cells = (n, planes_y, planes_z)

    halo = (3, n, planes_z)
    strata = porosity.shape[0]
    hbm = pl.BlockSpec(memory_space=pltpu.HBM)
    early, late, table, concentration, stratum = pl.pallas_call(
        pack_kernel,
        out_shape=[
            jax.ShapeDtypeStruct(halo, jnp.float32),
            jax.ShapeDtypeStruct(halo, jnp.float32),
            jax.ShapeDtypeStruct((2 * SUB, LANE), jnp.float32),
            jax.ShapeDtypeStruct(concentration.shape, jnp.float32),
            jax.ShapeDtypeStruct(cells, jnp.int32),
        ],
        in_specs=[hbm] * 7,
        scratch_shapes=[
            pltpu.VMEM((1, strata), jnp.float32),
            pltpu.VMEM((2, strata), jnp.float32),
            pltpu.VMEM((1, strata), jnp.float32),
            pltpu.VMEM((1, strata), jnp.float32),
            pltpu.VMEM((1, strata), jnp.float32),
            pltpu.VMEM((SUB, LANE), jnp.float32),
            pltpu.SemaphoreType.DMA((8,)),
        ],
        compiler_params=pltpu.CompilerParams(vmem_limit_bytes=VMEM_LIMIT),
    )(
        *[
            pltpu.with_memory_space_constraint(value, pltpu.HBM)
            for value in (
                concentration,
                stratum,
                porosity[None],
                dispersion_table.T,
                transverse_table[None],
                exchange_table[None],
                decay_table[None],
            )
        ]
    )
    groups = lax.axis_size("trans")
    def swap(value, start):
        low = range(start, groups - 1, 2)
        pairs = [(i, i + 1) for i in low] + [(i + 1, i) for i in low]
        if start:
            pairs += [(0, groups - 1), (groups - 1, 0)]
        return lax.ppermute(value, "trans", pairs)

    beyond_early, beyond_late = swap(early, 0), swap(late, 1)

    def exchange(value, stride):
        return lax.ppermute(value, "flow", [(i, i ^ stride) for i in range(peers)])

    half_cells = (n, half, planes_z)
    block_shape = (QUANTITIES, half, planes_z)

    def local(kept):
        pay, edge, *rest = call(
            functools.partial(local_kernel, kept),
            [
                (PIECES,) + block_shape,
                (6, n, planes_z),
                *[half_cells] * 4,
                (2, PIECES, half, planes_z),
                *[half_cells] * 2,
            ],
            [half_cells] * 9,
        )(table, stratum, concentration)
        pay, parts, flow = call(
            functools.partial(border_kernel, kept),
            [block_shape, (PIECES - 1, KEPT, half, planes_z), (2, n, planes_z)],
        )(table, early, late, beyond_early, beyond_late, edge, pay)
        return pay, (*rest, parts, flow)

    send, sent_rest = local(False)
    block, kept_rest = local(True)
    kept = []
    for stride in strides[:-1]:
        other = exchange(send, stride)
        last = stride == strides[-2]
        block, keep, *face = call(
            functools.partial(merge_kernel, stride, last),
            [block_shape, (KEPT, half, planes_z)] + [(5, half, planes_z)] * last,
        )(block, other)
        kept.append(keep)
        send = face[0] if last else block
    ends_shape = (CURRENTS, half, planes_z)
    mine, send = call(functools.partial(close_kernel, strides), [ends_shape, ends_shape])(
        block, exchange(send, strides[-1]), *kept
    )
    currents = exchange(send, 1)
    def final(kept, rest, currents, *before):
        whole = jax.ShapeDtypeStruct((4,) + cells, jnp.float32)
        vmem = pl.BlockSpec(memory_space=pltpu.VMEM)
        return pl.pallas_call(
            functools.partial(final_kernel, kept),
            out_shape=whole,
            in_specs=[vmem] * 13 + [hbm] * len(before),
            out_specs=hbm,
            scratch_shapes=[
                pltpu.VMEM(half_cells, jnp.float32),
                pltpu.VMEM(half_cells, jnp.float32),
                pltpu.VMEM((4,) + half_cells, jnp.float32),
                pltpu.SemaphoreType.DMA((n,)),
            ],
            input_output_aliases={13: 0} if before else {},
            compiler_params=pltpu.CompilerParams(vmem_limit_bytes=VMEM_LIMIT),
        )(table, stratum, concentration, *rest, currents, *before)

    out = final(True, kept_rest, mine)
    return final(False, sent_rest, currents, out)


def solution(mesh):
    in_specs = (P(None, "flow", "trans", None), P("flow", "trans", None), P(), P(), P(), P(), P())
    out_specs = P(None, "flow", "trans", None)
    return jax.shard_map(
        per_device, mesh=mesh, in_specs=in_specs, out_specs=out_specs, check_vma=False
    )
```

```python
import functools

import jax
import jax.numpy as jnp
from jax import lax
from jax.experimental import pallas as pl
from jax.experimental.pallas import tpu as pltpu
from jax.sharding import PartitionSpec as P

SUB, LANE = 8, 128
ZA_LL, ZA_LR, ZA_RR, ZB_LL, ZB_LR, ZB_RR, C_LL, C_LR, C_RL, C_RR, FA_L, FA_R, FB_L, FB_R = range(14)
QUANTITIES = 14
CURRENTS = 4
KEPT = 8
PIECES = 4
VMEM_LIMIT = 40 * 1024 * 1024


def recip(x):
    return 1.0 / x


def lookup(row, index):
    tiles = []
    for y in range(0, index.shape[0], SUB):
        across = [
            jnp.take_along_axis(
                row, index[y : y + SUB, z : z + LANE], axis=1, mode="promise_in_bounds"
            )
            for z in range(0, index.shape[1], LANE)
        ]
        tiles.append(jnp.concatenate(across, axis=1))
    return jnp.concatenate(tiles, axis=0)


NUMBERS = (
    "por",
    "shunt_a",
    "shunt_b",
    "half_a",
    "half_b",
    "half_t",
    "beta",
    "gamma",
    "alpha_a",
    "alpha_b",
    "kappa",
    "delta",
    "free_b",
    "share_b",
    "decay_b",
)


def derive(por, disp_a, disp_b, trans, exch, decay):
    immobile = 1.0 - por
    over_a = 1.0 / (immobile + exch + decay)
    over_b = 1.0 / (immobile + exch)
    beta = immobile * over_a
    gamma = exch * over_a
    share_b = exch * over_b
    return dict(
        por=por,
        shunt_a=por + decay + exch * (immobile + decay) * over_a,
        shunt_b=por + exch * immobile * over_b,
        half_a=0.5 / disp_a,
        half_b=0.5 / disp_b,
        half_t=0.5 / trans,
        beta=beta,
        gamma=gamma,
        alpha_a=exch * beta,
        alpha_b=share_b * immobile,
        kappa=decay + share_b * decay * gamma,
        delta=share_b * decay * beta,
        free_b=immobile * over_b,
        share_b=share_b,
        decay_b=decay * over_b,
    )


class Numbers:
    def __init__(self, tab_ref):
        self.tab_ref = tab_ref

    def __call__(self, name, index):
        k = NUMBERS.index(name)
        row = jnp.broadcast_to(self.tab_ref[k : k + 1, :], (SUB, LANE))
        return lookup(row, index)


def shifted_difference(value, axis):
    return pltpu.roll(value, value.shape[axis] - 1, axis) - value


def side_of(axis, stride):
    return (lax.axis_index(axis) // stride) % 2 == 1


def pack_kernel(
    conc_hbm,
    stratum_hbm,
    por_hbm,
    disp_hbm,
    trans_hbm,
    exch_hbm,
    decay_hbm,
    early_ref,
    late_ref,
    tab_ref,
    conc_ref,
    stratum_ref,
    por_ref,
    disp_ref,
    trans_ref,
    exch_ref,
    decay_ref,
    raw,
    sems,
):
    moves = [
        (stratum_hbm, stratum_ref),
        (conc_hbm.at[0:2], conc_ref.at[0:2]),
        (por_hbm, por_ref),
        (disp_hbm, disp_ref),
        (trans_hbm, trans_ref),
        (exch_hbm, exch_ref),
        (decay_hbm, decay_ref),
        (conc_hbm.at[2:4], conc_ref.at[2:4]),
    ]
    copies = [pltpu.make_async_copy(src, dst, sems.at[k]) for k, (src, dst) in enumerate(moves)]
    for copy in copies:
        copy.start()
    raw[...] = jnp.full(raw.shape, 0.5, jnp.float32)
    for copy in copies[2:7]:
        copy.wait()
    strata = por_ref.shape[1]
    raw[0:1, 0:strata] = por_ref[...]
    raw[1:3, 0:strata] = disp_ref[...]
    raw[3:4, 0:strata] = trans_ref[...]
    raw[4:5, 0:strata] = exch_ref[...]
    raw[5:6, 0:strata] = decay_ref[...]
    made = derive(*[raw[k : k + 1, :] for k in range(6)])
    for k, name in enumerate(NUMBERS):
        tab_ref[k : k + 1, :] = made[name]
    tab_ref[len(NUMBERS) : 2 * SUB, :] = raw[0 : 2 * SUB - len(NUMBERS), :]
    odd = side_of("trans", 1)
    last = stratum_ref.shape[1] - 1

    def put(k, low, high):
        early_ref[k] = jnp.where(odd, low, high)
        late_ref[k] = jnp.where(odd, high, low)

    copies[0].wait()
    numbered = [(stratum_ref[:, y, :] + 1).astype(jnp.float32) for y in (0, last)]
    put(2, *numbered)
    copies[1].wait()
    for k in (0, 1):
        put(k, conc_ref[k, :, 0, :], conc_ref[k, :, last, :])
    copies[7].wait()


def half_of(kept):
    second = lax.axis_index("flow") % 2
    return second if kept else 1 - second


def local_kernel(
    kept,
    tab_ref,
    stratum_ref,
    conc_ref,
    pay_ref,
    edge_ref,
    pass_a_ref,
    drop_a_ref,
    pass_b_ref,
    drop_b_ref,
    over_ref,
    source_a_ref,
    source_b_ref,
    head_a,
    head_b,
    kappa_ref,
    left_a,
    right_a,
    left_b,
    right_b,
    adj_l,
    adj_r,
):
    n, planes_y, planes_z = stratum_ref.shape
    half = planes_y // 2
    which = half_of(kept)
    rows = pl.ds(pl.multiple_of(which * half, half), half)
    other_rows = pl.ds(pl.multiple_of((1 - which) * half, half), half)
    number = Numbers(tab_ref)

    pieces = range(PIECES)
    m = n // PIECES
    shape = (half, planes_z)
    zero, one = jnp.zeros(shape, jnp.float32), jnp.ones(shape, jnp.float32)

    def from_left(j, carry):
        after = []
        for s, (cond_a, cond_b, half_a, half_b, through_a, through_b) in zip(pieces, carry):
            i = s * m + j
            index = stratum_ref[i, rows, :]
            new_a, new_b = number("half_a", index), number("half_b", index)
            face_a, face_b = half_a + new_a, half_b + new_b
            pass_a, pass_b = recip(1.0 + face_a * cond_a), recip(1.0 + face_b * cond_b)
            cond_a = number("shunt_a", index) + cond_a * pass_a
            cond_b = number("shunt_b", index) + cond_b * pass_b
            through_a, through_b = through_a * pass_a, through_b * pass_b
            kappa_ref[i] = number("kappa", index)
            pass_a_ref[i], pass_b_ref[i] = pass_a, pass_b
            drop_a_ref[i], drop_b_ref[i] = face_a * pass_a, face_b * pass_b
            head_a[i], head_b[i] = through_a, through_b
            after.append((cond_a, cond_b, new_a, new_b, through_a, through_b))
        return after

    ahead = lax.fori_loop(0, m, from_left, [(zero, zero, zero, zero, one, one)] * PIECES)
    over_a, over_b = [recip(c[0]) for c in ahead], [recip(c[1]) for c in ahead]
    for s in pieces:
        over_ref[0, s], over_ref[1, s] = over_a[s], over_b[s]

    def from_right(back, carry):
        after = []
        for s, (next_pass, next_drop, next_pass_b, next_drop_b, l_a, r_a, l_b, r_b, *couple) in zip(
            pieces, carry
        ):
            i = s * m + (m - 1 - back)
            l_a = next_pass * l_a + next_drop * head_a[i]
            l_b = next_pass_b * l_b + next_drop_b * head_b[i]
            r_a, r_b = next_pass * r_a, next_pass_b * r_b
            left_a[i], right_a[i], left_b[i], right_b[i] = l_a, r_a, l_b, r_b
            kappa = kappa_ref[i]
            k_l, k_r = kappa * l_a, kappa * r_a
            terms = [l_b * k_l, l_b * k_r, r_b * k_l, r_b * k_r]
            couple = [c + t for c, t in zip(couple, terms)]
            passes = (pass_a_ref[i], drop_a_ref[i], pass_b_ref[i], drop_b_ref[i])
            after.append((*passes, l_a, r_a, l_b, r_b, *couple))
        return after

    responses = lax.fori_loop(
        0,
        m,
        from_right,
        [(one, a, one, b, zero, a, zero, b, zero, zero, zero, zero) for a, b in zip(over_a, over_b)],
    )

    def share(j, carry):
        after = []
        for s, (g_l, g_r) in zip(pieces, carry):
            i = s * m + j
            kappa, pass_a = kappa_ref[i], pass_a_ref[i]
            g_l = kappa * left_b[i] + pass_a * g_l
            g_r = kappa * right_b[i] + pass_a * g_r
            adj_l[i], adj_r[i] = g_l, g_r
            after.append((g_l, g_r))
        return after

    lax.fori_loop(0, m, share, [(zero, zero)] * PIECES)

    lane = lax.broadcasted_iota(jnp.int32, shape, 1)
    line = lax.broadcasted_iota(jnp.int32, shape, 0)
    inside = (line < half - 1, lane < planes_z - 1)
    meets = line == (half - 1) * (1 - which)
    shift = jnp.where(which == 0, half - 1, 1)

    def sources(back, carry):
        after = []
        for s, (next_pass, next_drop, w_l, w_r, *free) in zip(pieces, carry):
            i = s * m + (m - 1 - back)
            w_l = next_pass * w_l + next_drop * adj_l[i]
            w_r = next_pass * w_r + next_drop * adj_r[i]
            adj_l[i], adj_r[i] = w_l, w_r
            index = stratum_ref[i, rows, :]
            half_t = number("half_t", index)
            por = number("por", index)
            c0, c1, c2, c3 = [conc_ref[k, i, rows, :] for k in range(4)]
            source_a = por * c0 + number("alpha_a", index) * c2
            source_b = por * c1 + number("alpha_b", index) * c3 + number("delta", index) * c2
            for axis in (0, 1):
                last = half_t.shape[axis] - 1
                face = jnp.where(
                    inside[axis], recip(half_t + pltpu.roll(half_t, last, axis)), 0.0
                )
                flow_a = face * shifted_difference(c0, axis)
                flow_b = face * shifted_difference(c1, axis)
                source_a = source_a + (flow_a - pltpu.roll(flow_a, 1, axis))
                source_b = source_b + (flow_b - pltpu.roll(flow_b, 1, axis))
            beyond_t = pltpu.roll(number("half_t", stratum_ref[i, other_rows, :]), shift, 0)
            face = jnp.where(meets, recip(half_t + beyond_t), 0.0)
            beyond_a = pltpu.roll(conc_ref[0, i, other_rows, :], shift, 0)
            beyond_b = pltpu.roll(conc_ref[1, i, other_rows, :], shift, 0)
            source_a = source_a + face * (beyond_a - c0)
            source_b = source_b + face * (beyond_b - c1)
            source_a_ref[i], source_b_ref[i] = source_a, source_b
            terms = [
                left_a[i] * source_a,
                right_a[i] * source_a,
                left_b[i] * source_b + w_l * source_a,
                right_b[i] * source_b + w_r * source_a,
            ]
            free = [f + t for f, t in zip(free, terms)]
            after.append((pass_a_ref[i], drop_a_ref[i], w_l, w_r, *free))
        return after

    totals = lax.fori_loop(0, m, sources, [(one, a) + (zero,) * 6 for a in over_a])
    for s in pieces:
        l_a, r_a, l_b, r_b, *couple = responses[s][4:]
        first = stratum_ref[s * m, rows, :]
        quantities = [
            l_a + number("half_a", first),
            r_a,
            over_a[s] + ahead[s][2],
            l_b + number("half_b", first),
            r_b,
            over_b[s] + ahead[s][3],
            *couple,
            *totals[s][4:],
        ]
        for q, value in enumerate(quantities):
            pay_ref[s, q] = value
    for k, ref in enumerate((left_a, right_a, left_b, right_b, adj_l, adj_r)):
        edge_ref[k] = jnp.where(which == 0, ref[:, 0, :], ref[:, half - 1, :])


def border_kernel(
    kept,
    tab_ref,
    early_ref,
    late_ref,
    beyond_late_ref,
    beyond_early_ref,
    edge_ref,
    pay_ref,
    out_ref,
    kept_ref,
    flow_ref,
):
    number = Numbers(tab_ref)
    n, planes_z = edge_ref.shape[1:]
    m = n // PIECES
    half = pay_ref.shape[2]
    low = half_of(kept) == 0
    early = side_of("trans", 1) == low
    own = jnp.where(early, early_ref[...], late_ref[...])
    beyond = jnp.where(early, beyond_early_ref[...], beyond_late_ref[...])
    own_id = own[2].astype(jnp.int32) - 1
    next_id = beyond[2].astype(jnp.int32) - 1
    resist = number("half_t", own_id) + number("half_t", next_id)
    end = jnp.where(low, 0, lax.axis_size("trans") - 1)
    face = jnp.where(lax.axis_index("trans") != end, recip(resist), 0.0)
    flow_a = face * (beyond[0] - own[0])
    flow_b = face * (beyond[1] - own[1])
    flow_ref[0], flow_ref[1] = flow_a, flow_b
    l_a, r_a, l_b, r_b, w_l, w_r = [edge_ref[k] for k in range(6)]
    changes = {
        FA_L: l_a * flow_a,
        FA_R: r_a * flow_a,
        FB_L: l_b * flow_b + w_l * flow_a,
        FB_R: r_b * flow_b + w_r * flow_a,
    }
    line = lax.broadcasted_iota(jnp.int32, (half, planes_z), 0)
    outer = line == jnp.where(low, 0, half - 1)
    blocks = []
    for s in range(PIECES):
        values = {q: pay_ref[s, q] for q in range(QUANTITIES)}
        for q, change in changes.items():
            total = jnp.sum(change[s * m : (s + 1) * m], axis=0, keepdims=True)
            values[q] = values[q] + jnp.where(outer, total, 0.0)
        blocks.append(values)
    slot = 0
    while len(blocks) > 1:
        joined = []
        for one, two in zip(blocks[::2], blocks[1::2]):
            merged, parts = merge(one, two)
            for k, value in enumerate(parts):
                kept_ref[slot, k] = value
            slot += 1
            joined.append(merged)
        blocks = joined
    for q in range(QUANTITIES):
        out_ref[q] = blocks[0][q]


FACE_L = (ZA_LL, ZB_LL, C_LL, FA_L, FB_L)
FACE_R = (ZA_RR, ZB_RR, C_RR, FA_R, FB_R)


def merge(one, two):
    over_a = recip(one[ZA_RR] + two[ZA_LL])
    over_b = recip(one[ZB_RR] + two[ZB_LL])
    across = one[C_RR] + two[C_LL]
    free_a = over_a * (one[FA_R] - two[FA_L])
    from_l, from_r = over_a * one[ZA_LR], over_a * two[ZA_LR]
    free_b = over_b * (one[FB_R] - two[FB_L] - across * free_a)
    from_l_b, from_r_b = over_b * one[ZB_LR], over_b * two[ZB_LR]
    cross_l = over_b * (one[C_RL] - across * from_l)
    cross_r = over_b * (two[C_LR] - across * from_r)
    merged = {
        ZA_LL: one[ZA_LL] - one[ZA_LR] * from_l,
        ZA_LR: one[ZA_LR] * from_r,
        ZA_RR: two[ZA_RR] - two[ZA_LR] * from_r,
        ZB_LL: one[ZB_LL] - one[ZB_LR] * from_l_b,
        ZB_LR: one[ZB_LR] * from_r_b,
        ZB_RR: two[ZB_RR] - two[ZB_LR] * from_r_b,
        C_LL: one[C_LL] - one[ZB_LR] * cross_l - one[C_LR] * from_l,
        C_LR: one[ZB_LR] * cross_r + one[C_LR] * from_r,
        C_RL: two[ZB_LR] * cross_l + two[C_RL] * from_l,
        C_RR: two[C_RR] - two[ZB_LR] * cross_r - two[C_RL] * from_r,
        FA_L: one[FA_L] - one[ZA_LR] * free_a,
        FA_R: two[FA_R] + two[ZA_LR] * free_a,
        FB_L: one[FB_L] - one[ZB_LR] * free_b - one[C_LR] * free_a,
        FB_R: two[FB_R] + two[ZB_LR] * free_b + two[C_RL] * free_a,
    }
    return merged, (free_a, from_l, from_r, free_b, from_l_b, from_r_b, cross_l, cross_r)


def between(kept, ends):
    free_a, from_l, from_r, free_b, from_l_b, from_r_b, cross_l, cross_r = kept
    l_a, r_a, l_b, r_b = ends
    middle_a = free_a + from_l * l_a - from_r * r_a
    middle_b = free_b + from_l_b * l_b - from_r_b * r_b + cross_l * l_a - cross_r * r_a
    return middle_a, middle_b


def merge_kernel(stride, last, own_ref, other_ref, out_ref, kept_ref, *face_ref):
    second = side_of("flow", stride)
    own = [own_ref[q] for q in range(QUANTITIES)]
    other = [other_ref[q] for q in range(QUANTITIES)]
    one = [jnp.where(second, b, a) for a, b in zip(own, other)]
    two = [jnp.where(second, a, b) for a, b in zip(own, other)]
    merged, kept = merge(one, two)
    for q, value in merged.items():
        out_ref[q] = value
    for k, value in enumerate(kept):
        kept_ref[k] = value
    if last:
        after = side_of("flow", 2 * stride)
        for k, (l, r) in enumerate(zip(FACE_L, FACE_R)):
            face_ref[0][k] = jnp.where(after, merged[l], merged[r])


def close_kernel(strides, own_ref, other_ref, *refs):
    kept_refs, mine_ref, send_ref = refs[:-2], refs[-2], refs[-1]
    stride = strides[-1]
    second = side_of("flow", stride)
    own = [jnp.where(second, own_ref[l], own_ref[r]) for l, r in zip(FACE_L, FACE_R)]
    z_a, z_b, couple, f_a, f_b = [own[k] + other_ref[k] for k in range(3)] + [
        jnp.where(second, other_ref[k] - own[k], own[k] - other_ref[k]) for k in (3, 4)
    ]
    current_a = recip(z_a) * f_a
    current_b = recip(z_b) * (f_b - couple * current_a)
    nothing = jnp.zeros_like(current_a)

    def side_ends(after, middle_a, middle_b, ends):
        l_a, r_a, l_b, r_b = ends
        return (
            jnp.where(after, middle_a, l_a),
            jnp.where(after, r_a, -middle_a),
            jnp.where(after, middle_b, l_b),
            jnp.where(after, r_b, -middle_b),
        )

    ends = side_ends(second, current_a, current_b, (nothing,) * 4)
    for stride, kept_ref in reversed(list(zip(strides[:-1], kept_refs))):
        middle_a, middle_b = between([kept_ref[k] for k in range(KEPT)], ends)
        after = side_of("flow", stride)
        if stride == 1:
            other_ends = side_ends(jnp.logical_not(after), middle_a, middle_b, ends)
            for q, value in enumerate(other_ends):
                send_ref[q] = value
        ends = side_ends(after, middle_a, middle_b, ends)
    for q, value in enumerate(ends):
        mine_ref[q] = value


def final_kernel(
    kept,
    tab_ref,
    stratum_ref,
    conc_ref,
    pass_a_ref,
    drop_a_ref,
    pass_b_ref,
    drop_b_ref,
    over_ref,
    source_a_ref,
    source_b_ref,
    kept_ref,
    flow_ref,
    current_ref,
    *refs,
):
    out_hbm, gather_a, gather_b, made, sems = refs[-5:]
    n, planes_y, planes_z = stratum_ref.shape
    half = planes_y // 2
    which = half_of(kept)
    rows = pl.ds(pl.multiple_of(which * half, half), half)
    number = Numbers(tab_ref)
    line = lax.broadcasted_iota(jnp.int32, (half, planes_z), 0)
    outer = line == (half - 1) * which

    def with_border(source, component, i):
        flow = jnp.broadcast_to(flow_ref[component, pl.ds(i, 1), :], source.shape)
        return source + jnp.where(outer, flow, 0.0)

    ends = [tuple(current_ref[q] for q in range(CURRENTS))]
    slot = PIECES - 1
    while len(ends) < PIECES:
        slot -= len(ends)
        parts = []
        for k, (l_a, r_a, l_b, r_b) in enumerate(ends):
            values = [kept_ref[slot + k, v] for v in range(KEPT)]
            middle_a, middle_b = between(values, (l_a, r_a, l_b, r_b))
            parts += [(l_a, -middle_a, l_b, -middle_b), (middle_a, r_a, middle_b, r_b)]
        ends = parts

    pieces = range(PIECES)
    m = n // PIECES
    values = [ends[s][0] for s in pieces]
    for j in range(m):
        for s in pieces:
            i = s * m + j
            values[s] = with_border(source_a_ref[i], 0, i) + values[s]
            if j < m - 1:
                gather_a[i] = values[s]
                values[s] = pass_a_ref[i + 1] * values[s]
    x = [(values[s] + ends[s][1]) * over_ref[0, s] for s in pieces]
    for j in reversed(range(m)):
        for s in pieces:
            i = s * m + j
            if j < m - 1:
                x[s] = pass_a_ref[i + 1] * x[s] + drop_a_ref[i + 1] * gather_a[i]
            made[0, i] = x[s]
    values = [ends[s][2] for s in pieces]
    for j in range(m):
        for s in pieces:
            i = s * m + j
            kappa = number("kappa", stratum_ref[i, rows, :])
            values[s] = with_border(source_b_ref[i], 1, i) + kappa * made[0, i] + values[s]
            if j < m - 1:
                gather_b[i] = values[s]
                values[s] = pass_b_ref[i + 1] * values[s]
    x = [(values[s] + ends[s][3]) * over_ref[1, s] for s in pieces]
    copies = []
    for j in reversed(range(m)):
        for s in pieces:
            i = s * m + j
            if j < m - 1:
                x[s] = pass_b_ref[i + 1] * x[s] + drop_b_ref[i + 1] * gather_b[i]
            made[1, i] = x[s]
            index = stratum_ref[i, rows, :]
            x2 = (
                number("beta", index) * conc_ref[2, i, rows, :]
                + number("gamma", index) * made[0, i]
            )
            made[2, i] = x2
            made[3, i] = (
                number("free_b", index) * conc_ref[3, i, rows, :]
                + number("share_b", index) * x[s]
                + number("decay_b", index) * x2
            )
            copies.append(
                pltpu.make_async_copy(made.at[:, i], out_hbm.at[:, i, rows, :], sems.at[i])
            )
            copies[-1].start()
    for copy in copies:
        copy.wait()


def call(kernel, outs, scratch=()):
    return pl.pallas_call(
        kernel,
        out_shape=[jax.ShapeDtypeStruct(shape, jnp.float32) for shape in outs],
        scratch_shapes=[pltpu.VMEM(shape, jnp.float32) for shape in scratch],
        compiler_params=pltpu.CompilerParams(vmem_limit_bytes=VMEM_LIMIT),
    )


def per_device(
    concentration,
    stratum,
    porosity,
    dispersion_table,
    transverse_table,
    exchange_table,
    decay_table,
):
    n, planes_y, planes_z = stratum.shape
    peers = lax.axis_size("flow")
    half = planes_y // 2
    strides = [1 << k for k in range(peers.bit_length() - 1)]
    cells = (n, planes_y, planes_z)

    halo = (3, n, planes_z)
    strata = porosity.shape[0]
    hbm = pl.BlockSpec(memory_space=pltpu.HBM)
    early, late, table, concentration, stratum = pl.pallas_call(
        pack_kernel,
        out_shape=[
            jax.ShapeDtypeStruct(halo, jnp.float32),
            jax.ShapeDtypeStruct(halo, jnp.float32),
            jax.ShapeDtypeStruct((2 * SUB, LANE), jnp.float32),
            jax.ShapeDtypeStruct(concentration.shape, jnp.float32),
            jax.ShapeDtypeStruct(cells, jnp.int32),
        ],
        in_specs=[hbm] * 7,
        scratch_shapes=[
            pltpu.VMEM((1, strata), jnp.float32),
            pltpu.VMEM((2, strata), jnp.float32),
            pltpu.VMEM((1, strata), jnp.float32),
            pltpu.VMEM((1, strata), jnp.float32),
            pltpu.VMEM((1, strata), jnp.float32),
            pltpu.VMEM((SUB, LANE), jnp.float32),
            pltpu.SemaphoreType.DMA((8,)),
        ],
        compiler_params=pltpu.CompilerParams(vmem_limit_bytes=VMEM_LIMIT),
    )(
        *[
            pltpu.with_memory_space_constraint(value, pltpu.HBM)
            for value in (
                concentration,
                stratum,
                porosity[None],
                dispersion_table.T,
                transverse_table[None],
                exchange_table[None],
                decay_table[None],
            )
        ]
    )
    groups = lax.axis_size("trans")
    def swap(value, start):
        low = range(start, groups - 1, 2)
        pairs = [(i, i + 1) for i in low] + [(i + 1, i) for i in low]
        if start:
            pairs += [(0, groups - 1), (groups - 1, 0)]
        return lax.ppermute(value, "trans", pairs)

    beyond_late = swap(late, 1)
    beyond_early = swap(early, 0)

    def exchange(value, stride):
        return lax.ppermute(value, "flow", [(i, i ^ stride) for i in range(peers)])

    half_cells = (n, half, planes_z)
    block_shape = (QUANTITIES, half, planes_z)

    def local(kept):
        pay, edge, *rest = call(
            functools.partial(local_kernel, kept),
            [
                (PIECES,) + block_shape,
                (6, n, planes_z),
                *[half_cells] * 4,
                (2, PIECES, half, planes_z),
                *[half_cells] * 2,
            ],
            [half_cells] * 9,
        )(table, stratum, concentration)
        pay, parts, flow = call(
            functools.partial(border_kernel, kept),
            [block_shape, (PIECES - 1, KEPT, half, planes_z), (2, n, planes_z)],
        )(table, early, late, beyond_late, beyond_early, edge, pay)
        return pay, (*rest, parts, flow)

    send, sent_rest = local(False)
    block, kept_rest = local(True)
    kept = []
    for stride in strides[:-1]:
        other = exchange(send, stride)
        last = stride == strides[-2]
        block, keep, *face = call(
            functools.partial(merge_kernel, stride, last),
            [block_shape, (KEPT, half, planes_z)] + [(5, half, planes_z)] * last,
        )(block, other)
        kept.append(keep)
        send = face[0] if last else block
    ends_shape = (CURRENTS, half, planes_z)
    mine, send = call(functools.partial(close_kernel, strides), [ends_shape, ends_shape])(
        block, exchange(send, strides[-1]), *kept
    )
    currents = exchange(send, 1)
    def final(kept, rest, currents, *before):
        whole = jax.ShapeDtypeStruct((4,) + cells, jnp.float32)
        vmem = pl.BlockSpec(memory_space=pltpu.VMEM)
        return pl.pallas_call(
            functools.partial(final_kernel, kept),
            out_shape=whole,
            in_specs=[vmem] * 13 + [hbm] * len(before),
            out_specs=hbm,
            scratch_shapes=[
                pltpu.VMEM(half_cells, jnp.float32),
                pltpu.VMEM(half_cells, jnp.float32),
                pltpu.VMEM((4,) + half_cells, jnp.float32),
                pltpu.SemaphoreType.DMA((n,)),
            ],
            input_output_aliases={13: 0} if before else {},
            compiler_params=pltpu.CompilerParams(vmem_limit_bytes=VMEM_LIMIT),
        )(table, stratum, concentration, *rest, currents, *before)

    out = final(True, kept_rest, mine)
    return final(False, sent_rest, currents, out)


def solution(mesh):
    in_specs = (P(None, "flow", "trans", None), P("flow", "trans", None), P(), P(), P(), P(), P())
    out_specs = P(None, "flow", "trans", None)
    return jax.shard_map(
        per_device, mesh=mesh, in_specs=in_specs, out_specs=out_specs, check_vma=False
    )
```

```python
import functools

import jax
import jax.numpy as jnp
from jax import lax
from jax.experimental import pallas as pl
from jax.experimental.pallas import tpu as pltpu
from jax.sharding import PartitionSpec as P

SUB, LANE = 8, 128
ZA_LL, ZA_LR, ZA_RR, ZB_LL, ZB_LR, ZB_RR, C_LL, C_LR, C_RL, C_RR, FA_L, FA_R, FB_L, FB_R = range(14)
QUANTITIES = 14
CURRENTS = 4
KEPT = 8
CLOSING = 10
PIECES = 4
VMEM_LIMIT = 40 * 1024 * 1024


def recip(x):
    return 1.0 / x


def lookup(row, index):
    tiles = []
    for y in range(0, index.shape[0], SUB):
        across = [
            jnp.take_along_axis(
                row, index[y : y + SUB, z : z + LANE], axis=1, mode="promise_in_bounds"
            )
            for z in range(0, index.shape[1], LANE)
        ]
        tiles.append(jnp.concatenate(across, axis=1))
    return jnp.concatenate(tiles, axis=0)


NUMBERS = (
    "por",
    "shunt_a",
    "shunt_b",
    "half_a",
    "half_b",
    "half_t",
    "beta",
    "gamma",
    "alpha_a",
    "alpha_b",
    "kappa",
    "delta",
    "free_b",
    "share_b",
    "decay_b",
)


def derive(por, disp_a, disp_b, trans, exch, decay):
    immobile = 1.0 - por
    over_a = 1.0 / (immobile + exch + decay)
    over_b = 1.0 / (immobile + exch)
    beta = immobile * over_a
    gamma = exch * over_a
    share_b = exch * over_b
    return dict(
        por=por,
        shunt_a=por + decay + exch * (immobile + decay) * over_a,
        shunt_b=por + exch * immobile * over_b,
        half_a=0.5 / disp_a,
        half_b=0.5 / disp_b,
        half_t=0.5 / trans,
        beta=beta,
        gamma=gamma,
        alpha_a=exch * beta,
        alpha_b=share_b * immobile,
        kappa=decay + share_b * decay * gamma,
        delta=share_b * decay * beta,
        free_b=immobile * over_b,
        share_b=share_b,
        decay_b=decay * over_b,
    )


class Numbers:
    def __init__(self, tab_ref):
        self.tab_ref = tab_ref

    def __call__(self, name, index):
        k = NUMBERS.index(name)
        row = jnp.broadcast_to(self.tab_ref[k : k + 1, :], (SUB, LANE))
        return lookup(row, index)


def shifted_difference(value, axis):
    return pltpu.roll(value, value.shape[axis] - 1, axis) - value


def side_of(axis, stride):
    return (lax.axis_index(axis) // stride) % 2 == 1


def pack_kernel(
    conc_hbm,
    stratum_hbm,
    por_hbm,
    disp_hbm,
    trans_hbm,
    exch_hbm,
    decay_hbm,
    early_ref,
    late_ref,
    tab_ref,
    conc_ref,
    stratum_ref,
    por_ref,
    disp_ref,
    trans_ref,
    exch_ref,
    decay_ref,
    raw,
    sems,
):
    moves = [
        (stratum_hbm, stratum_ref),
        (conc_hbm.at[0:2], conc_ref.at[0:2]),
        (por_hbm, por_ref),
        (disp_hbm, disp_ref),
        (trans_hbm, trans_ref),
        (exch_hbm, exch_ref),
        (decay_hbm, decay_ref),
        (conc_hbm.at[2:4], conc_ref.at[2:4]),
    ]
    copies = [pltpu.make_async_copy(src, dst, sems.at[k]) for k, (src, dst) in enumerate(moves)]
    for copy in copies:
        copy.start()
    raw[...] = jnp.full(raw.shape, 0.5, jnp.float32)
    for copy in copies[2:7]:
        copy.wait()
    strata = por_ref.shape[1]
    raw[0:1, 0:strata] = por_ref[...]
    raw[1:3, 0:strata] = disp_ref[...]
    raw[3:4, 0:strata] = trans_ref[...]
    raw[4:5, 0:strata] = exch_ref[...]
    raw[5:6, 0:strata] = decay_ref[...]
    made = derive(*[raw[k : k + 1, :] for k in range(6)])
    for k, name in enumerate(NUMBERS):
        tab_ref[k : k + 1, :] = made[name]
    tab_ref[len(NUMBERS) : 2 * SUB, :] = raw[0 : 2 * SUB - len(NUMBERS), :]
    odd = side_of("trans", 1)
    last = stratum_ref.shape[1] - 1

    def put(k, low, high):
        early_ref[k] = jnp.where(odd, low, high)
        late_ref[k] = jnp.where(odd, high, low)

    copies[0].wait()
    numbered = [(stratum_ref[:, y, :] + 1).astype(jnp.float32) for y in (0, last)]
    put(2, *numbered)
    copies[1].wait()
    for k in (0, 1):
        put(k, conc_ref[k, :, 0, :], conc_ref[k, :, last, :])
    copies[7].wait()


def half_of(kept):
    second = lax.axis_index("flow") % 2
    return second if kept else 1 - second


def local_kernel(
    kept,
    tab_ref,
    stratum_ref,
    conc_ref,
    pay_ref,
    edge_ref,
    pass_a_ref,
    drop_a_ref,
    pass_b_ref,
    drop_b_ref,
    over_ref,
    source_a_ref,
    source_b_ref,
    head_a,
    head_b,
    kappa_ref,
    left_a,
    right_a,
    left_b,
    right_b,
    adj_l,
    adj_r,
):
    n, planes_y, planes_z = stratum_ref.shape
    half = planes_y // 2
    which = half_of(kept)
    rows = pl.ds(pl.multiple_of(which * half, half), half)
    other_rows = pl.ds(pl.multiple_of((1 - which) * half, half), half)
    number = Numbers(tab_ref)

    pieces = range(PIECES)
    m = n // PIECES
    shape = (half, planes_z)
    zero, one = jnp.zeros(shape, jnp.float32), jnp.ones(shape, jnp.float32)

    def from_left(j, carry):
        after = []
        for s, (cond_a, cond_b, half_a, half_b, through_a, through_b) in zip(pieces, carry):
            i = s * m + j
            index = stratum_ref[i, rows, :]
            new_a, new_b = number("half_a", index), number("half_b", index)
            face_a, face_b = half_a + new_a, half_b + new_b
            pass_a, pass_b = recip(1.0 + face_a * cond_a), recip(1.0 + face_b * cond_b)
            cond_a = number("shunt_a", index) + cond_a * pass_a
            cond_b = number("shunt_b", index) + cond_b * pass_b
            through_a, through_b = through_a * pass_a, through_b * pass_b
            kappa_ref[i] = number("kappa", index)
            pass_a_ref[i], pass_b_ref[i] = pass_a, pass_b
            drop_a_ref[i], drop_b_ref[i] = face_a * pass_a, face_b * pass_b
            head_a[i], head_b[i] = through_a, through_b
            after.append((cond_a, cond_b, new_a, new_b, through_a, through_b))
        return after

    ahead = lax.fori_loop(0, m, from_left, [(zero, zero, zero, zero, one, one)] * PIECES)
    over_a, over_b = [recip(c[0]) for c in ahead], [recip(c[1]) for c in ahead]
    for s in pieces:
        over_ref[0, s], over_ref[1, s] = over_a[s], over_b[s]

    def from_right(back, carry):
        after = []
        for s, (next_pass, next_drop, next_pass_b, next_drop_b, l_a, r_a, l_b, r_b, *couple) in zip(
            pieces, carry
        ):
            i = s * m + (m - 1 - back)
            l_a = next_pass * l_a + next_drop * head_a[i]
            l_b = next_pass_b * l_b + next_drop_b * head_b[i]
            r_a, r_b = next_pass * r_a, next_pass_b * r_b
            left_a[i], right_a[i], left_b[i], right_b[i] = l_a, r_a, l_b, r_b
            kappa = kappa_ref[i]
            k_l, k_r = kappa * l_a, kappa * r_a
            terms = [l_b * k_l, l_b * k_r, r_b * k_l, r_b * k_r]
            couple = [c + t for c, t in zip(couple, terms)]
            passes = (pass_a_ref[i], drop_a_ref[i], pass_b_ref[i], drop_b_ref[i])
            after.append((*passes, l_a, r_a, l_b, r_b, *couple))
        return after

    responses = lax.fori_loop(
        0,
        m,
        from_right,
        [(one, a, one, b, zero, a, zero, b, zero, zero, zero, zero) for a, b in zip(over_a, over_b)],
    )

    def share(j, carry):
        after = []
        for s, (g_l, g_r) in zip(pieces, carry):
            i = s * m + j
            kappa, pass_a = kappa_ref[i], pass_a_ref[i]
            g_l = kappa * left_b[i] + pass_a * g_l
            g_r = kappa * right_b[i] + pass_a * g_r
            adj_l[i], adj_r[i] = g_l, g_r
            after.append((g_l, g_r))
        return after

    lax.fori_loop(0, m, share, [(zero, zero)] * PIECES)

    lane = lax.broadcasted_iota(jnp.int32, shape, 1)
    line = lax.broadcasted_iota(jnp.int32, shape, 0)
    inside = (line < half - 1, lane < planes_z - 1)
    meets = line == (half - 1) * (1 - which)
    shift = jnp.where(which == 0, half - 1, 1)

    def sources(back, carry):
        after = []
        for s, (next_pass, next_drop, w_l, w_r, *free) in zip(pieces, carry):
            i = s * m + (m - 1 - back)
            w_l = next_pass * w_l + next_drop * adj_l[i]
            w_r = next_pass * w_r + next_drop * adj_r[i]
            adj_l[i], adj_r[i] = w_l, w_r
            index = stratum_ref[i, rows, :]
            half_t = number("half_t", index)
            por = number("por", index)
            c0, c1, c2, c3 = [conc_ref[k, i, rows, :] for k in range(4)]
            source_a = por * c0 + number("alpha_a", index) * c2
            source_b = por * c1 + number("alpha_b", index) * c3 + number("delta", index) * c2
            for axis in (0, 1):
                last = half_t.shape[axis] - 1
                face = jnp.where(
                    inside[axis], recip(half_t + pltpu.roll(half_t, last, axis)), 0.0
                )
                flow_a = face * shifted_difference(c0, axis)
                flow_b = face * shifted_difference(c1, axis)
                source_a = source_a + (flow_a - pltpu.roll(flow_a, 1, axis))
                source_b = source_b + (flow_b - pltpu.roll(flow_b, 1, axis))
            beyond_t = pltpu.roll(number("half_t", stratum_ref[i, other_rows, :]), shift, 0)
            face = jnp.where(meets, recip(half_t + beyond_t), 0.0)
            beyond_a = pltpu.roll(conc_ref[0, i, other_rows, :], shift, 0)
            beyond_b = pltpu.roll(conc_ref[1, i, other_rows, :], shift, 0)
            source_a = source_a + face * (beyond_a - c0)
            source_b = source_b + face * (beyond_b - c1)
            source_a_ref[i], source_b_ref[i] = source_a, source_b
            terms = [
                left_a[i] * source_a,
                right_a[i] * source_a,
                left_b[i] * source_b + w_l * source_a,
                right_b[i] * source_b + w_r * source_a,
            ]
            free = [f + t for f, t in zip(free, terms)]
            after.append((pass_a_ref[i], drop_a_ref[i], w_l, w_r, *free))
        return after

    totals = lax.fori_loop(0, m, sources, [(one, a) + (zero,) * 6 for a in over_a])
    for s in pieces:
        l_a, r_a, l_b, r_b, *couple = responses[s][4:]
        first = stratum_ref[s * m, rows, :]
        quantities = [
            l_a + number("half_a", first),
            r_a,
            over_a[s] + ahead[s][2],
            l_b + number("half_b", first),
            r_b,
            over_b[s] + ahead[s][3],
            *couple,
            *totals[s][4:],
        ]
        for q, value in enumerate(quantities):
            pay_ref[s, q] = value
    for k, ref in enumerate((left_a, right_a, left_b, right_b, adj_l, adj_r)):
        edge_ref[k] = jnp.where(which == 0, ref[:, 0, :], ref[:, half - 1, :])


def border_kernel(
    kept,
    tab_ref,
    early_ref,
    late_ref,
    beyond_late_ref,
    beyond_early_ref,
    edge_ref,
    pay_ref,
    out_ref,
    kept_ref,
    flow_ref,
):
    number = Numbers(tab_ref)
    n, planes_z = edge_ref.shape[1:]
    m = n // PIECES
    half = pay_ref.shape[2]
    low = half_of(kept) == 0
    early = side_of("trans", 1) == low
    own = jnp.where(early, early_ref[...], late_ref[...])
    beyond = jnp.where(early, beyond_early_ref[...], beyond_late_ref[...])
    own_id = own[2].astype(jnp.int32) - 1
    next_id = beyond[2].astype(jnp.int32) - 1
    resist = number("half_t", own_id) + number("half_t", next_id)
    end = jnp.where(low, 0, lax.axis_size("trans") - 1)
    face = jnp.where(lax.axis_index("trans") != end, recip(resist), 0.0)
    flow_a = face * (beyond[0] - own[0])
    flow_b = face * (beyond[1] - own[1])
    flow_ref[0], flow_ref[1] = flow_a, flow_b
    l_a, r_a, l_b, r_b, w_l, w_r = [edge_ref[k] for k in range(6)]
    changes = {
        FA_L: l_a * flow_a,
        FA_R: r_a * flow_a,
        FB_L: l_b * flow_b + w_l * flow_a,
        FB_R: r_b * flow_b + w_r * flow_a,
    }
    line = lax.broadcasted_iota(jnp.int32, (half, planes_z), 0)
    outer = line == jnp.where(low, 0, half - 1)
    blocks = []
    for s in range(PIECES):
        values = {q: pay_ref[s, q] for q in range(QUANTITIES)}
        for q, change in changes.items():
            total = jnp.sum(change[s * m : (s + 1) * m], axis=0, keepdims=True)
            values[q] = values[q] + jnp.where(outer, total, 0.0)
        blocks.append(values)
    slot = 0
    while len(blocks) > 1:
        joined = []
        for one, two in zip(blocks[::2], blocks[1::2]):
            merged, parts = merge(one, two)
            for k, value in enumerate(parts):
                kept_ref[slot, k] = value
            slot += 1
            joined.append(merged)
        blocks = joined
    for q in range(QUANTITIES):
        out_ref[q] = blocks[0][q]


FACE_L = (ZA_LL, ZB_LL, C_LL, FA_L, FB_L)
FACE_R = (ZA_RR, ZB_RR, C_RR, FA_R, FB_R)


def merge(one, two):
    over_a = recip(one[ZA_RR] + two[ZA_LL])
    over_b = recip(one[ZB_RR] + two[ZB_LL])
    across = one[C_RR] + two[C_LL]
    free_a = over_a * (one[FA_R] - two[FA_L])
    from_l, from_r = over_a * one[ZA_LR], over_a * two[ZA_LR]
    free_b = over_b * (one[FB_R] - two[FB_L] - across * free_a)
    from_l_b, from_r_b = over_b * one[ZB_LR], over_b * two[ZB_LR]
    cross_l = over_b * (one[C_RL] - across * from_l)
    cross_r = over_b * (two[C_LR] - across * from_r)
    merged = {
        ZA_LL: one[ZA_LL] - one[ZA_LR] * from_l,
        ZA_LR: one[ZA_LR] * from_r,
        ZA_RR: two[ZA_RR] - two[ZA_LR] * from_r,
        ZB_LL: one[ZB_LL] - one[ZB_LR] * from_l_b,
        ZB_LR: one[ZB_LR] * from_r_b,
        ZB_RR: two[ZB_RR] - two[ZB_LR] * from_r_b,
        C_LL: one[C_LL] - one[ZB_LR] * cross_l - one[C_LR] * from_l,
        C_LR: one[ZB_LR] * cross_r + one[C_LR] * from_r,
        C_RL: two[ZB_LR] * cross_l + two[C_RL] * from_l,
        C_RR: two[C_RR] - two[ZB_LR] * cross_r - two[C_RL] * from_r,
        FA_L: one[FA_L] - one[ZA_LR] * free_a,
        FA_R: two[FA_R] + two[ZA_LR] * free_a,
        FB_L: one[FB_L] - one[ZB_LR] * free_b - one[C_LR] * free_a,
        FB_R: two[FB_R] + two[ZB_LR] * free_b + two[C_RL] * free_a,
    }
    return merged, (free_a, from_l, from_r, free_b, from_l_b, from_r_b, cross_l, cross_r)


def between(kept, ends):
    free_a, from_l, from_r, free_b, from_l_b, from_r_b, cross_l, cross_r = kept
    l_a, r_a, l_b, r_b = ends
    middle_a = free_a + from_l * l_a - from_r * r_a
    middle_b = free_b + from_l_b * l_b - from_r_b * r_b + cross_l * l_a - cross_r * r_a
    return middle_a, middle_b


def merge_kernel(stride, last, own_ref, other_ref, *refs):
    second = side_of("flow", stride)
    own = [own_ref[q] for q in range(QUANTITIES)]
    other = [other_ref[q] for q in range(QUANTITIES)]
    one = [jnp.where(second, b, a) for a, b in zip(own, other)]
    two = [jnp.where(second, a, b) for a, b in zip(own, other)]
    merged, kept = merge(one, two)
    if not last:
        out_ref, kept_ref = refs
        for q, value in merged.items():
            out_ref[q] = value
        for k, value in enumerate(kept):
            kept_ref[k] = value
        return
    kept_refs, face_ref, closing_ref = refs[:-2], refs[-2], refs[-1]
    free_a, from_l, from_r, free_b, from_l_b, from_r_b, cross_l, cross_r = kept
    after = side_of("flow", 2 * stride)
    for k, (l, r) in enumerate(zip(FACE_L, FACE_R)):
        face_ref[k] = closing_ref[k] = jnp.where(after, merged[l], merged[r])
    closing_ref[5] = free_a
    closing_ref[6] = jnp.where(after, from_l, from_r)
    closing_ref[7] = free_b
    closing_ref[8] = jnp.where(after, from_l_b, from_r_b)
    closing_ref[9] = jnp.where(after, cross_l, cross_r)
    for k, kept_ref in enumerate(kept_refs):
        closing_ref[CLOSING + k * KEPT : CLOSING + (k + 1) * KEPT] = kept_ref[...]


def close_kernel(strides, other_ref, closing_ref, out_ref):
    second = side_of("flow", strides[-1])
    own = [closing_ref[k] for k in range(CLOSING)]
    z_a, z_b, couple = [own[k] + other_ref[k] for k in range(3)]
    f_a, f_b = [
        jnp.where(second, other_ref[k] - own[k], own[k] - other_ref[k]) for k in (3, 4)
    ]
    current_a = recip(z_a) * f_a
    current_b = recip(z_b) * (f_b - couple * current_a)
    nothing = jnp.zeros_like(current_a)

    def side_ends(stride, middle_a, middle_b, ends):
        after = side_of("flow", stride)
        l_a, r_a, l_b, r_b = ends
        return (
            jnp.where(after, middle_a, l_a),
            jnp.where(after, r_a, -middle_a),
            jnp.where(after, middle_b, l_b),
            jnp.where(after, r_b, -middle_b),
        )

    ends = side_ends(strides[-1], current_a, current_b, (nothing,) * 4)
    middle_a = own[5] + own[6] * current_a
    middle_b = own[7] + own[8] * current_b + own[9] * current_a
    ends = side_ends(strides[-2], middle_a, middle_b, ends)
    for level in reversed(range(len(strides) - 2)):
        stride, base = strides[level], CLOSING + level * KEPT
        middle_a, middle_b = between([closing_ref[base + k] for k in range(KEPT)], ends)
        ends = side_ends(stride, middle_a, middle_b, ends)
    for q, value in enumerate(ends):
        out_ref[q] = value


def final_kernel(
    kept,
    tab_ref,
    stratum_ref,
    conc_ref,
    pass_a_ref,
    drop_a_ref,
    pass_b_ref,
    drop_b_ref,
    over_ref,
    source_a_ref,
    source_b_ref,
    kept_ref,
    flow_ref,
    current_ref,
    *refs,
):
    out_hbm, gather_a, gather_b, made, sems = refs[-5:]
    n, planes_y, planes_z = stratum_ref.shape
    half = planes_y // 2
    which = half_of(kept)
    rows = pl.ds(pl.multiple_of(which * half, half), half)
    number = Numbers(tab_ref)
    line = lax.broadcasted_iota(jnp.int32, (half, planes_z), 0)
    outer = line == (half - 1) * which

    def with_border(source, component, i):
        flow = jnp.broadcast_to(flow_ref[component, pl.ds(i, 1), :], source.shape)
        return source + jnp.where(outer, flow, 0.0)

    ends = [tuple(current_ref[q] for q in range(CURRENTS))]
    slot = PIECES - 1
    while len(ends) < PIECES:
        slot -= len(ends)
        parts = []
        for k, (l_a, r_a, l_b, r_b) in enumerate(ends):
            values = [kept_ref[slot + k, v] for v in range(KEPT)]
            middle_a, middle_b = between(values, (l_a, r_a, l_b, r_b))
            parts += [(l_a, -middle_a, l_b, -middle_b), (middle_a, r_a, middle_b, r_b)]
        ends = parts

    pieces = range(PIECES)
    m = n // PIECES
    values = [ends[s][0] for s in pieces]
    for j in range(m):
        for s in pieces:
            i = s * m + j
            values[s] = with_border(source_a_ref[i], 0, i) + values[s]
            if j < m - 1:
                gather_a[i] = values[s]
                values[s] = pass_a_ref[i + 1] * values[s]
    x = [(values[s] + ends[s][1]) * over_ref[0, s] for s in pieces]
    for j in reversed(range(m)):
        for s in pieces:
            i = s * m + j
            if j < m - 1:
                x[s] = pass_a_ref[i + 1] * x[s] + drop_a_ref[i + 1] * gather_a[i]
            made[0, i] = x[s]
    values = [ends[s][2] for s in pieces]
    for j in range(m):
        for s in pieces:
            i = s * m + j
            kappa = number("kappa", stratum_ref[i, rows, :])
            values[s] = with_border(source_b_ref[i], 1, i) + kappa * made[0, i] + values[s]
            if j < m - 1:
                gather_b[i] = values[s]
                values[s] = pass_b_ref[i + 1] * values[s]
    x = [(values[s] + ends[s][3]) * over_ref[1, s] for s in pieces]
    copies = []
    for j in reversed(range(m)):
        for s in pieces:
            i = s * m + j
            if j < m - 1:
                x[s] = pass_b_ref[i + 1] * x[s] + drop_b_ref[i + 1] * gather_b[i]
            made[1, i] = x[s]
            index = stratum_ref[i, rows, :]
            x2 = (
                number("beta", index) * conc_ref[2, i, rows, :]
                + number("gamma", index) * made[0, i]
            )
            made[2, i] = x2
            made[3, i] = (
                number("free_b", index) * conc_ref[3, i, rows, :]
                + number("share_b", index) * x[s]
                + number("decay_b", index) * x2
            )
            copies.append(
                pltpu.make_async_copy(made.at[:, i], out_hbm.at[:, i, rows, :], sems.at[i])
            )
            copies[-1].start()
    for copy in copies:
        copy.wait()


def call(kernel, outs, scratch=()):
    return pl.pallas_call(
        kernel,
        out_shape=[jax.ShapeDtypeStruct(shape, jnp.float32) for shape in outs],
        scratch_shapes=[pltpu.VMEM(shape, jnp.float32) for shape in scratch],
        compiler_params=pltpu.CompilerParams(vmem_limit_bytes=VMEM_LIMIT),
    )


def per_device(
    concentration,
    stratum,
    porosity,
    dispersion_table,
    transverse_table,
    exchange_table,
    decay_table,
):
    n, planes_y, planes_z = stratum.shape
    peers = lax.axis_size("flow")
    half = planes_y // 2
    strides = [1 << k for k in range(peers.bit_length() - 1)]
    cells = (n, planes_y, planes_z)

    halo = (3, n, planes_z)
    strata = porosity.shape[0]
    hbm = pl.BlockSpec(memory_space=pltpu.HBM)
    early, late, table, concentration, stratum = pl.pallas_call(
        pack_kernel,
        out_shape=[
            jax.ShapeDtypeStruct(halo, jnp.float32),
            jax.ShapeDtypeStruct(halo, jnp.float32),
            jax.ShapeDtypeStruct((2 * SUB, LANE), jnp.float32),
            jax.ShapeDtypeStruct(concentration.shape, jnp.float32),
            jax.ShapeDtypeStruct(cells, jnp.int32),
        ],
        in_specs=[hbm] * 7,
        scratch_shapes=[
            pltpu.VMEM((1, strata), jnp.float32),
            pltpu.VMEM((2, strata), jnp.float32),
            pltpu.VMEM((1, strata), jnp.float32),
            pltpu.VMEM((1, strata), jnp.float32),
            pltpu.VMEM((1, strata), jnp.float32),
            pltpu.VMEM((SUB, LANE), jnp.float32),
            pltpu.SemaphoreType.DMA((8,)),
        ],
        compiler_params=pltpu.CompilerParams(vmem_limit_bytes=VMEM_LIMIT),
    )(
        *[
            pltpu.with_memory_space_constraint(value, pltpu.HBM)
            for value in (
                concentration,
                stratum,
                porosity[None],
                dispersion_table.T,
                transverse_table[None],
                exchange_table[None],
                decay_table[None],
            )
        ]
    )
    groups = lax.axis_size("trans")
    def swap(value, start):
        low = range(start, groups - 1, 2)
        pairs = [(i, i + 1) for i in low] + [(i + 1, i) for i in low]
        if start:
            pairs += [(0, groups - 1), (groups - 1, 0)]
        return lax.ppermute(value, "trans", pairs)

    beyond_late = swap(late, 1)
    beyond_early = swap(early, 0)

    def exchange(value, stride):
        return lax.ppermute(value, "flow", [(i, i ^ stride) for i in range(peers)])

    half_cells = (n, half, planes_z)
    block_shape = (QUANTITIES, half, planes_z)

    def local(kept):
        pay, edge, *rest = call(
            functools.partial(local_kernel, kept),
            [
                (PIECES,) + block_shape,
                (6, n, planes_z),
                *[half_cells] * 4,
                (2, PIECES, half, planes_z),
                *[half_cells] * 2,
            ],
            [half_cells] * 9,
        )(table, stratum, concentration)
        pay, parts, flow = call(
            functools.partial(border_kernel, kept),
            [block_shape, (PIECES - 1, KEPT, half, planes_z), (2, n, planes_z)],
        )(table, early, late, beyond_late, beyond_early, edge, pay)
        return pay, (*rest, parts, flow)

    send, sent_rest = local(False)
    block, kept_rest = local(True)
    own_kept = []
    for stride in strides[:-2]:
        send, keep = call(
            functools.partial(merge_kernel, stride, False), [block_shape, (KEPT, half, planes_z)]
        )(block, exchange(send, stride))
        block = send
        own_kept.append(keep)
    face, closing = call(
        functools.partial(merge_kernel, strides[-2], True),
        [(5, half, planes_z), (CLOSING + KEPT * len(own_kept), half, planes_z)],
    )(block, exchange(send, strides[-2]), *own_kept)
    close = call(functools.partial(close_kernel, strides), [(CURRENTS, half, planes_z)])
    (mine,) = close(exchange(face, strides[-1]), closing)
    (currents,) = close(exchange(face, strides[-1] ^ 1), exchange(closing, 1))

    def final(kept, rest, currents, *before):
        whole = jax.ShapeDtypeStruct((4,) + cells, jnp.float32)
        vmem = pl.BlockSpec(memory_space=pltpu.VMEM)
        return pl.pallas_call(
            functools.partial(final_kernel, kept),
            out_shape=whole,
            in_specs=[vmem] * 13 + [hbm] * len(before),
            out_specs=hbm,
            scratch_shapes=[
                pltpu.VMEM(half_cells, jnp.float32),
                pltpu.VMEM(half_cells, jnp.float32),
                pltpu.VMEM((4,) + half_cells, jnp.float32),
                pltpu.SemaphoreType.DMA((n,)),
            ],
            input_output_aliases={13: 0} if before else {},
            compiler_params=pltpu.CompilerParams(vmem_limit_bytes=VMEM_LIMIT),
        )(table, stratum, concentration, *rest, currents, *before)

    out = final(True, kept_rest, mine)
    return final(False, sent_rest, currents, out)


def solution(mesh):
    in_specs = (P(None, "flow", "trans", None), P("flow", "trans", None), P(), P(), P(), P(), P())
    out_specs = P(None, "flow", "trans", None)
    return jax.shard_map(
        per_device, mesh=mesh, in_specs=in_specs, out_specs=out_specs, check_vma=False
    )
```

```python
import functools

import jax
import jax.numpy as jnp
from jax import lax
from jax.experimental import pallas as pl
from jax.experimental.pallas import tpu as pltpu
from jax.sharding import PartitionSpec as P

SUB, LANE = 8, 128
ZA_LL, ZA_LR, ZA_RR, ZB_LL, ZB_LR, ZB_RR, C_LL, C_LR, C_RL, C_RR, FA_L, FA_R, FB_L, FB_R = range(14)
QUANTITIES = 14
CURRENTS = 4
KEPT = 8
PIECES = 4
VMEM_LIMIT = 40 * 1024 * 1024


def recip(x):
    return 1.0 / x


def lookup(row, index):
    tiles = []
    for y in range(0, index.shape[0], SUB):
        across = [
            jnp.take_along_axis(
                row, index[y : y + SUB, z : z + LANE], axis=1, mode="promise_in_bounds"
            )
            for z in range(0, index.shape[1], LANE)
        ]
        tiles.append(jnp.concatenate(across, axis=1))
    return jnp.concatenate(tiles, axis=0)


NUMBERS = (
    "por",
    "shunt_a",
    "shunt_b",
    "half_a",
    "half_b",
    "half_t",
    "beta",
    "gamma",
    "alpha_a",
    "alpha_b",
    "kappa",
    "delta",
    "free_b",
    "share_b",
    "decay_b",
)


def derive(por, disp_a, disp_b, trans, exch, decay):
    immobile = 1.0 - por
    over_a = 1.0 / (immobile + exch + decay)
    over_b = 1.0 / (immobile + exch)
    beta = immobile * over_a
    gamma = exch * over_a
    share_b = exch * over_b
    return dict(
        por=por,
        shunt_a=por + decay + exch * (immobile + decay) * over_a,
        shunt_b=por + exch * immobile * over_b,
        half_a=0.5 / disp_a,
        half_b=0.5 / disp_b,
        half_t=0.5 / trans,
        beta=beta,
        gamma=gamma,
        alpha_a=exch * beta,
        alpha_b=share_b * immobile,
        kappa=decay + share_b * decay * gamma,
        delta=share_b * decay * beta,
        free_b=immobile * over_b,
        share_b=share_b,
        decay_b=decay * over_b,
    )


class Numbers:
    def __init__(self, tab_ref):
        self.tab_ref = tab_ref

    def __call__(self, name, index):
        k = NUMBERS.index(name)
        row = jnp.broadcast_to(self.tab_ref[k : k + 1, :], (SUB, LANE))
        return lookup(row, index)


def shifted_difference(value, axis):
    return pltpu.roll(value, value.shape[axis] - 1, axis) - value


def side_of(axis, stride):
    return (lax.axis_index(axis) // stride) % 2 == 1


def pack_kernel(
    conc_hbm,
    stratum_hbm,
    por_hbm,
    disp_hbm,
    trans_hbm,
    exch_hbm,
    decay_hbm,
    early_ref,
    late_ref,
    tab_ref,
    conc_ref,
    stratum_ref,
    por_ref,
    disp_ref,
    trans_ref,
    exch_ref,
    decay_ref,
    raw,
    sems,
):
    moves = [
        (stratum_hbm, stratum_ref),
        (conc_hbm.at[0:2], conc_ref.at[0:2]),
        (por_hbm, por_ref),
        (disp_hbm, disp_ref),
        (trans_hbm, trans_ref),
        (exch_hbm, exch_ref),
        (decay_hbm, decay_ref),
        (conc_hbm.at[2:4], conc_ref.at[2:4]),
    ]
    copies = [pltpu.make_async_copy(src, dst, sems.at[k]) for k, (src, dst) in enumerate(moves)]
    for copy in copies:
        copy.start()
    raw[...] = jnp.full(raw.shape, 0.5, jnp.float32)
    for copy in copies[2:7]:
        copy.wait()
    strata = por_ref.shape[1]
    raw[0:1, 0:strata] = por_ref[...]
    raw[1:3, 0:strata] = disp_ref[...]
    raw[3:4, 0:strata] = trans_ref[...]
    raw[4:5, 0:strata] = exch_ref[...]
    raw[5:6, 0:strata] = decay_ref[...]
    made = derive(*[raw[k : k + 1, :] for k in range(6)])
    for k, name in enumerate(NUMBERS):
        tab_ref[k : k + 1, :] = made[name]
    tab_ref[len(NUMBERS) : 2 * SUB, :] = raw[0 : 2 * SUB - len(NUMBERS), :]
    odd = side_of("trans", 1)
    last = stratum_ref.shape[1] - 1

    def put(k, low, high):
        early_ref[k] = jnp.where(odd, low, high)
        late_ref[k] = jnp.where(odd, high, low)

    copies[0].wait()
    numbered = [(stratum_ref[:, y, :] + 1).astype(jnp.float32) for y in (0, last)]
    put(2, *numbered)
    copies[1].wait()
    for k in (0, 1):
        put(k, conc_ref[k, :, 0, :], conc_ref[k, :, last, :])
    copies[7].wait()


def half_of(kept):
    second = lax.axis_index("flow") % 2
    return second if kept else 1 - second


def local_kernel(
    kept,
    tab_ref,
    stratum_ref,
    conc_ref,
    pay_ref,
    edge_ref,
    pass_a_ref,
    drop_a_ref,
    pass_b_ref,
    drop_b_ref,
    over_ref,
    source_a_ref,
    source_b_ref,
    left_a,
    right_a,
    left_b,
    right_b,
    head_a,
    head_b,
    kappa_ref,
    adj_l,
    adj_r,
):
    n, planes_y, planes_z = stratum_ref.shape
    half = planes_y // 2
    which = half_of(kept)
    rows = pl.ds(pl.multiple_of(which * half, half), half)
    other_rows = pl.ds(pl.multiple_of((1 - which) * half, half), half)
    number = Numbers(tab_ref)

    pieces = range(PIECES)
    m = n // PIECES
    shape = (half, planes_z)
    zero, one = jnp.zeros(shape, jnp.float32), jnp.ones(shape, jnp.float32)

    def from_left(j, carry):
        after = []
        for s, (cond_a, cond_b, half_a, half_b, through_a, through_b) in zip(pieces, carry):
            i = s * m + j
            index = stratum_ref[i, rows, :]
            new_a, new_b = number("half_a", index), number("half_b", index)
            face_a, face_b = half_a + new_a, half_b + new_b
            pass_a, pass_b = recip(1.0 + face_a * cond_a), recip(1.0 + face_b * cond_b)
            cond_a = number("shunt_a", index) + cond_a * pass_a
            cond_b = number("shunt_b", index) + cond_b * pass_b
            through_a, through_b = through_a * pass_a, through_b * pass_b
            kappa_ref[i] = number("kappa", index)
            pass_a_ref[i], pass_b_ref[i] = pass_a, pass_b
            drop_a_ref[i], drop_b_ref[i] = face_a * pass_a, face_b * pass_b
            head_a[i], head_b[i] = through_a, through_b
            after.append((cond_a, cond_b, new_a, new_b, through_a, through_b))
        return after

    ahead = lax.fori_loop(0, m, from_left, [(zero, zero, zero, zero, one, one)] * PIECES)
    over_a, over_b = [recip(c[0]) for c in ahead], [recip(c[1]) for c in ahead]
    for s in pieces:
        over_ref[0, s], over_ref[1, s] = over_a[s], over_b[s]

    def from_right(back, carry):
        after = []
        for s, (next_pass, next_drop, next_pass_b, next_drop_b, l_a, r_a, l_b, r_b, *couple) in zip(
            pieces, carry
        ):
            i = s * m + (m - 1 - back)
            l_a = next_pass * l_a + next_drop * head_a[i]
            l_b = next_pass_b * l_b + next_drop_b * head_b[i]
            r_a, r_b = next_pass * r_a, next_pass_b * r_b
            left_a[i], right_a[i], left_b[i], right_b[i] = l_a, r_a, l_b, r_b
            kappa = kappa_ref[i]
            k_l, k_r = kappa * l_a, kappa * r_a
            terms = [l_b * k_l, l_b * k_r, r_b * k_l, r_b * k_r]
            couple = [c + t for c, t in zip(couple, terms)]
            passes = (pass_a_ref[i], drop_a_ref[i], pass_b_ref[i], drop_b_ref[i])
            after.append((*passes, l_a, r_a, l_b, r_b, *couple))
        return after

    responses = lax.fori_loop(
        0,
        m,
        from_right,
        [(one, a, one, b, zero, a, zero, b, zero, zero, zero, zero) for a, b in zip(over_a, over_b)],
    )

    def share(j, carry):
        after = []
        for s, (g_l, g_r) in zip(pieces, carry):
            i = s * m + j
            kappa, pass_a = kappa_ref[i], pass_a_ref[i]
            g_l = kappa * left_b[i] + pass_a * g_l
            g_r = kappa * right_b[i] + pass_a * g_r
            adj_l[i], adj_r[i] = g_l, g_r
            after.append((g_l, g_r))
        return after

    lax.fori_loop(0, m, share, [(zero, zero)] * PIECES)

    lane = lax.broadcasted_iota(jnp.int32, shape, 1)
    line = lax.broadcasted_iota(jnp.int32, shape, 0)
    inside = (line < half - 1, lane < planes_z - 1)
    meets = line == (half - 1) * (1 - which)
    shift = jnp.where(which == 0, half - 1, 1)

    def sources(back, carry):
        after = []
        for s, (next_pass, next_drop, w_l, w_r, *free) in zip(pieces, carry):
            i = s * m + (m - 1 - back)
            w_l = next_pass * w_l + next_drop * adj_l[i]
            w_r = next_pass * w_r + next_drop * adj_r[i]
            adj_l[i], adj_r[i] = w_l, w_r
            index = stratum_ref[i, rows, :]
            half_t = number("half_t", index)
            por = number("por", index)
            c0, c1, c2, c3 = [conc_ref[k, i, rows, :] for k in range(4)]
            source_a = por * c0 + number("alpha_a", index) * c2
            source_b = por * c1 + number("alpha_b", index) * c3 + number("delta", index) * c2
            for axis in (0, 1):
                last = half_t.shape[axis] - 1
                face = jnp.where(
                    inside[axis], recip(half_t + pltpu.roll(half_t, last, axis)), 0.0
                )
                flow_a = face * shifted_difference(c0, axis)
                flow_b = face * shifted_difference(c1, axis)
                source_a = source_a + (flow_a - pltpu.roll(flow_a, 1, axis))
                source_b = source_b + (flow_b - pltpu.roll(flow_b, 1, axis))
            beyond_t = pltpu.roll(number("half_t", stratum_ref[i, other_rows, :]), shift, 0)
            face = jnp.where(meets, recip(half_t + beyond_t), 0.0)
            beyond_a = pltpu.roll(conc_ref[0, i, other_rows, :], shift, 0)
            beyond_b = pltpu.roll(conc_ref[1, i, other_rows, :], shift, 0)
            source_a = source_a + face * (beyond_a - c0)
            source_b = source_b + face * (beyond_b - c1)
            source_a_ref[i], source_b_ref[i] = source_a, source_b
            terms = [
                left_a[i] * source_a,
                right_a[i] * source_a,
                left_b[i] * source_b + w_l * source_a,
                right_b[i] * source_b + w_r * source_a,
            ]
            free = [f + t for f, t in zip(free, terms)]
            after.append((pass_a_ref[i], drop_a_ref[i], w_l, w_r, *free))
        return after

    totals = lax.fori_loop(0, m, sources, [(one, a) + (zero,) * 6 for a in over_a])
    for s in pieces:
        l_a, r_a, l_b, r_b, *couple = responses[s][4:]
        first = stratum_ref[s * m, rows, :]
        quantities = [
            l_a + number("half_a", first),
            r_a,
            over_a[s] + ahead[s][2],
            l_b + number("half_b", first),
            r_b,
            over_b[s] + ahead[s][3],
            *couple,
            *totals[s][4:],
        ]
        for q, value in enumerate(quantities):
            pay_ref[s, q] = value
    for k, ref in enumerate((left_a, right_a, left_b, right_b, adj_l, adj_r)):
        edge_ref[k] = jnp.where(which == 0, ref[:, 0, :], ref[:, half - 1, :])


def border_kernel(
    kept,
    tab_ref,
    early_ref,
    late_ref,
    beyond_late_ref,
    beyond_early_ref,
    edge_ref,
    pay_ref,
    out_ref,
    kept_ref,
    flow_ref,
):
    number = Numbers(tab_ref)
    n, planes_z = edge_ref.shape[1:]
    m = n // PIECES
    half = pay_ref.shape[2]
    low = half_of(kept) == 0
    early = side_of("trans", 1) == low
    own = jnp.where(early, early_ref[...], late_ref[...])
    beyond = jnp.where(early, beyond_early_ref[...], beyond_late_ref[...])
    own_id = own[2].astype(jnp.int32) - 1
    next_id = beyond[2].astype(jnp.int32) - 1
    resist = number("half_t", own_id) + number("half_t", next_id)
    end = jnp.where(low, 0, lax.axis_size("trans") - 1)
    face = jnp.where(lax.axis_index("trans") != end, recip(resist), 0.0)
    flow_a = face * (beyond[0] - own[0])
    flow_b = face * (beyond[1] - own[1])
    flow_ref[0], flow_ref[1] = flow_a, flow_b
    l_a, r_a, l_b, r_b, w_l, w_r = [edge_ref[k] for k in range(6)]
    changes = {
        FA_L: l_a * flow_a,
        FA_R: r_a * flow_a,
        FB_L: l_b * flow_b + w_l * flow_a,
        FB_R: r_b * flow_b + w_r * flow_a,
    }
    line = lax.broadcasted_iota(jnp.int32, (half, planes_z), 0)
    outer = line == jnp.where(low, 0, half - 1)
    blocks = []
    for s in range(PIECES):
        values = {q: pay_ref[s, q] for q in range(QUANTITIES)}
        for q, change in changes.items():
            total = jnp.sum(change[s * m : (s + 1) * m], axis=0, keepdims=True)
            values[q] = values[q] + jnp.where(outer, total, 0.0)
        blocks.append(values)
    slot = 0
    while len(blocks) > 1:
        joined = []
        for one, two in zip(blocks[::2], blocks[1::2]):
            merged, parts = merge(one, two)
            for k, value in enumerate(parts):
                kept_ref[slot, k] = value
            slot += 1
            joined.append(merged)
        blocks = joined
    for q in range(QUANTITIES):
        out_ref[q] = blocks[0][q]


FACE_L = (ZA_LL, ZB_LL, C_LL, FA_L, FB_L)
FACE_R = (ZA_RR, ZB_RR, C_RR, FA_R, FB_R)


def merge(one, two):
    over_a = recip(one[ZA_RR] + two[ZA_LL])
    over_b = recip(one[ZB_RR] + two[ZB_LL])
    across = one[C_RR] + two[C_LL]
    free_a = over_a * (one[FA_R] - two[FA_L])
    from_l, from_r = over_a * one[ZA_LR], over_a * two[ZA_LR]
    free_b = over_b * (one[FB_R] - two[FB_L] - across * free_a)
    from_l_b, from_r_b = over_b * one[ZB_LR], over_b * two[ZB_LR]
    cross_l = over_b * (one[C_RL] - across * from_l)
    cross_r = over_b * (two[C_LR] - across * from_r)
    merged = {
        ZA_LL: one[ZA_LL] - one[ZA_LR] * from_l,
        ZA_LR: one[ZA_LR] * from_r,
        ZA_RR: two[ZA_RR] - two[ZA_LR] * from_r,
        ZB_LL: one[ZB_LL] - one[ZB_LR] * from_l_b,
        ZB_LR: one[ZB_LR] * from_r_b,
        ZB_RR: two[ZB_RR] - two[ZB_LR] * from_r_b,
        C_LL: one[C_LL] - one[ZB_LR] * cross_l - one[C_LR] * from_l,
        C_LR: one[ZB_LR] * cross_r + one[C_LR] * from_r,
        C_RL: two[ZB_LR] * cross_l + two[C_RL] * from_l,
        C_RR: two[C_RR] - two[ZB_LR] * cross_r - two[C_RL] * from_r,
        FA_L: one[FA_L] - one[ZA_LR] * free_a,
        FA_R: two[FA_R] + two[ZA_LR] * free_a,
        FB_L: one[FB_L] - one[ZB_LR] * free_b - one[C_LR] * free_a,
        FB_R: two[FB_R] + two[ZB_LR] * free_b + two[C_RL] * free_a,
    }
    return merged, (free_a, from_l, from_r, free_b, from_l_b, from_r_b, cross_l, cross_r)


def between(kept, ends):
    free_a, from_l, from_r, free_b, from_l_b, from_r_b, cross_l, cross_r = kept
    l_a, r_a, l_b, r_b = ends
    middle_a = free_a + from_l * l_a - from_r * r_a
    middle_b = free_b + from_l_b * l_b - from_r_b * r_b + cross_l * l_a - cross_r * r_a
    return middle_a, middle_b


def merge_kernel(stride, last, own_ref, other_ref, out_ref, kept_ref, *face_ref):
    second = side_of("flow", stride)
    own = [own_ref[q] for q in range(QUANTITIES)]
    other = [other_ref[q] for q in range(QUANTITIES)]
    one = [jnp.where(second, b, a) for a, b in zip(own, other)]
    two = [jnp.where(second, a, b) for a, b in zip(own, other)]
    merged, kept = merge(one, two)
    for q, value in merged.items():
        out_ref[q] = value
    for k, value in enumerate(kept):
        kept_ref[k] = value
    if last:
        after = side_of("flow", 2 * stride)
        for k, (l, r) in enumerate(zip(FACE_L, FACE_R)):
            face_ref[0][k] = jnp.where(after, merged[l], merged[r])


def close_kernel(strides, ready_ref, own_ref, other_ref, *refs):
    kept_refs, mine_ref, send_ref = refs[:-2], refs[-2], refs[-1]
    stride = strides[-1]
    second = side_of("flow", stride)
    own = [jnp.where(second, own_ref[l], own_ref[r]) for l, r in zip(FACE_L, FACE_R)]
    z_a, z_b, couple, f_a, f_b = [own[k] + other_ref[k] for k in range(3)] + [
        jnp.where(second, other_ref[k] - own[k], own[k] - other_ref[k]) for k in (3, 4)
    ]
    current_a = recip(z_a) * f_a
    current_b = recip(z_b) * (f_b - couple * current_a)
    nothing = jnp.zeros_like(current_a)

    def side_ends(after, middle_a, middle_b, ends):
        l_a, r_a, l_b, r_b = ends
        return (
            jnp.where(after, middle_a, l_a),
            jnp.where(after, r_a, -middle_a),
            jnp.where(after, middle_b, l_b),
            jnp.where(after, r_b, -middle_b),
        )

    ends = side_ends(second, current_a, current_b, (nothing,) * 4)
    for stride, kept_ref in reversed(list(zip(strides[:-1], kept_refs))):
        middle_a, middle_b = between([kept_ref[k] for k in range(KEPT)], ends)
        after = side_of("flow", stride)
        if stride == 1:
            other_ends = side_ends(jnp.logical_not(after), middle_a, middle_b, ends)
            for q, value in enumerate(other_ends):
                send_ref[q] = value
        ends = side_ends(after, middle_a, middle_b, ends)
    for q, value in enumerate(ends):
        mine_ref[q] = value


def piece_ends(kept_ref, current_ref):
    ends = [tuple(current_ref[q] for q in range(CURRENTS))]
    slot = PIECES - 1
    while len(ends) < PIECES:
        slot -= len(ends)
        parts = []
        for k, (l_a, r_a, l_b, r_b) in enumerate(ends):
            values = [kept_ref[slot + k, v] for v in range(KEPT)]
            middle_a, middle_b = between(values, (l_a, r_a, l_b, r_b))
            parts += [(l_a, -middle_a, l_b, -middle_b), (middle_a, r_a, middle_b, r_b)]
        ends = parts
    return ends


def prepare_kernel(
    kept,
    tab_ref,
    stratum_ref,
    conc_ref,
    pass_a_ref,
    drop_a_ref,
    pass_b_ref,
    drop_b_ref,
    over_ref,
    source_a_ref,
    source_b_ref,
    flow_ref,
    left_a,
    right_a,
    free_a_ref,
    free_b_ref,
    cross_l_ref,
    cross_r_ref,
    own_2_ref,
    own_3_ref,
    gamma_ref,
    share_ref,
    decay_ref,
):
    n, planes_y, planes_z = stratum_ref.shape
    half = planes_y // 2
    which = half_of(kept)
    rows = pl.ds(pl.multiple_of(which * half, half), half)
    number = Numbers(tab_ref)
    line = lax.broadcasted_iota(jnp.int32, (half, planes_z), 0)
    outer = line == (half - 1) * which
    zero = jnp.zeros((half, planes_z), jnp.float32)
    m = n // PIECES

    def with_border(source, component, i):
        flow = jnp.broadcast_to(flow_ref[component, i : i + 1, :], source.shape)
        return source + jnp.where(outer, flow, 0.0)

    def solve(s, forcing, pass_ref, drop_ref, over, out_ref):
        value, gathered = zero, []
        for j in range(m):
            value = forcing(s * m + j) + (pass_ref[s * m + j] * value if j else 0.0)
            gathered.append(value)
        x = gathered[-1] * over
        for j in reversed(range(m)):
            i = s * m + j
            if j < m - 1:
                x = pass_ref[i + 1] * x + drop_ref[i + 1] * gathered[j]
            out_ref[i] = x

    for i in range(n):
        index = stratum_ref[i, rows, :]
        own_2_ref[i] = number("beta", index) * conc_ref[2, i, rows, :]
        own_3_ref[i] = number("free_b", index) * conc_ref[3, i, rows, :]
        gamma_ref[i] = number("gamma", index)
        share_ref[i] = number("share_b", index)
        decay_ref[i] = number("decay_b", index)
    for s in range(PIECES):
        kappa = {}
        for i in range(s * m, s * m + m):
            kappa[i] = number("kappa", stratum_ref[i, rows, :])
        solve(
            s,
            lambda i: with_border(source_a_ref[i], 0, i),
            pass_a_ref,
            drop_a_ref,
            over_ref[0, s],
            free_a_ref,
        )
        forcings = (
            (lambda i: with_border(source_b_ref[i], 1, i) + kappa[i] * free_a_ref[i], free_b_ref),
            (lambda i: kappa[i] * left_a[i], cross_l_ref),
            (lambda i: kappa[i] * right_a[i], cross_r_ref),
        )
        for forcing, out_ref in forcings:
            solve(s, forcing, pass_b_ref, drop_b_ref, over_ref[1, s], out_ref)


def add_kernel(
    kept,
    kept_ref,
    current_ref,
    free_a_ref,
    free_b_ref,
    cross_l_ref,
    cross_r_ref,
    own_2_ref,
    own_3_ref,
    gamma_ref,
    share_ref,
    decay_ref,
    left_a,
    right_a,
    left_b,
    right_b,
    before_hbm,
    out_hbm,
    made,
    sems,
):
    n, half, planes_z = free_a_ref.shape
    rows = pl.ds(pl.multiple_of(half_of(kept) * half, half), half)
    ends = piece_ends(kept_ref, current_ref)
    m = n // PIECES
    copies = []
    for i in range(n):
        l_a, r_a, l_b, r_b = ends[i // m]
        x0 = free_a_ref[i] + left_a[i] * l_a + right_a[i] * r_a
        x1 = (free_b_ref[i] + cross_l_ref[i] * l_a + cross_r_ref[i] * r_a) + (
            left_b[i] * l_b + right_b[i] * r_b
        )
        x2 = own_2_ref[i] + gamma_ref[i] * x0
        made[0, i], made[1, i], made[2, i] = x0, x1, x2
        made[3, i] = own_3_ref[i] + share_ref[i] * x1 + decay_ref[i] * x2
        copies.append(
            pltpu.make_async_copy(made.at[:, i], out_hbm.at[:, i, rows, :], sems.at[i])
        )
        copies[-1].start()
    for copy in copies:
        copy.wait()


def final_kernel(
    kept,
    tab_ref,
    stratum_ref,
    conc_ref,
    pass_a_ref,
    drop_a_ref,
    pass_b_ref,
    drop_b_ref,
    over_ref,
    source_a_ref,
    source_b_ref,
    kept_ref,
    flow_ref,
    current_ref,
    *refs,
):
    out_hbm, gather_a, gather_b, made, sems = refs[-5:]
    n, planes_y, planes_z = stratum_ref.shape
    half = planes_y // 2
    which = half_of(kept)
    rows = pl.ds(pl.multiple_of(which * half, half), half)
    number = Numbers(tab_ref)
    line = lax.broadcasted_iota(jnp.int32, (half, planes_z), 0)
    outer = line == (half - 1) * which

    def with_border(source, component, i):
        flow = jnp.broadcast_to(flow_ref[component, pl.ds(i, 1), :], source.shape)
        return source + jnp.where(outer, flow, 0.0)

    ends = piece_ends(kept_ref, current_ref)
    pieces = range(PIECES)
    m = n // PIECES
    values = [ends[s][0] for s in pieces]
    for j in range(m):
        for s in pieces:
            i = s * m + j
            values[s] = with_border(source_a_ref[i], 0, i) + values[s]
            if j < m - 1:
                gather_a[i] = values[s]
                values[s] = pass_a_ref[i + 1] * values[s]
    x = [(values[s] + ends[s][1]) * over_ref[0, s] for s in pieces]
    for j in reversed(range(m)):
        for s in pieces:
            i = s * m + j
            if j < m - 1:
                x[s] = pass_a_ref[i + 1] * x[s] + drop_a_ref[i + 1] * gather_a[i]
            made[0, i] = x[s]
    values = [ends[s][2] for s in pieces]
    for j in range(m):
        for s in pieces:
            i = s * m + j
            kappa = number("kappa", stratum_ref[i, rows, :])
            values[s] = with_border(source_b_ref[i], 1, i) + kappa * made[0, i] + values[s]
            if j < m - 1:
                gather_b[i] = values[s]
                values[s] = pass_b_ref[i + 1] * values[s]
    x = [(values[s] + ends[s][3]) * over_ref[1, s] for s in pieces]
    copies = []
    for j in reversed(range(m)):
        for s in pieces:
            i = s * m + j
            if j < m - 1:
                x[s] = pass_b_ref[i + 1] * x[s] + drop_b_ref[i + 1] * gather_b[i]
            made[1, i] = x[s]
            index = stratum_ref[i, rows, :]
            x2 = (
                number("beta", index) * conc_ref[2, i, rows, :]
                + number("gamma", index) * made[0, i]
            )
            made[2, i] = x2
            made[3, i] = (
                number("free_b", index) * conc_ref[3, i, rows, :]
                + number("share_b", index) * x[s]
                + number("decay_b", index) * x2
            )
            copies.append(
                pltpu.make_async_copy(made.at[:, i], out_hbm.at[:, i, rows, :], sems.at[i])
            )
            copies[-1].start()
    for copy in copies:
        copy.wait()


def call(kernel, outs, scratch=()):
    return pl.pallas_call(
        kernel,
        out_shape=[jax.ShapeDtypeStruct(shape, jnp.float32) for shape in outs],
        scratch_shapes=[pltpu.VMEM(shape, jnp.float32) for shape in scratch],
        compiler_params=pltpu.CompilerParams(vmem_limit_bytes=VMEM_LIMIT),
    )


def per_device(
    concentration,
    stratum,
    porosity,
    dispersion_table,
    transverse_table,
    exchange_table,
    decay_table,
):
    n, planes_y, planes_z = stratum.shape
    peers = lax.axis_size("flow")
    half = planes_y // 2
    strides = [1 << k for k in range(peers.bit_length() - 1)]
    cells = (n, planes_y, planes_z)

    halo = (3, n, planes_z)
    strata = porosity.shape[0]
    hbm = pl.BlockSpec(memory_space=pltpu.HBM)
    early, late, table, concentration, stratum = pl.pallas_call(
        pack_kernel,
        out_shape=[
            jax.ShapeDtypeStruct(halo, jnp.float32),
            jax.ShapeDtypeStruct(halo, jnp.float32),
            jax.ShapeDtypeStruct((2 * SUB, LANE), jnp.float32),
            jax.ShapeDtypeStruct(concentration.shape, jnp.float32),
            jax.ShapeDtypeStruct(cells, jnp.int32),
        ],
        in_specs=[hbm] * 7,
        scratch_shapes=[
            pltpu.VMEM((1, strata), jnp.float32),
            pltpu.VMEM((2, strata), jnp.float32),
            pltpu.VMEM((1, strata), jnp.float32),
            pltpu.VMEM((1, strata), jnp.float32),
            pltpu.VMEM((1, strata), jnp.float32),
            pltpu.VMEM((SUB, LANE), jnp.float32),
            pltpu.SemaphoreType.DMA((8,)),
        ],
        compiler_params=pltpu.CompilerParams(vmem_limit_bytes=VMEM_LIMIT),
    )(
        *[
            pltpu.with_memory_space_constraint(value, pltpu.HBM)
            for value in (
                concentration,
                stratum,
                porosity[None],
                dispersion_table.T,
                transverse_table[None],
                exchange_table[None],
                decay_table[None],
            )
        ]
    )
    groups = lax.axis_size("trans")
    def swap(value, start):
        low = range(start, groups - 1, 2)
        pairs = [(i, i + 1) for i in low] + [(i + 1, i) for i in low]
        if start:
            pairs += [(0, groups - 1), (groups - 1, 0)]
        return lax.ppermute(value, "trans", pairs)

    beyond_late = swap(late, 1)
    beyond_early = swap(early, 0)

    def exchange(value, stride):
        return lax.ppermute(value, "flow", [(i, i ^ stride) for i in range(peers)])

    half_cells = (n, half, planes_z)
    block_shape = (QUANTITIES, half, planes_z)

    def local(kept):
        pay, edge, *rest = call(
            functools.partial(local_kernel, kept),
            [
                (PIECES,) + block_shape,
                (6, n, planes_z),
                *[half_cells] * 4,
                (2, PIECES, half, planes_z),
                *[half_cells] * 6,
            ],
            [half_cells] * 5,
        )(table, stratum, concentration)
        pay, parts, flow = call(
            functools.partial(border_kernel, kept),
            [block_shape, (PIECES - 1, KEPT, half, planes_z), (2, n, planes_z)],
        )(table, early, late, beyond_late, beyond_early, edge, pay)
        return pay, rest[:7], rest[7:], parts, flow

    send, sent_rest, sent_responses, sent_parts, sent_flow = local(False)
    block, kept_rest, _, kept_parts, kept_flow = local(True)
    kept = []
    for stride in strides[:-1]:
        other = exchange(send, stride)
        last = stride == strides[-2]
        block, keep, *face = call(
            functools.partial(merge_kernel, stride, last),
            [block_shape, (KEPT, half, planes_z)] + [(5, half, planes_z)] * last,
        )(block, other)
        kept.append(keep)
        send = face[0] if last else block
    prepared = call(functools.partial(prepare_kernel, False), [half_cells] * 9)(
        table, stratum, concentration, *sent_rest, sent_flow, *sent_responses[:2]
    )
    ends_shape = jax.ShapeDtypeStruct((CURRENTS, half, planes_z), jnp.float32)
    vmem = pl.BlockSpec(memory_space=pltpu.VMEM)
    limit = pltpu.CompilerParams(vmem_limit_bytes=VMEM_LIMIT)
    mine, send = pl.pallas_call(
        functools.partial(close_kernel, strides),
        out_shape=[ends_shape, ends_shape],
        in_specs=[pl.BlockSpec(memory_space=pl.ANY)] + [vmem] * (2 + len(kept)),
        compiler_params=limit,
    )(prepared[0], block, exchange(send, strides[-1]), *kept)
    currents = exchange(send, 1)
    whole = jax.ShapeDtypeStruct((4,) + cells, jnp.float32)
    results = [pltpu.VMEM((4,) + half_cells, jnp.float32), pltpu.SemaphoreType.DMA((n,))]
    out = pl.pallas_call(
        functools.partial(final_kernel, True),
        out_shape=whole,
        in_specs=[vmem] * 13,
        out_specs=hbm,
        scratch_shapes=[pltpu.VMEM(half_cells, jnp.float32)] * 2 + results,
        compiler_params=limit,
    )(table, stratum, concentration, *kept_rest, kept_parts, kept_flow, mine)
    return pl.pallas_call(
        functools.partial(add_kernel, False),
        out_shape=whole,
        in_specs=[vmem] * 15 + [hbm],
        out_specs=hbm,
        scratch_shapes=results,
        input_output_aliases={15: 0},
        compiler_params=limit,
    )(sent_parts, currents, *prepared, *sent_responses, out)


def solution(mesh):
    in_specs = (P(None, "flow", "trans", None), P("flow", "trans", None), P(), P(), P(), P(), P())
    out_specs = P(None, "flow", "trans", None)
    return jax.shard_map(
        per_device, mesh=mesh, in_specs=in_specs, out_specs=out_specs, check_vma=False
    )
```

```python
import functools

import jax
import jax.numpy as jnp
from jax import lax
from jax.experimental import pallas as pl
from jax.experimental.pallas import tpu as pltpu
from jax.sharding import PartitionSpec as P

SUB, LANE = 8, 128
ZA_LL, ZA_LR, ZA_RR, ZB_LL, ZB_LR, ZB_RR, C_LL, C_LR, C_RL, C_RR, FA_L, FA_R, FB_L, FB_R = range(14)
QUANTITIES = 14
CURRENTS = 4
KEPT = 8
PIECES = 4
VMEM_LIMIT = 40 * 1024 * 1024


def recip(x):
    return 1.0 / x


def lookup(row, index):
    tiles = []
    for y in range(0, index.shape[0], SUB):
        across = [
            jnp.take_along_axis(
                row, index[y : y + SUB, z : z + LANE], axis=1, mode="promise_in_bounds"
            )
            for z in range(0, index.shape[1], LANE)
        ]
        tiles.append(jnp.concatenate(across, axis=1))
    return jnp.concatenate(tiles, axis=0)


NUMBERS = (
    "por",
    "shunt_a",
    "shunt_b",
    "half_a",
    "half_b",
    "half_t",
    "beta",
    "gamma",
    "alpha_a",
    "alpha_b",
    "kappa",
    "delta",
    "free_b",
    "share_b",
    "decay_b",
)


def derive(por, disp_a, disp_b, trans, exch, decay):
    immobile = 1.0 - por
    over_a = 1.0 / (immobile + exch + decay)
    over_b = 1.0 / (immobile + exch)
    beta = immobile * over_a
    gamma = exch * over_a
    share_b = exch * over_b
    return dict(
        por=por,
        shunt_a=por + decay + exch * (immobile + decay) * over_a,
        shunt_b=por + exch * immobile * over_b,
        half_a=0.5 / disp_a,
        half_b=0.5 / disp_b,
        half_t=0.5 / trans,
        beta=beta,
        gamma=gamma,
        alpha_a=exch * beta,
        alpha_b=share_b * immobile,
        kappa=decay + share_b * decay * gamma,
        delta=share_b * decay * beta,
        free_b=immobile * over_b,
        share_b=share_b,
        decay_b=decay * over_b,
    )


class Numbers:
    def __init__(self, tab_ref):
        self.tab_ref = tab_ref

    def __call__(self, name, index):
        k = NUMBERS.index(name)
        row = jnp.broadcast_to(self.tab_ref[k : k + 1, :], (SUB, LANE))
        return lookup(row, index)


def shifted_difference(value, axis):
    return pltpu.roll(value, value.shape[axis] - 1, axis) - value


def side_of(axis, stride):
    return (lax.axis_index(axis) // stride) % 2 == 1


def pack_kernel(
    conc_hbm,
    stratum_hbm,
    por_hbm,
    disp_hbm,
    trans_hbm,
    exch_hbm,
    decay_hbm,
    early_ref,
    late_ref,
    tab_ref,
    conc_ref,
    stratum_ref,
    por_ref,
    disp_ref,
    trans_ref,
    exch_ref,
    decay_ref,
    raw,
    sems,
):
    moves = [
        (stratum_hbm, stratum_ref),
        (conc_hbm.at[0:2], conc_ref.at[0:2]),
        (por_hbm, por_ref),
        (disp_hbm, disp_ref),
        (trans_hbm, trans_ref),
        (exch_hbm, exch_ref),
        (decay_hbm, decay_ref),
        (conc_hbm.at[2:4], conc_ref.at[2:4]),
    ]
    copies = [pltpu.make_async_copy(src, dst, sems.at[k]) for k, (src, dst) in enumerate(moves)]
    for copy in copies:
        copy.start()
    raw[...] = jnp.full(raw.shape, 0.5, jnp.float32)
    for copy in copies[2:7]:
        copy.wait()
    strata = por_ref.shape[1]
    raw[0:1, 0:strata] = por_ref[...]
    raw[1:3, 0:strata] = disp_ref[...]
    raw[3:4, 0:strata] = trans_ref[...]
    raw[4:5, 0:strata] = exch_ref[...]
    raw[5:6, 0:strata] = decay_ref[...]
    made = derive(*[raw[k : k + 1, :] for k in range(6)])
    for k, name in enumerate(NUMBERS):
        tab_ref[k : k + 1, :] = made[name]
    tab_ref[len(NUMBERS) : 2 * SUB, :] = raw[0 : 2 * SUB - len(NUMBERS), :]
    odd = side_of("trans", 1)
    last = stratum_ref.shape[1] - 1

    def put(k, low, high):
        early_ref[k] = jnp.where(odd, low, high)
        late_ref[k] = jnp.where(odd, high, low)

    copies[0].wait()
    numbered = [(stratum_ref[:, y, :] + 1).astype(jnp.float32) for y in (0, last)]
    put(2, *numbered)
    copies[1].wait()
    for k in (0, 1):
        put(k, conc_ref[k, :, 0, :], conc_ref[k, :, last, :])
    copies[7].wait()


def half_of(kept):
    second = lax.axis_index("flow") % 2
    return second if kept else 1 - second


def local_kernel(
    kept,
    tab_ref,
    stratum_ref,
    conc_ref,
    pay_ref,
    edge_ref,
    pass_a_ref,
    drop_a_ref,
    pass_b_ref,
    drop_b_ref,
    over_ref,
    source_a_ref,
    source_b_ref,
    left_a,
    right_a,
    left_b,
    right_b,
    head_a,
    head_b,
    kappa_ref,
    adj_l,
    adj_r,
):
    n, planes_y, planes_z = stratum_ref.shape
    half = planes_y // 2
    which = half_of(kept)
    rows = pl.ds(pl.multiple_of(which * half, half), half)
    other_rows = pl.ds(pl.multiple_of((1 - which) * half, half), half)
    number = Numbers(tab_ref)

    pieces = range(PIECES)
    m = n // PIECES
    shape = (half, planes_z)
    zero, one = jnp.zeros(shape, jnp.float32), jnp.ones(shape, jnp.float32)

    def from_left(j, carry):
        after = []
        for s, (cond_a, cond_b, half_a, half_b, through_a, through_b) in zip(pieces, carry):
            i = s * m + j
            index = stratum_ref[i, rows, :]
            new_a, new_b = number("half_a", index), number("half_b", index)
            face_a, face_b = half_a + new_a, half_b + new_b
            pass_a, pass_b = recip(1.0 + face_a * cond_a), recip(1.0 + face_b * cond_b)
            cond_a = number("shunt_a", index) + cond_a * pass_a
            cond_b = number("shunt_b", index) + cond_b * pass_b
            through_a, through_b = through_a * pass_a, through_b * pass_b
            kappa_ref[i] = number("kappa", index)
            pass_a_ref[i], pass_b_ref[i] = pass_a, pass_b
            drop_a_ref[i], drop_b_ref[i] = face_a * pass_a, face_b * pass_b
            head_a[i], head_b[i] = through_a, through_b
            after.append((cond_a, cond_b, new_a, new_b, through_a, through_b))
        return after

    ahead = lax.fori_loop(0, m, from_left, [(zero, zero, zero, zero, one, one)] * PIECES)
    over_a, over_b = [recip(c[0]) for c in ahead], [recip(c[1]) for c in ahead]
    for s in pieces:
        over_ref[0, s], over_ref[1, s] = over_a[s], over_b[s]

    def from_right(back, carry):
        after = []
        for s, (next_pass, next_drop, next_pass_b, next_drop_b, l_a, r_a, l_b, r_b, *couple) in zip(
            pieces, carry
        ):
            i = s * m + (m - 1 - back)
            l_a = next_pass * l_a + next_drop * head_a[i]
            l_b = next_pass_b * l_b + next_drop_b * head_b[i]
            r_a, r_b = next_pass * r_a, next_pass_b * r_b
            left_a[i], right_a[i], left_b[i], right_b[i] = l_a, r_a, l_b, r_b
            kappa = kappa_ref[i]
            k_l, k_r = kappa * l_a, kappa * r_a
            terms = [l_b * k_l, l_b * k_r, r_b * k_l, r_b * k_r]
            couple = [c + t for c, t in zip(couple, terms)]
            passes = (pass_a_ref[i], drop_a_ref[i], pass_b_ref[i], drop_b_ref[i])
            after.append((*passes, l_a, r_a, l_b, r_b, *couple))
        return after

    responses = lax.fori_loop(
        0,
        m,
        from_right,
        [(one, a, one, b, zero, a, zero, b, zero, zero, zero, zero) for a, b in zip(over_a, over_b)],
    )

    def share(j, carry):
        after = []
        for s, (g_l, g_r) in zip(pieces, carry):
            i = s * m + j
            kappa, pass_a = kappa_ref[i], pass_a_ref[i]
            g_l = kappa * left_b[i] + pass_a * g_l
            g_r = kappa * right_b[i] + pass_a * g_r
            adj_l[i], adj_r[i] = g_l, g_r
            after.append((g_l, g_r))
        return after

    lax.fori_loop(0, m, share, [(zero, zero)] * PIECES)

    lane = lax.broadcasted_iota(jnp.int32, shape, 1)
    line = lax.broadcasted_iota(jnp.int32, shape, 0)
    inside = (line < half - 1, lane < planes_z - 1)
    meets = line == (half - 1) * (1 - which)
    shift = jnp.where(which == 0, half - 1, 1)

    def sources(back, carry):
        after = []
        for s, (next_pass, next_drop, w_l, w_r, *free) in zip(pieces, carry):
            i = s * m + (m - 1 - back)
            w_l = next_pass * w_l + next_drop * adj_l[i]
            w_r = next_pass * w_r + next_drop * adj_r[i]
            adj_l[i], adj_r[i] = w_l, w_r
            index = stratum_ref[i, rows, :]
            half_t = number("half_t", index)
            por = number("por", index)
            c0, c1, c2, c3 = [conc_ref[k, i, rows, :] for k in range(4)]
            source_a = por * c0 + number("alpha_a", index) * c2
            source_b = por * c1 + number("alpha_b", index) * c3 + number("delta", index) * c2
            for axis in (0, 1):
                last = half_t.shape[axis] - 1
                face = jnp.where(
                    inside[axis], recip(half_t + pltpu.roll(half_t, last, axis)), 0.0
                )
                flow_a = face * shifted_difference(c0, axis)
                flow_b = face * shifted_difference(c1, axis)
                source_a = source_a + (flow_a - pltpu.roll(flow_a, 1, axis))
                source_b = source_b + (flow_b - pltpu.roll(flow_b, 1, axis))
            beyond_t = pltpu.roll(number("half_t", stratum_ref[i, other_rows, :]), shift, 0)
            face = jnp.where(meets, recip(half_t + beyond_t), 0.0)
            beyond_a = pltpu.roll(conc_ref[0, i, other_rows, :], shift, 0)
            beyond_b = pltpu.roll(conc_ref[1, i, other_rows, :], shift, 0)
            source_a = source_a + face * (beyond_a - c0)
            source_b = source_b + face * (beyond_b - c1)
            source_a_ref[i], source_b_ref[i] = source_a, source_b
            terms = [
                left_a[i] * source_a,
                right_a[i] * source_a,
                left_b[i] * source_b + w_l * source_a,
                right_b[i] * source_b + w_r * source_a,
            ]
            free = [f + t for f, t in zip(free, terms)]
            after.append((pass_a_ref[i], drop_a_ref[i], w_l, w_r, *free))
        return after

    totals = lax.fori_loop(0, m, sources, [(one, a) + (zero,) * 6 for a in over_a])
    for s in pieces:
        l_a, r_a, l_b, r_b, *couple = responses[s][4:]
        first = stratum_ref[s * m, rows, :]
        quantities = [
            l_a + number("half_a", first),
            r_a,
            over_a[s] + ahead[s][2],
            l_b + number("half_b", first),
            r_b,
            over_b[s] + ahead[s][3],
            *couple,
            *totals[s][4:],
        ]
        for q, value in enumerate(quantities):
            pay_ref[s, q] = value
    for k, ref in enumerate((left_a, right_a, left_b, right_b, adj_l, adj_r)):
        edge_ref[k] = jnp.where(which == 0, ref[:, 0, :], ref[:, half - 1, :])


def border_kernel(
    kept,
    tab_ref,
    early_ref,
    late_ref,
    beyond_late_ref,
    beyond_early_ref,
    edge_ref,
    pay_ref,
    out_ref,
    kept_ref,
    flow_ref,
):
    number = Numbers(tab_ref)
    n, planes_z = edge_ref.shape[1:]
    m = n // PIECES
    half = pay_ref.shape[2]
    low = half_of(kept) == 0
    early = side_of("trans", 1) == low
    own = jnp.where(early, early_ref[...], late_ref[...])
    beyond = jnp.where(early, beyond_early_ref[...], beyond_late_ref[...])
    own_id = own[2].astype(jnp.int32) - 1
    next_id = beyond[2].astype(jnp.int32) - 1
    resist = number("half_t", own_id) + number("half_t", next_id)
    end = jnp.where(low, 0, lax.axis_size("trans") - 1)
    face = jnp.where(lax.axis_index("trans") != end, recip(resist), 0.0)
    flow_a = face * (beyond[0] - own[0])
    flow_b = face * (beyond[1] - own[1])
    flow_ref[0], flow_ref[1] = flow_a, flow_b
    l_a, r_a, l_b, r_b, w_l, w_r = [edge_ref[k] for k in range(6)]
    changes = {
        FA_L: l_a * flow_a,
        FA_R: r_a * flow_a,
        FB_L: l_b * flow_b + w_l * flow_a,
        FB_R: r_b * flow_b + w_r * flow_a,
    }
    line = lax.broadcasted_iota(jnp.int32, (half, planes_z), 0)
    outer = line == jnp.where(low, 0, half - 1)
    blocks = []
    for s in range(PIECES):
        values = {q: pay_ref[s, q] for q in range(QUANTITIES)}
        for q, change in changes.items():
            total = jnp.sum(change[s * m : (s + 1) * m], axis=0, keepdims=True)
            values[q] = values[q] + jnp.where(outer, total, 0.0)
        blocks.append(values)
    slot = 0
    while len(blocks) > 1:
        joined = []
        for one, two in zip(blocks[::2], blocks[1::2]):
            merged, parts = merge(one, two)
            for k, value in enumerate(parts):
                kept_ref[slot, k] = value
            slot += 1
            joined.append(merged)
        blocks = joined
    for q in range(QUANTITIES):
        out_ref[q] = blocks[0][q]


FACE_L = (ZA_LL, ZB_LL, C_LL, FA_L, FB_L)
FACE_R = (ZA_RR, ZB_RR, C_RR, FA_R, FB_R)


def merge(one, two):
    over_a = recip(one[ZA_RR] + two[ZA_LL])
    over_b = recip(one[ZB_RR] + two[ZB_LL])
    across = one[C_RR] + two[C_LL]
    free_a = over_a * (one[FA_R] - two[FA_L])
    from_l, from_r = over_a * one[ZA_LR], over_a * two[ZA_LR]
    free_b = over_b * (one[FB_R] - two[FB_L] - across * free_a)
    from_l_b, from_r_b = over_b * one[ZB_LR], over_b * two[ZB_LR]
    cross_l = over_b * (one[C_RL] - across * from_l)
    cross_r = over_b * (two[C_LR] - across * from_r)
    merged = {
        ZA_LL: one[ZA_LL] - one[ZA_LR] * from_l,
        ZA_LR: one[ZA_LR] * from_r,
        ZA_RR: two[ZA_RR] - two[ZA_LR] * from_r,
        ZB_LL: one[ZB_LL] - one[ZB_LR] * from_l_b,
        ZB_LR: one[ZB_LR] * from_r_b,
        ZB_RR: two[ZB_RR] - two[ZB_LR] * from_r_b,
        C_LL: one[C_LL] - one[ZB_LR] * cross_l - one[C_LR] * from_l,
        C_LR: one[ZB_LR] * cross_r + one[C_LR] * from_r,
        C_RL: two[ZB_LR] * cross_l + two[C_RL] * from_l,
        C_RR: two[C_RR] - two[ZB_LR] * cross_r - two[C_RL] * from_r,
        FA_L: one[FA_L] - one[ZA_LR] * free_a,
        FA_R: two[FA_R] + two[ZA_LR] * free_a,
        FB_L: one[FB_L] - one[ZB_LR] * free_b - one[C_LR] * free_a,
        FB_R: two[FB_R] + two[ZB_LR] * free_b + two[C_RL] * free_a,
    }
    return merged, (free_a, from_l, from_r, free_b, from_l_b, from_r_b, cross_l, cross_r)


def between(kept, ends):
    free_a, from_l, from_r, free_b, from_l_b, from_r_b, cross_l, cross_r = kept
    l_a, r_a, l_b, r_b = ends
    middle_a = free_a + from_l * l_a - from_r * r_a
    middle_b = free_b + from_l_b * l_b - from_r_b * r_b + cross_l * l_a - cross_r * r_a
    return middle_a, middle_b


def merge_kernel(stride, last, own_ref, other_ref, out_ref, kept_ref, *face_ref):
    second = side_of("flow", stride)
    own = [own_ref[q] for q in range(QUANTITIES)]
    other = [other_ref[q] for q in range(QUANTITIES)]
    one = [jnp.where(second, b, a) for a, b in zip(own, other)]
    two = [jnp.where(second, a, b) for a, b in zip(own, other)]
    merged, kept = merge(one, two)
    for q, value in merged.items():
        out_ref[q] = value
    for k, value in enumerate(kept):
        kept_ref[k] = value
    if last:
        after = side_of("flow", 2 * stride)
        for k, (l, r) in enumerate(zip(FACE_L, FACE_R)):
            face_ref[0][k] = jnp.where(after, merged[l], merged[r])


def close_kernel(strides, ready_ref, own_ref, other_ref, *refs):
    kept_refs, mine_ref, send_ref = refs[:-2], refs[-2], refs[-1]
    stride = strides[-1]
    second = side_of("flow", stride)
    own = [jnp.where(second, own_ref[l], own_ref[r]) for l, r in zip(FACE_L, FACE_R)]
    z_a, z_b, couple, f_a, f_b = [own[k] + other_ref[k] for k in range(3)] + [
        jnp.where(second, other_ref[k] - own[k], own[k] - other_ref[k]) for k in (3, 4)
    ]
    current_a = recip(z_a) * f_a
    current_b = recip(z_b) * (f_b - couple * current_a)
    nothing = jnp.zeros_like(current_a)

    def side_ends(after, middle_a, middle_b, ends):
        l_a, r_a, l_b, r_b = ends
        return (
            jnp.where(after, middle_a, l_a),
            jnp.where(after, r_a, -middle_a),
            jnp.where(after, middle_b, l_b),
            jnp.where(after, r_b, -middle_b),
        )

    ends = side_ends(second, current_a, current_b, (nothing,) * 4)
    for stride, kept_ref in reversed(list(zip(strides[:-1], kept_refs))):
        middle_a, middle_b = between([kept_ref[k] for k in range(KEPT)], ends)
        after = side_of("flow", stride)
        if stride == 1:
            other_ends = side_ends(jnp.logical_not(after), middle_a, middle_b, ends)
            for q, value in enumerate(other_ends):
                send_ref[q] = value
        ends = side_ends(after, middle_a, middle_b, ends)
    for q, value in enumerate(ends):
        mine_ref[q] = value


def piece_ends(kept_ref, current_ref):
    ends = [tuple(current_ref[q] for q in range(CURRENTS))]
    slot = PIECES - 1
    while len(ends) < PIECES:
        slot -= len(ends)
        parts = []
        for k, (l_a, r_a, l_b, r_b) in enumerate(ends):
            values = [kept_ref[slot + k, v] for v in range(KEPT)]
            middle_a, middle_b = between(values, (l_a, r_a, l_b, r_b))
            parts += [(l_a, -middle_a, l_b, -middle_b), (middle_a, r_a, middle_b, r_b)]
        ends = parts
    return ends


def prepare_kernel(
    kept,
    tab_ref,
    stratum_ref,
    conc_ref,
    pass_a_ref,
    drop_a_ref,
    pass_b_ref,
    drop_b_ref,
    over_ref,
    source_a_ref,
    source_b_ref,
    flow_ref,
    left_a,
    right_a,
    free_a_ref,
    free_b_ref,
    cross_l_ref,
    cross_r_ref,
    own_2_ref,
    own_3_ref,
    gamma_ref,
    share_ref,
    decay_ref,
):
    n, planes_y, planes_z = stratum_ref.shape
    half = planes_y // 2
    which = half_of(kept)
    rows = pl.ds(pl.multiple_of(which * half, half), half)
    number = Numbers(tab_ref)
    line = lax.broadcasted_iota(jnp.int32, (half, planes_z), 0)
    outer = line == (half - 1) * which
    zero = jnp.zeros((half, planes_z), jnp.float32)
    m = n // PIECES

    def with_border(source, component, i):
        flow = jnp.broadcast_to(flow_ref[component, i : i + 1, :], source.shape)
        return source + jnp.where(outer, flow, 0.0)

    def solve(s, forcing, pass_ref, drop_ref, over, out_ref):
        value, gathered = zero, []
        for j in range(m):
            value = forcing(s * m + j) + (pass_ref[s * m + j] * value if j else 0.0)
            gathered.append(value)
        x = gathered[-1] * over
        for j in reversed(range(m)):
            i = s * m + j
            if j < m - 1:
                x = pass_ref[i + 1] * x + drop_ref[i + 1] * gathered[j]
            out_ref[i] = x

    for i in range(n):
        index = stratum_ref[i, rows, :]
        own_2_ref[i] = number("beta", index) * conc_ref[2, i, rows, :]
        own_3_ref[i] = number("free_b", index) * conc_ref[3, i, rows, :]
        gamma_ref[i] = number("gamma", index)
        share_ref[i] = number("share_b", index)
        decay_ref[i] = number("decay_b", index)
    for s in range(PIECES):
        kappa = {}
        for i in range(s * m, s * m + m):
            kappa[i] = number("kappa", stratum_ref[i, rows, :])
        solve(
            s,
            lambda i: with_border(source_a_ref[i], 0, i),
            pass_a_ref,
            drop_a_ref,
            over_ref[0, s],
            free_a_ref,
        )
        forcings = (
            (lambda i: with_border(source_b_ref[i], 1, i) + kappa[i] * free_a_ref[i], free_b_ref),
            (lambda i: kappa[i] * left_a[i], cross_l_ref),
            (lambda i: kappa[i] * right_a[i], cross_r_ref),
        )
        for forcing, out_ref in forcings:
            solve(s, forcing, pass_b_ref, drop_b_ref, over_ref[1, s], out_ref)


def add_kernel(
    kept,
    kept_ref,
    current_ref,
    free_a_ref,
    free_b_ref,
    cross_l_ref,
    cross_r_ref,
    own_2_ref,
    own_3_ref,
    gamma_ref,
    share_ref,
    decay_ref,
    left_a,
    right_a,
    left_b,
    right_b,
    before_hbm,
    out_hbm,
    made,
    sems,
):
    n, half, planes_z = free_a_ref.shape
    rows = pl.ds(pl.multiple_of(half_of(kept) * half, half), half)
    ends = piece_ends(kept_ref, current_ref)
    m = n // PIECES
    copies = []
    for i in range(n):
        l_a, r_a, l_b, r_b = ends[i // m]
        x0 = free_a_ref[i] + left_a[i] * l_a + right_a[i] * r_a
        x1 = (free_b_ref[i] + cross_l_ref[i] * l_a + cross_r_ref[i] * r_a) + (
            left_b[i] * l_b + right_b[i] * r_b
        )
        x2 = own_2_ref[i] + gamma_ref[i] * x0
        made[0, i], made[1, i], made[2, i] = x0, x1, x2
        made[3, i] = own_3_ref[i] + share_ref[i] * x1 + decay_ref[i] * x2
        copies.append(
            pltpu.make_async_copy(made.at[:, i], out_hbm.at[:, i, rows, :], sems.at[i])
        )
        copies[-1].start()
    for copy in copies:
        copy.wait()


def final_kernel(
    kept,
    tab_ref,
    stratum_ref,
    conc_ref,
    pass_a_ref,
    drop_a_ref,
    pass_b_ref,
    drop_b_ref,
    over_ref,
    source_a_ref,
    source_b_ref,
    kept_ref,
    flow_ref,
    current_ref,
    *refs,
):
    out_hbm, gather_a, gather_b, made, sems = refs[-5:]
    n, planes_y, planes_z = stratum_ref.shape
    half = planes_y // 2
    which = half_of(kept)
    rows = pl.ds(pl.multiple_of(which * half, half), half)
    number = Numbers(tab_ref)
    line = lax.broadcasted_iota(jnp.int32, (half, planes_z), 0)
    outer = line == (half - 1) * which

    def with_border(source, component, i):
        flow = jnp.broadcast_to(flow_ref[component, pl.ds(i, 1), :], source.shape)
        return source + jnp.where(outer, flow, 0.0)

    ends = piece_ends(kept_ref, current_ref)
    pieces = range(PIECES)
    m = n // PIECES
    values = [ends[s][0] for s in pieces]
    for j in range(m):
        for s in pieces:
            i = s * m + j
            values[s] = with_border(source_a_ref[i], 0, i) + values[s]
            if j < m - 1:
                gather_a[i] = values[s]
                values[s] = pass_a_ref[i + 1] * values[s]
    x = [(values[s] + ends[s][1]) * over_ref[0, s] for s in pieces]
    for j in reversed(range(m)):
        for s in pieces:
            i = s * m + j
            if j < m - 1:
                x[s] = pass_a_ref[i + 1] * x[s] + drop_a_ref[i + 1] * gather_a[i]
            made[0, i] = x[s]
    values = [ends[s][2] for s in pieces]
    for j in range(m):
        for s in pieces:
            i = s * m + j
            kappa = number("kappa", stratum_ref[i, rows, :])
            values[s] = with_border(source_b_ref[i], 1, i) + kappa * made[0, i] + values[s]
            if j < m - 1:
                gather_b[i] = values[s]
                values[s] = pass_b_ref[i + 1] * values[s]
    x = [(values[s] + ends[s][3]) * over_ref[1, s] for s in pieces]
    copies = []
    for j in reversed(range(m)):
        for s in pieces:
            i = s * m + j
            if j < m - 1:
                x[s] = pass_b_ref[i + 1] * x[s] + drop_b_ref[i + 1] * gather_b[i]
            made[1, i] = x[s]
            index = stratum_ref[i, rows, :]
            x2 = (
                number("beta", index) * conc_ref[2, i, rows, :]
                + number("gamma", index) * made[0, i]
            )
            made[2, i] = x2
            made[3, i] = (
                number("free_b", index) * conc_ref[3, i, rows, :]
                + number("share_b", index) * x[s]
                + number("decay_b", index) * x2
            )
            copies.append(
                pltpu.make_async_copy(made.at[:, i], out_hbm.at[:, i, rows, :], sems.at[i])
            )
            copies[-1].start()
    for copy in copies:
        copy.wait()


def call(kernel, outs, scratch=()):
    return pl.pallas_call(
        kernel,
        out_shape=[jax.ShapeDtypeStruct(shape, jnp.float32) for shape in outs],
        scratch_shapes=[pltpu.VMEM(shape, jnp.float32) for shape in scratch],
        compiler_params=pltpu.CompilerParams(vmem_limit_bytes=VMEM_LIMIT),
    )


def per_device(
    concentration,
    stratum,
    porosity,
    dispersion_table,
    transverse_table,
    exchange_table,
    decay_table,
):
    n, planes_y, planes_z = stratum.shape
    peers = lax.axis_size("flow")
    half = planes_y // 2
    strides = [1 << k for k in range(peers.bit_length() - 1)]
    cells = (n, planes_y, planes_z)

    halo = (3, n, planes_z)
    strata = porosity.shape[0]
    hbm = pl.BlockSpec(memory_space=pltpu.HBM)
    early, late, table, concentration, stratum = pl.pallas_call(
        pack_kernel,
        out_shape=[
            jax.ShapeDtypeStruct(halo, jnp.float32),
            jax.ShapeDtypeStruct(halo, jnp.float32),
            jax.ShapeDtypeStruct((2 * SUB, LANE), jnp.float32),
            jax.ShapeDtypeStruct(concentration.shape, jnp.float32),
            jax.ShapeDtypeStruct(cells, jnp.int32),
        ],
        in_specs=[hbm] * 7,
        scratch_shapes=[
            pltpu.VMEM((1, strata), jnp.float32),
            pltpu.VMEM((2, strata), jnp.float32),
            pltpu.VMEM((1, strata), jnp.float32),
            pltpu.VMEM((1, strata), jnp.float32),
            pltpu.VMEM((1, strata), jnp.float32),
            pltpu.VMEM((SUB, LANE), jnp.float32),
            pltpu.SemaphoreType.DMA((8,)),
        ],
        compiler_params=pltpu.CompilerParams(vmem_limit_bytes=VMEM_LIMIT),
    )(
        *[
            pltpu.with_memory_space_constraint(value, pltpu.HBM)
            for value in (
                concentration,
                stratum,
                porosity[None],
                dispersion_table.T,
                transverse_table[None],
                exchange_table[None],
                decay_table[None],
            )
        ]
    )
    groups = lax.axis_size("trans")
    def swap(value, start):
        low = range(start, groups - 1, 2)
        pairs = [(i, i + 1) for i in low] + [(i + 1, i) for i in low]
        if start:
            pairs += [(0, 0), (groups - 1, groups - 1)]
        return lax.ppermute(value, "trans", pairs)

    beyond_late = swap(late, 1)
    beyond_early = swap(early, 0)

    def exchange(value, stride):
        return lax.ppermute(value, "flow", [(i, i ^ stride) for i in range(peers)])

    half_cells = (n, half, planes_z)
    block_shape = (QUANTITIES, half, planes_z)

    def local(kept):
        pay, edge, *rest = call(
            functools.partial(local_kernel, kept),
            [
                (PIECES,) + block_shape,
                (6, n, planes_z),
                *[half_cells] * 4,
                (2, PIECES, half, planes_z),
                *[half_cells] * 6,
            ],
            [half_cells] * 5,
        )(table, stratum, concentration)
        pay, parts, flow = call(
            functools.partial(border_kernel, kept),
            [block_shape, (PIECES - 1, KEPT, half, planes_z), (2, n, planes_z)],
        )(table, early, late, beyond_late, beyond_early, edge, pay)
        return pay, rest[:7], rest[7:], parts, flow

    send, sent_rest, sent_responses, sent_parts, sent_flow = local(False)
    block, kept_rest, _, kept_parts, kept_flow = local(True)
    kept = []
    for stride in strides[:-1]:
        other = exchange(send, stride)
        last = stride == strides[-2]
        block, keep, *face = call(
            functools.partial(merge_kernel, stride, last),
            [block_shape, (KEPT, half, planes_z)] + [(5, half, planes_z)] * last,
        )(block, other)
        kept.append(keep)
        send = face[0] if last else block
    prepared = call(functools.partial(prepare_kernel, False), [half_cells] * 9)(
        table, stratum, concentration, *sent_rest, sent_flow, *sent_responses[:2]
    )
    ends_shape = jax.ShapeDtypeStruct((CURRENTS, half, planes_z), jnp.float32)
    vmem = pl.BlockSpec(memory_space=pltpu.VMEM)
    limit = pltpu.CompilerParams(vmem_limit_bytes=VMEM_LIMIT)
    mine, send = pl.pallas_call(
        functools.partial(close_kernel, strides),
        out_shape=[ends_shape, ends_shape],
        in_specs=[pl.BlockSpec(memory_space=pl.ANY)] + [vmem] * (2 + len(kept)),
        compiler_params=limit,
    )(prepared[0], block, exchange(send, strides[-1]), *kept)
    currents = exchange(send, 1)
    whole = jax.ShapeDtypeStruct((4,) + cells, jnp.float32)
    results = [pltpu.VMEM((4,) + half_cells, jnp.float32), pltpu.SemaphoreType.DMA((n,))]
    out = pl.pallas_call(
        functools.partial(final_kernel, True),
        out_shape=whole,
        in_specs=[vmem] * 13,
        out_specs=hbm,
        scratch_shapes=[pltpu.VMEM(half_cells, jnp.float32)] * 2 + results,
        compiler_params=limit,
    )(table, stratum, concentration, *kept_rest, kept_parts, kept_flow, mine)
    return pl.pallas_call(
        functools.partial(add_kernel, False),
        out_shape=whole,
        in_specs=[vmem] * 15 + [hbm],
        out_specs=hbm,
        scratch_shapes=results,
        input_output_aliases={15: 0},
        compiler_params=limit,
    )(sent_parts, currents, *prepared, *sent_responses, out)


def solution(mesh):
    in_specs = (P(None, "flow", "trans", None), P("flow", "trans", None), P(), P(), P(), P(), P())
    out_specs = P(None, "flow", "trans", None)
    return jax.shard_map(
        per_device, mesh=mesh, in_specs=in_specs, out_specs=out_specs, check_vma=False
    )
```

```python
import functools

import jax
import jax.numpy as jnp
from jax import lax
from jax.experimental import pallas as pl
from jax.experimental.pallas import tpu as pltpu
from jax.sharding import PartitionSpec as P

SUB, LANE = 8, 128
ZA_LL, ZA_LR, ZA_RR, ZB_LL, ZB_LR, ZB_RR, C_LL, C_LR, C_RL, C_RR, FA_L, FA_R, FB_L, FB_R = range(14)
QUANTITIES = 14
CURRENTS = 4
KEPT = 8
PIECES = 4
VMEM_LIMIT = 40 * 1024 * 1024


def recip(x):
    return 1.0 / x


def lookup(row, index):
    tiles = []
    for y in range(0, index.shape[0], SUB):
        across = [
            jnp.take_along_axis(
                row, index[y : y + SUB, z : z + LANE], axis=1, mode="promise_in_bounds"
            )
            for z in range(0, index.shape[1], LANE)
        ]
        tiles.append(jnp.concatenate(across, axis=1))
    return jnp.concatenate(tiles, axis=0)


NUMBERS = (
    "por",
    "shunt_a",
    "shunt_b",
    "half_a",
    "half_b",
    "half_t",
    "beta",
    "gamma",
    "alpha_a",
    "alpha_b",
    "kappa",
    "delta",
    "free_b",
    "share_b",
    "decay_b",
)


def derive(por, disp_a, disp_b, trans, exch, decay):
    immobile = 1.0 - por
    over_a = 1.0 / (immobile + exch + decay)
    over_b = 1.0 / (immobile + exch)
    beta = immobile * over_a
    gamma = exch * over_a
    share_b = exch * over_b
    return dict(
        por=por,
        shunt_a=por + decay + exch * (immobile + decay) * over_a,
        shunt_b=por + exch * immobile * over_b,
        half_a=0.5 / disp_a,
        half_b=0.5 / disp_b,
        half_t=0.5 / trans,
        beta=beta,
        gamma=gamma,
        alpha_a=exch * beta,
        alpha_b=share_b * immobile,
        kappa=decay + share_b * decay * gamma,
        delta=share_b * decay * beta,
        free_b=immobile * over_b,
        share_b=share_b,
        decay_b=decay * over_b,
    )


class Numbers:
    def __init__(self, tab_ref):
        self.tab_ref = tab_ref

    def __call__(self, name, index):
        k = NUMBERS.index(name)
        row = jnp.broadcast_to(self.tab_ref[k : k + 1, :], (SUB, LANE))
        return lookup(row, index)


def shifted_difference(value, axis):
    return pltpu.roll(value, value.shape[axis] - 1, axis) - value


def side_of(axis, stride):
    return (lax.axis_index(axis) // stride) % 2 == 1


def pack_kernel(
    conc_hbm,
    stratum_hbm,
    por_hbm,
    disp_hbm,
    trans_hbm,
    exch_hbm,
    decay_hbm,
    early_ref,
    late_ref,
    tab_ref,
    conc_ref,
    stratum_ref,
    por_ref,
    disp_ref,
    trans_ref,
    exch_ref,
    decay_ref,
    raw,
    sems,
):
    moves = [
        (stratum_hbm, stratum_ref),
        (conc_hbm.at[0:2], conc_ref.at[0:2]),
        (por_hbm, por_ref),
        (disp_hbm, disp_ref),
        (trans_hbm, trans_ref),
        (exch_hbm, exch_ref),
        (decay_hbm, decay_ref),
        (conc_hbm.at[2:4], conc_ref.at[2:4]),
    ]
    copies = [pltpu.make_async_copy(src, dst, sems.at[k]) for k, (src, dst) in enumerate(moves)]
    for copy in copies:
        copy.start()
    raw[...] = jnp.full(raw.shape, 0.5, jnp.float32)
    for copy in copies[2:7]:
        copy.wait()
    strata = por_ref.shape[1]
    raw[0:1, 0:strata] = por_ref[...]
    raw[1:3, 0:strata] = disp_ref[...]
    raw[3:4, 0:strata] = trans_ref[...]
    raw[4:5, 0:strata] = exch_ref[...]
    raw[5:6, 0:strata] = decay_ref[...]
    made = derive(*[raw[k : k + 1, :] for k in range(6)])
    for k, name in enumerate(NUMBERS):
        tab_ref[k : k + 1, :] = made[name]
    tab_ref[len(NUMBERS) : 2 * SUB, :] = raw[0 : 2 * SUB - len(NUMBERS), :]
    odd = side_of("trans", 1)
    last = stratum_ref.shape[1] - 1

    def put(k, low, high):
        early_ref[k] = jnp.where(odd, low, high)
        late_ref[k] = jnp.where(odd, high, low)

    copies[0].wait()
    numbered = [(stratum_ref[:, y, :] + 1).astype(jnp.float32) for y in (0, last)]
    put(2, *numbered)
    copies[1].wait()
    for k in (0, 1):
        put(k, conc_ref[k, :, 0, :], conc_ref[k, :, last, :])
    copies[7].wait()


def half_of(kept):
    second = lax.axis_index("flow") % 2
    return second if kept else 1 - second


def local_kernel(
    kept,
    tab_ref,
    stratum_ref,
    conc_ref,
    pay_ref,
    edge_ref,
    pass_a_ref,
    drop_a_ref,
    pass_b_ref,
    drop_b_ref,
    over_ref,
    source_a_ref,
    source_b_ref,
    left_a,
    right_a,
    left_b,
    right_b,
    head_a,
    head_b,
    kappa_ref,
    adj_l,
    adj_r,
):
    n, planes_y, planes_z = stratum_ref.shape
    half = planes_y // 2
    which = half_of(kept)
    rows = pl.ds(pl.multiple_of(which * half, half), half)
    other_rows = pl.ds(pl.multiple_of((1 - which) * half, half), half)
    number = Numbers(tab_ref)

    pieces = range(PIECES)
    m = n // PIECES
    shape = (half, planes_z)
    zero, one = jnp.zeros(shape, jnp.float32), jnp.ones(shape, jnp.float32)

    def from_left(j, carry):
        after = []
        for s, (cond_a, cond_b, half_a, half_b, through_a, through_b) in zip(pieces, carry):
            i = s * m + j
            index = stratum_ref[i, rows, :]
            new_a, new_b = number("half_a", index), number("half_b", index)
            face_a, face_b = half_a + new_a, half_b + new_b
            pass_a, pass_b = recip(1.0 + face_a * cond_a), recip(1.0 + face_b * cond_b)
            cond_a = number("shunt_a", index) + cond_a * pass_a
            cond_b = number("shunt_b", index) + cond_b * pass_b
            through_a, through_b = through_a * pass_a, through_b * pass_b
            kappa_ref[i] = number("kappa", index)
            pass_a_ref[i], pass_b_ref[i] = pass_a, pass_b
            drop_a_ref[i], drop_b_ref[i] = face_a * pass_a, face_b * pass_b
            head_a[i], head_b[i] = through_a, through_b
            after.append((cond_a, cond_b, new_a, new_b, through_a, through_b))
        return after

    ahead = lax.fori_loop(0, m, from_left, [(zero, zero, zero, zero, one, one)] * PIECES)
    over_a, over_b = [recip(c[0]) for c in ahead], [recip(c[1]) for c in ahead]
    for s in pieces:
        over_ref[0, s], over_ref[1, s] = over_a[s], over_b[s]

    def from_right(back, carry):
        after = []
        for s, (next_pass, next_drop, next_pass_b, next_drop_b, l_a, r_a, l_b, r_b, *couple) in zip(
            pieces, carry
        ):
            i = s * m + (m - 1 - back)
            l_a = next_pass * l_a + next_drop * head_a[i]
            l_b = next_pass_b * l_b + next_drop_b * head_b[i]
            r_a, r_b = next_pass * r_a, next_pass_b * r_b
            left_a[i], right_a[i], left_b[i], right_b[i] = l_a, r_a, l_b, r_b
            kappa = kappa_ref[i]
            k_l, k_r = kappa * l_a, kappa * r_a
            terms = [l_b * k_l, l_b * k_r, r_b * k_l, r_b * k_r]
            couple = [c + t for c, t in zip(couple, terms)]
            passes = (pass_a_ref[i], drop_a_ref[i], pass_b_ref[i], drop_b_ref[i])
            after.append((*passes, l_a, r_a, l_b, r_b, *couple))
        return after

    responses = lax.fori_loop(
        0,
        m,
        from_right,
        [(one, a, one, b, zero, a, zero, b, zero, zero, zero, zero) for a, b in zip(over_a, over_b)],
    )

    def share(j, carry):
        after = []
        for s, (g_l, g_r) in zip(pieces, carry):
            i = s * m + j
            kappa, pass_a = kappa_ref[i], pass_a_ref[i]
            g_l = kappa * left_b[i] + pass_a * g_l
            g_r = kappa * right_b[i] + pass_a * g_r
            adj_l[i], adj_r[i] = g_l, g_r
            after.append((g_l, g_r))
        return after

    lax.fori_loop(0, m, share, [(zero, zero)] * PIECES)

    lane = lax.broadcasted_iota(jnp.int32, shape, 1)
    line = lax.broadcasted_iota(jnp.int32, shape, 0)
    inside = (line < half - 1, lane < planes_z - 1)
    meets = line == (half - 1) * (1 - which)
    shift = jnp.where(which == 0, half - 1, 1)

    def sources(back, carry):
        after = []
        for s, (next_pass, next_drop, w_l, w_r, *free) in zip(pieces, carry):
            i = s * m + (m - 1 - back)
            w_l = next_pass * w_l + next_drop * adj_l[i]
            w_r = next_pass * w_r + next_drop * adj_r[i]
            adj_l[i], adj_r[i] = w_l, w_r
            index = stratum_ref[i, rows, :]
            half_t = number("half_t", index)
            por = number("por", index)
            c0, c1, c2, c3 = [conc_ref[k, i, rows, :] for k in range(4)]
            source_a = por * c0 + number("alpha_a", index) * c2
            source_b = por * c1 + number("alpha_b", index) * c3 + number("delta", index) * c2
            for axis in (0, 1):
                last = half_t.shape[axis] - 1
                face = jnp.where(
                    inside[axis], recip(half_t + pltpu.roll(half_t, last, axis)), 0.0
                )
                flow_a = face * shifted_difference(c0, axis)
                flow_b = face * shifted_difference(c1, axis)
                source_a = source_a + (flow_a - pltpu.roll(flow_a, 1, axis))
                source_b = source_b + (flow_b - pltpu.roll(flow_b, 1, axis))
            beyond_t = pltpu.roll(number("half_t", stratum_ref[i, other_rows, :]), shift, 0)
            face = jnp.where(meets, recip(half_t + beyond_t), 0.0)
            beyond_a = pltpu.roll(conc_ref[0, i, other_rows, :], shift, 0)
            beyond_b = pltpu.roll(conc_ref[1, i, other_rows, :], shift, 0)
            source_a = source_a + face * (beyond_a - c0)
            source_b = source_b + face * (beyond_b - c1)
            source_a_ref[i], source_b_ref[i] = source_a, source_b
            terms = [
                left_a[i] * source_a,
                right_a[i] * source_a,
                left_b[i] * source_b + w_l * source_a,
                right_b[i] * source_b + w_r * source_a,
            ]
            free = [f + t for f, t in zip(free, terms)]
            after.append((pass_a_ref[i], drop_a_ref[i], w_l, w_r, *free))
        return after

    totals = lax.fori_loop(0, m, sources, [(one, a) + (zero,) * 6 for a in over_a])
    for s in pieces:
        l_a, r_a, l_b, r_b, *couple = responses[s][4:]
        first = stratum_ref[s * m, rows, :]
        quantities = [
            l_a + number("half_a", first),
            r_a,
            over_a[s] + ahead[s][2],
            l_b + number("half_b", first),
            r_b,
            over_b[s] + ahead[s][3],
            *couple,
            *totals[s][4:],
        ]
        for q, value in enumerate(quantities):
            pay_ref[s, q] = value
    for k, ref in enumerate((left_a, right_a, left_b, right_b, adj_l, adj_r)):
        edge_ref[k] = jnp.where(which == 0, ref[:, 0, :], ref[:, half - 1, :])


def border_kernel(
    kept,
    tab_ref,
    early_ref,
    late_ref,
    beyond_late_ref,
    beyond_early_ref,
    edge_ref,
    pay_ref,
    out_ref,
    kept_ref,
    flow_ref,
):
    number = Numbers(tab_ref)
    n, planes_z = edge_ref.shape[1:]
    m = n // PIECES
    half = pay_ref.shape[2]
    low = half_of(kept) == 0
    early = side_of("trans", 1) == low
    own = jnp.where(early, early_ref[...], late_ref[...])
    beyond = jnp.where(early, beyond_early_ref[...], beyond_late_ref[...])
    own_id = own[2].astype(jnp.int32) - 1
    next_id = beyond[2].astype(jnp.int32) - 1
    resist = number("half_t", own_id) + number("half_t", next_id)
    end = jnp.where(low, 0, lax.axis_size("trans") - 1)
    face = jnp.where(lax.axis_index("trans") != end, recip(resist), 0.0)
    flow_a = face * (beyond[0] - own[0])
    flow_b = face * (beyond[1] - own[1])
    flow_ref[0], flow_ref[1] = flow_a, flow_b
    l_a, r_a, l_b, r_b, w_l, w_r = [edge_ref[k] for k in range(6)]
    changes = {
        FA_L: l_a * flow_a,
        FA_R: r_a * flow_a,
        FB_L: l_b * flow_b + w_l * flow_a,
        FB_R: r_b * flow_b + w_r * flow_a,
    }
    line = lax.broadcasted_iota(jnp.int32, (half, planes_z), 0)
    outer = line == jnp.where(low, 0, half - 1)
    blocks = []
    for s in range(PIECES):
        values = {q: pay_ref[s, q] for q in range(QUANTITIES)}
        for q, change in changes.items():
            total = jnp.sum(change[s * m : (s + 1) * m], axis=0, keepdims=True)
            values[q] = values[q] + jnp.where(outer, total, 0.0)
        blocks.append(values)
    slot = 0
    while len(blocks) > 1:
        joined = []
        for one, two in zip(blocks[::2], blocks[1::2]):
            merged, parts = merge(one, two)
            for k, value in enumerate(parts):
                kept_ref[slot, k] = value
            slot += 1
            joined.append(merged)
        blocks = joined
    for q in range(QUANTITIES):
        out_ref[q] = blocks[0][q]


FACE_L = (ZA_LL, ZB_LL, C_LL, FA_L, FB_L)
FACE_R = (ZA_RR, ZB_RR, C_RR, FA_R, FB_R)


def merge(one, two):
    over_a = recip(one[ZA_RR] + two[ZA_LL])
    over_b = recip(one[ZB_RR] + two[ZB_LL])
    across = one[C_RR] + two[C_LL]
    free_a = over_a * (one[FA_R] - two[FA_L])
    from_l, from_r = over_a * one[ZA_LR], over_a * two[ZA_LR]
    free_b = over_b * (one[FB_R] - two[FB_L] - across * free_a)
    from_l_b, from_r_b = over_b * one[ZB_LR], over_b * two[ZB_LR]
    cross_l = over_b * (one[C_RL] - across * from_l)
    cross_r = over_b * (two[C_LR] - across * from_r)
    merged = {
        ZA_LL: one[ZA_LL] - one[ZA_LR] * from_l,
        ZA_LR: one[ZA_LR] * from_r,
        ZA_RR: two[ZA_RR] - two[ZA_LR] * from_r,
        ZB_LL: one[ZB_LL] - one[ZB_LR] * from_l_b,
        ZB_LR: one[ZB_LR] * from_r_b,
        ZB_RR: two[ZB_RR] - two[ZB_LR] * from_r_b,
        C_LL: one[C_LL] - one[ZB_LR] * cross_l - one[C_LR] * from_l,
        C_LR: one[ZB_LR] * cross_r + one[C_LR] * from_r,
        C_RL: two[ZB_LR] * cross_l + two[C_RL] * from_l,
        C_RR: two[C_RR] - two[ZB_LR] * cross_r - two[C_RL] * from_r,
        FA_L: one[FA_L] - one[ZA_LR] * free_a,
        FA_R: two[FA_R] + two[ZA_LR] * free_a,
        FB_L: one[FB_L] - one[ZB_LR] * free_b - one[C_LR] * free_a,
        FB_R: two[FB_R] + two[ZB_LR] * free_b + two[C_RL] * free_a,
    }
    return merged, (free_a, from_l, from_r, free_b, from_l_b, from_r_b, cross_l, cross_r)


def between(kept, ends):
    free_a, from_l, from_r, free_b, from_l_b, from_r_b, cross_l, cross_r = kept
    l_a, r_a, l_b, r_b = ends
    middle_a = free_a + from_l * l_a - from_r * r_a
    middle_b = free_b + from_l_b * l_b - from_r_b * r_b + cross_l * l_a - cross_r * r_a
    return middle_a, middle_b


def merge_kernel(stride, last, own_ref, other_ref, out_ref, kept_ref, *face_ref):
    second = side_of("flow", stride)
    own = [own_ref[q] for q in range(QUANTITIES)]
    other = [other_ref[q] for q in range(QUANTITIES)]
    one = [jnp.where(second, b, a) for a, b in zip(own, other)]
    two = [jnp.where(second, a, b) for a, b in zip(own, other)]
    merged, kept = merge(one, two)
    for q, value in merged.items():
        out_ref[q] = value
    for k, value in enumerate(kept):
        kept_ref[k] = value
    if last:
        after = side_of("flow", 2 * stride)
        for k, (l, r) in enumerate(zip(FACE_L, FACE_R)):
            face_ref[0][k] = jnp.where(after, merged[l], merged[r])


def close_kernel(strides, ready_ref, own_ref, other_ref, *refs):
    kept_refs, mine_ref, send_ref = refs[:-2], refs[-2], refs[-1]
    stride = strides[-1]
    second = side_of("flow", stride)
    own = [jnp.where(second, own_ref[l], own_ref[r]) for l, r in zip(FACE_L, FACE_R)]
    z_a, z_b, couple, f_a, f_b = [own[k] + other_ref[k] for k in range(3)] + [
        jnp.where(second, other_ref[k] - own[k], own[k] - other_ref[k]) for k in (3, 4)
    ]
    current_a = recip(z_a) * f_a
    current_b = recip(z_b) * (f_b - couple * current_a)
    nothing = jnp.zeros_like(current_a)

    def side_ends(after, middle_a, middle_b, ends):
        l_a, r_a, l_b, r_b = ends
        return (
            jnp.where(after, middle_a, l_a),
            jnp.where(after, r_a, -middle_a),
            jnp.where(after, middle_b, l_b),
            jnp.where(after, r_b, -middle_b),
        )

    ends = side_ends(second, current_a, current_b, (nothing,) * 4)
    for stride, kept_ref in reversed(list(zip(strides[:-1], kept_refs))):
        middle_a, middle_b = between([kept_ref[k] for k in range(KEPT)], ends)
        after = side_of("flow", stride)
        if stride == 1:
            other_ends = side_ends(jnp.logical_not(after), middle_a, middle_b, ends)
            for q, value in enumerate(other_ends):
                send_ref[q] = value
        ends = side_ends(after, middle_a, middle_b, ends)
    for q, value in enumerate(ends):
        mine_ref[q] = value


def piece_ends(kept_ref, current_ref):
    ends = [tuple(current_ref[q] for q in range(CURRENTS))]
    slot = PIECES - 1
    while len(ends) < PIECES:
        slot -= len(ends)
        parts = []
        for k, (l_a, r_a, l_b, r_b) in enumerate(ends):
            values = [kept_ref[slot + k, v] for v in range(KEPT)]
            middle_a, middle_b = between(values, (l_a, r_a, l_b, r_b))
            parts += [(l_a, -middle_a, l_b, -middle_b), (middle_a, r_a, middle_b, r_b)]
        ends = parts
    return ends


def prepare_kernel(
    kept,
    tab_ref,
    stratum_ref,
    conc_ref,
    pass_a_ref,
    drop_a_ref,
    pass_b_ref,
    drop_b_ref,
    over_ref,
    source_a_ref,
    source_b_ref,
    flow_ref,
    left_a,
    right_a,
    free_a_ref,
    free_b_ref,
    cross_l_ref,
    cross_r_ref,
    own_2_ref,
    own_3_ref,
    gamma_ref,
    share_ref,
    decay_ref,
):
    n, planes_y, planes_z = stratum_ref.shape
    half = planes_y // 2
    which = half_of(kept)
    rows = pl.ds(pl.multiple_of(which * half, half), half)
    number = Numbers(tab_ref)
    line = lax.broadcasted_iota(jnp.int32, (half, planes_z), 0)
    outer = line == (half - 1) * which
    zero = jnp.zeros((half, planes_z), jnp.float32)
    m = n // PIECES

    def with_border(source, component, i):
        flow = jnp.broadcast_to(flow_ref[component, i : i + 1, :], source.shape)
        return source + jnp.where(outer, flow, 0.0)

    def solve(s, forcing, pass_ref, drop_ref, over, out_ref):
        value, gathered = zero, []
        for j in range(m):
            value = forcing(s * m + j) + (pass_ref[s * m + j] * value if j else 0.0)
            gathered.append(value)
        x = gathered[-1] * over
        for j in reversed(range(m)):
            i = s * m + j
            if j < m - 1:
                x = pass_ref[i + 1] * x + drop_ref[i + 1] * gathered[j]
            out_ref[i] = x

    for i in range(n):
        index = stratum_ref[i, rows, :]
        own_2_ref[i] = number("beta", index) * conc_ref[2, i, rows, :]
        own_3_ref[i] = number("free_b", index) * conc_ref[3, i, rows, :]
        gamma_ref[i] = number("gamma", index)
        share_ref[i] = number("share_b", index)
        decay_ref[i] = number("decay_b", index)
    for s in range(PIECES):
        kappa = {}
        for i in range(s * m, s * m + m):
            kappa[i] = number("kappa", stratum_ref[i, rows, :])
        solve(
            s,
            lambda i: with_border(source_a_ref[i], 0, i),
            pass_a_ref,
            drop_a_ref,
            over_ref[0, s],
            free_a_ref,
        )
        forcings = (
            (lambda i: with_border(source_b_ref[i], 1, i) + kappa[i] * free_a_ref[i], free_b_ref),
            (lambda i: kappa[i] * left_a[i], cross_l_ref),
            (lambda i: kappa[i] * right_a[i], cross_r_ref),
        )
        for forcing, out_ref in forcings:
            solve(s, forcing, pass_b_ref, drop_b_ref, over_ref[1, s], out_ref)


def add_kernel(
    kept,
    kept_ref,
    current_ref,
    free_a_ref,
    free_b_ref,
    cross_l_ref,
    cross_r_ref,
    own_2_ref,
    own_3_ref,
    gamma_ref,
    share_ref,
    decay_ref,
    left_a,
    right_a,
    left_b,
    right_b,
    before_hbm,
    out_hbm,
    made,
    sems,
):
    n, half, planes_z = free_a_ref.shape
    rows = pl.ds(pl.multiple_of(half_of(kept) * half, half), half)
    ends = piece_ends(kept_ref, current_ref)
    m = n // PIECES
    copies = []
    for i in range(n):
        l_a, r_a, l_b, r_b = ends[i // m]
        x0 = free_a_ref[i] + left_a[i] * l_a + right_a[i] * r_a
        x1 = (free_b_ref[i] + cross_l_ref[i] * l_a + cross_r_ref[i] * r_a) + (
            left_b[i] * l_b + right_b[i] * r_b
        )
        x2 = own_2_ref[i] + gamma_ref[i] * x0
        made[0, i], made[1, i], made[2, i] = x0, x1, x2
        made[3, i] = own_3_ref[i] + share_ref[i] * x1 + decay_ref[i] * x2
        copies.append(
            pltpu.make_async_copy(made.at[:, i], out_hbm.at[:, i, rows, :], sems.at[i])
        )
        copies[-1].start()
    for copy in copies:
        copy.wait()


def final_kernel(
    kept,
    tab_ref,
    stratum_ref,
    conc_ref,
    pass_a_ref,
    drop_a_ref,
    pass_b_ref,
    drop_b_ref,
    over_ref,
    source_a_ref,
    source_b_ref,
    kept_ref,
    flow_ref,
    current_ref,
    *refs,
):
    out_hbm, gather_a, gather_b, made, sems = refs[-5:]
    n, planes_y, planes_z = stratum_ref.shape
    half = planes_y // 2
    which = half_of(kept)
    rows = pl.ds(pl.multiple_of(which * half, half), half)
    number = Numbers(tab_ref)
    line = lax.broadcasted_iota(jnp.int32, (half, planes_z), 0)
    outer = line == (half - 1) * which

    def with_border(source, component, i):
        flow = jnp.broadcast_to(flow_ref[component, pl.ds(i, 1), :], source.shape)
        return source + jnp.where(outer, flow, 0.0)

    ends = piece_ends(kept_ref, current_ref)
    pieces = range(PIECES)
    m = n // PIECES
    values = [ends[s][0] for s in pieces]
    for j in range(m):
        for s in pieces:
            i = s * m + j
            values[s] = with_border(source_a_ref[i], 0, i) + values[s]
            if j < m - 1:
                gather_a[i] = values[s]
                values[s] = pass_a_ref[i + 1] * values[s]
    x = [(values[s] + ends[s][1]) * over_ref[0, s] for s in pieces]
    for j in reversed(range(m)):
        for s in pieces:
            i = s * m + j
            if j < m - 1:
                x[s] = pass_a_ref[i + 1] * x[s] + drop_a_ref[i + 1] * gather_a[i]
            made[0, i] = x[s]
    values = [ends[s][2] for s in pieces]
    for j in range(m):
        for s in pieces:
            i = s * m + j
            kappa = number("kappa", stratum_ref[i, rows, :])
            values[s] = with_border(source_b_ref[i], 1, i) + kappa * made[0, i] + values[s]
            if j < m - 1:
                gather_b[i] = values[s]
                values[s] = pass_b_ref[i + 1] * values[s]
    x = [(values[s] + ends[s][3]) * over_ref[1, s] for s in pieces]
    copies = []
    for j in reversed(range(m)):
        for s in pieces:
            i = s * m + j
            if j < m - 1:
                x[s] = pass_b_ref[i + 1] * x[s] + drop_b_ref[i + 1] * gather_b[i]
            made[1, i] = x[s]
            index = stratum_ref[i, rows, :]
            x2 = (
                number("beta", index) * conc_ref[2, i, rows, :]
                + number("gamma", index) * made[0, i]
            )
            made[2, i] = x2
            made[3, i] = (
                number("free_b", index) * conc_ref[3, i, rows, :]
                + number("share_b", index) * x[s]
                + number("decay_b", index) * x2
            )
            copies.append(
                pltpu.make_async_copy(made.at[:, i], out_hbm.at[:, i, rows, :], sems.at[i])
            )
            copies[-1].start()
    for copy in copies:
        copy.wait()


def call(kernel, outs, scratch=()):
    return pl.pallas_call(
        kernel,
        out_shape=[jax.ShapeDtypeStruct(shape, jnp.float32) for shape in outs],
        scratch_shapes=[pltpu.VMEM(shape, jnp.float32) for shape in scratch],
        compiler_params=pltpu.CompilerParams(vmem_limit_bytes=VMEM_LIMIT),
    )


def per_device(
    concentration,
    stratum,
    porosity,
    dispersion_table,
    transverse_table,
    exchange_table,
    decay_table,
):
    n, planes_y, planes_z = stratum.shape
    peers = lax.axis_size("flow")
    half = planes_y // 2
    strides = [1 << k for k in range(peers.bit_length() - 1)]
    cells = (n, planes_y, planes_z)

    halo = (3, n, planes_z)
    strata = porosity.shape[0]
    hbm = pl.BlockSpec(memory_space=pltpu.HBM)
    early, late, table, concentration, stratum = pl.pallas_call(
        pack_kernel,
        out_shape=[
            jax.ShapeDtypeStruct(halo, jnp.float32),
            jax.ShapeDtypeStruct(halo, jnp.float32),
            jax.ShapeDtypeStruct((2 * SUB, LANE), jnp.float32),
            jax.ShapeDtypeStruct(concentration.shape, jnp.float32),
            jax.ShapeDtypeStruct(cells, jnp.int32),
        ],
        in_specs=[hbm] * 7,
        scratch_shapes=[
            pltpu.VMEM((1, strata), jnp.float32),
            pltpu.VMEM((2, strata), jnp.float32),
            pltpu.VMEM((1, strata), jnp.float32),
            pltpu.VMEM((1, strata), jnp.float32),
            pltpu.VMEM((1, strata), jnp.float32),
            pltpu.VMEM((SUB, LANE), jnp.float32),
            pltpu.SemaphoreType.DMA((8,)),
        ],
        compiler_params=pltpu.CompilerParams(vmem_limit_bytes=VMEM_LIMIT),
    )(
        *[
            pltpu.with_memory_space_constraint(value, pltpu.HBM)
            for value in (
                concentration,
                stratum,
                porosity[None],
                dispersion_table.T,
                transverse_table[None],
                exchange_table[None],
                decay_table[None],
            )
        ]
    )
    groups = lax.axis_size("trans")
    def swap(value, start):
        pairs = []
        for f in range(peers):
            for t in range(groups):
                other = t + 1 if (t - start) % 2 == 0 else t - 1
                if 0 <= other < groups:
                    pairs.append((f * groups + t, f * groups + other))
                else:
                    pairs.append((f * groups + t, (f ^ 1) * groups + t))
        return lax.ppermute(value, ("flow", "trans"), pairs)

    beyond_late = swap(late, 1)
    beyond_early = swap(early, 0)

    def exchange(value, stride):
        return lax.ppermute(value, "flow", [(i, i ^ stride) for i in range(peers)])

    half_cells = (n, half, planes_z)
    block_shape = (QUANTITIES, half, planes_z)

    def local(kept):
        pay, edge, *rest = call(
            functools.partial(local_kernel, kept),
            [
                (PIECES,) + block_shape,
                (6, n, planes_z),
                *[half_cells] * 4,
                (2, PIECES, half, planes_z),
                *[half_cells] * 6,
            ],
            [half_cells] * 5,
        )(table, stratum, concentration)
        pay, parts, flow = call(
            functools.partial(border_kernel, kept),
            [block_shape, (PIECES - 1, KEPT, half, planes_z), (2, n, planes_z)],
        )(table, early, late, beyond_late, beyond_early, edge, pay)
        return pay, rest[:7], rest[7:], parts, flow

    send, sent_rest, sent_responses, sent_parts, sent_flow = local(False)
    block, kept_rest, _, kept_parts, kept_flow = local(True)
    kept = []
    for stride in strides[:-1]:
        other = exchange(send, stride)
        last = stride == strides[-2]
        block, keep, *face = call(
            functools.partial(merge_kernel, stride, last),
            [block_shape, (KEPT, half, planes_z)] + [(5, half, planes_z)] * last,
        )(block, other)
        kept.append(keep)
        send = face[0] if last else block
    prepared = call(functools.partial(prepare_kernel, False), [half_cells] * 9)(
        table, stratum, concentration, *sent_rest, sent_flow, *sent_responses[:2]
    )
    ends_shape = jax.ShapeDtypeStruct((CURRENTS, half, planes_z), jnp.float32)
    vmem = pl.BlockSpec(memory_space=pltpu.VMEM)
    limit = pltpu.CompilerParams(vmem_limit_bytes=VMEM_LIMIT)
    mine, send = pl.pallas_call(
        functools.partial(close_kernel, strides),
        out_shape=[ends_shape, ends_shape],
        in_specs=[pl.BlockSpec(memory_space=pl.ANY)] + [vmem] * (2 + len(kept)),
        compiler_params=limit,
    )(prepared[0], block, exchange(send, strides[-1]), *kept)
    currents = exchange(send, 1)
    whole = jax.ShapeDtypeStruct((4,) + cells, jnp.float32)
    results = [pltpu.VMEM((4,) + half_cells, jnp.float32), pltpu.SemaphoreType.DMA((n,))]
    out = pl.pallas_call(
        functools.partial(final_kernel, True),
        out_shape=whole,
        in_specs=[vmem] * 13,
        out_specs=hbm,
        scratch_shapes=[pltpu.VMEM(half_cells, jnp.float32)] * 2 + results,
        compiler_params=limit,
    )(table, stratum, concentration, *kept_rest, kept_parts, kept_flow, mine)
    return pl.pallas_call(
        functools.partial(add_kernel, False),
        out_shape=whole,
        in_specs=[vmem] * 15 + [hbm],
        out_specs=hbm,
        scratch_shapes=results,
        input_output_aliases={15: 0},
        compiler_params=limit,
    )(sent_parts, currents, *prepared, *sent_responses, out)


def solution(mesh):
    in_specs = (P(None, "flow", "trans", None), P("flow", "trans", None), P(), P(), P(), P(), P())
    out_specs = P(None, "flow", "trans", None)
    return jax.shard_map(
        per_device, mesh=mesh, in_specs=in_specs, out_specs=out_specs, check_vma=False
    )
```

```python
import functools

import jax
import jax.numpy as jnp
from jax import lax
from jax.experimental import pallas as pl
from jax.experimental.pallas import tpu as pltpu
from jax.sharding import PartitionSpec as P

SUB, LANE = 8, 128
ZA_LL, ZA_LR, ZA_RR, ZB_LL, ZB_LR, ZB_RR, C_LL, C_LR, C_RL, C_RR, FA_L, FA_R, FB_L, FB_R = range(14)
QUANTITIES = 14
CURRENTS = 4
KEPT = 8
PIECES = 4
VMEM_LIMIT = 40 * 1024 * 1024


def recip(x):
    return 1.0 / x


def lookup(row, index):
    tiles = []
    for y in range(0, index.shape[0], SUB):
        across = [
            jnp.take_along_axis(
                row, index[y : y + SUB, z : z + LANE], axis=1, mode="promise_in_bounds"
            )
            for z in range(0, index.shape[1], LANE)
        ]
        tiles.append(jnp.concatenate(across, axis=1))
    return jnp.concatenate(tiles, axis=0)


NUMBERS = (
    "por",
    "shunt_a",
    "shunt_b",
    "half_a",
    "half_b",
    "half_t",
    "beta",
    "gamma",
    "alpha_a",
    "alpha_b",
    "kappa",
    "delta",
    "free_b",
    "share_b",
    "decay_b",
)


def derive(por, disp_a, disp_b, trans, exch, decay):
    immobile = 1.0 - por
    over_a = 1.0 / (immobile + exch + decay)
    over_b = 1.0 / (immobile + exch)
    beta = immobile * over_a
    gamma = exch * over_a
    share_b = exch * over_b
    return dict(
        por=por,
        shunt_a=por + decay + exch * (immobile + decay) * over_a,
        shunt_b=por + exch * immobile * over_b,
        half_a=0.5 / disp_a,
        half_b=0.5 / disp_b,
        half_t=0.5 / trans,
        beta=beta,
        gamma=gamma,
        alpha_a=exch * beta,
        alpha_b=share_b * immobile,
        kappa=decay + share_b * decay * gamma,
        delta=share_b * decay * beta,
        free_b=immobile * over_b,
        share_b=share_b,
        decay_b=decay * over_b,
    )


class Numbers:
    def __init__(self, tab_ref):
        self.tab_ref = tab_ref

    def __call__(self, name, index):
        k = NUMBERS.index(name)
        row = jnp.broadcast_to(self.tab_ref[k : k + 1, :], (SUB, LANE))
        return lookup(row, index)


def shifted_difference(value, axis):
    return pltpu.roll(value, value.shape[axis] - 1, axis) - value


def side_of(axis, stride):
    return (lax.axis_index(axis) // stride) % 2 == 1


def pack_kernel(
    conc_hbm,
    stratum_hbm,
    por_hbm,
    disp_hbm,
    trans_hbm,
    exch_hbm,
    decay_hbm,
    early_ref,
    late_ref,
    tab_ref,
    conc_ref,
    stratum_ref,
    por_ref,
    disp_ref,
    trans_ref,
    exch_ref,
    decay_ref,
    raw,
    sems,
):
    moves = [
        (stratum_hbm, stratum_ref),
        (conc_hbm.at[0:2], conc_ref.at[0:2]),
        (por_hbm, por_ref),
        (disp_hbm, disp_ref),
        (trans_hbm, trans_ref),
        (exch_hbm, exch_ref),
        (decay_hbm, decay_ref),
        (conc_hbm.at[2:4], conc_ref.at[2:4]),
    ]
    copies = [pltpu.make_async_copy(src, dst, sems.at[k]) for k, (src, dst) in enumerate(moves)]
    for copy in copies:
        copy.start()
    raw[...] = jnp.full(raw.shape, 0.5, jnp.float32)
    for copy in copies[2:7]:
        copy.wait()
    strata = por_ref.shape[1]
    raw[0:1, 0:strata] = por_ref[...]
    raw[1:3, 0:strata] = disp_ref[...]
    raw[3:4, 0:strata] = trans_ref[...]
    raw[4:5, 0:strata] = exch_ref[...]
    raw[5:6, 0:strata] = decay_ref[...]
    made = derive(*[raw[k : k + 1, :] for k in range(6)])
    for k, name in enumerate(NUMBERS):
        tab_ref[k : k + 1, :] = made[name]
    tab_ref[len(NUMBERS) : 2 * SUB, :] = raw[0 : 2 * SUB - len(NUMBERS), :]
    odd = side_of("trans", 1)
    last = stratum_ref.shape[1] - 1

    def put(k, low, high):
        early_ref[k] = jnp.where(odd, low, high)
        late_ref[k] = jnp.where(odd, high, low)

    copies[0].wait()
    numbered = [(stratum_ref[:, y, :] + 1).astype(jnp.float32) for y in (0, last)]
    put(2, *numbered)
    copies[1].wait()
    for k in (0, 1):
        put(k, conc_ref[k, :, 0, :], conc_ref[k, :, last, :])
    copies[7].wait()


def half_of(kept):
    second = lax.axis_index("flow") % 2
    return second if kept else 1 - second


def local_kernel(
    kept,
    tab_ref,
    stratum_ref,
    conc_ref,
    pay_ref,
    edge_ref,
    pass_a_ref,
    drop_a_ref,
    pass_b_ref,
    drop_b_ref,
    over_ref,
    source_a_ref,
    source_b_ref,
    left_a,
    right_a,
    left_b,
    right_b,
    head_a,
    head_b,
    kappa_ref,
    adj_l,
    adj_r,
):
    n, planes_y, planes_z = stratum_ref.shape
    half = planes_y // 2
    which = half_of(kept)
    rows = pl.ds(pl.multiple_of(which * half, half), half)
    other_rows = pl.ds(pl.multiple_of((1 - which) * half, half), half)
    number = Numbers(tab_ref)

    pieces = range(PIECES)
    m = n // PIECES
    shape = (half, planes_z)
    zero, one = jnp.zeros(shape, jnp.float32), jnp.ones(shape, jnp.float32)

    def from_left(j, carry):
        after = []
        for s, (cond_a, cond_b, half_a, half_b, through_a, through_b) in zip(pieces, carry):
            i = s * m + j
            index = stratum_ref[i, rows, :]
            new_a, new_b = number("half_a", index), number("half_b", index)
            face_a, face_b = half_a + new_a, half_b + new_b
            pass_a, pass_b = recip(1.0 + face_a * cond_a), recip(1.0 + face_b * cond_b)
            cond_a = number("shunt_a", index) + cond_a * pass_a
            cond_b = number("shunt_b", index) + cond_b * pass_b
            through_a, through_b = through_a * pass_a, through_b * pass_b
            kappa_ref[i] = number("kappa", index)
            pass_a_ref[i], pass_b_ref[i] = pass_a, pass_b
            drop_a_ref[i], drop_b_ref[i] = face_a * pass_a, face_b * pass_b
            head_a[i], head_b[i] = through_a, through_b
            after.append((cond_a, cond_b, new_a, new_b, through_a, through_b))
        return after

    start = [(zero, zero, zero, zero, one, one)] * PIECES
    ahead = lax.fori_loop(0, m, from_left, start, unroll=2)
    over_a, over_b = [recip(c[0]) for c in ahead], [recip(c[1]) for c in ahead]
    for s in pieces:
        over_ref[0, s], over_ref[1, s] = over_a[s], over_b[s]

    def from_right(back, carry):
        after = []
        for s, (next_pass, next_drop, next_pass_b, next_drop_b, l_a, r_a, l_b, r_b, *couple) in zip(
            pieces, carry
        ):
            i = s * m + (m - 1 - back)
            l_a = next_pass * l_a + next_drop * head_a[i]
            l_b = next_pass_b * l_b + next_drop_b * head_b[i]
            r_a, r_b = next_pass * r_a, next_pass_b * r_b
            left_a[i], right_a[i], left_b[i], right_b[i] = l_a, r_a, l_b, r_b
            kappa = kappa_ref[i]
            k_l, k_r = kappa * l_a, kappa * r_a
            terms = [l_b * k_l, l_b * k_r, r_b * k_l, r_b * k_r]
            couple = [c + t for c, t in zip(couple, terms)]
            passes = (pass_a_ref[i], drop_a_ref[i], pass_b_ref[i], drop_b_ref[i])
            after.append((*passes, l_a, r_a, l_b, r_b, *couple))
        return after

    responses = lax.fori_loop(
        0,
        m,
        from_right,
        [(one, a, one, b, zero, a, zero, b, zero, zero, zero, zero) for a, b in zip(over_a, over_b)],
        unroll=2,
    )

    def share(j, carry):
        after = []
        for s, (g_l, g_r) in zip(pieces, carry):
            i = s * m + j
            kappa, pass_a = kappa_ref[i], pass_a_ref[i]
            g_l = kappa * left_b[i] + pass_a * g_l
            g_r = kappa * right_b[i] + pass_a * g_r
            adj_l[i], adj_r[i] = g_l, g_r
            after.append((g_l, g_r))
        return after

    lax.fori_loop(0, m, share, [(zero, zero)] * PIECES, unroll=2)

    lane = lax.broadcasted_iota(jnp.int32, shape, 1)
    line = lax.broadcasted_iota(jnp.int32, shape, 0)
    inside = (line < half - 1, lane < planes_z - 1)
    meets = line == (half - 1) * (1 - which)
    shift = jnp.where(which == 0, half - 1, 1)

    def sources(back, carry):
        after = []
        for s, (next_pass, next_drop, w_l, w_r, *free) in zip(pieces, carry):
            i = s * m + (m - 1 - back)
            w_l = next_pass * w_l + next_drop * adj_l[i]
            w_r = next_pass * w_r + next_drop * adj_r[i]
            adj_l[i], adj_r[i] = w_l, w_r
            index = stratum_ref[i, rows, :]
            half_t = number("half_t", index)
            por = number("por", index)
            c0, c1, c2, c3 = [conc_ref[k, i, rows, :] for k in range(4)]
            source_a = por * c0 + number("alpha_a", index) * c2
            source_b = por * c1 + number("alpha_b", index) * c3 + number("delta", index) * c2
            for axis in (0, 1):
                last = half_t.shape[axis] - 1
                face = jnp.where(
                    inside[axis], recip(half_t + pltpu.roll(half_t, last, axis)), 0.0
                )
                flow_a = face * shifted_difference(c0, axis)
                flow_b = face * shifted_difference(c1, axis)
                source_a = source_a + (flow_a - pltpu.roll(flow_a, 1, axis))
                source_b = source_b + (flow_b - pltpu.roll(flow_b, 1, axis))
            beyond_t = pltpu.roll(number("half_t", stratum_ref[i, other_rows, :]), shift, 0)
            face = jnp.where(meets, recip(half_t + beyond_t), 0.0)
            beyond_a = pltpu.roll(conc_ref[0, i, other_rows, :], shift, 0)
            beyond_b = pltpu.roll(conc_ref[1, i, other_rows, :], shift, 0)
            source_a = source_a + face * (beyond_a - c0)
            source_b = source_b + face * (beyond_b - c1)
            source_a_ref[i], source_b_ref[i] = source_a, source_b
            terms = [
                left_a[i] * source_a,
                right_a[i] * source_a,
                left_b[i] * source_b + w_l * source_a,
                right_b[i] * source_b + w_r * source_a,
            ]
            free = [f + t for f, t in zip(free, terms)]
            after.append((pass_a_ref[i], drop_a_ref[i], w_l, w_r, *free))
        return after

    totals = lax.fori_loop(0, m, sources, [(one, a) + (zero,) * 6 for a in over_a], unroll=2)
    for s in pieces:
        l_a, r_a, l_b, r_b, *couple = responses[s][4:]
        first = stratum_ref[s * m, rows, :]
        quantities = [
            l_a + number("half_a", first),
            r_a,
            over_a[s] + ahead[s][2],
            l_b + number("half_b", first),
            r_b,
            over_b[s] + ahead[s][3],
            *couple,
            *totals[s][4:],
        ]
        for q, value in enumerate(quantities):
            pay_ref[s, q] = value
    for k, ref in enumerate((left_a, right_a, left_b, right_b, adj_l, adj_r)):
        edge_ref[k] = jnp.where(which == 0, ref[:, 0, :], ref[:, half - 1, :])


def border_kernel(
    kept,
    tab_ref,
    early_ref,
    late_ref,
    beyond_late_ref,
    beyond_early_ref,
    edge_ref,
    pay_ref,
    out_ref,
    kept_ref,
    flow_ref,
):
    number = Numbers(tab_ref)
    n, planes_z = edge_ref.shape[1:]
    m = n // PIECES
    half = pay_ref.shape[2]
    low = half_of(kept) == 0
    early = side_of("trans", 1) == low
    own = jnp.where(early, early_ref[...], late_ref[...])
    beyond = jnp.where(early, beyond_early_ref[...], beyond_late_ref[...])
    own_id = own[2].astype(jnp.int32) - 1
    next_id = beyond[2].astype(jnp.int32) - 1
    resist = number("half_t", own_id) + number("half_t", next_id)
    end = jnp.where(low, 0, lax.axis_size("trans") - 1)
    face = jnp.where(lax.axis_index("trans") != end, recip(resist), 0.0)
    flow_a = face * (beyond[0] - own[0])
    flow_b = face * (beyond[1] - own[1])
    flow_ref[0], flow_ref[1] = flow_a, flow_b
    l_a, r_a, l_b, r_b, w_l, w_r = [edge_ref[k] for k in range(6)]
    changes = {
        FA_L: l_a * flow_a,
        FA_R: r_a * flow_a,
        FB_L: l_b * flow_b + w_l * flow_a,
        FB_R: r_b * flow_b + w_r * flow_a,
    }
    line = lax.broadcasted_iota(jnp.int32, (half, planes_z), 0)
    outer = line == jnp.where(low, 0, half - 1)
    blocks = []
    for s in range(PIECES):
        values = {q: pay_ref[s, q] for q in range(QUANTITIES)}
        for q, change in changes.items():
            total = jnp.sum(change[s * m : (s + 1) * m], axis=0, keepdims=True)
            values[q] = values[q] + jnp.where(outer, total, 0.0)
        blocks.append(values)
    slot = 0
    while len(blocks) > 1:
        joined = []
        for one, two in zip(blocks[::2], blocks[1::2]):
            merged, parts = merge(one, two)
            for k, value in enumerate(parts):
                kept_ref[slot, k] = value
            slot += 1
            joined.append(merged)
        blocks = joined
    for q in range(QUANTITIES):
        out_ref[q] = blocks[0][q]


FACE_L = (ZA_LL, ZB_LL, C_LL, FA_L, FB_L)
FACE_R = (ZA_RR, ZB_RR, C_RR, FA_R, FB_R)


def merge(one, two):
    over_a = recip(one[ZA_RR] + two[ZA_LL])
    over_b = recip(one[ZB_RR] + two[ZB_LL])
    across = one[C_RR] + two[C_LL]
    free_a = over_a * (one[FA_R] - two[FA_L])
    from_l, from_r = over_a * one[ZA_LR], over_a * two[ZA_LR]
    free_b = over_b * (one[FB_R] - two[FB_L] - across * free_a)
    from_l_b, from_r_b = over_b * one[ZB_LR], over_b * two[ZB_LR]
    cross_l = over_b * (one[C_RL] - across * from_l)
    cross_r = over_b * (two[C_LR] - across * from_r)
    merged = {
        ZA_LL: one[ZA_LL] - one[ZA_LR] * from_l,
        ZA_LR: one[ZA_LR] * from_r,
        ZA_RR: two[ZA_RR] - two[ZA_LR] * from_r,
        ZB_LL: one[ZB_LL] - one[ZB_LR] * from_l_b,
        ZB_LR: one[ZB_LR] * from_r_b,
        ZB_RR: two[ZB_RR] - two[ZB_LR] * from_r_b,
        C_LL: one[C_LL] - one[ZB_LR] * cross_l - one[C_LR] * from_l,
        C_LR: one[ZB_LR] * cross_r + one[C_LR] * from_r,
        C_RL: two[ZB_LR] * cross_l + two[C_RL] * from_l,
        C_RR: two[C_RR] - two[ZB_LR] * cross_r - two[C_RL] * from_r,
        FA_L: one[FA_L] - one[ZA_LR] * free_a,
        FA_R: two[FA_R] + two[ZA_LR] * free_a,
        FB_L: one[FB_L] - one[ZB_LR] * free_b - one[C_LR] * free_a,
        FB_R: two[FB_R] + two[ZB_LR] * free_b + two[C_RL] * free_a,
    }
    return merged, (free_a, from_l, from_r, free_b, from_l_b, from_r_b, cross_l, cross_r)


def between(kept, ends):
    free_a, from_l, from_r, free_b, from_l_b, from_r_b, cross_l, cross_r = kept
    l_a, r_a, l_b, r_b = ends
    middle_a = free_a + from_l * l_a - from_r * r_a
    middle_b = free_b + from_l_b * l_b - from_r_b * r_b + cross_l * l_a - cross_r * r_a
    return middle_a, middle_b


def merge_kernel(stride, last, own_ref, other_ref, out_ref, kept_ref, *face_ref):
    second = side_of("flow", stride)
    own = [own_ref[q] for q in range(QUANTITIES)]
    other = [other_ref[q] for q in range(QUANTITIES)]
    one = [jnp.where(second, b, a) for a, b in zip(own, other)]
    two = [jnp.where(second, a, b) for a, b in zip(own, other)]
    merged, kept = merge(one, two)
    for q, value in merged.items():
        out_ref[q] = value
    for k, value in enumerate(kept):
        kept_ref[k] = value
    if last:
        after = side_of("flow", 2 * stride)
        for k, (l, r) in enumerate(zip(FACE_L, FACE_R)):
            face_ref[0][k] = jnp.where(after, merged[l], merged[r])


def close_kernel(strides, ready_ref, own_ref, other_ref, *refs):
    kept_refs, mine_ref, send_ref = refs[:-2], refs[-2], refs[-1]
    stride = strides[-1]
    second = side_of("flow", stride)
    own = [jnp.where(second, own_ref[l], own_ref[r]) for l, r in zip(FACE_L, FACE_R)]
    z_a, z_b, couple, f_a, f_b = [own[k] + other_ref[k] for k in range(3)] + [
        jnp.where(second, other_ref[k] - own[k], own[k] - other_ref[k]) for k in (3, 4)
    ]
    current_a = recip(z_a) * f_a
    current_b = recip(z_b) * (f_b - couple * current_a)
    nothing = jnp.zeros_like(current_a)

    def side_ends(after, middle_a, middle_b, ends):
        l_a, r_a, l_b, r_b = ends
        return (
            jnp.where(after, middle_a, l_a),
            jnp.where(after, r_a, -middle_a),
            jnp.where(after, middle_b, l_b),
            jnp.where(after, r_b, -middle_b),
        )

    ends = side_ends(second, current_a, current_b, (nothing,) * 4)
    for stride, kept_ref in reversed(list(zip(strides[:-1], kept_refs))):
        middle_a, middle_b = between([kept_ref[k] for k in range(KEPT)], ends)
        after = side_of("flow", stride)
        if stride == 1:
            other_ends = side_ends(jnp.logical_not(after), middle_a, middle_b, ends)
            for q, value in enumerate(other_ends):
                send_ref[q] = value
        ends = side_ends(after, middle_a, middle_b, ends)
    for q, value in enumerate(ends):
        mine_ref[q] = value


def piece_ends(kept_ref, current_ref):
    ends = [tuple(current_ref[q] for q in range(CURRENTS))]
    slot = PIECES - 1
    while len(ends) < PIECES:
        slot -= len(ends)
        parts = []
        for k, (l_a, r_a, l_b, r_b) in enumerate(ends):
            values = [kept_ref[slot + k, v] for v in range(KEPT)]
            middle_a, middle_b = between(values, (l_a, r_a, l_b, r_b))
            parts += [(l_a, -middle_a, l_b, -middle_b), (middle_a, r_a, middle_b, r_b)]
        ends = parts
    return ends


def prepare_kernel(
    kept,
    tab_ref,
    stratum_ref,
    conc_ref,
    pass_a_ref,
    drop_a_ref,
    pass_b_ref,
    drop_b_ref,
    over_ref,
    source_a_ref,
    source_b_ref,
    flow_ref,
    left_a,
    right_a,
    free_a_ref,
    free_b_ref,
    cross_l_ref,
    cross_r_ref,
    own_2_ref,
    own_3_ref,
    gamma_ref,
    share_ref,
    decay_ref,
):
    n, planes_y, planes_z = stratum_ref.shape
    half = planes_y // 2
    which = half_of(kept)
    rows = pl.ds(pl.multiple_of(which * half, half), half)
    number = Numbers(tab_ref)
    line = lax.broadcasted_iota(jnp.int32, (half, planes_z), 0)
    outer = line == (half - 1) * which
    zero = jnp.zeros((half, planes_z), jnp.float32)
    m = n // PIECES

    def with_border(source, component, i):
        flow = jnp.broadcast_to(flow_ref[component, i : i + 1, :], source.shape)
        return source + jnp.where(outer, flow, 0.0)

    def solve(s, forcing, pass_ref, drop_ref, over, out_ref):
        value, gathered = zero, []
        for j in range(m):
            value = forcing(s * m + j) + (pass_ref[s * m + j] * value if j else 0.0)
            gathered.append(value)
        x = gathered[-1] * over
        for j in reversed(range(m)):
            i = s * m + j
            if j < m - 1:
                x = pass_ref[i + 1] * x + drop_ref[i + 1] * gathered[j]
            out_ref[i] = x

    for i in range(n):
        index = stratum_ref[i, rows, :]
        own_2_ref[i] = number("beta", index) * conc_ref[2, i, rows, :]
        own_3_ref[i] = number("free_b", index) * conc_ref[3, i, rows, :]
        gamma_ref[i] = number("gamma", index)
        share_ref[i] = number("share_b", index)
        decay_ref[i] = number("decay_b", index)
    for s in range(PIECES):
        kappa = {}
        for i in range(s * m, s * m + m):
            kappa[i] = number("kappa", stratum_ref[i, rows, :])
        solve(
            s,
            lambda i: with_border(source_a_ref[i], 0, i),
            pass_a_ref,
            drop_a_ref,
            over_ref[0, s],
            free_a_ref,
        )
        forcings = (
            (lambda i: with_border(source_b_ref[i], 1, i) + kappa[i] * free_a_ref[i], free_b_ref),
            (lambda i: kappa[i] * left_a[i], cross_l_ref),
            (lambda i: kappa[i] * right_a[i], cross_r_ref),
        )
        for forcing, out_ref in forcings:
            solve(s, forcing, pass_b_ref, drop_b_ref, over_ref[1, s], out_ref)


def add_kernel(
    kept,
    kept_ref,
    current_ref,
    free_a_ref,
    free_b_ref,
    cross_l_ref,
    cross_r_ref,
    own_2_ref,
    own_3_ref,
    gamma_ref,
    share_ref,
    decay_ref,
    left_a,
    right_a,
    left_b,
    right_b,
    before_hbm,
    out_hbm,
    made,
    sems,
):
    n, half, planes_z = free_a_ref.shape
    rows = pl.ds(pl.multiple_of(half_of(kept) * half, half), half)
    ends = piece_ends(kept_ref, current_ref)
    m = n // PIECES
    copies = []
    for i in range(n):
        l_a, r_a, l_b, r_b = ends[i // m]
        x0 = free_a_ref[i] + left_a[i] * l_a + right_a[i] * r_a
        x1 = (free_b_ref[i] + cross_l_ref[i] * l_a + cross_r_ref[i] * r_a) + (
            left_b[i] * l_b + right_b[i] * r_b
        )
        x2 = own_2_ref[i] + gamma_ref[i] * x0
        made[0, i], made[1, i], made[2, i] = x0, x1, x2
        made[3, i] = own_3_ref[i] + share_ref[i] * x1 + decay_ref[i] * x2
        copies.append(
            pltpu.make_async_copy(made.at[:, i], out_hbm.at[:, i, rows, :], sems.at[i])
        )
        copies[-1].start()
    for copy in copies:
        copy.wait()


def final_kernel(
    kept,
    tab_ref,
    stratum_ref,
    conc_ref,
    pass_a_ref,
    drop_a_ref,
    pass_b_ref,
    drop_b_ref,
    over_ref,
    source_a_ref,
    source_b_ref,
    kept_ref,
    flow_ref,
    current_ref,
    *refs,
):
    out_hbm, gather_a, gather_b, made, sems = refs[-5:]
    n, planes_y, planes_z = stratum_ref.shape
    half = planes_y // 2
    which = half_of(kept)
    rows = pl.ds(pl.multiple_of(which * half, half), half)
    number = Numbers(tab_ref)
    line = lax.broadcasted_iota(jnp.int32, (half, planes_z), 0)
    outer = line == (half - 1) * which

    def with_border(source, component, i):
        flow = jnp.broadcast_to(flow_ref[component, pl.ds(i, 1), :], source.shape)
        return source + jnp.where(outer, flow, 0.0)

    ends = piece_ends(kept_ref, current_ref)
    pieces = range(PIECES)
    m = n // PIECES
    values = [ends[s][0] for s in pieces]
    for j in range(m):
        for s in pieces:
            i = s * m + j
            values[s] = with_border(source_a_ref[i], 0, i) + values[s]
            if j < m - 1:
                gather_a[i] = values[s]
                values[s] = pass_a_ref[i + 1] * values[s]
    x = [(values[s] + ends[s][1]) * over_ref[0, s] for s in pieces]
    for j in reversed(range(m)):
        for s in pieces:
            i = s * m + j
            if j < m - 1:
                x[s] = pass_a_ref[i + 1] * x[s] + drop_a_ref[i + 1] * gather_a[i]
            made[0, i] = x[s]
    values = [ends[s][2] for s in pieces]
    for j in range(m):
        for s in pieces:
            i = s * m + j
            kappa = number("kappa", stratum_ref[i, rows, :])
            values[s] = with_border(source_b_ref[i], 1, i) + kappa * made[0, i] + values[s]
            if j < m - 1:
                gather_b[i] = values[s]
                values[s] = pass_b_ref[i + 1] * values[s]
    x = [(values[s] + ends[s][3]) * over_ref[1, s] for s in pieces]
    copies = []
    for j in reversed(range(m)):
        for s in pieces:
            i = s * m + j
            if j < m - 1:
                x[s] = pass_b_ref[i + 1] * x[s] + drop_b_ref[i + 1] * gather_b[i]
            made[1, i] = x[s]
            index = stratum_ref[i, rows, :]
            x2 = (
                number("beta", index) * conc_ref[2, i, rows, :]
                + number("gamma", index) * made[0, i]
            )
            made[2, i] = x2
            made[3, i] = (
                number("free_b", index) * conc_ref[3, i, rows, :]
                + number("share_b", index) * x[s]
                + number("decay_b", index) * x2
            )
            copies.append(
                pltpu.make_async_copy(made.at[:, i], out_hbm.at[:, i, rows, :], sems.at[i])
            )
            copies[-1].start()
    for copy in copies:
        copy.wait()


def call(kernel, outs, scratch=()):
    return pl.pallas_call(
        kernel,
        out_shape=[jax.ShapeDtypeStruct(shape, jnp.float32) for shape in outs],
        scratch_shapes=[pltpu.VMEM(shape, jnp.float32) for shape in scratch],
        compiler_params=pltpu.CompilerParams(vmem_limit_bytes=VMEM_LIMIT),
    )


def per_device(
    concentration,
    stratum,
    porosity,
    dispersion_table,
    transverse_table,
    exchange_table,
    decay_table,
):
    n, planes_y, planes_z = stratum.shape
    peers = lax.axis_size("flow")
    half = planes_y // 2
    strides = [1 << k for k in range(peers.bit_length() - 1)]
    cells = (n, planes_y, planes_z)

    halo = (3, n, planes_z)
    strata = porosity.shape[0]
    hbm = pl.BlockSpec(memory_space=pltpu.HBM)
    early, late, table, concentration, stratum = pl.pallas_call(
        pack_kernel,
        out_shape=[
            jax.ShapeDtypeStruct(halo, jnp.float32),
            jax.ShapeDtypeStruct(halo, jnp.float32),
            jax.ShapeDtypeStruct((2 * SUB, LANE), jnp.float32),
            jax.ShapeDtypeStruct(concentration.shape, jnp.float32),
            jax.ShapeDtypeStruct(cells, jnp.int32),
        ],
        in_specs=[hbm] * 7,
        scratch_shapes=[
            pltpu.VMEM((1, strata), jnp.float32),
            pltpu.VMEM((2, strata), jnp.float32),
            pltpu.VMEM((1, strata), jnp.float32),
            pltpu.VMEM((1, strata), jnp.float32),
            pltpu.VMEM((1, strata), jnp.float32),
            pltpu.VMEM((SUB, LANE), jnp.float32),
            pltpu.SemaphoreType.DMA((8,)),
        ],
        compiler_params=pltpu.CompilerParams(vmem_limit_bytes=VMEM_LIMIT),
    )(
        *[
            pltpu.with_memory_space_constraint(value, pltpu.HBM)
            for value in (
                concentration,
                stratum,
                porosity[None],
                dispersion_table.T,
                transverse_table[None],
                exchange_table[None],
                decay_table[None],
            )
        ]
    )
    groups = lax.axis_size("trans")
    def swap(value, start):
        low = range(start, groups - 1, 2)
        pairs = [(i, i + 1) for i in low] + [(i + 1, i) for i in low]
        if start:
            pairs += [(0, groups - 1), (groups - 1, 0)]
        return lax.ppermute(value, "trans", pairs)

    beyond_late = swap(late, 1)
    beyond_early = swap(early, 0)

    def exchange(value, stride):
        return lax.ppermute(value, "flow", [(i, i ^ stride) for i in range(peers)])

    half_cells = (n, half, planes_z)
    block_shape = (QUANTITIES, half, planes_z)

    def local(kept):
        pay, edge, *rest = call(
            functools.partial(local_kernel, kept),
            [
                (PIECES,) + block_shape,
                (6, n, planes_z),
                *[half_cells] * 4,
                (2, PIECES, half, planes_z),
                *[half_cells] * 6,
            ],
            [half_cells] * 5,
        )(table, stratum, concentration)
        pay, parts, flow = call(
            functools.partial(border_kernel, kept),
            [block_shape, (PIECES - 1, KEPT, half, planes_z), (2, n, planes_z)],
        )(table, early, late, beyond_late, beyond_early, edge, pay)
        return pay, rest[:7], rest[7:], parts, flow

    send, sent_rest, sent_responses, sent_parts, sent_flow = local(False)
    block, kept_rest, _, kept_parts, kept_flow = local(True)
    kept = []
    for stride in strides[:-1]:
        other = exchange(send, stride)
        last = stride == strides[-2]
        block, keep, *face = call(
            functools.partial(merge_kernel, stride, last),
            [block_shape, (KEPT, half, planes_z)] + [(5, half, planes_z)] * last,
        )(block, other)
        kept.append(keep)
        send = face[0] if last else block
    prepared = call(functools.partial(prepare_kernel, False), [half_cells] * 9)(
        table, stratum, concentration, *sent_rest, sent_flow, *sent_responses[:2]
    )
    ends_shape = jax.ShapeDtypeStruct((CURRENTS, half, planes_z), jnp.float32)
    vmem = pl.BlockSpec(memory_space=pltpu.VMEM)
    limit = pltpu.CompilerParams(vmem_limit_bytes=VMEM_LIMIT)
    mine, send = pl.pallas_call(
        functools.partial(close_kernel, strides),
        out_shape=[ends_shape, ends_shape],
        in_specs=[pl.BlockSpec(memory_space=pl.ANY)] + [vmem] * (2 + len(kept)),
        compiler_params=limit,
    )(prepared[0], block, exchange(send, strides[-1]), *kept)
    currents = exchange(send, 1)
    whole = jax.ShapeDtypeStruct((4,) + cells, jnp.float32)
    results = [pltpu.VMEM((4,) + half_cells, jnp.float32), pltpu.SemaphoreType.DMA((n,))]
    out = pl.pallas_call(
        functools.partial(final_kernel, True),
        out_shape=whole,
        in_specs=[vmem] * 13,
        out_specs=hbm,
        scratch_shapes=[pltpu.VMEM(half_cells, jnp.float32)] * 2 + results,
        compiler_params=limit,
    )(table, stratum, concentration, *kept_rest, kept_parts, kept_flow, mine)
    return pl.pallas_call(
        functools.partial(add_kernel, False),
        out_shape=whole,
        in_specs=[vmem] * 15 + [hbm],
        out_specs=hbm,
        scratch_shapes=results,
        input_output_aliases={15: 0},
        compiler_params=limit,
    )(sent_parts, currents, *prepared, *sent_responses, out)


def solution(mesh):
    in_specs = (P(None, "flow", "trans", None), P("flow", "trans", None), P(), P(), P(), P(), P())
    out_specs = P(None, "flow", "trans", None)
    return jax.shard_map(
        per_device, mesh=mesh, in_specs=in_specs, out_specs=out_specs, check_vma=False
    )
```

```python
import functools

import jax
import jax.numpy as jnp
from jax import lax
from jax.experimental import pallas as pl
from jax.experimental.pallas import tpu as pltpu
from jax.sharding import PartitionSpec as P

SUB, LANE = 8, 128
ZA_LL, ZA_LR, ZA_RR, ZB_LL, ZB_LR, ZB_RR, C_LL, C_LR, C_RL, C_RR, FA_L, FA_R, FB_L, FB_R = range(14)
QUANTITIES = 14
CURRENTS = 4
KEPT = 8
PIECES = 4
VMEM_LIMIT = 40 * 1024 * 1024


def recip(x):
    return 1.0 / x


def lookup(row, index):
    tiles = []
    for y in range(0, index.shape[0], SUB):
        across = [
            jnp.take_along_axis(
                row, index[y : y + SUB, z : z + LANE], axis=1, mode="promise_in_bounds"
            )
            for z in range(0, index.shape[1], LANE)
        ]
        tiles.append(jnp.concatenate(across, axis=1))
    return jnp.concatenate(tiles, axis=0)


NUMBERS = (
    "por",
    "shunt_a",
    "shunt_b",
    "half_a",
    "half_b",
    "half_t",
    "beta",
    "gamma",
    "alpha_a",
    "alpha_b",
    "kappa",
    "delta",
    "free_b",
    "share_b",
    "decay_b",
)


def derive(por, disp_a, disp_b, trans, exch, decay):
    immobile = 1.0 - por
    over_a = 1.0 / (immobile + exch + decay)
    over_b = 1.0 / (immobile + exch)
    beta = immobile * over_a
    gamma = exch * over_a
    share_b = exch * over_b
    return dict(
        por=por,
        shunt_a=por + decay + exch * (immobile + decay) * over_a,
        shunt_b=por + exch * immobile * over_b,
        half_a=0.5 / disp_a,
        half_b=0.5 / disp_b,
        half_t=0.5 / trans,
        beta=beta,
        gamma=gamma,
        alpha_a=exch * beta,
        alpha_b=share_b * immobile,
        kappa=decay + share_b * decay * gamma,
        delta=share_b * decay * beta,
        free_b=immobile * over_b,
        share_b=share_b,
        decay_b=decay * over_b,
    )


class Numbers:
    def __init__(self, tab_ref):
        self.tab_ref = tab_ref

    def __call__(self, name, index):
        k = NUMBERS.index(name)
        row = jnp.broadcast_to(self.tab_ref[k : k + 1, :], (SUB, LANE))
        return lookup(row, index)


def shifted_difference(value, axis):
    return pltpu.roll(value, value.shape[axis] - 1, axis) - value


def side_of(axis, stride):
    return (lax.axis_index(axis) // stride) % 2 == 1


def pack_kernel(
    conc_hbm,
    stratum_hbm,
    por_hbm,
    disp_hbm,
    trans_hbm,
    exch_hbm,
    decay_hbm,
    early_ref,
    late_ref,
    tab_ref,
    conc_ref,
    stratum_ref,
    por_ref,
    disp_ref,
    trans_ref,
    exch_ref,
    decay_ref,
    raw,
    sems,
):
    moves = [
        (stratum_hbm, stratum_ref),
        (conc_hbm.at[0:2], conc_ref.at[0:2]),
        (por_hbm, por_ref),
        (disp_hbm, disp_ref),
        (trans_hbm, trans_ref),
        (exch_hbm, exch_ref),
        (decay_hbm, decay_ref),
        (conc_hbm.at[2:4], conc_ref.at[2:4]),
    ]
    copies = [pltpu.make_async_copy(src, dst, sems.at[k]) for k, (src, dst) in enumerate(moves)]
    for copy in copies:
        copy.start()
    raw[...] = jnp.full(raw.shape, 0.5, jnp.float32)
    for copy in copies[2:7]:
        copy.wait()
    strata = por_ref.shape[1]
    raw[0:1, 0:strata] = por_ref[...]
    raw[1:3, 0:strata] = disp_ref[...]
    raw[3:4, 0:strata] = trans_ref[...]
    raw[4:5, 0:strata] = exch_ref[...]
    raw[5:6, 0:strata] = decay_ref[...]
    made = derive(*[raw[k : k + 1, :] for k in range(6)])
    for k, name in enumerate(NUMBERS):
        tab_ref[k : k + 1, :] = made[name]
    tab_ref[len(NUMBERS) : 2 * SUB, :] = raw[0 : 2 * SUB - len(NUMBERS), :]
    odd = side_of("trans", 1)
    last = stratum_ref.shape[1] - 1

    def put(k, low, high):
        early_ref[k] = jnp.where(odd, low, high)
        late_ref[k] = jnp.where(odd, high, low)

    copies[0].wait()
    numbered = [(stratum_ref[:, y, :] + 1).astype(jnp.float32) for y in (0, last)]
    put(2, *numbered)
    copies[1].wait()
    for k in (0, 1):
        put(k, conc_ref[k, :, 0, :], conc_ref[k, :, last, :])
    copies[7].wait()


def half_of(kept):
    second = lax.axis_index("flow") % 2
    return second if kept else 1 - second


def local_kernel(
    kept,
    tab_ref,
    stratum_ref,
    conc_ref,
    pay_ref,
    edge_ref,
    pass_a_ref,
    drop_a_ref,
    pass_b_ref,
    drop_b_ref,
    over_ref,
    source_a_ref,
    source_b_ref,
    left_a,
    right_a,
    left_b,
    right_b,
    head_a,
    head_b,
    kappa_ref,
    adj_l,
    adj_r,
):
    n, planes_y, planes_z = stratum_ref.shape
    half = planes_y // 2
    which = half_of(kept)
    rows = pl.ds(pl.multiple_of(which * half, half), half)
    other_rows = pl.ds(pl.multiple_of((1 - which) * half, half), half)
    number = Numbers(tab_ref)

    pieces = range(PIECES)
    m = n // PIECES
    shape = (half, planes_z)
    zero, one = jnp.zeros(shape, jnp.float32), jnp.ones(shape, jnp.float32)

    def from_left(j, carry):
        after = []
        for s, (cond_a, cond_b, half_a, half_b, through_a, through_b) in zip(pieces, carry):
            i = s * m + j
            index = stratum_ref[i, rows, :]
            new_a, new_b = number("half_a", index), number("half_b", index)
            face_a, face_b = half_a + new_a, half_b + new_b
            pass_a, pass_b = recip(1.0 + face_a * cond_a), recip(1.0 + face_b * cond_b)
            cond_a = number("shunt_a", index) + cond_a * pass_a
            cond_b = number("shunt_b", index) + cond_b * pass_b
            through_a, through_b = through_a * pass_a, through_b * pass_b
            kappa_ref[i] = number("kappa", index)
            pass_a_ref[i], pass_b_ref[i] = pass_a, pass_b
            drop_a_ref[i], drop_b_ref[i] = face_a * pass_a, face_b * pass_b
            head_a[i], head_b[i] = through_a, through_b
            after.append((cond_a, cond_b, new_a, new_b, through_a, through_b))
        return after

    start = [(zero, zero, zero, zero, one, one)] * PIECES
    ahead = lax.fori_loop(0, m, from_left, start, unroll=4)
    over_a, over_b = [recip(c[0]) for c in ahead], [recip(c[1]) for c in ahead]
    for s in pieces:
        over_ref[0, s], over_ref[1, s] = over_a[s], over_b[s]

    def from_right(back, carry):
        after = []
        for s, (next_pass, next_drop, next_pass_b, next_drop_b, l_a, r_a, l_b, r_b, *couple) in zip(
            pieces, carry
        ):
            i = s * m + (m - 1 - back)
            l_a = next_pass * l_a + next_drop * head_a[i]
            l_b = next_pass_b * l_b + next_drop_b * head_b[i]
            r_a, r_b = next_pass * r_a, next_pass_b * r_b
            left_a[i], right_a[i], left_b[i], right_b[i] = l_a, r_a, l_b, r_b
            kappa = kappa_ref[i]
            k_l, k_r = kappa * l_a, kappa * r_a
            terms = [l_b * k_l, l_b * k_r, r_b * k_l, r_b * k_r]
            couple = [c + t for c, t in zip(couple, terms)]
            passes = (pass_a_ref[i], drop_a_ref[i], pass_b_ref[i], drop_b_ref[i])
            after.append((*passes, l_a, r_a, l_b, r_b, *couple))
        return after

    responses = lax.fori_loop(
        0,
        m,
        from_right,
        [(one, a, one, b, zero, a, zero, b, zero, zero, zero, zero) for a, b in zip(over_a, over_b)],
        unroll=4,
    )

    def share(j, carry):
        after = []
        for s, (g_l, g_r) in zip(pieces, carry):
            i = s * m + j
            kappa, pass_a = kappa_ref[i], pass_a_ref[i]
            g_l = kappa * left_b[i] + pass_a * g_l
            g_r = kappa * right_b[i] + pass_a * g_r
            adj_l[i], adj_r[i] = g_l, g_r
            after.append((g_l, g_r))
        return after

    lax.fori_loop(0, m, share, [(zero, zero)] * PIECES, unroll=4)

    lane = lax.broadcasted_iota(jnp.int32, shape, 1)
    line = lax.broadcasted_iota(jnp.int32, shape, 0)
    inside = (line < half - 1, lane < planes_z - 1)
    meets = line == (half - 1) * (1 - which)
    shift = jnp.where(which == 0, half - 1, 1)

    def sources(back, carry):
        after = []
        for s, (next_pass, next_drop, w_l, w_r, *free) in zip(pieces, carry):
            i = s * m + (m - 1 - back)
            w_l = next_pass * w_l + next_drop * adj_l[i]
            w_r = next_pass * w_r + next_drop * adj_r[i]
            adj_l[i], adj_r[i] = w_l, w_r
            index = stratum_ref[i, rows, :]
            half_t = number("half_t", index)
            por = number("por", index)
            c0, c1, c2, c3 = [conc_ref[k, i, rows, :] for k in range(4)]
            source_a = por * c0 + number("alpha_a", index) * c2
            source_b = por * c1 + number("alpha_b", index) * c3 + number("delta", index) * c2
            for axis in (0, 1):
                last = half_t.shape[axis] - 1
                face = jnp.where(
                    inside[axis], recip(half_t + pltpu.roll(half_t, last, axis)), 0.0
                )
                flow_a = face * shifted_difference(c0, axis)
                flow_b = face * shifted_difference(c1, axis)
                source_a = source_a + (flow_a - pltpu.roll(flow_a, 1, axis))
                source_b = source_b + (flow_b - pltpu.roll(flow_b, 1, axis))
            beyond_t = pltpu.roll(number("half_t", stratum_ref[i, other_rows, :]), shift, 0)
            face = jnp.where(meets, recip(half_t + beyond_t), 0.0)
            beyond_a = pltpu.roll(conc_ref[0, i, other_rows, :], shift, 0)
            beyond_b = pltpu.roll(conc_ref[1, i, other_rows, :], shift, 0)
            source_a = source_a + face * (beyond_a - c0)
            source_b = source_b + face * (beyond_b - c1)
            source_a_ref[i], source_b_ref[i] = source_a, source_b
            terms = [
                left_a[i] * source_a,
                right_a[i] * source_a,
                left_b[i] * source_b + w_l * source_a,
                right_b[i] * source_b + w_r * source_a,
            ]
            free = [f + t for f, t in zip(free, terms)]
            after.append((pass_a_ref[i], drop_a_ref[i], w_l, w_r, *free))
        return after

    totals = lax.fori_loop(0, m, sources, [(one, a) + (zero,) * 6 for a in over_a], unroll=4)
    for s in pieces:
        l_a, r_a, l_b, r_b, *couple = responses[s][4:]
        first = stratum_ref[s * m, rows, :]
        quantities = [
            l_a + number("half_a", first),
            r_a,
            over_a[s] + ahead[s][2],
            l_b + number("half_b", first),
            r_b,
            over_b[s] + ahead[s][3],
            *couple,
            *totals[s][4:],
        ]
        for q, value in enumerate(quantities):
            pay_ref[s, q] = value
    for k, ref in enumerate((left_a, right_a, left_b, right_b, adj_l, adj_r)):
        edge_ref[k] = jnp.where(which == 0, ref[:, 0, :], ref[:, half - 1, :])


def border_kernel(
    kept,
    tab_ref,
    early_ref,
    late_ref,
    beyond_late_ref,
    beyond_early_ref,
    edge_ref,
    pay_ref,
    out_ref,
    kept_ref,
    flow_ref,
):
    number = Numbers(tab_ref)
    n, planes_z = edge_ref.shape[1:]
    m = n // PIECES
    half = pay_ref.shape[2]
    low = half_of(kept) == 0
    early = side_of("trans", 1) == low
    own = jnp.where(early, early_ref[...], late_ref[...])
    beyond = jnp.where(early, beyond_early_ref[...], beyond_late_ref[...])
    own_id = own[2].astype(jnp.int32) - 1
    next_id = beyond[2].astype(jnp.int32) - 1
    resist = number("half_t", own_id) + number("half_t", next_id)
    end = jnp.where(low, 0, lax.axis_size("trans") - 1)
    face = jnp.where(lax.axis_index("trans") != end, recip(resist), 0.0)
    flow_a = face * (beyond[0] - own[0])
    flow_b = face * (beyond[1] - own[1])
    flow_ref[0], flow_ref[1] = flow_a, flow_b
    l_a, r_a, l_b, r_b, w_l, w_r = [edge_ref[k] for k in range(6)]
    changes = {
        FA_L: l_a * flow_a,
        FA_R: r_a * flow_a,
        FB_L: l_b * flow_b + w_l * flow_a,
        FB_R: r_b * flow_b + w_r * flow_a,
    }
    line = lax.broadcasted_iota(jnp.int32, (half, planes_z), 0)
    outer = line == jnp.where(low, 0, half - 1)
    blocks = []
    for s in range(PIECES):
        values = {q: pay_ref[s, q] for q in range(QUANTITIES)}
        for q, change in changes.items():
            total = jnp.sum(change[s * m : (s + 1) * m], axis=0, keepdims=True)
            values[q] = values[q] + jnp.where(outer, total, 0.0)
        blocks.append(values)
    slot = 0
    while len(blocks) > 1:
        joined = []
        for one, two in zip(blocks[::2], blocks[1::2]):
            merged, parts = merge(one, two)
            for k, value in enumerate(parts):
                kept_ref[slot, k] = value
            slot += 1
            joined.append(merged)
        blocks = joined
    for q in range(QUANTITIES):
        out_ref[q] = blocks[0][q]


FACE_L = (ZA_LL, ZB_LL, C_LL, FA_L, FB_L)
FACE_R = (ZA_RR, ZB_RR, C_RR, FA_R, FB_R)


def merge(one, two):
    over_a = recip(one[ZA_RR] + two[ZA_LL])
    over_b = recip(one[ZB_RR] + two[ZB_LL])
    across = one[C_RR] + two[C_LL]
    free_a = over_a * (one[FA_R] - two[FA_L])
    from_l, from_r = over_a * one[ZA_LR], over_a * two[ZA_LR]
    free_b = over_b * (one[FB_R] - two[FB_L] - across * free_a)
    from_l_b, from_r_b = over_b * one[ZB_LR], over_b * two[ZB_LR]
    cross_l = over_b * (one[C_RL] - across * from_l)
    cross_r = over_b * (two[C_LR] - across * from_r)
    merged = {
        ZA_LL: one[ZA_LL] - one[ZA_LR] * from_l,
        ZA_LR: one[ZA_LR] * from_r,
        ZA_RR: two[ZA_RR] - two[ZA_LR] * from_r,
        ZB_LL: one[ZB_LL] - one[ZB_LR] * from_l_b,
        ZB_LR: one[ZB_LR] * from_r_b,
        ZB_RR: two[ZB_RR] - two[ZB_LR] * from_r_b,
        C_LL: one[C_LL] - one[ZB_LR] * cross_l - one[C_LR] * from_l,
        C_LR: one[ZB_LR] * cross_r + one[C_LR] * from_r,
        C_RL: two[ZB_LR] * cross_l + two[C_RL] * from_l,
        C_RR: two[C_RR] - two[ZB_LR] * cross_r - two[C_RL] * from_r,
        FA_L: one[FA_L] - one[ZA_LR] * free_a,
        FA_R: two[FA_R] + two[ZA_LR] * free_a,
        FB_L: one[FB_L] - one[ZB_LR] * free_b - one[C_LR] * free_a,
        FB_R: two[FB_R] + two[ZB_LR] * free_b + two[C_RL] * free_a,
    }
    return merged, (free_a, from_l, from_r, free_b, from_l_b, from_r_b, cross_l, cross_r)


def between(kept, ends):
    free_a, from_l, from_r, free_b, from_l_b, from_r_b, cross_l, cross_r = kept
    l_a, r_a, l_b, r_b = ends
    middle_a = free_a + from_l * l_a - from_r * r_a
    middle_b = free_b + from_l_b * l_b - from_r_b * r_b + cross_l * l_a - cross_r * r_a
    return middle_a, middle_b


def merge_kernel(stride, last, own_ref, other_ref, out_ref, kept_ref, *face_ref):
    second = side_of("flow", stride)
    own = [own_ref[q] for q in range(QUANTITIES)]
    other = [other_ref[q] for q in range(QUANTITIES)]
    one = [jnp.where(second, b, a) for a, b in zip(own, other)]
    two = [jnp.where(second, a, b) for a, b in zip(own, other)]
    merged, kept = merge(one, two)
    for q, value in merged.items():
        out_ref[q] = value
    for k, value in enumerate(kept):
        kept_ref[k] = value
    if last:
        after = side_of("flow", 2 * stride)
        for k, (l, r) in enumerate(zip(FACE_L, FACE_R)):
            face_ref[0][k] = jnp.where(after, merged[l], merged[r])


def close_kernel(strides, ready_ref, own_ref, other_ref, *refs):
    kept_refs, mine_ref, send_ref = refs[:-2], refs[-2], refs[-1]
    stride = strides[-1]
    second = side_of("flow", stride)
    own = [jnp.where(second, own_ref[l], own_ref[r]) for l, r in zip(FACE_L, FACE_R)]
    z_a, z_b, couple, f_a, f_b = [own[k] + other_ref[k] for k in range(3)] + [
        jnp.where(second, other_ref[k] - own[k], own[k] - other_ref[k]) for k in (3, 4)
    ]
    current_a = recip(z_a) * f_a
    current_b = recip(z_b) * (f_b - couple * current_a)
    nothing = jnp.zeros_like(current_a)

    def side_ends(after, middle_a, middle_b, ends):
        l_a, r_a, l_b, r_b = ends
        return (
            jnp.where(after, middle_a, l_a),
            jnp.where(after, r_a, -middle_a),
            jnp.where(after, middle_b, l_b),
            jnp.where(after, r_b, -middle_b),
        )

    ends = side_ends(second, current_a, current_b, (nothing,) * 4)
    for stride, kept_ref in reversed(list(zip(strides[:-1], kept_refs))):
        middle_a, middle_b = between([kept_ref[k] for k in range(KEPT)], ends)
        after = side_of("flow", stride)
        if stride == 1:
            other_ends = side_ends(jnp.logical_not(after), middle_a, middle_b, ends)
            for q, value in enumerate(other_ends):
                send_ref[q] = value
        ends = side_ends(after, middle_a, middle_b, ends)
    for q, value in enumerate(ends):
        mine_ref[q] = value


def piece_ends(kept_ref, current_ref):
    ends = [tuple(current_ref[q] for q in range(CURRENTS))]
    slot = PIECES - 1
    while len(ends) < PIECES:
        slot -= len(ends)
        parts = []
        for k, (l_a, r_a, l_b, r_b) in enumerate(ends):
            values = [kept_ref[slot + k, v] for v in range(KEPT)]
            middle_a, middle_b = between(values, (l_a, r_a, l_b, r_b))
            parts += [(l_a, -middle_a, l_b, -middle_b), (middle_a, r_a, middle_b, r_b)]
        ends = parts
    return ends


def prepare_kernel(
    kept,
    tab_ref,
    stratum_ref,
    conc_ref,
    pass_a_ref,
    drop_a_ref,
    pass_b_ref,
    drop_b_ref,
    over_ref,
    source_a_ref,
    source_b_ref,
    flow_ref,
    left_a,
    right_a,
    free_a_ref,
    free_b_ref,
    cross_l_ref,
    cross_r_ref,
    own_2_ref,
    own_3_ref,
    gamma_ref,
    share_ref,
    decay_ref,
):
    n, planes_y, planes_z = stratum_ref.shape
    half = planes_y // 2
    which = half_of(kept)
    rows = pl.ds(pl.multiple_of(which * half, half), half)
    number = Numbers(tab_ref)
    line = lax.broadcasted_iota(jnp.int32, (half, planes_z), 0)
    outer = line == (half - 1) * which
    zero = jnp.zeros((half, planes_z), jnp.float32)
    m = n // PIECES

    def with_border(source, component, i):
        flow = jnp.broadcast_to(flow_ref[component, i : i + 1, :], source.shape)
        return source + jnp.where(outer, flow, 0.0)

    def solve(s, forcing, pass_ref, drop_ref, over, out_ref):
        value, gathered = zero, []
        for j in range(m):
            value = forcing(s * m + j) + (pass_ref[s * m + j] * value if j else 0.0)
            gathered.append(value)
        x = gathered[-1] * over
        for j in reversed(range(m)):
            i = s * m + j
            if j < m - 1:
                x = pass_ref[i + 1] * x + drop_ref[i + 1] * gathered[j]
            out_ref[i] = x

    for i in range(n):
        index = stratum_ref[i, rows, :]
        own_2_ref[i] = number("beta", index) * conc_ref[2, i, rows, :]
        own_3_ref[i] = number("free_b", index) * conc_ref[3, i, rows, :]
        gamma_ref[i] = number("gamma", index)
        share_ref[i] = number("share_b", index)
        decay_ref[i] = number("decay_b", index)
    for s in range(PIECES):
        kappa = {}
        for i in range(s * m, s * m + m):
            kappa[i] = number("kappa", stratum_ref[i, rows, :])
        solve(
            s,
            lambda i: with_border(source_a_ref[i], 0, i),
            pass_a_ref,
            drop_a_ref,
            over_ref[0, s],
            free_a_ref,
        )
        forcings = (
            (lambda i: with_border(source_b_ref[i], 1, i) + kappa[i] * free_a_ref[i], free_b_ref),
            (lambda i: kappa[i] * left_a[i], cross_l_ref),
            (lambda i: kappa[i] * right_a[i], cross_r_ref),
        )
        for forcing, out_ref in forcings:
            solve(s, forcing, pass_b_ref, drop_b_ref, over_ref[1, s], out_ref)


def add_kernel(
    kept,
    kept_ref,
    current_ref,
    free_a_ref,
    free_b_ref,
    cross_l_ref,
    cross_r_ref,
    own_2_ref,
    own_3_ref,
    gamma_ref,
    share_ref,
    decay_ref,
    left_a,
    right_a,
    left_b,
    right_b,
    before_hbm,
    out_hbm,
    made,
    sems,
):
    n, half, planes_z = free_a_ref.shape
    rows = pl.ds(pl.multiple_of(half_of(kept) * half, half), half)
    ends = piece_ends(kept_ref, current_ref)
    m = n // PIECES
    copies = []
    for i in range(n):
        l_a, r_a, l_b, r_b = ends[i // m]
        x0 = free_a_ref[i] + left_a[i] * l_a + right_a[i] * r_a
        x1 = (free_b_ref[i] + cross_l_ref[i] * l_a + cross_r_ref[i] * r_a) + (
            left_b[i] * l_b + right_b[i] * r_b
        )
        x2 = own_2_ref[i] + gamma_ref[i] * x0
        made[0, i], made[1, i], made[2, i] = x0, x1, x2
        made[3, i] = own_3_ref[i] + share_ref[i] * x1 + decay_ref[i] * x2
        copies.append(
            pltpu.make_async_copy(made.at[:, i], out_hbm.at[:, i, rows, :], sems.at[i])
        )
        copies[-1].start()
    for copy in copies:
        copy.wait()


def final_kernel(
    kept,
    tab_ref,
    stratum_ref,
    conc_ref,
    pass_a_ref,
    drop_a_ref,
    pass_b_ref,
    drop_b_ref,
    over_ref,
    source_a_ref,
    source_b_ref,
    kept_ref,
    flow_ref,
    current_ref,
    *refs,
):
    out_hbm, gather_a, gather_b, made, sems = refs[-5:]
    n, planes_y, planes_z = stratum_ref.shape
    half = planes_y // 2
    which = half_of(kept)
    rows = pl.ds(pl.multiple_of(which * half, half), half)
    number = Numbers(tab_ref)
    line = lax.broadcasted_iota(jnp.int32, (half, planes_z), 0)
    outer = line == (half - 1) * which

    def with_border(source, component, i):
        flow = jnp.broadcast_to(flow_ref[component, pl.ds(i, 1), :], source.shape)
        return source + jnp.where(outer, flow, 0.0)

    ends = piece_ends(kept_ref, current_ref)
    pieces = range(PIECES)
    m = n // PIECES
    values = [ends[s][0] for s in pieces]
    for j in range(m):
        for s in pieces:
            i = s * m + j
            values[s] = with_border(source_a_ref[i], 0, i) + values[s]
            if j < m - 1:
                gather_a[i] = values[s]
                values[s] = pass_a_ref[i + 1] * values[s]
    x = [(values[s] + ends[s][1]) * over_ref[0, s] for s in pieces]
    for j in reversed(range(m)):
        for s in pieces:
            i = s * m + j
            if j < m - 1:
                x[s] = pass_a_ref[i + 1] * x[s] + drop_a_ref[i + 1] * gather_a[i]
            made[0, i] = x[s]
    values = [ends[s][2] for s in pieces]
    for j in range(m):
        for s in pieces:
            i = s * m + j
            kappa = number("kappa", stratum_ref[i, rows, :])
            values[s] = with_border(source_b_ref[i], 1, i) + kappa * made[0, i] + values[s]
            if j < m - 1:
                gather_b[i] = values[s]
                values[s] = pass_b_ref[i + 1] * values[s]
    x = [(values[s] + ends[s][3]) * over_ref[1, s] for s in pieces]
    copies = []
    for j in reversed(range(m)):
        for s in pieces:
            i = s * m + j
            if j < m - 1:
                x[s] = pass_b_ref[i + 1] * x[s] + drop_b_ref[i + 1] * gather_b[i]
            made[1, i] = x[s]
            index = stratum_ref[i, rows, :]
            x2 = (
                number("beta", index) * conc_ref[2, i, rows, :]
                + number("gamma", index) * made[0, i]
            )
            made[2, i] = x2
            made[3, i] = (
                number("free_b", index) * conc_ref[3, i, rows, :]
                + number("share_b", index) * x[s]
                + number("decay_b", index) * x2
            )
            copies.append(
                pltpu.make_async_copy(made.at[:, i], out_hbm.at[:, i, rows, :], sems.at[i])
            )
            copies[-1].start()
    for copy in copies:
        copy.wait()


def call(kernel, outs, scratch=()):
    return pl.pallas_call(
        kernel,
        out_shape=[jax.ShapeDtypeStruct(shape, jnp.float32) for shape in outs],
        scratch_shapes=[pltpu.VMEM(shape, jnp.float32) for shape in scratch],
        compiler_params=pltpu.CompilerParams(vmem_limit_bytes=VMEM_LIMIT),
    )


def per_device(
    concentration,
    stratum,
    porosity,
    dispersion_table,
    transverse_table,
    exchange_table,
    decay_table,
):
    n, planes_y, planes_z = stratum.shape
    peers = lax.axis_size("flow")
    half = planes_y // 2
    strides = [1 << k for k in range(peers.bit_length() - 1)]
    cells = (n, planes_y, planes_z)

    halo = (3, n, planes_z)
    strata = porosity.shape[0]
    hbm = pl.BlockSpec(memory_space=pltpu.HBM)
    early, late, table, concentration, stratum = pl.pallas_call(
        pack_kernel,
        out_shape=[
            jax.ShapeDtypeStruct(halo, jnp.float32),
            jax.ShapeDtypeStruct(halo, jnp.float32),
            jax.ShapeDtypeStruct((2 * SUB, LANE), jnp.float32),
            jax.ShapeDtypeStruct(concentration.shape, jnp.float32),
            jax.ShapeDtypeStruct(cells, jnp.int32),
        ],
        in_specs=[hbm] * 7,
        scratch_shapes=[
            pltpu.VMEM((1, strata), jnp.float32),
            pltpu.VMEM((2, strata), jnp.float32),
            pltpu.VMEM((1, strata), jnp.float32),
            pltpu.VMEM((1, strata), jnp.float32),
            pltpu.VMEM((1, strata), jnp.float32),
            pltpu.VMEM((SUB, LANE), jnp.float32),
            pltpu.SemaphoreType.DMA((8,)),
        ],
        compiler_params=pltpu.CompilerParams(vmem_limit_bytes=VMEM_LIMIT),
    )(
        *[
            pltpu.with_memory_space_constraint(value, pltpu.HBM)
            for value in (
                concentration,
                stratum,
                porosity[None],
                dispersion_table.T,
                transverse_table[None],
                exchange_table[None],
                decay_table[None],
            )
        ]
    )
    groups = lax.axis_size("trans")
    def swap(value, start):
        low = range(start, groups - 1, 2)
        pairs = [(i, i + 1) for i in low] + [(i + 1, i) for i in low]
        if start:
            pairs += [(0, groups - 1), (groups - 1, 0)]
        return lax.ppermute(value, "trans", pairs)

    beyond_late = swap(late, 1)
    beyond_early = swap(early, 0)

    def exchange(value, stride):
        return lax.ppermute(value, "flow", [(i, i ^ stride) for i in range(peers)])

    half_cells = (n, half, planes_z)
    block_shape = (QUANTITIES, half, planes_z)

    def local(kept):
        pay, edge, *rest = call(
            functools.partial(local_kernel, kept),
            [
                (PIECES,) + block_shape,
                (6, n, planes_z),
                *[half_cells] * 4,
                (2, PIECES, half, planes_z),
                *[half_cells] * 6,
            ],
            [half_cells] * 5,
        )(table, stratum, concentration)
        pay, parts, flow = call(
            functools.partial(border_kernel, kept),
            [block_shape, (PIECES - 1, KEPT, half, planes_z), (2, n, planes_z)],
        )(table, early, late, beyond_late, beyond_early, edge, pay)
        return pay, rest[:7], rest[7:], parts, flow

    send, sent_rest, sent_responses, sent_parts, sent_flow = local(False)
    block, kept_rest, _, kept_parts, kept_flow = local(True)
    kept = []
    for stride in strides[:-1]:
        other = exchange(send, stride)
        last = stride == strides[-2]
        block, keep, *face = call(
            functools.partial(merge_kernel, stride, last),
            [block_shape, (KEPT, half, planes_z)] + [(5, half, planes_z)] * last,
        )(block, other)
        kept.append(keep)
        send = face[0] if last else block
    prepared = call(functools.partial(prepare_kernel, False), [half_cells] * 9)(
        table, stratum, concentration, *sent_rest, sent_flow, *sent_responses[:2]
    )
    ends_shape = jax.ShapeDtypeStruct((CURRENTS, half, planes_z), jnp.float32)
    vmem = pl.BlockSpec(memory_space=pltpu.VMEM)
    limit = pltpu.CompilerParams(vmem_limit_bytes=VMEM_LIMIT)
    mine, send = pl.pallas_call(
        functools.partial(close_kernel, strides),
        out_shape=[ends_shape, ends_shape],
        in_specs=[pl.BlockSpec(memory_space=pl.ANY)] + [vmem] * (2 + len(kept)),
        compiler_params=limit,
    )(prepared[0], block, exchange(send, strides[-1]), *kept)
    currents = exchange(send, 1)
    whole = jax.ShapeDtypeStruct((4,) + cells, jnp.float32)
    results = [pltpu.VMEM((4,) + half_cells, jnp.float32), pltpu.SemaphoreType.DMA((n,))]
    out = pl.pallas_call(
        functools.partial(final_kernel, True),
        out_shape=whole,
        in_specs=[vmem] * 13,
        out_specs=hbm,
        scratch_shapes=[pltpu.VMEM(half_cells, jnp.float32)] * 2 + results,
        compiler_params=limit,
    )(table, stratum, concentration, *kept_rest, kept_parts, kept_flow, mine)
    return pl.pallas_call(
        functools.partial(add_kernel, False),
        out_shape=whole,
        in_specs=[vmem] * 15 + [hbm],
        out_specs=hbm,
        scratch_shapes=results,
        input_output_aliases={15: 0},
        compiler_params=limit,
    )(sent_parts, currents, *prepared, *sent_responses, out)


def solution(mesh):
    in_specs = (P(None, "flow", "trans", None), P("flow", "trans", None), P(), P(), P(), P(), P())
    out_specs = P(None, "flow", "trans", None)
    return jax.shard_map(
        per_device, mesh=mesh, in_specs=in_specs, out_specs=out_specs, check_vma=False
    )
```

```python
import functools

import jax
import jax.numpy as jnp
from jax import lax
from jax.experimental import pallas as pl
from jax.experimental.pallas import tpu as pltpu
from jax.sharding import PartitionSpec as P

SUB, LANE = 8, 128
ZA_LL, ZA_LR, ZA_RR, ZB_LL, ZB_LR, ZB_RR, C_LL, C_LR, C_RL, C_RR, FA_L, FA_R, FB_L, FB_R = range(14)
QUANTITIES = 14
CURRENTS = 4
KEPT = 8
PIECES = 2
VMEM_LIMIT = 40 * 1024 * 1024


def recip(x):
    return 1.0 / x


def lookup(row, index):
    tiles = []
    for y in range(0, index.shape[0], SUB):
        across = [
            jnp.take_along_axis(
                row, index[y : y + SUB, z : z + LANE], axis=1, mode="promise_in_bounds"
            )
            for z in range(0, index.shape[1], LANE)
        ]
        tiles.append(jnp.concatenate(across, axis=1))
    return jnp.concatenate(tiles, axis=0)


NUMBERS = (
    "por",
    "shunt_a",
    "shunt_b",
    "half_a",
    "half_b",
    "half_t",
    "beta",
    "gamma",
    "alpha_a",
    "alpha_b",
    "kappa",
    "delta",
    "free_b",
    "share_b",
    "decay_b",
)


def derive(por, disp_a, disp_b, trans, exch, decay):
    immobile = 1.0 - por
    over_a = 1.0 / (immobile + exch + decay)
    over_b = 1.0 / (immobile + exch)
    beta = immobile * over_a
    gamma = exch * over_a
    share_b = exch * over_b
    return dict(
        por=por,
        shunt_a=por + decay + exch * (immobile + decay) * over_a,
        shunt_b=por + exch * immobile * over_b,
        half_a=0.5 / disp_a,
        half_b=0.5 / disp_b,
        half_t=0.5 / trans,
        beta=beta,
        gamma=gamma,
        alpha_a=exch * beta,
        alpha_b=share_b * immobile,
        kappa=decay + share_b * decay * gamma,
        delta=share_b * decay * beta,
        free_b=immobile * over_b,
        share_b=share_b,
        decay_b=decay * over_b,
    )


class Numbers:
    def __init__(self, tab_ref):
        self.tab_ref = tab_ref

    def __call__(self, name, index):
        k = NUMBERS.index(name)
        row = jnp.broadcast_to(self.tab_ref[k : k + 1, :], (SUB, LANE))
        return lookup(row, index)


def shifted_difference(value, axis):
    return pltpu.roll(value, value.shape[axis] - 1, axis) - value


def side_of(axis, stride):
    return (lax.axis_index(axis) // stride) % 2 == 1


def pack_kernel(
    conc_hbm,
    stratum_hbm,
    por_hbm,
    disp_hbm,
    trans_hbm,
    exch_hbm,
    decay_hbm,
    early_ref,
    late_ref,
    tab_ref,
    conc_ref,
    stratum_ref,
    por_ref,
    disp_ref,
    trans_ref,
    exch_ref,
    decay_ref,
    raw,
    sems,
):
    moves = [
        (stratum_hbm, stratum_ref),
        (conc_hbm.at[0:2], conc_ref.at[0:2]),
        (por_hbm, por_ref),
        (disp_hbm, disp_ref),
        (trans_hbm, trans_ref),
        (exch_hbm, exch_ref),
        (decay_hbm, decay_ref),
        (conc_hbm.at[2:4], conc_ref.at[2:4]),
    ]
    copies = [pltpu.make_async_copy(src, dst, sems.at[k]) for k, (src, dst) in enumerate(moves)]
    for copy in copies:
        copy.start()
    raw[...] = jnp.full(raw.shape, 0.5, jnp.float32)
    for copy in copies[2:7]:
        copy.wait()
    strata = por_ref.shape[1]
    raw[0:1, 0:strata] = por_ref[...]
    raw[1:3, 0:strata] = disp_ref[...]
    raw[3:4, 0:strata] = trans_ref[...]
    raw[4:5, 0:strata] = exch_ref[...]
    raw[5:6, 0:strata] = decay_ref[...]
    made = derive(*[raw[k : k + 1, :] for k in range(6)])
    for k, name in enumerate(NUMBERS):
        tab_ref[k : k + 1, :] = made[name]
    tab_ref[len(NUMBERS) : 2 * SUB, :] = raw[0 : 2 * SUB - len(NUMBERS), :]
    odd = side_of("trans", 1)
    last = stratum_ref.shape[1] - 1

    def put(k, low, high):
        early_ref[k] = jnp.where(odd, low, high)
        late_ref[k] = jnp.where(odd, high, low)

    copies[0].wait()
    numbered = [(stratum_ref[:, y, :] + 1).astype(jnp.float32) for y in (0, last)]
    put(2, *numbered)
    copies[1].wait()
    for k in (0, 1):
        put(k, conc_ref[k, :, 0, :], conc_ref[k, :, last, :])
    copies[7].wait()


def half_of(kept):
    second = lax.axis_index("flow") % 2
    return second if kept else 1 - second


def local_kernel(
    kept,
    tab_ref,
    stratum_ref,
    conc_ref,
    pay_ref,
    edge_ref,
    pass_a_ref,
    drop_a_ref,
    pass_b_ref,
    drop_b_ref,
    over_ref,
    source_a_ref,
    source_b_ref,
    left_a,
    right_a,
    left_b,
    right_b,
    head_a,
    head_b,
    kappa_ref,
    adj_l,
    adj_r,
):
    n, planes_y, planes_z = stratum_ref.shape
    half = planes_y // 2
    which = half_of(kept)
    rows = pl.ds(pl.multiple_of(which * half, half), half)
    other_rows = pl.ds(pl.multiple_of((1 - which) * half, half), half)
    number = Numbers(tab_ref)

    pieces = range(PIECES)
    m = n // PIECES
    shape = (half, planes_z)
    zero, one = jnp.zeros(shape, jnp.float32), jnp.ones(shape, jnp.float32)

    def from_left(j, carry):
        after = []
        for s, (cond_a, cond_b, half_a, half_b, through_a, through_b) in zip(pieces, carry):
            i = s * m + j
            index = stratum_ref[i, rows, :]
            new_a, new_b = number("half_a", index), number("half_b", index)
            face_a, face_b = half_a + new_a, half_b + new_b
            pass_a, pass_b = recip(1.0 + face_a * cond_a), recip(1.0 + face_b * cond_b)
            cond_a = number("shunt_a", index) + cond_a * pass_a
            cond_b = number("shunt_b", index) + cond_b * pass_b
            through_a, through_b = through_a * pass_a, through_b * pass_b
            kappa_ref[i] = number("kappa", index)
            pass_a_ref[i], pass_b_ref[i] = pass_a, pass_b
            drop_a_ref[i], drop_b_ref[i] = face_a * pass_a, face_b * pass_b
            head_a[i], head_b[i] = through_a, through_b
            after.append((cond_a, cond_b, new_a, new_b, through_a, through_b))
        return after

    start = [(zero, zero, zero, zero, one, one)] * PIECES
    ahead = lax.fori_loop(0, m, from_left, start, unroll=2)
    over_a, over_b = [recip(c[0]) for c in ahead], [recip(c[1]) for c in ahead]
    for s in pieces:
        over_ref[0, s], over_ref[1, s] = over_a[s], over_b[s]

    def from_right(back, carry):
        after = []
        for s, (next_pass, next_drop, next_pass_b, next_drop_b, l_a, r_a, l_b, r_b, *couple) in zip(
            pieces, carry
        ):
            i = s * m + (m - 1 - back)
            l_a = next_pass * l_a + next_drop * head_a[i]
            l_b = next_pass_b * l_b + next_drop_b * head_b[i]
            r_a, r_b = next_pass * r_a, next_pass_b * r_b
            left_a[i], right_a[i], left_b[i], right_b[i] = l_a, r_a, l_b, r_b
            kappa = kappa_ref[i]
            k_l, k_r = kappa * l_a, kappa * r_a
            terms = [l_b * k_l, l_b * k_r, r_b * k_l, r_b * k_r]
            couple = [c + t for c, t in zip(couple, terms)]
            passes = (pass_a_ref[i], drop_a_ref[i], pass_b_ref[i], drop_b_ref[i])
            after.append((*passes, l_a, r_a, l_b, r_b, *couple))
        return after

    responses = lax.fori_loop(
        0,
        m,
        from_right,
        [(one, a, one, b, zero, a, zero, b, zero, zero, zero, zero) for a, b in zip(over_a, over_b)],
        unroll=2,
    )

    def share(j, carry):
        after = []
        for s, (g_l, g_r) in zip(pieces, carry):
            i = s * m + j
            kappa, pass_a = kappa_ref[i], pass_a_ref[i]
            g_l = kappa * left_b[i] + pass_a * g_l
            g_r = kappa * right_b[i] + pass_a * g_r
            adj_l[i], adj_r[i] = g_l, g_r
            after.append((g_l, g_r))
        return after

    lax.fori_loop(0, m, share, [(zero, zero)] * PIECES, unroll=2)

    lane = lax.broadcasted_iota(jnp.int32, shape, 1)
    line = lax.broadcasted_iota(jnp.int32, shape, 0)
    inside = (line < half - 1, lane < planes_z - 1)
    meets = line == (half - 1) * (1 - which)
    shift = jnp.where(which == 0, half - 1, 1)

    def sources(back, carry):
        after = []
        for s, (next_pass, next_drop, w_l, w_r, *free) in zip(pieces, carry):
            i = s * m + (m - 1 - back)
            w_l = next_pass * w_l + next_drop * adj_l[i]
            w_r = next_pass * w_r + next_drop * adj_r[i]
            adj_l[i], adj_r[i] = w_l, w_r
            index = stratum_ref[i, rows, :]
            half_t = number("half_t", index)
            por = number("por", index)
            c0, c1, c2, c3 = [conc_ref[k, i, rows, :] for k in range(4)]
            source_a = por * c0 + number("alpha_a", index) * c2
            source_b = por * c1 + number("alpha_b", index) * c3 + number("delta", index) * c2
            for axis in (0, 1):
                last = half_t.shape[axis] - 1
                face = jnp.where(
                    inside[axis], recip(half_t + pltpu.roll(half_t, last, axis)), 0.0
                )
                flow_a = face * shifted_difference(c0, axis)
                flow_b = face * shifted_difference(c1, axis)
                source_a = source_a + (flow_a - pltpu.roll(flow_a, 1, axis))
                source_b = source_b + (flow_b - pltpu.roll(flow_b, 1, axis))
            beyond_t = pltpu.roll(number("half_t", stratum_ref[i, other_rows, :]), shift, 0)
            face = jnp.where(meets, recip(half_t + beyond_t), 0.0)
            beyond_a = pltpu.roll(conc_ref[0, i, other_rows, :], shift, 0)
            beyond_b = pltpu.roll(conc_ref[1, i, other_rows, :], shift, 0)
            source_a = source_a + face * (beyond_a - c0)
            source_b = source_b + face * (beyond_b - c1)
            source_a_ref[i], source_b_ref[i] = source_a, source_b
            terms = [
                left_a[i] * source_a,
                right_a[i] * source_a,
                left_b[i] * source_b + w_l * source_a,
                right_b[i] * source_b + w_r * source_a,
            ]
            free = [f + t for f, t in zip(free, terms)]
            after.append((pass_a_ref[i], drop_a_ref[i], w_l, w_r, *free))
        return after

    totals = lax.fori_loop(0, m, sources, [(one, a) + (zero,) * 6 for a in over_a], unroll=2)
    for s in pieces:
        l_a, r_a, l_b, r_b, *couple = responses[s][4:]
        first = stratum_ref[s * m, rows, :]
        quantities = [
            l_a + number("half_a", first),
            r_a,
            over_a[s] + ahead[s][2],
            l_b + number("half_b", first),
            r_b,
            over_b[s] + ahead[s][3],
            *couple,
            *totals[s][4:],
        ]
        for q, value in enumerate(quantities):
            pay_ref[s, q] = value
    for k, ref in enumerate((left_a, right_a, left_b, right_b, adj_l, adj_r)):
        edge_ref[k] = jnp.where(which == 0, ref[:, 0, :], ref[:, half - 1, :])


def border_kernel(
    kept,
    tab_ref,
    early_ref,
    late_ref,
    beyond_late_ref,
    beyond_early_ref,
    edge_ref,
    pay_ref,
    out_ref,
    kept_ref,
    flow_ref,
):
    number = Numbers(tab_ref)
    n, planes_z = edge_ref.shape[1:]
    m = n // PIECES
    half = pay_ref.shape[2]
    low = half_of(kept) == 0
    early = side_of("trans", 1) == low
    own = jnp.where(early, early_ref[...], late_ref[...])
    beyond = jnp.where(early, beyond_early_ref[...], beyond_late_ref[...])
    own_id = own[2].astype(jnp.int32) - 1
    next_id = beyond[2].astype(jnp.int32) - 1
    resist = number("half_t", own_id) + number("half_t", next_id)
    end = jnp.where(low, 0, lax.axis_size("trans") - 1)
    face = jnp.where(lax.axis_index("trans") != end, recip(resist), 0.0)
    flow_a = face * (beyond[0] - own[0])
    flow_b = face * (beyond[1] - own[1])
    flow_ref[0], flow_ref[1] = flow_a, flow_b
    l_a, r_a, l_b, r_b, w_l, w_r = [edge_ref[k] for k in range(6)]
    changes = {
        FA_L: l_a * flow_a,
        FA_R: r_a * flow_a,
        FB_L: l_b * flow_b + w_l * flow_a,
        FB_R: r_b * flow_b + w_r * flow_a,
    }
    line = lax.broadcasted_iota(jnp.int32, (half, planes_z), 0)
    outer = line == jnp.where(low, 0, half - 1)
    blocks = []
    for s in range(PIECES):
        values = {q: pay_ref[s, q] for q in range(QUANTITIES)}
        for q, change in changes.items():
            total = jnp.sum(change[s * m : (s + 1) * m], axis=0, keepdims=True)
            values[q] = values[q] + jnp.where(outer, total, 0.0)
        blocks.append(values)
    slot = 0
    while len(blocks) > 1:
        joined = []
        for one, two in zip(blocks[::2], blocks[1::2]):
            merged, parts = merge(one, two)
            for k, value in enumerate(parts):
                kept_ref[slot, k] = value
            slot += 1
            joined.append(merged)
        blocks = joined
    for q in range(QUANTITIES):
        out_ref[q] = blocks[0][q]


FACE_L = (ZA_LL, ZB_LL, C_LL, FA_L, FB_L)
FACE_R = (ZA_RR, ZB_RR, C_RR, FA_R, FB_R)


def merge(one, two):
    over_a = recip(one[ZA_RR] + two[ZA_LL])
    over_b = recip(one[ZB_RR] + two[ZB_LL])
    across = one[C_RR] + two[C_LL]
    free_a = over_a * (one[FA_R] - two[FA_L])
    from_l, from_r = over_a * one[ZA_LR], over_a * two[ZA_LR]
    free_b = over_b * (one[FB_R] - two[FB_L] - across * free_a)
    from_l_b, from_r_b = over_b * one[ZB_LR], over_b * two[ZB_LR]
    cross_l = over_b * (one[C_RL] - across * from_l)
    cross_r = over_b * (two[C_LR] - across * from_r)
    merged = {
        ZA_LL: one[ZA_LL] - one[ZA_LR] * from_l,
        ZA_LR: one[ZA_LR] * from_r,
        ZA_RR: two[ZA_RR] - two[ZA_LR] * from_r,
        ZB_LL: one[ZB_LL] - one[ZB_LR] * from_l_b,
        ZB_LR: one[ZB_LR] * from_r_b,
        ZB_RR: two[ZB_RR] - two[ZB_LR] * from_r_b,
        C_LL: one[C_LL] - one[ZB_LR] * cross_l - one[C_LR] * from_l,
        C_LR: one[ZB_LR] * cross_r + one[C_LR] * from_r,
        C_RL: two[ZB_LR] * cross_l + two[C_RL] * from_l,
        C_RR: two[C_RR] - two[ZB_LR] * cross_r - two[C_RL] * from_r,
        FA_L: one[FA_L] - one[ZA_LR] * free_a,
        FA_R: two[FA_R] + two[ZA_LR] * free_a,
        FB_L: one[FB_L] - one[ZB_LR] * free_b - one[C_LR] * free_a,
        FB_R: two[FB_R] + two[ZB_LR] * free_b + two[C_RL] * free_a,
    }
    return merged, (free_a, from_l, from_r, free_b, from_l_b, from_r_b, cross_l, cross_r)


def between(kept, ends):
    free_a, from_l, from_r, free_b, from_l_b, from_r_b, cross_l, cross_r = kept
    l_a, r_a, l_b, r_b = ends
    middle_a = free_a + from_l * l_a - from_r * r_a
    middle_b = free_b + from_l_b * l_b - from_r_b * r_b + cross_l * l_a - cross_r * r_a
    return middle_a, middle_b


def merge_kernel(stride, last, own_ref, other_ref, out_ref, kept_ref, *face_ref):
    second = side_of("flow", stride)
    own = [own_ref[q] for q in range(QUANTITIES)]
    other = [other_ref[q] for q in range(QUANTITIES)]
    one = [jnp.where(second, b, a) for a, b in zip(own, other)]
    two = [jnp.where(second, a, b) for a, b in zip(own, other)]
    merged, kept = merge(one, two)
    for q, value in merged.items():
        out_ref[q] = value
    for k, value in enumerate(kept):
        kept_ref[k] = value
    if last:
        after = side_of("flow", 2 * stride)
        for k, (l, r) in enumerate(zip(FACE_L, FACE_R)):
            face_ref[0][k] = jnp.where(after, merged[l], merged[r])


def close_kernel(strides, ready_ref, own_ref, other_ref, *refs):
    kept_refs, mine_ref, send_ref = refs[:-2], refs[-2], refs[-1]
    stride = strides[-1]
    second = side_of("flow", stride)
    own = [jnp.where(second, own_ref[l], own_ref[r]) for l, r in zip(FACE_L, FACE_R)]
    z_a, z_b, couple, f_a, f_b = [own[k] + other_ref[k] for k in range(3)] + [
        jnp.where(second, other_ref[k] - own[k], own[k] - other_ref[k]) for k in (3, 4)
    ]
    current_a = recip(z_a) * f_a
    current_b = recip(z_b) * (f_b - couple * current_a)
    nothing = jnp.zeros_like(current_a)

    def side_ends(after, middle_a, middle_b, ends):
        l_a, r_a, l_b, r_b = ends
        return (
            jnp.where(after, middle_a, l_a),
            jnp.where(after, r_a, -middle_a),
            jnp.where(after, middle_b, l_b),
            jnp.where(after, r_b, -middle_b),
        )

    ends = side_ends(second, current_a, current_b, (nothing,) * 4)
    for stride, kept_ref in reversed(list(zip(strides[:-1], kept_refs))):
        middle_a, middle_b = between([kept_ref[k] for k in range(KEPT)], ends)
        after = side_of("flow", stride)
        if stride == 1:
            other_ends = side_ends(jnp.logical_not(after), middle_a, middle_b, ends)
            for q, value in enumerate(other_ends):
                send_ref[q] = value
        ends = side_ends(after, middle_a, middle_b, ends)
    for q, value in enumerate(ends):
        mine_ref[q] = value


def piece_ends(kept_ref, current_ref):
    ends = [tuple(current_ref[q] for q in range(CURRENTS))]
    slot = PIECES - 1
    while len(ends) < PIECES:
        slot -= len(ends)
        parts = []
        for k, (l_a, r_a, l_b, r_b) in enumerate(ends):
            values = [kept_ref[slot + k, v] for v in range(KEPT)]
            middle_a, middle_b = between(values, (l_a, r_a, l_b, r_b))
            parts += [(l_a, -middle_a, l_b, -middle_b), (middle_a, r_a, middle_b, r_b)]
        ends = parts
    return ends


def prepare_kernel(
    kept,
    tab_ref,
    stratum_ref,
    conc_ref,
    pass_a_ref,
    drop_a_ref,
    pass_b_ref,
    drop_b_ref,
    over_ref,
    source_a_ref,
    source_b_ref,
    flow_ref,
    left_a,
    right_a,
    free_a_ref,
    free_b_ref,
    cross_l_ref,
    cross_r_ref,
    own_2_ref,
    own_3_ref,
    gamma_ref,
    share_ref,
    decay_ref,
):
    n, planes_y, planes_z = stratum_ref.shape
    half = planes_y // 2
    which = half_of(kept)
    rows = pl.ds(pl.multiple_of(which * half, half), half)
    number = Numbers(tab_ref)
    line = lax.broadcasted_iota(jnp.int32, (half, planes_z), 0)
    outer = line == (half - 1) * which
    zero = jnp.zeros((half, planes_z), jnp.float32)
    m = n // PIECES

    def with_border(source, component, i):
        flow = jnp.broadcast_to(flow_ref[component, i : i + 1, :], source.shape)
        return source + jnp.where(outer, flow, 0.0)

    def solve(s, forcing, pass_ref, drop_ref, over, out_ref):
        value, gathered = zero, []
        for j in range(m):
            value = forcing(s * m + j) + (pass_ref[s * m + j] * value if j else 0.0)
            gathered.append(value)
        x = gathered[-1] * over
        for j in reversed(range(m)):
            i = s * m + j
            if j < m - 1:
                x = pass_ref[i + 1] * x + drop_ref[i + 1] * gathered[j]
            out_ref[i] = x

    for i in range(n):
        index = stratum_ref[i, rows, :]
        own_2_ref[i] = number("beta", index) * conc_ref[2, i, rows, :]
        own_3_ref[i] = number("free_b", index) * conc_ref[3, i, rows, :]
        gamma_ref[i] = number("gamma", index)
        share_ref[i] = number("share_b", index)
        decay_ref[i] = number("decay_b", index)
    for s in range(PIECES):
        kappa = {}
        for i in range(s * m, s * m + m):
            kappa[i] = number("kappa", stratum_ref[i, rows, :])
        solve(
            s,
            lambda i: with_border(source_a_ref[i], 0, i),
            pass_a_ref,
            drop_a_ref,
            over_ref[0, s],
            free_a_ref,
        )
        forcings = (
            (lambda i: with_border(source_b_ref[i], 1, i) + kappa[i] * free_a_ref[i], free_b_ref),
            (lambda i: kappa[i] * left_a[i], cross_l_ref),
            (lambda i: kappa[i] * right_a[i], cross_r_ref),
        )
        for forcing, out_ref in forcings:
            solve(s, forcing, pass_b_ref, drop_b_ref, over_ref[1, s], out_ref)


def add_kernel(
    kept,
    kept_ref,
    current_ref,
    free_a_ref,
    free_b_ref,
    cross_l_ref,
    cross_r_ref,
    own_2_ref,
    own_3_ref,
    gamma_ref,
    share_ref,
    decay_ref,
    left_a,
    right_a,
    left_b,
    right_b,
    before_hbm,
    out_hbm,
    made,
    sems,
):
    n, half, planes_z = free_a_ref.shape
    rows = pl.ds(pl.multiple_of(half_of(kept) * half, half), half)
    ends = piece_ends(kept_ref, current_ref)
    m = n // PIECES
    copies = []
    for i in range(n):
        l_a, r_a, l_b, r_b = ends[i // m]
        x0 = free_a_ref[i] + left_a[i] * l_a + right_a[i] * r_a
        x1 = (free_b_ref[i] + cross_l_ref[i] * l_a + cross_r_ref[i] * r_a) + (
            left_b[i] * l_b + right_b[i] * r_b
        )
        x2 = own_2_ref[i] + gamma_ref[i] * x0
        made[0, i], made[1, i], made[2, i] = x0, x1, x2
        made[3, i] = own_3_ref[i] + share_ref[i] * x1 + decay_ref[i] * x2
        copies.append(
            pltpu.make_async_copy(made.at[:, i], out_hbm.at[:, i, rows, :], sems.at[i])
        )
        copies[-1].start()
    for copy in copies:
        copy.wait()


def final_kernel(
    kept,
    tab_ref,
    stratum_ref,
    conc_ref,
    pass_a_ref,
    drop_a_ref,
    pass_b_ref,
    drop_b_ref,
    over_ref,
    source_a_ref,
    source_b_ref,
    kept_ref,
    flow_ref,
    current_ref,
    *refs,
):
    out_hbm, gather_a, gather_b, made, sems = refs[-5:]
    n, planes_y, planes_z = stratum_ref.shape
    half = planes_y // 2
    which = half_of(kept)
    rows = pl.ds(pl.multiple_of(which * half, half), half)
    number = Numbers(tab_ref)
    line = lax.broadcasted_iota(jnp.int32, (half, planes_z), 0)
    outer = line == (half - 1) * which

    def with_border(source, component, i):
        flow = jnp.broadcast_to(flow_ref[component, pl.ds(i, 1), :], source.shape)
        return source + jnp.where(outer, flow, 0.0)

    ends = piece_ends(kept_ref, current_ref)
    pieces = range(PIECES)
    m = n // PIECES
    values = [ends[s][0] for s in pieces]
    for j in range(m):
        for s in pieces:
            i = s * m + j
            values[s] = with_border(source_a_ref[i], 0, i) + values[s]
            if j < m - 1:
                gather_a[i] = values[s]
                values[s] = pass_a_ref[i + 1] * values[s]
    x = [(values[s] + ends[s][1]) * over_ref[0, s] for s in pieces]
    for j in reversed(range(m)):
        for s in pieces:
            i = s * m + j
            if j < m - 1:
                x[s] = pass_a_ref[i + 1] * x[s] + drop_a_ref[i + 1] * gather_a[i]
            made[0, i] = x[s]
    values = [ends[s][2] for s in pieces]
    for j in range(m):
        for s in pieces:
            i = s * m + j
            kappa = number("kappa", stratum_ref[i, rows, :])
            values[s] = with_border(source_b_ref[i], 1, i) + kappa * made[0, i] + values[s]
            if j < m - 1:
                gather_b[i] = values[s]
                values[s] = pass_b_ref[i + 1] * values[s]
    x = [(values[s] + ends[s][3]) * over_ref[1, s] for s in pieces]
    copies = []
    for j in reversed(range(m)):
        for s in pieces:
            i = s * m + j
            if j < m - 1:
                x[s] = pass_b_ref[i + 1] * x[s] + drop_b_ref[i + 1] * gather_b[i]
            made[1, i] = x[s]
            index = stratum_ref[i, rows, :]
            x2 = (
                number("beta", index) * conc_ref[2, i, rows, :]
                + number("gamma", index) * made[0, i]
            )
            made[2, i] = x2
            made[3, i] = (
                number("free_b", index) * conc_ref[3, i, rows, :]
                + number("share_b", index) * x[s]
                + number("decay_b", index) * x2
            )
            copies.append(
                pltpu.make_async_copy(made.at[:, i], out_hbm.at[:, i, rows, :], sems.at[i])
            )
            copies[-1].start()
    for copy in copies:
        copy.wait()


def call(kernel, outs, scratch=()):
    return pl.pallas_call(
        kernel,
        out_shape=[jax.ShapeDtypeStruct(shape, jnp.float32) for shape in outs],
        scratch_shapes=[pltpu.VMEM(shape, jnp.float32) for shape in scratch],
        compiler_params=pltpu.CompilerParams(vmem_limit_bytes=VMEM_LIMIT),
    )


def per_device(
    concentration,
    stratum,
    porosity,
    dispersion_table,
    transverse_table,
    exchange_table,
    decay_table,
):
    n, planes_y, planes_z = stratum.shape
    peers = lax.axis_size("flow")
    half = planes_y // 2
    strides = [1 << k for k in range(peers.bit_length() - 1)]
    cells = (n, planes_y, planes_z)

    halo = (3, n, planes_z)
    strata = porosity.shape[0]
    hbm = pl.BlockSpec(memory_space=pltpu.HBM)
    early, late, table, concentration, stratum = pl.pallas_call(
        pack_kernel,
        out_shape=[
            jax.ShapeDtypeStruct(halo, jnp.float32),
            jax.ShapeDtypeStruct(halo, jnp.float32),
            jax.ShapeDtypeStruct((2 * SUB, LANE), jnp.float32),
            jax.ShapeDtypeStruct(concentration.shape, jnp.float32),
            jax.ShapeDtypeStruct(cells, jnp.int32),
        ],
        in_specs=[hbm] * 7,
        scratch_shapes=[
            pltpu.VMEM((1, strata), jnp.float32),
            pltpu.VMEM((2, strata), jnp.float32),
            pltpu.VMEM((1, strata), jnp.float32),
            pltpu.VMEM((1, strata), jnp.float32),
            pltpu.VMEM((1, strata), jnp.float32),
            pltpu.VMEM((SUB, LANE), jnp.float32),
            pltpu.SemaphoreType.DMA((8,)),
        ],
        compiler_params=pltpu.CompilerParams(vmem_limit_bytes=VMEM_LIMIT),
    )(
        *[
            pltpu.with_memory_space_constraint(value, pltpu.HBM)
            for value in (
                concentration,
                stratum,
                porosity[None],
                dispersion_table.T,
                transverse_table[None],
                exchange_table[None],
                decay_table[None],
            )
        ]
    )
    groups = lax.axis_size("trans")
    def swap(value, start):
        low = range(start, groups - 1, 2)
        pairs = [(i, i + 1) for i in low] + [(i + 1, i) for i in low]
        if start:
            pairs += [(0, groups - 1), (groups - 1, 0)]
        return lax.ppermute(value, "trans", pairs)

    beyond_late = swap(late, 1)
    beyond_early = swap(early, 0)

    def exchange(value, stride):
        return lax.ppermute(value, "flow", [(i, i ^ stride) for i in range(peers)])

    half_cells = (n, half, planes_z)
    block_shape = (QUANTITIES, half, planes_z)

    def local(kept):
        pay, edge, *rest = call(
            functools.partial(local_kernel, kept),
            [
                (PIECES,) + block_shape,
                (6, n, planes_z),
                *[half_cells] * 4,
                (2, PIECES, half, planes_z),
                *[half_cells] * 6,
            ],
            [half_cells] * 5,
        )(table, stratum, concentration)
        pay, parts, flow = call(
            functools.partial(border_kernel, kept),
            [block_shape, (PIECES - 1, KEPT, half, planes_z), (2, n, planes_z)],
        )(table, early, late, beyond_late, beyond_early, edge, pay)
        return pay, rest[:7], rest[7:], parts, flow

    send, sent_rest, sent_responses, sent_parts, sent_flow = local(False)
    block, kept_rest, _, kept_parts, kept_flow = local(True)
    kept = []
    for stride in strides[:-1]:
        other = exchange(send, stride)
        last = stride == strides[-2]
        block, keep, *face = call(
            functools.partial(merge_kernel, stride, last),
            [block_shape, (KEPT, half, planes_z)] + [(5, half, planes_z)] * last,
        )(block, other)
        kept.append(keep)
        send = face[0] if last else block
    prepared = call(functools.partial(prepare_kernel, False), [half_cells] * 9)(
        table, stratum, concentration, *sent_rest, sent_flow, *sent_responses[:2]
    )
    ends_shape = jax.ShapeDtypeStruct((CURRENTS, half, planes_z), jnp.float32)
    vmem = pl.BlockSpec(memory_space=pltpu.VMEM)
    limit = pltpu.CompilerParams(vmem_limit_bytes=VMEM_LIMIT)
    mine, send = pl.pallas_call(
        functools.partial(close_kernel, strides),
        out_shape=[ends_shape, ends_shape],
        in_specs=[pl.BlockSpec(memory_space=pl.ANY)] + [vmem] * (2 + len(kept)),
        compiler_params=limit,
    )(prepared[0], block, exchange(send, strides[-1]), *kept)
    currents = exchange(send, 1)
    whole = jax.ShapeDtypeStruct((4,) + cells, jnp.float32)
    results = [pltpu.VMEM((4,) + half_cells, jnp.float32), pltpu.SemaphoreType.DMA((n,))]
    out = pl.pallas_call(
        functools.partial(final_kernel, True),
        out_shape=whole,
        in_specs=[vmem] * 13,
        out_specs=hbm,
        scratch_shapes=[pltpu.VMEM(half_cells, jnp.float32)] * 2 + results,
        compiler_params=limit,
    )(table, stratum, concentration, *kept_rest, kept_parts, kept_flow, mine)
    return pl.pallas_call(
        functools.partial(add_kernel, False),
        out_shape=whole,
        in_specs=[vmem] * 15 + [hbm],
        out_specs=hbm,
        scratch_shapes=results,
        input_output_aliases={15: 0},
        compiler_params=limit,
    )(sent_parts, currents, *prepared, *sent_responses, out)


def solution(mesh):
    in_specs = (P(None, "flow", "trans", None), P("flow", "trans", None), P(), P(), P(), P(), P())
    out_specs = P(None, "flow", "trans", None)
    return jax.shard_map(
        per_device, mesh=mesh, in_specs=in_specs, out_specs=out_specs, check_vma=False
    )
```
